256 devices in a mesh: slab: 8 (over x, core), space: 32 (over y, z).
Axes of the slice: x: 4, y: 4, z: 8, core: 2. Of those that a mesh axis runs over, the one named last changes fastest.
Arguments:
- positions: float32 [8, 1536, 3, 128], P('slab', 'space'), may hold values from -1 to 1
- masses: float32 [8, 1536, 128], P('slab', 'space'), may hold values from 0.0005 to 0.005
- counts: int32 [8, 32, 48], P('slab', 'space'), may hold values from 1 to 128, 4608 in all within a row
- dest_ids: int32 [8, 1536], P('slab', 'space'), may hold values from 0 to 31, as said below
- near_list: int32 [8, 1536, 4], P('slab', 'space'), may hold values from 0 to 143
- cell_list: int32 [8, 1536, 32], P('slab', 'space'), may hold values from 0 to 16383
- cell_centers: float32 [3, 16384], P(None, 'slab'), may hold values from -6 to 6
- cell_mass: float32 [16384], P('slab'), may hold values from 0.5 to 5
Outputs:
- accel: float32 [8, 1536, 3, 128], P('slab', 'space')
The draws below stay inside these ranges and needn't reach their ends.
Inputs may be any that keep to these rules, and one draw needn't show every extreme that they name: `dest_ids`: of one device's 48 buckets at most 6 name any one destination, and in every slab one destination, drawn from the seed, is named by exactly 6 buckets of every device of that slab.
All inputs are finite; a program needn't handle non-finite values.
Results may differ from the reference program's by a relative error of at most 0.0003.
Values sent between devices are 32-bit elements; how exact they have to be, the bound alone decides.
No kernel may reach another device: no remote copies, remote signals or barrier semaphores. Data moves between devices by JAX's collectives and lax.ppermute only.
A program may use at most 64 MiB of HBM per device.

```python
import math
import jax
import jax.numpy as jnp
import numpy as np
from jax import lax

P_SIZE = 128
NB = 48
CAP = 6
K = 4
LC = 32
LEAVES = 1536
CELLS = 16384
N_SLAB = 8
N_SPACE = 32


def draw_dest_ids(key, part):
    key = jax.random.fold_in(key, 11)
    hottest = jax.random.randint(jax.random.fold_in(key, 1), (N_SLAB,), 0, N_SPACE).astype(jnp.int32)
    device_keys = jax.random.split(jax.random.fold_in(key, 2), N_SLAB * N_SPACE)
    hot_each = jnp.repeat(hottest, N_SPACE)

    def one_device(device_key, hot):
        chosen = jax.random.permutation(device_key, (N_SPACE - 1) * CAP)[:NB - CAP].astype(jnp.int32)
        target = chosen // CAP
        target = target + (target >= hot).astype(jnp.int32)
        joined = jnp.concatenate([jnp.full((CAP,), hot, jnp.int32), target])
        return jax.random.permutation(jax.random.fold_in(device_key, 5), joined).astype(jnp.int32)
    result = jax.vmap(one_device)(device_keys, hot_each)
    return result.reshape(N_SLAB, N_SPACE * NB).astype(jnp.int32)


def touch_ends(values, own_key, low, top_value):
    longest = values.shape.index(max(values.shape))
    spots = []
    for shift in (0, 1):
        where = [jax.random.randint(jax.random.fold_in(own_key, axis), (), 0, length) for axis, length in enumerate(values.shape)]
        where[longest] = (where[longest] + shift) % values.shape[longest]
        spots.append(tuple(where))
    return values.at[spots[0]].set(low).at[spots[1]].set(top_value)


def block_scale(rng, dims, cuts, smallest, top_value):
    def one(axis_at, parts):
        heights = jax.random.uniform(jax.random.fold_in(jax.random.fold_in(rng, 6), axis_at), (parts,), jnp.float32, smallest / len(cuts), top_value / len(cuts))
        return jnp.repeat(jnp.exp(heights), dims[axis_at] // parts).reshape((-1,) + (1,) * (len(dims) - axis_at - 1))

    gain = one(*cuts[0])
    for cut in cuts[1:]:
        gain = gain * one(*cut)
    return gain


def split_up(number_of, total, most, lean):
    portions = [(1 << 20) // math.isqrt(rank ** lean) + 1 for rank in range(2, number_of + 1)]
    rest, given = total - most - (number_of - 1), [1] * (number_of - 1)
    while rest > 0:
        candidates = [i for i in range(number_of - 1) if given[i] < most]
        whole, left = sum([portions[i] for i in candidates]), rest
        for i in candidates:
            addition = min(most - given[i], max(1, left * portions[i] // whole), rest)
            given[i] = given[i] + addition
            rest = rest - addition
    return np.array([most] + given)


def ragged_sizes(rng, number_of, total, limit, lean):
    if number_of == 2:
        one = jax.random.randint(rng, (), max(1, total - limit), min(limit, total - 1) + 1)
        return jnp.stack([one, total - one])
    sizes = jnp.asarray(split_up(number_of, total, limit, lean), jnp.int32)
    couples = (number_of - 1) // 2
    donor, receiver = sizes[1:1 + 2 * couples:2], sizes[2:2 + 2 * couples:2]
    room = jnp.minimum(donor - 1, limit - receiver)
    moved = jax.random.randint(jax.random.fold_in(rng, 1), (couples,), 0, 1 << 20) % (room + 1)
    sizes = sizes.at[1:1 + 2 * couples:2].set(donor - moved).at[2:2 + 2 * couples:2].set(receiver + moved)
    return sizes[jax.random.permutation(jax.random.fold_in(rng, 2), number_of)]


def setup_inputs(seed: int = 0) -> dict:
    key_list = jax.random.split(jax.random.key(seed), 9)
    positions = jnp.clip(jax.random.uniform(key_list[0], (N_SLAB, LEAVES, 3, P_SIZE), jnp.float32, -1.0, 1.0) * block_scale(key_list[0], (N_SLAB, LEAVES, 3, P_SIZE), ((0, 8), (1, 32)), -0.4, 0.0), -1.0, 1.0)
    masses = jnp.clip(jnp.exp(math.log(0.005) - 2.30258502 * jax.random.uniform(key_list[1], (N_SLAB, LEAVES, P_SIZE), jnp.float32) ** block_scale(key_list[1], (N_SLAB, LEAVES, P_SIZE), ((0, 8), (1, 32)), -0.2, 0.2)), 0.0005, 0.005)
    counts = jax.vmap(lambda own: ragged_sizes(own, NB, NB * 96, 128, 1))(jax.random.split(key_list[2], N_SLAB * N_SPACE)).reshape((N_SLAB, N_SPACE, NB)).astype(jnp.int32)
    dest_ids = draw_dest_ids(jax.random.fold_in(key_list[8], 71), 0)
    near_list = touch_ends(jax.random.randint(key_list[4], (N_SLAB, LEAVES, K), 0, 3 * NB), jax.random.fold_in(key_list[4], 1), 0, (3 * NB) - 1).astype(jnp.int32)
    cell_list = touch_ends(jax.random.randint(key_list[5], (N_SLAB, LEAVES, LC), 0, CELLS), jax.random.fold_in(key_list[5], 1), 0, CELLS - 1).astype(jnp.int32)
    cell_centers = jnp.clip(jax.random.uniform(key_list[6], (3, CELLS), jnp.float32, -6.0, 6.0) * block_scale(key_list[6], (3, CELLS), ((1, 8),), -0.4, 0.0), -6.0, 6.0)
    cell_mass = jnp.clip(jnp.exp(math.log(5.0) - 2.3025851 * jax.random.uniform(key_list[7], (CELLS,), jnp.float32) ** block_scale(key_list[7], (CELLS,), ((0, 8),), -0.2, 0.2)), 0.5, 5.0)
    return dict(positions=positions, masses=masses, counts=counts, dest_ids=dest_ids, near_list=near_list, cell_list=cell_list, cell_centers=cell_centers, cell_mass=cell_mass)


soft_near = 0.01
block_rows = 16


def center_of(packed):
    alive = (packed[:, 3] > 0.0).astype(jnp.float32)
    total = jnp.sum(alive, axis=-1)
    center = jnp.sum(packed[:, :3] * alive[:, None], axis=-1) / jnp.maximum(total, 1.0)[:, None]
    return center, alive


def pair_block(targets, sources):
    rel = sources[:, :, :3, None, :] - targets[:, None, :3, :, None]
    dist_sq = jnp.sum(rel * rel, axis=2) + soft_near
    weight = sources[:, :, 3][:, :, None, :] * dist_sq ** -1.5
    return jnp.sum(rel * weight[:, :, None], axis=(1, 4))


def moment_terms(center, cell_pos, cell_weight):
    rel = center[:, :, None] - cell_pos
    dist_sq = jnp.sum(rel * rel, axis=0) + 1.0
    inverse_cube = cell_weight * dist_sq ** -1.5
    inverse_fifth = 3.0 * cell_weight * dist_sq ** -2.5
    field = -jnp.sum(inverse_cube[None] * rel, axis=2)
    terms = []
    for first, second in ((0, 0), (1, 1), (2, 2), (0, 1), (0, 2), (1, 2)):
        value = inverse_fifth * rel[first] * rel[second]
        if first == second:
            value = value - inverse_cube
        terms.append(jnp.sum(value, axis=1))
    return field, jnp.stack(terms)


def apply_local(field, tidal, offset):
    acc_x = field[0][:, None] + tidal[0][:, None] * offset[:, 0] + tidal[3][:, None] * offset[:, 1] + tidal[4][:, None] * offset[:, 2]
    acc_y = field[1][:, None] + tidal[3][:, None] * offset[:, 0] + tidal[1][:, None] * offset[:, 1] + tidal[5][:, None] * offset[:, 2]
    acc_z = field[2][:, None] + tidal[4][:, None] * offset[:, 0] + tidal[5][:, None] * offset[:, 1] + tidal[2][:, None] * offset[:, 2]
    return jnp.stack([acc_x, acc_y, acc_z], axis=1)


def reference(positions, masses, counts, dest_ids, near_list, cell_list, cell_centers, cell_mass):
    alive = (jnp.arange(P_SIZE, dtype=jnp.int32)[None, None, :] < counts.reshape(N_SLAB, LEAVES)[:, :, None]).astype(jnp.float32)
    packed = jnp.concatenate([positions, (masses * alive)[:, :, None, :]], axis=2)
    home_dev = (dest_ids[:, :, None] + near_list // NB - 1) % N_SPACE
    slab_base = (jnp.arange(N_SLAB, dtype=jnp.int32) * LEAVES)[:, None, None]
    global_ids = (slab_base + home_dev * NB + near_list % NB).astype(jnp.int32)
    flat = packed.reshape(N_SLAB * LEAVES, 4, P_SIZE)
    blocks = N_SLAB * LEAVES // block_rows

    def one_block(inputs):
        targets, leaf_ids, cell_ids = inputs
        sources = flat[leaf_ids]
        near = pair_block(targets, sources)
        center, live_block = center_of(targets)
        cell_pos = cell_centers[:, cell_ids]
        field, tidal = moment_terms(center.T, cell_pos, cell_mass[cell_ids])
        offset = targets[:, :3] - center[:, :, None]
        return (near + apply_local(field, tidal, offset)) * live_block[:, None, :]

    result = lax.map(one_block, (flat.reshape(blocks, block_rows, 4, P_SIZE), global_ids.reshape(blocks, block_rows, K), cell_list.reshape(blocks, block_rows, LC)))
    return result.reshape(N_SLAB, LEAVES, 3, P_SIZE)
```

```python
import jax
import jax.numpy as jnp
from jax import lax
from jax.experimental import pallas as pl
from jax.experimental.pallas import tpu as pltpu
from jax.sharding import PartitionSpec as P

NB = 48
PL = 128
K = 4
LC = 32
NY = 4
NZ = 8
NX = 4
SOFT = 0.01
F32 = jnp.float32
I32 = jnp.int32
BF16 = jnp.bfloat16
VMEM = pltpu.VMEM
SMEM = pltpu.SMEM


def vspec():
    return pl.BlockSpec(memory_space=VMEM)


def sspec():
    return pl.BlockSpec(memory_space=SMEM)


def column_of(row, n):
    square = jnp.broadcast_to(row, (n, n))
    diag = lax.broadcasted_iota(I32, (n, n), 0) == lax.broadcasted_iota(I32, (n, n), 1)
    return jnp.sum(jnp.where(diag, square, 0), axis=1, keepdims=True)


def pack_kernel(pos_ref, mass_ref, cnt_ref, dest_ref, near_ref, src_ref, tgt_ref):
    cnt = column_of(cnt_ref[...], NB)
    dest = column_of(dest_ref[...], NB)
    lane = lax.broadcasted_iota(I32, (NB, PL), 1)
    weight = jnp.where(lane < cnt, mass_ref[...], 0.0)
    near = near_ref[...]
    off = (near >= NB).astype(I32) + (near >= 2 * NB).astype(I32)
    dev = (dest + off - 1) & (NY * NZ - 1)
    code = (dev & (NZ - 1)) * NB + (near - off * NB)
    row = dev >> 3
    info = jnp.zeros((NB, PL), I32)
    for k in range(K):
        info = jnp.where(lane == k, code[:, k : k + 1], info)
        info = jnp.where(lane == 8 + k, row[:, k : k + 1], info)
    info = jnp.where(lane == 4, cnt, info)
    for y in range(NY):
        n = jnp.sum((row == y).astype(I32), axis=1, keepdims=True)
        info = jnp.where(lane == 12 + y, n, info)
    info = info.astype(F32)
    for c in range(3):
        value = pos_ref[:, c, :]
        tgt_ref[:, c, :] = value
        for z in range(NZ):
            src_ref[z, :, c, :] = value
    tgt_ref[:, 3, :] = info
    for z in range(NZ):
        src_ref[z, :, 3, :] = weight


def far_kernel(xc_ref, pos_ref, cnt_ref, list_ref, tab_ref, out_ref, pad):
    xs, cs = xc_ref[0], xc_ref[1]
    lane = lax.broadcasted_iota(I32, (NB, PL), 1)
    cnt = column_of(cnt_ref[...], NB)
    live = lane < cnt
    total = jnp.maximum(cnt, 1).astype(F32)
    pos = [pos_ref[:, c, :] for c in range(3)]
    centre = [jnp.sum(jnp.where(live, v, 0.0), axis=1, keepdims=True) / total for v in pos]
    block = jnp.zeros((NB, PL), F32)
    for c in range(3):
        block = jnp.where(lane == LC + c, centre[c], block)
    pad[...] = jnp.zeros((PL, PL), F32)
    pad[0:NB, :] = block
    pad[0:NB, 0:LC] = list_ref[...].astype(F32)
    turned = pad[...].T
    twice = turned + pltpu.roll(turned, 64, 1)
    half = lax.broadcasted_iota(I32, (1, PL), 1) < 64
    ids = [jnp.where(half, twice[2 * j : 2 * j + 1], twice[2 * j + 1 : 2 * j + 2]) for j in range(LC // 2)]
    ids = jnp.concatenate(ids, axis=0).astype(I32)
    ctr = [twice[LC + c : LC + c + 1] for c in range(3)]
    slab = ids >> 11
    dx = ((slab >> 1) - xs) & (NX - 1)
    order = jnp.where(dx == 3, 1, jnp.where(dx == 0, 0, dx + 1))
    rows = (order * 2 + ((slab & 1) ^ cs)) * 16 + ((ids >> 7) & 15)
    lanes = ids & (PL - 1)
    tables = []
    for c in range(4):
        whole = jnp.concatenate([tab_ref[o, i, c] for o in range(NX) for i in range(2)], axis=0)
        whole = whole.T
        high = whole.astype(BF16)
        low = (whole - high.astype(F32)).astype(BF16)
        tables.append(jnp.concatenate([high, low], axis=1))
    tables = jnp.concatenate(tables, axis=0)
    sub = lax.broadcasted_iota(I32, (PL, 2 * PL), 0)
    got = [[] for _ in range(4)]
    for j in range(0, LC // 2, 2):
        r2 = jnp.concatenate([rows[j : j + 1], rows[j + 1 : j + 2]], axis=1)
        l2 = jnp.concatenate([lanes[j : j + 1], lanes[j + 1 : j + 2]], axis=1)
        hot = jnp.where(sub == r2, 1.0, 0.0).astype(BF16)
        hot = jnp.concatenate([hot, hot], axis=0)
        found = jnp.dot(tables, hot, preferred_element_type=F32)
        pick = sub == l2
        for c in range(4):
            value = jnp.sum(jnp.where(pick, found[c * PL : (c + 1) * PL], 0.0), axis=0, keepdims=True)
            got[c] += [value[:, :PL], value[:, PL:]]
    cells = [jnp.concatenate(v, axis=0) for v in got]
    rel = [ctr[c] - cells[c] for c in range(3)]
    dist = rel[0] * rel[0] + rel[1] * rel[1] + rel[2] * rel[2] + 1.0
    inv = lax.rsqrt(dist)
    cube = cells[3] * (inv * inv * inv)
    fifth = 3.0 * cube * (inv * inv)
    terms = [-(cube * rel[c]) for c in range(3)]
    for a, b in ((0, 0), (1, 1), (2, 2), (0, 1), (0, 2), (1, 2)):
        value = fifth * rel[a] * rel[b]
        if a == b:
            value = value - cube
        terms.append(value)
    terms = [jnp.sum(v, axis=0, keepdims=True) for v in terms]
    pad[...] = jnp.zeros((PL, PL), F32)
    for i, v in enumerate(terms):
        pad[i : i + 1, :] = v + pltpu.roll(v, 64, 1)
    back = pad[...].T
    field = [back[0:NB, i : i + 1] for i in range(3)]
    tide = [back[0:NB, 3 + i : 4 + i] for i in range(6)]
    offset = [pos[c] - centre[c] for c in range(3)]
    for c, (i, j, k) in enumerate(((0, 3, 4), (3, 1, 5), (4, 5, 2))):
        out_ref[:, c, :] = field[c] + tide[i] * offset[0] + tide[j] * offset[1] + tide[k] * offset[2]


def near_kernel(info_ref, y_ref, t0, t1, t2, t3, src_ref, o0, o1, o2, o3, col, res):
    me = y_ref[0]
    lane8 = lax.broadcasted_iota(I32, (8, PL), 1)

    def groups_body(groups, picks, flags):
        srcs = [src_ref[p] for p in picks]
        rows = []
        for s, f in zip(srcs, flags):
            rows.append(
                (
                    jnp.broadcast_to(s[0:1], (8, PL)),
                    jnp.broadcast_to(s[1:2], (8, PL)),
                    jnp.broadcast_to(s[2:3], (8, PL)),
                    jnp.broadcast_to(s[3:4] * f, (8, PL)),
                )
            )
        for g in range(groups):
            part = col[8 * g : 8 * g + 8, :]
            tx, ty, tz = [jnp.broadcast_to(part[:, c : c + 1], (8, PL)) for c in range(3)]
            ax = ay = az = None
            for sx, sy, sz, w in rows:
                dx, dy, dz = sx - tx, sy - ty, sz - tz
                inv = lax.rsqrt(dx * dx + dy * dy + (dz * dz + SOFT))
                f = w * inv * (inv * inv)
                if ax is None:
                    ax, ay, az = f * dx, f * dy, f * dz
                else:
                    ax, ay, az = ax + f * dx, ay + f * dy, az + f * dz
            sums = [jnp.sum(v, axis=1, keepdims=True) for v in (ax, ay, az)]
            res[8 * g : 8 * g + 8, :] = jnp.where(lane8 == 0, sums[0], jnp.where(lane8 == 1, sums[1], sums[2]))

    for which, (t, o) in enumerate(((t0, o0), (t1, o1), (t2, o2), (t3, o3))):
        o[...] = jnp.zeros((NB, 3, PL), F32)

        def bucket(b, _, t=t, o=o, which=which):
            r = which * NB + b

            @pl.when(info_ref[r, 12 + me] > 0)
            def _():
                cnt = info_ref[r, 4]
                picks, flags = [], []
                for k in range(K):
                    picks.append(info_ref[r, k])
                    flags.append((info_ref[r, 8 + k] == me).astype(F32))
                tile = t[b]
                col[:, 0:8] = jnp.concatenate([tile, tile], axis=0).T
                for n in (4, 8, 12, 16):
                    @pl.when((cnt > 8 * (n - 4)) & (cnt <= 8 * n))
                    def _(n=n):
                        groups_body(n, picks, flags)
                o[b] = jnp.where(
                    lax.broadcasted_iota(I32, (3, PL), 1) < cnt, res[...].T[0:3], 0.0
                )

        lax.fori_loop(0, NB, bucket, None)


def ring(n, k):
    return [(i, (i + k) % n) for i in range(n)]


def along_y(k):
    return [(NZ * y + z, NZ * ((y + k) % NY) + z) for y in range(NY) for z in range(NZ)]


def along_x(k):
    return [(2 * x + c, 2 * ((x + k) % NX) + c) for x in range(NX) for c in range(2)]


def per_device(positions, masses, counts, dest_ids, near_list, cell_list, cell_centers, cell_mass):
    pos, cnt = positions[0], counts[0]
    src, tgt = pl.pallas_call(
        pack_kernel,
        out_shape=(
            jax.ShapeDtypeStruct((NZ, NB, 4, PL), F32),
            jax.ShapeDtypeStruct((NB, 4, PL), F32),
        ),
        in_specs=[vspec()] * 5,
        out_specs=[vspec()] * 2,
        name="pack",
    )(pos, masses[0], cnt, dest_ids, near_list[0])
    rows = [[NZ * y + z for z in range(NZ)] for y in range(NY)]
    window = lax.all_to_all(src, "space", 0, 0, axis_index_groups=rows, tiled=True)
    tgts = [tgt] + [lax.ppermute(tgt, "space", along_y(k)) for k in (1, -1, 2)]
    cells = jnp.concatenate([cell_centers, cell_mass[None]], axis=0).reshape(4, 16, PL)
    pair = jnp.stack([cells, lax.ppermute(cells, "slab", [(i, i ^ 1) for i in range(2 * NX)])])
    tab = jnp.stack([pair] + [lax.ppermute(pair, "slab", along_x(k)) for k in (1, -1, 2)])
    slab = lax.axis_index("slab")
    place = jnp.stack([slab >> 1, slab & 1]).astype(I32)
    far = pl.pallas_call(
        far_kernel,
        out_shape=jax.ShapeDtypeStruct((NB, 3, PL), F32),
        in_specs=[sspec()] + [vspec()] * 4,
        out_specs=vspec(),
        scratch_shapes=[pltpu.VMEM((PL, PL), F32)],
        name="far",
    )(place, pos, cnt, cell_list[0], tab)
    info = jnp.concatenate([t[:, 3, :16] for t in tgts], axis=0).astype(I32)
    me = (lax.axis_index("space") // NZ).astype(I32).reshape(1)
    parts = pl.pallas_call(
        near_kernel,
        out_shape=[jax.ShapeDtypeStruct((NB, 3, PL), F32)] * 4,
        in_specs=[sspec(), sspec()] + [vspec()] * 5,
        out_specs=[vspec()] * 4,
        scratch_shapes=[pltpu.VMEM((PL, PL), F32), pltpu.VMEM((PL, PL), F32)],
        name="near",
    )(info, me, *tgts, window.reshape(NZ * NB, 4, PL))
    back = [parts[0]] + [lax.ppermute(parts[1 + i], "space", along_y(-k)) for i, k in enumerate((1, -1, 2))]
    live = lax.broadcasted_iota(I32, (NB, 1, PL), 2) < cnt[0][:, None, None]
    out = jnp.where(live, far + ((back[0] + back[1]) + (back[2] + back[3])), 0.0)
    return out[None]


def solution(mesh):
    in_specs = (
        P("slab", "space", None, None),
        P("slab", "space", None),
        P("slab", "space", None),
        P("slab", "space"),
        P("slab", "space", None),
        P("slab", "space", None),
        P(None, "slab"),
        P("slab"),
    )
    return jax.shard_map(
        per_device,
        mesh=mesh,
        in_specs=in_specs,
        out_specs=P("slab", "space", None, None),
        check_vma=False,
    )
```

```python
import jax
import jax.numpy as jnp
from jax import lax
from jax.experimental import pallas as pl
from jax.experimental.pallas import tpu as pltpu
from jax.sharding import PartitionSpec as P

NB = 48
PL = 128
K = 4
LC = 32
NY = 4
NZ = 8
NX = 4
SOFT = 0.01
UNROLL = 4
LIST = 256
F32 = jnp.float32
I32 = jnp.int32
BF16 = jnp.bfloat16
VMEM = pltpu.VMEM
SMEM = pltpu.SMEM


def vspec():
    return pl.BlockSpec(memory_space=VMEM)


def sspec():
    return pl.BlockSpec(memory_space=SMEM)


def column_of(row, n):
    square = jnp.broadcast_to(row, (n, n))
    diag = lax.broadcasted_iota(I32, (n, n), 0) == lax.broadcasted_iota(I32, (n, n), 1)
    return jnp.sum(jnp.where(diag, square, 0), axis=1, keepdims=True)


def pack_kernel(pos_ref, mass_ref, cnt_ref, dest_ref, near_ref, src_ref, tgt_ref):
    cnt = column_of(cnt_ref[...], NB)
    dest = column_of(dest_ref[...], NB)
    lane = lax.broadcasted_iota(I32, (NB, PL), 1)
    weight = jnp.where(lane < cnt, mass_ref[...], 0.0)
    near = near_ref[...]
    off = (near >= NB).astype(I32) + (near >= 2 * NB).astype(I32)
    dev = (dest + off - 1) & (NY * NZ - 1)
    code = (dev & (NZ - 1)) * NB + (near - off * NB)
    row = dev >> 3
    info = jnp.zeros((NB, PL), I32)
    for k in range(K):
        info = jnp.where(lane == k, code[:, k : k + 1], info)
        info = jnp.where(lane == 8 + k, row[:, k : k + 1], info)
    info = jnp.where(lane == 4, cnt, info)
    for y in range(NY):
        n = jnp.sum((row == y).astype(I32), axis=1, keepdims=True)
        info = jnp.where(lane == 12 + y, n, info)
    info = info.astype(F32)
    for c in range(3):
        value = pos_ref[:, c, :]
        tgt_ref[:, c, :] = value
        for z in range(NZ):
            src_ref[z, :, c, :] = value
    tgt_ref[:, 3, :] = info
    for z in range(NZ):
        src_ref[z, :, 3, :] = weight


def far_kernel(xc_ref, pos_ref, cnt_ref, list_ref, tab_ref, out_ref, pad):
    xs, cs = xc_ref[0], xc_ref[1]
    lane = lax.broadcasted_iota(I32, (NB, PL), 1)
    cnt = column_of(cnt_ref[...], NB)
    live = lane < cnt
    total = jnp.maximum(cnt, 1).astype(F32)
    pos = [pos_ref[:, c, :] for c in range(3)]
    centre = [jnp.sum(jnp.where(live, v, 0.0), axis=1, keepdims=True) / total for v in pos]
    block = jnp.zeros((NB, PL), F32)
    for c in range(3):
        block = jnp.where(lane == LC + c, centre[c], block)
    pad[...] = jnp.zeros((PL, PL), F32)
    pad[0:NB, :] = block
    pad[0:NB, 0:LC] = list_ref[...].astype(F32)
    turned = pad[...].T
    twice = turned + pltpu.roll(turned, 64, 1)
    half = lax.broadcasted_iota(I32, (1, PL), 1) < 64
    ids = [jnp.where(half, twice[2 * j : 2 * j + 1], twice[2 * j + 1 : 2 * j + 2]) for j in range(LC // 2)]
    ids = jnp.concatenate(ids, axis=0).astype(I32)
    ctr = [twice[LC + c : LC + c + 1] for c in range(3)]
    slab = ids >> 11
    dx = ((slab >> 1) - xs) & (NX - 1)
    order = jnp.where(dx == 3, 1, jnp.where(dx == 0, 0, dx + 1))
    rows = (order * 2 + ((slab & 1) ^ cs)) * 16 + ((ids >> 7) & 15)
    lanes = ids & (PL - 1)
    tables = []
    for c in range(4):
        whole = jnp.concatenate([tab_ref[o, i, c] for o in range(NX) for i in range(2)], axis=0)
        whole = whole.T
        high = whole.astype(BF16)
        low = (whole - high.astype(F32)).astype(BF16)
        tables.append(jnp.concatenate([high, low], axis=1))
    tables = jnp.concatenate(tables, axis=0)
    sub = lax.broadcasted_iota(I32, (PL, 2 * PL), 0)
    got = [[] for _ in range(4)]
    for j in range(0, LC // 2, 2):
        r2 = jnp.concatenate([rows[j : j + 1], rows[j + 1 : j + 2]], axis=1)
        l2 = jnp.concatenate([lanes[j : j + 1], lanes[j + 1 : j + 2]], axis=1)
        hot = jnp.where(sub == r2, 1.0, 0.0).astype(BF16)
        hot = jnp.concatenate([hot, hot], axis=0)
        found = jnp.dot(tables, hot, preferred_element_type=F32)
        pick = sub == l2
        for c in range(4):
            value = jnp.sum(jnp.where(pick, found[c * PL : (c + 1) * PL], 0.0), axis=0, keepdims=True)
            got[c] += [value[:, :PL], value[:, PL:]]
    cells = [jnp.concatenate(v, axis=0) for v in got]
    rel = [ctr[c] - cells[c] for c in range(3)]
    dist = rel[0] * rel[0] + rel[1] * rel[1] + rel[2] * rel[2] + 1.0
    inv = lax.rsqrt(dist)
    cube = cells[3] * (inv * inv * inv)
    fifth = 3.0 * cube * (inv * inv)
    terms = [-(cube * rel[c]) for c in range(3)]
    for a, b in ((0, 0), (1, 1), (2, 2), (0, 1), (0, 2), (1, 2)):
        value = fifth * rel[a] * rel[b]
        if a == b:
            value = value - cube
        terms.append(value)
    terms = [jnp.sum(v, axis=0, keepdims=True) for v in terms]
    pad[...] = jnp.zeros((PL, PL), F32)
    for i, v in enumerate(terms):
        pad[i : i + 1, :] = v + pltpu.roll(v, 64, 1)
    back = pad[...].T
    field = [back[0:NB, i : i + 1] for i in range(3)]
    tide = [back[0:NB, 3 + i : 4 + i] for i in range(6)]
    offset = [pos[c] - centre[c] for c in range(3)]
    for c, (i, j, k) in enumerate(((0, 3, 4), (3, 1, 5), (4, 5, 2))):
        out_ref[:, c, :] = field[c] + tide[i] * offset[0] + tide[j] * offset[1] + tide[k] * offset[2]


def split3(v):
    high = v.astype(BF16).astype(F32)
    rest = v - high
    mid = rest.astype(BF16).astype(F32)
    return high, mid, rest - mid


def prep_kernel(info_ref, y_ref, t0, t1, t2, t3, tall, lst):
    me = y_ref[0]
    for i, t in enumerate((t0, t1, t2, t3)):
        tall[i * NB : (i + 1) * NB] = t[...]

    def scan(r, n):
        lst[n] = r
        return n + (info_ref[r, 12 + me] > 0).astype(I32)

    lst[LIST - 1] = lax.fori_loop(0, NY * NB, scan, jnp.int32(0), unroll=8)


def near_kernel(info_ref, y_ref, lst, tall, src_ref, o0, o1, o2, o3, oall):
    me = y_ref[0]
    n = lst[LIST - 1]
    oall[...] = jnp.zeros((NY * NB, 4, PL), F32)
    sub4 = lax.broadcasted_iota(I32, (4, PL), 0)
    lane4 = lax.broadcasted_iota(I32, (4, PL), 1)
    spatial = sub4 < 3
    one = jnp.ones((4, PL), F32)
    zero4 = jnp.zeros((4, PL), F32)
    zero8 = jnp.zeros((8, PL), F32)

    def square(v):
        return jnp.sum(jnp.where(spatial, v * v, 0.0), axis=0, keepdims=True)

    def mix(a, b):
        return jnp.where(spatial, a, b)

    def stack(*v):
        return jnp.concatenate(v, axis=0).astype(BF16)

    def job(r):
        t = tall[r]
        th, tm, tl = split3(t)
        qh, qm, ql = split3(square(t))
        u = stack(mix(th, one), mix(th, one), mix(tm, one), mix(tm, qh), mix(th, qm), mix(tl, ql), zero8)
        vs, gs = [], []
        for k in range(K):
            s = src_ref[info_ref[r, k]]
            flag = (info_ref[r, 8 + k] == me).astype(F32)
            sh, sm, sl = split3(-2.0 * s)
            qh, qm, ql = split3(square(s) + SOFT)
            vs.append(stack(mix(sh, qh), mix(sm, qm), mix(sh, ql), mix(sm, one), mix(sl, one), mix(sh, one), zero8))
            w = s[3:4] * flag
            gs.append(stack(*split3(mix(s * w, w)), zero4))
        v = jnp.concatenate(vs, axis=1)
        g = jnp.concatenate(gs, axis=1)
        dist = lax.dot_general(v, u, (((0,), (0,)), ((), ())), preferred_element_type=F32)
        inv = lax.rsqrt(dist)
        f = inv * inv * inv
        high = f.astype(BF16)
        low = (f - high.astype(F32)).astype(BF16)
        o = jnp.dot(g, high, preferred_element_type=F32) + jnp.dot(g, low, preferred_element_type=F32)
        a = o[0:4] + o[4:8] + o[8:12]
        oall[r] = jnp.where(lane4 < info_ref[r, 4], a - t * a[3:4], 0.0)

    def step(i, _):
        for j in range(UNROLL):
            job(lst[jnp.minimum(UNROLL * i + j, n - 1)])

    lax.fori_loop(0, (n + UNROLL - 1) // UNROLL, step, None)
    for i, o in enumerate((o0, o1, o2, o3)):
        o[...] = oall[i * NB : (i + 1) * NB, 0:3, :]


def ring(n, k):
    return [(i, (i + k) % n) for i in range(n)]


def along_y(k):
    return [(NZ * y + z, NZ * ((y + k) % NY) + z) for y in range(NY) for z in range(NZ)]


def along_x(k):
    return [(2 * x + c, 2 * ((x + k) % NX) + c) for x in range(NX) for c in range(2)]


def per_device(positions, masses, counts, dest_ids, near_list, cell_list, cell_centers, cell_mass):
    pos, cnt = positions[0], counts[0]
    src, tgt = pl.pallas_call(
        pack_kernel,
        out_shape=(
            jax.ShapeDtypeStruct((NZ, NB, 4, PL), F32),
            jax.ShapeDtypeStruct((NB, 4, PL), F32),
        ),
        in_specs=[vspec()] * 5,
        out_specs=[vspec()] * 2,
        name="pack",
    )(pos, masses[0], cnt, dest_ids, near_list[0])
    rows = [[NZ * y + z for z in range(NZ)] for y in range(NY)]
    window = lax.all_to_all(src, "space", 0, 0, axis_index_groups=rows, tiled=True)
    tgts = [tgt] + [lax.ppermute(tgt, "space", along_y(k)) for k in (1, -1, 2)]
    cells = jnp.concatenate([cell_centers, cell_mass[None]], axis=0).reshape(4, 16, PL)
    pair = jnp.stack([cells, lax.ppermute(cells, "slab", [(i, i ^ 1) for i in range(2 * NX)])])
    tab = jnp.stack([pair] + [lax.ppermute(pair, "slab", along_x(k)) for k in (1, -1, 2)])
    slab = lax.axis_index("slab")
    place = jnp.stack([slab >> 1, slab & 1]).astype(I32)
    far = pl.pallas_call(
        far_kernel,
        out_shape=jax.ShapeDtypeStruct((NB, 3, PL), F32),
        in_specs=[sspec()] + [vspec()] * 4,
        out_specs=vspec(),
        scratch_shapes=[pltpu.VMEM((PL, PL), F32)],
        name="far",
    )(place, pos, cnt, cell_list[0], tab)
    info = jnp.concatenate([t[:, 3, :16] for t in tgts], axis=0).astype(I32)
    me = (lax.axis_index("space") // NZ).astype(I32).reshape(1)
    tall, lst = pl.pallas_call(
        prep_kernel,
        out_shape=(
            jax.ShapeDtypeStruct((NY * NB, 4, PL), F32),
            jax.ShapeDtypeStruct((LIST,), I32),
        ),
        in_specs=[sspec(), sspec()] + [vspec()] * 4,
        out_specs=[vspec(), sspec()],
        name="prep",
    )(info, me, *tgts)
    far, tall = lax.optimization_barrier((far, tall))
    parts = pl.pallas_call(
        near_kernel,
        out_shape=[jax.ShapeDtypeStruct((NB, 3, PL), F32)] * 4,
        in_specs=[sspec()] * 3 + [vspec()] * 2,
        out_specs=[vspec()] * 4,
        scratch_shapes=[pltpu.VMEM((NY * NB, 4, PL), F32)],
        name="near",
    )(info, me, lst, tall, window.reshape(NZ * NB, 4, PL))
    back = [parts[0]] + [lax.ppermute(parts[1 + i], "space", along_y(-k)) for i, k in enumerate((1, -1, 2))]
    live = lax.broadcasted_iota(I32, (NB, 1, PL), 2) < cnt[0][:, None, None]
    out = jnp.where(live, far + ((back[0] + back[1]) + (back[2] + back[3])), 0.0)
    return out[None]


def solution(mesh):
    in_specs = (
        P("slab", "space", None, None),
        P("slab", "space", None),
        P("slab", "space", None),
        P("slab", "space"),
        P("slab", "space", None),
        P("slab", "space", None),
        P(None, "slab"),
        P("slab"),
    )
    return jax.shard_map(
        per_device,
        mesh=mesh,
        in_specs=in_specs,
        out_specs=P("slab", "space", None, None),
        check_vma=False,
    )
```

```python
import jax
import jax.numpy as jnp
from jax import lax
from jax.experimental import pallas as pl
from jax.experimental.pallas import tpu as pltpu
from jax.sharding import PartitionSpec as P

NB = 48
PL = 128
K = 4
LC = 32
NY = 4
NZ = 8
NX = 4
SOFT = 0.01
UNROLL = 8
FULL_AT = 7
HALF_AT = 8
PADDED = 256
F32 = jnp.float32
I32 = jnp.int32
BF16 = jnp.bfloat16
VMEM = pltpu.VMEM
SMEM = pltpu.SMEM


def vspec():
    return pl.BlockSpec(memory_space=VMEM)


def sspec():
    return pl.BlockSpec(memory_space=SMEM)


def column_of(row, n):
    square = jnp.broadcast_to(row, (n, n))
    diag = lax.broadcasted_iota(I32, (n, n), 0) == lax.broadcasted_iota(I32, (n, n), 1)
    return jnp.sum(jnp.where(diag, square, jnp.zeros_like(square)), axis=1, keepdims=True)


def pack_kernel(pos_ref, mass_ref, cnt_ref, dest_ref, near_ref, ctr_ref, cm_ref, src_ref, tgt_ref, cell_ref):
    cnt = column_of(cnt_ref[...], NB)
    near = near_ref[...]
    off = (near >= NB).astype(I32) + (near >= 2 * NB).astype(I32)
    dev = (dest_ref[...] + off - 1) & (NY * NZ - 1)
    code = (dev & (NZ - 1)) * NB + (near - off * NB)
    row = dev >> 3
    lane = lax.broadcasted_iota(I32, (NB, PL), 1)
    weight = jnp.where(lane < cnt, mass_ref[...], 0.0)
    info = jnp.where(lane == 4, cnt, 0)
    for k in range(K):
        info = jnp.where(lane == k, column_of(code[k : k + 1], NB), info)
        info = jnp.where(lane == 8 + k, column_of(row[k : k + 1], NB), info)
    info = info.astype(F32)
    for c in range(3):
        value = pos_ref[c]
        tgt_ref[:, c, :] = value
        for z in range(NZ):
            src_ref[z, :, c, :] = value
    tgt_ref[:, 3, :] = info
    for z in range(NZ):
        src_ref[z, :, 3, :] = weight
    for j in range(16):
        part = slice(j * PL, (j + 1) * PL)
        for c in range(3):
            cell_ref[c * 16 + j : c * 16 + j + 1, :] = ctr_ref[c : c + 1, part]
        cell_ref[48 + j : 49 + j, :] = cm_ref[0:1, part]
    cell_ref[64:PADDED, :] = jnp.zeros((PADDED - 64, PL), F32)


def far_kernel(pos_ref, cnt_ref, list_ref, cell_hbm, out_ref, pad, tab, sem):
    copies = [
        pltpu.make_async_copy(cell_hbm.at[pl.ds(i * PADDED, 64)], tab.at[i], sem.at[i]) for i in range(2 * NX)
    ]
    for copy in copies:
        copy.start()
    lane = lax.broadcasted_iota(I32, (NB, PL), 1)
    cnt = column_of(cnt_ref[...], NB)
    live = lane < cnt
    total = jnp.maximum(cnt, 1).astype(F32)
    pos = [pos_ref[c] for c in range(3)]
    centre = [jnp.sum(jnp.where(live, v, 0.0), axis=1, keepdims=True) / total for v in pos]
    diag = lax.broadcasted_iota(I32, (NB, PL), 0) == (lane & 63)
    ctr = [jnp.sum(jnp.where(diag, v, 0.0), axis=0, keepdims=True) for v in centre]
    wide = jnp.concatenate([list_ref[...], jnp.zeros((LC, PL - NB), I32)], axis=1)
    twice = wide + pltpu.roll(wide, 64, 1)
    half = lax.broadcasted_iota(I32, (1, PL), 1) < 64
    ids = [jnp.where(half, twice[2 * j : 2 * j + 1], twice[2 * j + 1 : 2 * j + 2]) for j in range(LC // 2)]
    ids = jnp.concatenate(ids, axis=0)
    rows = ids >> 7
    lanes = ids & (PL - 1)
    tables = []
    for copy in copies:
        copy.wait()
    for c in range(4):
        whole = jnp.concatenate([tab[i, 16 * c : 16 * c + 16, :] for i in range(2 * NX)], axis=0)
        whole = whole.T
        high = whole.astype(BF16)
        low = (whole - high.astype(F32)).astype(BF16)
        tables.append(jnp.concatenate([high, low], axis=1))
    tables = jnp.concatenate(tables, axis=0)
    sub = lax.broadcasted_iota(I32, (PL, 2 * PL), 0)
    got = [[] for _ in range(4)]
    for j in range(0, LC // 2, 2):
        r2 = jnp.concatenate([rows[j : j + 1], rows[j + 1 : j + 2]], axis=1)
        l2 = jnp.concatenate([lanes[j : j + 1], lanes[j + 1 : j + 2]], axis=1)
        hot = jnp.where(sub == r2, 1.0, 0.0).astype(BF16)
        hot = jnp.concatenate([hot, hot], axis=0)
        found = jnp.dot(tables, hot, preferred_element_type=F32)
        pick = sub == l2
        for c in range(4):
            value = jnp.sum(jnp.where(pick, found[c * PL : (c + 1) * PL], 0.0), axis=0, keepdims=True)
            got[c] += [value[:, :PL], value[:, PL:]]
    cells = [jnp.concatenate(v, axis=0) for v in got]
    rel = [ctr[c] - cells[c] for c in range(3)]
    dist = rel[0] * rel[0] + rel[1] * rel[1] + rel[2] * rel[2] + 1.0
    inv = lax.rsqrt(dist)
    cube = cells[3] * (inv * inv * inv)
    fifth = 3.0 * cube * (inv * inv)
    terms = [-(cube * rel[c]) for c in range(3)]
    for a, b in ((0, 0), (1, 1), (2, 2), (0, 1), (0, 2), (1, 2)):
        value = fifth * rel[a] * rel[b]
        if a == b:
            value = value - cube
        terms.append(value)
    terms = [jnp.sum(v, axis=0, keepdims=True) for v in terms]
    pad[...] = jnp.zeros((PL, PL), F32)
    for i, v in enumerate(terms):
        pad[i : i + 1, :] = v + pltpu.roll(v, 64, 1)
    back = pad[...].T
    field = [back[0:NB, i : i + 1] for i in range(3)]
    tide = [back[0:NB, 3 + i : 4 + i] for i in range(6)]
    offset = [pos[c] - centre[c] for c in range(3)]
    for c, (i, j, k) in enumerate(((0, 3, 4), (3, 1, 5), (4, 5, 2))):
        out_ref[c] = field[c] + tide[i] * offset[0] + tide[j] * offset[1] + tide[k] * offset[2]


def split3(v):
    high = v.astype(BF16).astype(F32)
    rest = v - high
    mid = rest.astype(BF16).astype(F32)
    return high, mid, rest - mid


def prep_kernel(y_ref, t0, t1, t2, t3, tall, tab, hold, sem):
    me = y_ref[0]
    n_all = NY * NB
    infos = []
    for i, t in enumerate((t0, t1, t2, t3)):
        tall[i * NB : (i + 1) * NB] = t[...]
        infos.append(t[:, 3, :])
    info = jnp.concatenate(infos, axis=0)
    sub = lax.broadcasted_iota(I32, (n_all, PL), 0)
    lane = lax.broadcasted_iota(I32, (n_all, PL), 1)
    here = me.astype(F32)
    flag = [(info[:, 8 + k : 9 + k] == here).astype(F32) for k in range(K)]
    code = [info[:, k : k + 1] for k in range(K)]
    count = (flag[0] + flag[1]) + (flag[2] + flag[3])
    full = (count > 2.5).astype(F32)
    half = ((count > 0.5) & (count < 2.5)).astype(F32)
    marks = jnp.where(lane == 0, full, jnp.where(lane == 1, half, 0.0))
    a = lax.broadcasted_iota(I32, (n_all, n_all), 0)
    b = lax.broadcasted_iota(I32, (n_all, n_all), 1)
    below = jnp.where(b < a, 1.0, 0.0).astype(BF16)
    before = jnp.dot(below, marks.astype(BF16), preferred_element_type=F32)
    n_full = jnp.sum(full, axis=0, keepdims=True)
    n_half = jnp.sum(half, axis=0, keepdims=True)
    place = jnp.where(full > 0.5, before[:, 0:1], jnp.where(half > 0.5, n_full + before[:, 1:2], -1.0))
    moved = jnp.where(b == place.astype(I32), 1.0, 0.0).astype(BF16)
    slot, ins, outs = [], jnp.zeros((n_all, 1), F32), jnp.zeros((n_all, 1), F32)
    for k in range(K):
        slot.append(jnp.where(flag[k] > 0.5, ins, count + outs))
        ins, outs = ins + flag[k], outs + (1.0 - flag[k])
    group = (sub >= NB).astype(I32) + (sub >= 2 * NB).astype(I32) + (sub >= 3 * NB).astype(I32)
    step = jnp.where(group == 2, -1, jnp.where(group == 3, 2, group))
    home = ((me - step) & (NY - 1)) * NB + (sub - group * NB)
    load = jnp.where(lane == 4, info, jnp.where(lane == 5, home.astype(F32), jnp.where(lane == 6, count, 0.0)))
    load = jnp.where(lane == 9, sub.astype(F32), load)
    for j in range(K):
        pick = jnp.zeros((n_all, 1), F32)
        for k in range(K):
            pick = pick + jnp.where(slot[k] == float(j), code[k], 0.0)
        load = jnp.where(lane == j, pick, load)
    high = load.astype(BF16)
    low = (load - high.astype(F32)).astype(BF16)
    dn = (((0,), (0,)), ((), ()))
    out = lax.dot_general(moved, high, dn, preferred_element_type=F32) + lax.dot_general(
        moved, low, dn, preferred_element_type=F32
    )
    out = jnp.where(lane == FULL_AT, n_full, jnp.where(lane == HALF_AT, n_half, out))
    hold[...] = out.astype(I32)
    copy = pltpu.make_async_copy(hold, tab, sem)
    copy.start()
    copy.wait()


def near_kernel(tab, tall, src_ref, out_ref):
    out_ref[...] = jnp.zeros((NY * NB, 3, PL), F32)
    sub4 = lax.broadcasted_iota(I32, (4, PL), 0)
    lane3 = lax.broadcasted_iota(I32, (3, PL), 1)
    spatial = sub4 < 3
    one = jnp.ones((4, PL), F32)
    zero4 = jnp.zeros((4, PL), F32)
    zero8 = jnp.zeros((8, PL), F32)

    def square(v):
        return jnp.sum(jnp.where(spatial, v * v, 0.0), axis=0, keepdims=True)

    def mix(a, b):
        return jnp.where(spatial, a, b)

    def stack(*v):
        return jnp.concatenate(v, axis=0).astype(BF16)

    def job(e, width):
        n = tab[e, 6]
        t = tall[tab[e, 9]]
        th, tm, tl = split3(t)
        qh, qm, ql = split3(square(t))
        u = stack(mix(th, one), mix(th, one), mix(tm, one), mix(tm, qh), mix(th, qm), mix(tl, ql), zero8)
        vs, gs = [], []
        for k in range(width):
            s = src_ref[tab[e, k]]
            flag = (k < n).astype(F32)
            sh, sm, sl = split3(-2.0 * s)
            qh, qm, ql = split3(square(s) + SOFT)
            vs.append(stack(mix(sh, qh), mix(sm, qm), mix(sh, ql), mix(sm, one), mix(sl, one), mix(sh, one), zero8))
            w = s[3:4] * flag
            gs.append(stack(*split3(mix(s * w, w)), zero4))
        v = jnp.concatenate(vs, axis=1)
        g = jnp.concatenate(gs, axis=1)
        dist = lax.dot_general(v, u, (((0,), (0,)), ((), ())), preferred_element_type=F32)
        inv = lax.rsqrt(dist)
        f = inv * inv * inv
        high = f.astype(BF16)
        low = (f - high.astype(F32)).astype(BF16)
        o = jnp.dot(g, high, preferred_element_type=F32) + jnp.dot(g, low, preferred_element_type=F32)
        a = o[0:4] + o[4:8] + o[8:12]
        out_ref[tab[e, 5]] = jnp.where(lane3 < tab[e, 4], a[0:3] - t[0:3] * a[3:4], 0.0)

    n_full = tab[0, FULL_AT]
    n_half = tab[0, HALF_AT]

    def whole(i, _):
        for j in range(UNROLL):
            job(jnp.minimum(UNROLL * i + j, n_full - 1), 4)

    def part(i, _):
        for j in range(UNROLL):
            job(n_full + jnp.minimum(UNROLL * i + j, n_half - 1), 2)

    lax.fori_loop(0, (n_full + UNROLL - 1) // UNROLL, whole, None)
    lax.fori_loop(0, (n_half + UNROLL - 1) // UNROLL, part, None)


def final_kernel(cnt_ref, far_ref, part_ref, out_ref):
    live = lax.broadcasted_iota(I32, (NB, PL), 1) < column_of(cnt_ref[...], NB)
    near = (part_ref[0] + part_ref[1]) + (part_ref[2] + part_ref[3])
    for c in range(3):
        out_ref[c] = jnp.where(live, far_ref[c] + near[:, c, :], 0.0)


def along_y(k):
    return [(NZ * y + z, NZ * ((y + k) % NY) + z) for y in range(NY) for z in range(NZ)]


def per_device(positions, masses, counts, dest_ids, near_list, cell_list, cell_centers, cell_mass):
    pos = jnp.transpose(positions[0], (1, 0, 2))
    cnt = counts[0]
    src, tgt, cells = pl.pallas_call(
        pack_kernel,
        out_shape=(
            jax.ShapeDtypeStruct((NZ, NB, 4, PL), F32),
            jax.ShapeDtypeStruct((NB, 4, PL), F32),
            jax.ShapeDtypeStruct((PADDED, PL), F32),
        ),
        in_specs=[vspec()] * 7,
        out_specs=[vspec()] * 3,
        name="pack",
    )(pos, masses[0], cnt, dest_ids, near_list[0].T, cell_centers, cell_mass[None])
    z_rows = [[NZ * y + z for z in range(NZ)] for y in range(NY)]
    y_rows = [[NZ * y + z for y in range(NY)] for z in range(NZ)]
    window = lax.all_to_all(src, "space", 0, 0, axis_index_groups=z_rows, tiled=True)
    tgts = [tgt] + [lax.ppermute(tgt, "space", along_y(k)) for k in (1, -1, 2)]
    table = lax.all_gather(cells, "slab", axis=0, tiled=True)
    me = (lax.axis_index("space") // NZ).astype(I32).reshape(1)
    tall, tab = pl.pallas_call(
        prep_kernel,
        out_shape=(
            jax.ShapeDtypeStruct((NY * NB, 4, PL), F32),
            jax.ShapeDtypeStruct((NY * NB, PL), I32),
        ),
        in_specs=[sspec()] + [vspec()] * 4,
        out_specs=[vspec(), sspec()],
        scratch_shapes=[pltpu.VMEM((NY * NB, PL), I32), pltpu.SemaphoreType.DMA],
        name="prep",
    )(me, *tgts)
    part = pl.pallas_call(
        near_kernel,
        out_shape=jax.ShapeDtypeStruct((NY * NB, 3, PL), F32),
        in_specs=[sspec()] + [vspec()] * 2,
        out_specs=vspec(),
        name="near",
    )(tab, tall, window.reshape(NZ * NB, 4, PL))
    table, part = lax.optimization_barrier((table, part))
    far = pl.pallas_call(
        far_kernel,
        out_shape=jax.ShapeDtypeStruct((3, NB, PL), F32),
        in_specs=[vspec()] * 3 + [pl.BlockSpec(memory_space=pl.ANY)],
        out_specs=vspec(),
        scratch_shapes=[
            pltpu.VMEM((PL, PL), F32),
            pltpu.VMEM((2 * NX, 64, PL), F32),
            pltpu.SemaphoreType.DMA((2 * NX,)),
        ],
        name="far",
    )(pos, cnt, cell_list[0].T, table)
    back = lax.all_to_all(
        part.reshape(NY, NB, 3, PL), "space", 0, 0, axis_index_groups=y_rows, tiled=True
    )
    out = pl.pallas_call(
        final_kernel,
        out_shape=jax.ShapeDtypeStruct((3, NB, PL), F32),
        in_specs=[vspec()] * 3,
        out_specs=vspec(),
        name="final",
    )(cnt, far, back)
    return jnp.transpose(out, (1, 0, 2))[None]


def solution(mesh):
    in_specs = (
        P("slab", "space", None, None),
        P("slab", "space", None),
        P("slab", "space", None),
        P("slab", "space"),
        P("slab", "space", None),
        P("slab", "space", None),
        P(None, "slab"),
        P("slab"),
    )
    return jax.shard_map(
        per_device,
        mesh=mesh,
        in_specs=in_specs,
        out_specs=P("slab", "space", None, None),
        check_vma=False,
    )
```

```python
import jax
import jax.numpy as jnp
from jax import lax
from jax.experimental import pallas as pl
from jax.experimental.pallas import tpu as pltpu
from jax.sharding import PartitionSpec as P

NB = 48
PL = 128
K = 4
LC = 32
NY = 4
NZ = 8
NX = 4
SOFT = 0.01
UNROLL = 8
MIB = 1 << 20
F32 = jnp.float32
I32 = jnp.int32
BF16 = jnp.bfloat16
VMEM = pltpu.VMEM
SMEM = pltpu.SMEM


def vspec():
    return pl.BlockSpec(memory_space=VMEM)


def sspec():
    return pl.BlockSpec(memory_space=SMEM)


def column_of(row, n):
    square = jnp.broadcast_to(row, (n, n))
    diag = lax.broadcasted_iota(I32, (n, n), 0) == lax.broadcasted_iota(I32, (n, n), 1)
    return jnp.sum(jnp.where(diag, square, jnp.zeros_like(square)), axis=1, keepdims=True)


def pack_kernel(pos_ref, mass_ref, cnt_ref, dest_ref, near_ref, ctr_ref, cm_ref, src_ref, tgt_ref, cell_ref):
    counts = cnt_ref[...]
    cnt = column_of(counts, NB)
    near = near_ref[...]
    off = (near >= NB).astype(I32) + (near >= 2 * NB).astype(I32)
    dev = (dest_ref[...] + off - 1) & (NY * NZ - 1)
    code = (dev >> 3) * 512 + (dev & (NZ - 1)) * NB + (near - off * NB)
    gap = jnp.zeros((4, 64 - NB), I32)
    info = jnp.concatenate([code, gap, jnp.broadcast_to(counts, (4, NB)), gap], axis=1)
    lane = lax.broadcasted_iota(I32, (NB, PL), 1)
    weight = jnp.where(lane < cnt, mass_ref[...], 0.0)
    for c in range(3):
        value = pos_ref[c]
        tgt_ref[0:NB, c, :] = value
        for z in range(NZ):
            src_ref[z, :, c, :] = value
    for z in range(NZ):
        src_ref[z, :, 3, :] = weight
    tgt_ref[0:NB, 3, :] = jnp.zeros((NB, PL), F32)
    tgt_ref[NB] = info.astype(F32)
    for j in range(16):
        part = slice(j * PL, (j + 1) * PL)
        cell_ref[j, 0:3, :] = ctr_ref[:, part]
        cell_ref[j, 3:4, :] = cm_ref[0:1, part]


def far_kernel(place_ref, pos_ref, cnt_ref, list_ref, c0, c1, c2, c3, out_ref, pad):
    xs, cs = place_ref[0] >> 1, place_ref[0] & 1
    lane = lax.broadcasted_iota(I32, (NB, PL), 1)
    cnt = column_of(cnt_ref[...], NB)
    live = lane < cnt
    total = jnp.maximum(cnt, 1).astype(F32)
    pos = [pos_ref[c] for c in range(3)]
    centre = [jnp.sum(jnp.where(live, v, 0.0), axis=1, keepdims=True) / total for v in pos]
    diag = lax.broadcasted_iota(I32, (NB, PL), 0) == (lane & 63)
    ctr = [jnp.sum(jnp.where(diag, v, 0.0), axis=0, keepdims=True) for v in centre]
    wide = jnp.concatenate([list_ref[...], jnp.zeros((LC, PL - NB), I32)], axis=1)
    twice = wide + pltpu.roll(wide, 64, 1)
    half = lax.broadcasted_iota(I32, (1, PL), 1) < 64
    ids = [jnp.where(half, twice[2 * j : 2 * j + 1], twice[2 * j + 1 : 2 * j + 2]) for j in range(LC // 2)]
    ids = jnp.concatenate(ids, axis=0)
    slab = ids >> 11
    dx = ((slab >> 1) - xs) & (NX - 1)
    order = jnp.where(dx == 3, 1, jnp.where(dx == 0, 0, dx + 1))
    rows = (order * 2 + ((slab & 1) ^ cs)) * 16 + ((ids >> 7) & 15)
    lanes = ids & (PL - 1)
    tables = []
    for c in range(4):
        whole = jnp.concatenate([ref[i, :, c, :] for ref in (c0, c1, c2, c3) for i in range(2)], axis=0)
        whole = whole.T
        high = whole.astype(BF16)
        low = (whole - high.astype(F32)).astype(BF16)
        tables.append(jnp.concatenate([high, low], axis=1))
    tables = jnp.concatenate(tables, axis=0)
    sub = lax.broadcasted_iota(I32, (PL, 2 * PL), 0)
    got = [[] for _ in range(4)]
    for j in range(0, LC // 2, 2):
        r2 = jnp.concatenate([rows[j : j + 1], rows[j + 1 : j + 2]], axis=1)
        l2 = jnp.concatenate([lanes[j : j + 1], lanes[j + 1 : j + 2]], axis=1)
        hot = jnp.where(sub == r2, 1.0, 0.0).astype(BF16)
        hot = jnp.concatenate([hot, hot], axis=0)
        found = jnp.dot(tables, hot, preferred_element_type=F32)
        pick = sub == l2
        for c in range(4):
            value = jnp.sum(jnp.where(pick, found[c * PL : (c + 1) * PL], 0.0), axis=0, keepdims=True)
            got[c] += [value[:, :PL], value[:, PL:]]
    cells = [jnp.concatenate(v, axis=0) for v in got]
    rel = [ctr[c] - cells[c] for c in range(3)]
    dist = rel[0] * rel[0] + rel[1] * rel[1] + rel[2] * rel[2] + 1.0
    inv = lax.rsqrt(dist)
    cube = cells[3] * (inv * inv * inv)
    fifth = 3.0 * cube * (inv * inv)
    terms = [-(cube * rel[c]) for c in range(3)]
    for a, b in ((0, 0), (1, 1), (2, 2), (0, 1), (0, 2), (1, 2)):
        value = fifth * rel[a] * rel[b]
        if a == b:
            value = value - cube
        terms.append(value)
    terms = [jnp.sum(v, axis=0, keepdims=True) for v in terms]
    pad[...] = jnp.zeros((PL, PL), F32)
    for i, v in enumerate(terms):
        pad[i : i + 1, :] = v + pltpu.roll(v, 64, 1)
    back = pad[...].T
    field = [back[0:NB, i : i + 1] for i in range(3)]
    tide = [back[0:NB, 3 + i : 4 + i] for i in range(6)]
    offset = [pos[c] - centre[c] for c in range(3)]
    for c, (i, j, k) in enumerate(((0, 3, 4), (3, 1, 5), (4, 5, 2))):
        out_ref[c] = field[c] + tide[i] * offset[0] + tide[j] * offset[1] + tide[k] * offset[2]


def split3(v):
    high = v.astype(BF16).astype(F32)
    rest = v - high
    mid = rest.astype(BF16).astype(F32)
    return high, mid, rest - mid


def prep_kernel(y_ref, t0, t1, t2, t3, tall, tab, hold, sem):
    me = y_ref[0]
    wide = 2 * PL
    tiles = []
    for i, t in enumerate((t0, t1, t2, t3)):
        tall[i * NB : (i + 1) * NB] = t[0:NB]
        tiles.append(t[NB])
    left = lax.broadcasted_iota(I32, (4, PL), 1) < 64
    code, cnt = [], []
    for a, b in ((tiles[0], tiles[1]), (tiles[2], tiles[3])):
        code.append(jnp.where(left, a, pltpu.roll(b, 64, 1)))
        cnt.append(jnp.where(left, pltpu.roll(a, 64, 1), b))
    code = jnp.concatenate(code, axis=1).astype(I32)
    cnt = jnp.concatenate(cnt, axis=1)[0:1]
    lane = lax.broadcasted_iota(I32, (1, wide), 1)
    valid = (lane & 63) < NB
    flag = [jnp.where(((code[k : k + 1] >> 9) == me) & valid, 1.0, 0.0) for k in range(K)]
    local = [(code[k : k + 1] & 511).astype(F32) for k in range(K)]
    count = (flag[0] + flag[1]) + (flag[2] + flag[3])
    full = jnp.where(count > 2.5, 1.0, 0.0)
    half = jnp.where((count > 0.5) & (count < 2.5), 1.0, 0.0)
    marks = jnp.concatenate([full, half, jnp.zeros((14, wide), F32)], axis=0).astype(BF16)
    a = lax.broadcasted_iota(I32, (wide, wide), 0)
    b = lax.broadcasted_iota(I32, (wide, wide), 1)
    before = jnp.dot(marks, jnp.where(a < b, 1.0, 0.0).astype(BF16), preferred_element_type=F32)
    n_full = jnp.sum(full, axis=1, keepdims=True)
    n_half = jnp.sum(half, axis=1, keepdims=True)
    place = jnp.where(full > 0.5, before[0:1], jnp.where(half > 0.5, n_full + before[1:2], -1.0))
    moved = jnp.where(a == place.astype(I32), 1.0, 0.0).astype(BF16)
    group = lane >> 6
    step = jnp.where(group == 2, -1, jnp.where(group == 3, 2, group))
    bucket = lane & 63
    home = ((me - step) & (NY - 1)) * NB + bucket
    slot, ins, outs = [], jnp.zeros((1, wide), F32), jnp.zeros((1, wide), F32)
    for k in range(K):
        slot.append(jnp.where(flag[k] > 0.5, ins, count + outs))
        ins, outs = ins + flag[k], outs + (1.0 - flag[k])
    fields = []
    for j in range(K):
        pick = jnp.zeros((1, wide), F32)
        for k in range(K):
            pick = pick + jnp.where(slot[k] == float(j), local[k], 0.0)
        fields.append(pick)
    fields += [cnt, home.astype(F32), count, (group * NB + bucket).astype(F32)]
    load = jnp.concatenate(fields, axis=0)
    high = load.astype(BF16).astype(F32)
    both = jnp.concatenate([high, load - high], axis=0).astype(BF16)
    out = lax.dot_general(both, moved, (((1,), (1,)), ((), ())), preferred_element_type=F32)
    out = out[0:8] + out[8:16]
    sizes = jnp.where(
        lax.broadcasted_iota(I32, (8, wide), 0) == 0,
        jnp.broadcast_to(n_full, (8, wide)),
        jnp.broadcast_to(n_half, (8, wide)),
    )
    hold[...] = jnp.concatenate([out, sizes], axis=0).astype(I32)
    copy = pltpu.make_async_copy(hold, tab, sem)
    copy.start()
    copy.wait()


def near_kernel(tab, tall, src_ref, out_ref):
    out_ref[...] = jnp.zeros((NY * NB, 4, PL), F32)
    sub4 = lax.broadcasted_iota(I32, (4, PL), 0)
    lane4 = lax.broadcasted_iota(I32, (4, PL), 1)
    spatial = sub4 < 3
    one = jnp.ones((4, PL), F32)
    zero4 = jnp.zeros((4, PL), F32)
    zero8 = jnp.zeros((8, PL), F32)

    def square(v):
        return jnp.sum(jnp.where(spatial, v * v, 0.0), axis=0, keepdims=True)

    def mix(a, b):
        return jnp.where(spatial, a, b)

    def stack(*v):
        return jnp.concatenate(v, axis=0).astype(BF16)

    def job(e, width):
        n = tab[6, e]
        t = tall[tab[7, e]]
        th, tm, tl = split3(t)
        qh, qm, ql = split3(square(t))
        u = stack(mix(th, one), mix(th, one), mix(tm, one), mix(tm, qh), mix(th, qm), mix(tl, ql), zero8)
        vs, gs = [], []
        for k in range(width):
            s = src_ref[tab[k, e]]
            flag = (k < n).astype(F32)
            sh, sm, sl = split3(-2.0 * s)
            qh, qm, ql = split3(square(s) + SOFT)
            vs.append(stack(mix(sh, qh), mix(sm, qm), mix(sh, ql), mix(sm, one), mix(sl, one), mix(sh, one), zero8))
            w = s[3:4] * flag
            gs.append(stack(*split3(mix(s * w, w)), zero4))
        v = jnp.concatenate(vs, axis=1)
        g = jnp.concatenate(gs, axis=1)
        dist = lax.dot_general(v, u, (((0,), (0,)), ((), ())), preferred_element_type=F32)
        inv = lax.rsqrt(dist)
        f = inv * inv * inv
        high = f.astype(BF16)
        low = (f - high.astype(F32)).astype(BF16)
        o = jnp.dot(g, high, preferred_element_type=F32) + jnp.dot(g, low, preferred_element_type=F32)
        a = o[0:4] + o[4:8] + o[8:12]
        out_ref[tab[5, e]] = jnp.where(lane4 < tab[4, e], a - t * a[3:4], 0.0)

    n_full = tab[8, 0]
    n_half = tab[9, 0]

    def whole(i, _):
        for j in range(UNROLL):
            job(jnp.minimum(UNROLL * i + j, n_full - 1), 4)

    def part(i, _):
        for j in range(UNROLL):
            job(n_full + jnp.minimum(UNROLL * i + j, n_half - 1), 2)

    lax.fori_loop(0, (n_full + UNROLL - 1) // UNROLL, whole, None)
    lax.fori_loop(0, (n_half + UNROLL - 1) // UNROLL, part, None)


def final_kernel(cnt_ref, far_ref, part_ref, out_ref):
    live = lax.broadcasted_iota(I32, (NB, PL), 1) < column_of(cnt_ref[...], NB)
    near = (part_ref[0] + part_ref[1]) + (part_ref[2] + part_ref[3])
    for c in range(3):
        out_ref[c] = jnp.where(live, far_ref[c] + near[:, c, :], 0.0)


def along_y(k):
    return [(NZ * y + z, NZ * ((y + k) % NY) + z) for y in range(NY) for z in range(NZ)]


def along_x(k):
    return [(2 * x + c, 2 * ((x + k) % NX) + c) for x in range(NX) for c in range(2)]


def call(kernel, outs, in_specs, out_specs, name, mib, scratch=()):
    return pl.pallas_call(
        kernel,
        out_shape=[jax.ShapeDtypeStruct(shape, dtype) for shape, dtype in outs],
        in_specs=in_specs,
        out_specs=out_specs,
        scratch_shapes=scratch,
        compiler_params=pltpu.CompilerParams(vmem_limit_bytes=mib * MIB),
        name=name,
    )


def per_device(positions, masses, counts, dest_ids, near_list, cell_list, cell_centers, cell_mass):
    pos = jnp.transpose(positions[0], (1, 0, 2))
    cnt = counts[0]
    src, tgt, cells = call(
        pack_kernel,
        (((NZ, NB, 4, PL), F32), ((NB + 1, 4, PL), F32), ((16, 4, PL), F32)),
        [vspec()] * 7,
        [vspec()] * 3,
        "pack",
        8,
    )(pos, masses[0], cnt, dest_ids, near_list[0].T, cell_centers, cell_mass[None])
    z_rows = [[NZ * y + z for z in range(NZ)] for y in range(NY)]
    y_rows = [[NZ * y + z for y in range(NY)] for z in range(NZ)]
    window = lax.all_to_all(src, "space", 0, 0, axis_index_groups=z_rows, tiled=True)
    tgts = [tgt] + [lax.ppermute(tgt, "space", along_y(k)) for k in (1, -1, 2)]
    pair = jnp.stack([cells, lax.ppermute(cells, "slab", [(i, i ^ 1) for i in range(2 * NX)])])
    pairs = [pair] + [lax.ppermute(pair, "slab", along_x(k)) for k in (1, -1, 2)]
    me = (lax.axis_index("space") // NZ).astype(I32).reshape(1)
    place = lax.axis_index("slab").astype(I32).reshape(1)
    tall, tab = call(
        prep_kernel,
        (((NY * NB, 4, PL), F32), ((16, 2 * PL), I32)),
        [sspec()] + [vspec()] * 4,
        [vspec(), sspec()],
        "prep",
        8,
        [pltpu.VMEM((16, 2 * PL), I32), pltpu.SemaphoreType.DMA],
    )(me, *tgts)
    (part,) = call(
        near_kernel,
        (((NY * NB, 4, PL), F32),),
        [sspec()] + [vspec()] * 2,
        [vspec()],
        "near",
        24,
    )(tab, tall, window.reshape(NZ * NB, 4, PL))
    *pairs, part = lax.optimization_barrier((*pairs, part))
    (far,) = call(
        far_kernel,
        (((3, NB, PL), F32),),
        [sspec()] + [vspec()] * 7,
        [vspec()],
        "far",
        16,
        [pltpu.VMEM((PL, PL), F32)],
    )(place, pos, cnt, cell_list[0].T, *pairs)
    back = lax.all_to_all(
        part.reshape(NY, NB, 4, PL), "space", 0, 0, axis_index_groups=y_rows, tiled=True
    )
    (out,) = call(
        final_kernel,
        (((3, NB, PL), F32),),
        [vspec()] * 3,
        [vspec()],
        "final",
        8,
    )(cnt, far, back)
    return jnp.transpose(out, (1, 0, 2))[None]


def solution(mesh):
    in_specs = (
        P("slab", "space", None, None),
        P("slab", "space", None),
        P("slab", "space", None),
        P("slab", "space"),
        P("slab", "space", None),
        P("slab", "space", None),
        P(None, "slab"),
        P("slab"),
    )
    return jax.shard_map(
        per_device,
        mesh=mesh,
        in_specs=in_specs,
        out_specs=P("slab", "space", None, None),
        check_vma=False,
    )
```

```python
import functools

import jax
import jax.numpy as jnp
from jax import lax
from jax.experimental import pallas as pl
from jax.experimental.pallas import tpu as pltpu
from jax.sharding import PartitionSpec as P

NB = 48
PL = 128
K = 4
LC = 32
NY = 4
NZ = 8
NX = 4
SOFT = 0.01
UNROLL = 8
MIB = 1 << 20
F32 = jnp.float32
I32 = jnp.int32
BF16 = jnp.bfloat16
VMEM = pltpu.VMEM
SMEM = pltpu.SMEM


def vspec():
    return pl.BlockSpec(memory_space=VMEM)


def sspec():
    return pl.BlockSpec(memory_space=SMEM)


def column_of(row, n):
    square = jnp.broadcast_to(row, (n, n))
    diag = lax.broadcasted_iota(I32, (n, n), 0) == lax.broadcasted_iota(I32, (n, n), 1)
    return jnp.sum(jnp.where(diag, square, jnp.zeros_like(square)), axis=1, keepdims=True)


def pack_kernel(*refs):
    ins, (src_ref, tgt_ref, cell_ref), holds, sem = refs[:7], refs[7:10], refs[10:17], refs[17]
    copies = [pltpu.make_async_copy(ins[i], holds[i], sem.at[i]) for i in range(7)]
    for copy in copies:
        copy.start()
    for copy in copies:
        copy.wait()
    pos_ref, mass_ref, cnt_ref, dest_ref, near_ref, ctr_ref, cm_ref = holds
    counts = cnt_ref[...]
    cnt = column_of(counts, NB)
    near = near_ref[...]
    off = (near >= NB).astype(I32) + (near >= 2 * NB).astype(I32)
    dev = (dest_ref[...] + off - 1) & (NY * NZ - 1)
    code = (dev >> 3) * 512 + (dev & (NZ - 1)) * NB + (near - off * NB)
    gap = jnp.zeros((4, 64 - NB), I32)
    info = jnp.concatenate([code, gap, jnp.broadcast_to(counts, (4, NB)), gap], axis=1)
    lane = lax.broadcasted_iota(I32, (NB, PL), 1)
    weight = jnp.where(lane < cnt, mass_ref[...], 0.0)
    for c in range(3):
        value = pos_ref[c]
        tgt_ref[0:NB, c, :] = value
        for z in range(NZ):
            src_ref[z, :, c, :] = value
    for z in range(NZ):
        src_ref[z, :, 3, :] = weight
    tgt_ref[0:NB, 3, :] = jnp.zeros((NB, PL), F32)
    tgt_ref[NB] = info.astype(F32)
    for j in range(16):
        part = slice(j * PL, (j + 1) * PL)
        cell_ref[j, 0:3, :] = ctr_ref[:, part]
        cell_ref[j, 3:4, :] = cm_ref[0:1, part]


def far_kernel(place_ref, pos_ref, cnt_ref, list_ref, c0, c1, c2, c3, out_ref, pad):
    xs, cs = place_ref[0] >> 1, place_ref[0] & 1
    lane = lax.broadcasted_iota(I32, (NB, PL), 1)
    cnt = column_of(cnt_ref[...], NB)
    live = lane < cnt
    total = jnp.maximum(cnt, 1).astype(F32)
    pos = [pos_ref[c] for c in range(3)]
    centre = [jnp.sum(jnp.where(live, v, 0.0), axis=1, keepdims=True) / total for v in pos]
    diag = lax.broadcasted_iota(I32, (NB, PL), 0) == (lane & 63)
    ctr = [jnp.sum(jnp.where(diag, v, 0.0), axis=0, keepdims=True) for v in centre]
    wide = jnp.concatenate([list_ref[...], jnp.zeros((LC, PL - NB), I32)], axis=1)
    twice = wide + pltpu.roll(wide, 64, 1)
    half = lax.broadcasted_iota(I32, (1, PL), 1) < 64
    ids = [jnp.where(half, twice[2 * j : 2 * j + 1], twice[2 * j + 1 : 2 * j + 2]) for j in range(LC // 2)]
    ids = jnp.concatenate(ids, axis=0)
    slab = ids >> 11
    dx = ((slab >> 1) - xs) & (NX - 1)
    order = jnp.where(dx == 3, 1, jnp.where(dx == 0, 0, dx + 1))
    rows = (order * 2 + ((slab & 1) ^ cs)) * 16 + ((ids >> 7) & 15)
    lanes = ids & (PL - 1)
    tables = []
    for c in range(4):
        whole = jnp.concatenate([ref[i, :, c, :] for ref in (c0, c1, c2, c3) for i in range(2)], axis=0)
        whole = whole.T
        high = whole.astype(BF16)
        low = (whole - high.astype(F32)).astype(BF16)
        tables.append(jnp.concatenate([high, low], axis=1))
    tables = jnp.concatenate(tables, axis=0)
    sub = lax.broadcasted_iota(I32, (PL, 2 * PL), 0)
    got = [[] for _ in range(4)]
    for j in range(0, LC // 2, 2):
        r2 = jnp.concatenate([rows[j : j + 1], rows[j + 1 : j + 2]], axis=1)
        l2 = jnp.concatenate([lanes[j : j + 1], lanes[j + 1 : j + 2]], axis=1)
        hot = jnp.where(sub == r2, 1.0, 0.0).astype(BF16)
        hot = jnp.concatenate([hot, hot], axis=0)
        found = jnp.dot(tables, hot, preferred_element_type=F32)
        pick = sub == l2
        for c in range(4):
            value = jnp.sum(jnp.where(pick, found[c * PL : (c + 1) * PL], 0.0), axis=0, keepdims=True)
            got[c] += [value[:, :PL], value[:, PL:]]
    cells = [jnp.concatenate(v, axis=0) for v in got]
    rel = [ctr[c] - cells[c] for c in range(3)]
    dist = rel[0] * rel[0] + rel[1] * rel[1] + rel[2] * rel[2] + 1.0
    inv = lax.rsqrt(dist)
    cube = cells[3] * (inv * inv * inv)
    fifth = 3.0 * cube * (inv * inv)
    terms = [-(cube * rel[c]) for c in range(3)]
    for a, b in ((0, 0), (1, 1), (2, 2), (0, 1), (0, 2), (1, 2)):
        value = fifth * rel[a] * rel[b]
        if a == b:
            value = value - cube
        terms.append(value)
    terms = [jnp.sum(v, axis=0, keepdims=True) for v in terms]
    pad[...] = jnp.zeros((PL, PL), F32)
    for i, v in enumerate(terms):
        pad[i : i + 1, :] = v + pltpu.roll(v, 64, 1)
    back = pad[...].T
    field = [back[0:NB, i : i + 1] for i in range(3)]
    tide = [back[0:NB, 3 + i : 4 + i] for i in range(6)]
    offset = [pos[c] - centre[c] for c in range(3)]
    for c, (i, j, k) in enumerate(((0, 3, 4), (3, 1, 5), (4, 5, 2))):
        out_ref[c] = field[c] + tide[i] * offset[0] + tide[j] * offset[1] + tide[k] * offset[2]


def split3(v):
    high = v.astype(BF16).astype(F32)
    rest = v - high
    mid = rest.astype(BF16).astype(F32)
    return high, mid, rest - mid


def prep_kernel(y_ref, t0, t1, t2, t3, tall, tab, hold, sem):
    me = y_ref[0]
    wide = 2 * PL
    tiles = []
    for i, t in enumerate((t0, t1, t2, t3)):
        tall[i * NB : (i + 1) * NB] = t[0:NB]
        tiles.append(t[NB])
    left = lax.broadcasted_iota(I32, (4, PL), 1) < 64
    code, cnt = [], []
    for a, b in ((tiles[0], tiles[1]), (tiles[2], tiles[3])):
        code.append(jnp.where(left, a, pltpu.roll(b, 64, 1)))
        cnt.append(jnp.where(left, pltpu.roll(a, 64, 1), b))
    code = jnp.concatenate(code, axis=1).astype(I32)
    cnt = jnp.concatenate(cnt, axis=1)[0:1]
    lane = lax.broadcasted_iota(I32, (1, wide), 1)
    valid = (lane & 63) < NB
    flag = [jnp.where(((code[k : k + 1] >> 9) == me) & valid, 1.0, 0.0) for k in range(K)]
    local = [(code[k : k + 1] & 511).astype(F32) for k in range(K)]
    count = (flag[0] + flag[1]) + (flag[2] + flag[3])
    full = jnp.where(count > 2.5, 1.0, 0.0)
    half = jnp.where((count > 0.5) & (count < 2.5), 1.0, 0.0)
    group = lane >> 6
    mine = group == 0
    lists = [jnp.where(mine, 0.0, v) for v in (full, half)] + [jnp.where(mine, v, 0.0) for v in (full, half)]
    marks = jnp.concatenate(lists + [jnp.zeros((12, wide), F32)], axis=0).astype(BF16)
    a = lax.broadcasted_iota(I32, (wide, wide), 0)
    b = lax.broadcasted_iota(I32, (wide, wide), 1)
    before = jnp.dot(marks, jnp.where(a < b, 1.0, 0.0).astype(BF16), preferred_element_type=F32)
    sizes = [jnp.sum(v, axis=1, keepdims=True) for v in lists]
    place, begin = jnp.full((1, wide), -1.0, F32), jnp.zeros((1, 1), F32)
    for i, v in enumerate(lists):
        place = jnp.where(v > 0.5, begin + before[i : i + 1], place)
        begin = begin + sizes[i]
    moved = jnp.where(a == place.astype(I32), 1.0, 0.0).astype(BF16)
    bucket = lane & 63
    home = jnp.where(mine, bucket, (group - 1) * NB + bucket)
    slot, ins, outs = [], jnp.zeros((1, wide), F32), jnp.zeros((1, wide), F32)
    for k in range(K):
        slot.append(jnp.where(flag[k] > 0.5, ins, count + outs))
        ins, outs = ins + flag[k], outs + (1.0 - flag[k])
    fields = []
    for j in range(K):
        pick = jnp.zeros((1, wide), F32)
        for k in range(K):
            pick = pick + jnp.where(slot[k] == float(j), local[k], 0.0)
        fields.append(pick)
    fields += [cnt, home.astype(F32), count, (group * NB + bucket).astype(F32)]
    load = jnp.concatenate(fields, axis=0)
    high = load.astype(BF16).astype(F32)
    both = jnp.concatenate([high, load - high], axis=0).astype(BF16)
    out = lax.dot_general(both, moved, (((1,), (1,)), ((), ())), preferred_element_type=F32)
    out = out[0:8] + out[8:16]
    sizes = jnp.concatenate([jnp.broadcast_to(v, (1, wide)) for v in sizes + [begin] * 4], axis=0)
    hold[...] = jnp.concatenate([out, sizes], axis=0).astype(I32)
    copy = pltpu.make_async_copy(hold, tab, sem)
    copy.start()
    copy.wait()


def near_kernel(first, tab, tall, src_ref, *refs):
    outs, out_ref = refs[:-1], refs[-1]
    out_ref[...] = jnp.zeros(out_ref.shape, F32)
    sub4 = lax.broadcasted_iota(I32, (4, PL), 0)
    lane4 = lax.broadcasted_iota(I32, (4, PL), 1)
    spatial = sub4 < 3
    one = jnp.ones((4, PL), F32)
    zero4 = jnp.zeros((4, PL), F32)
    zero8 = jnp.zeros((8, PL), F32)

    def square(v):
        return jnp.sum(jnp.where(spatial, v * v, 0.0), axis=0, keepdims=True)

    def mix(a, b):
        return jnp.where(spatial, a, b)

    def stack(*v):
        return jnp.concatenate(v, axis=0).astype(BF16)

    def job(e, width):
        n = tab[6, e]
        t = tall[tab[7, e]]
        th, tm, tl = split3(t)
        qh, qm, ql = split3(square(t))
        u = stack(mix(th, one), mix(th, one), mix(tm, one), mix(tm, qh), mix(th, qm), mix(tl, ql), zero8)
        vs, gs = [], []
        for k in range(width):
            s = src_ref[tab[k, e]]
            flag = (k < n).astype(F32)
            sh, sm, sl = split3(-2.0 * s)
            qh, qm, ql = split3(square(s) + SOFT)
            vs.append(stack(mix(sh, qh), mix(sm, qm), mix(sh, ql), mix(sm, one), mix(sl, one), mix(sh, one), zero8))
            w = s[3:4] * flag
            gs.append(stack(*split3(mix(s * w, w)), zero4))
        v = jnp.concatenate(vs, axis=1)
        g = jnp.concatenate(gs, axis=1)
        dist = lax.dot_general(v, u, (((0,), (0,)), ((), ())), preferred_element_type=F32)
        inv = lax.rsqrt(dist)
        f = inv * inv * inv
        high = f.astype(BF16)
        low = (f - high.astype(F32)).astype(BF16)
        o = jnp.dot(g, jnp.concatenate([high, low], axis=1), preferred_element_type=F32)
        o = o[:, :PL] + o[:, PL:]
        a = o[0:4] + o[4:8] + o[8:12]
        out_ref[tab[5, e]] = jnp.where(lane4 < tab[4, e], a - t * a[3:4], 0.0)

    sizes = [tab[8 + i, 0] for i in range(4)]

    def run(begin, size, width, step):
        def body(i, _):
            for j in range(step):
                job(begin + jnp.minimum(step * i + j, size - 1), width)

        lax.fori_loop(0, (size + step - 1) // step, body, None)

    begin = jnp.int32(0) if first else sizes[0] + sizes[1]
    n_full, n_half = (sizes[0], sizes[1]) if first else (sizes[2], sizes[3])
    run(begin, n_full, 4, UNROLL)
    run(begin + n_full, n_half, 2, UNROLL // 2)
    for i, o in enumerate(outs):
        o[...] = out_ref[i * NB : (i + 1) * NB]


def final_kernel(cnt_ref, far_ref, p0, p1, p2, p3, out_ref):
    live = lax.broadcasted_iota(I32, (NB, PL), 1) < column_of(cnt_ref[...], NB)
    for c in range(3):
        near = (p0[:, c, :] + p1[:, c, :]) + (p2[:, c, :] + p3[:, c, :])
        out_ref[c] = jnp.where(live, far_ref[c] + near, 0.0)


def along_y(k):
    return [(NZ * y + z, NZ * ((y + k) % NY) + z) for y in range(NY) for z in range(NZ)]


def along_x(k):
    return [(2 * x + c, 2 * ((x + k) % NX) + c) for x in range(NX) for c in range(2)]


def call(kernel, outs, in_specs, out_specs, name, mib, scratch=()):
    return pl.pallas_call(
        kernel,
        out_shape=[jax.ShapeDtypeStruct(shape, dtype) for shape, dtype in outs],
        in_specs=in_specs,
        out_specs=out_specs,
        scratch_shapes=scratch,
        compiler_params=pltpu.CompilerParams(vmem_limit_bytes=mib * MIB),
        name=name,
    )


def per_device(positions, masses, counts, dest_ids, near_list, cell_list, cell_centers, cell_mass):
    pos = jnp.transpose(positions[0], (1, 0, 2))
    cnt = counts[0]
    src, tgt, cells = call(
        pack_kernel,
        (((NZ, NB, 4, PL), F32), ((NB + 1, 4, PL), F32), ((16, 4, PL), F32)),
        [pl.BlockSpec(memory_space=pltpu.HBM)] * 7,
        [vspec()] * 3,
        "pack",
        60,
        [
            pltpu.VMEM((3, NB, PL), F32),
            pltpu.VMEM((NB, PL), F32),
            pltpu.VMEM((1, NB), I32),
            pltpu.VMEM((1, NB), I32),
            pltpu.VMEM((K, NB), I32),
            pltpu.VMEM((3, 2048), F32),
            pltpu.VMEM((1, 2048), F32),
            pltpu.SemaphoreType.DMA((7,)),
        ],
    )(pos, masses[0], cnt, dest_ids, near_list[0].T, cell_centers, cell_mass[None])
    z_rows = [[NZ * y + z for z in range(NZ)] for y in range(NY)]
    window = lax.all_to_all(src, "space", 0, 0, axis_index_groups=z_rows, tiled=True)
    tgts = [tgt] + [lax.ppermute(tgt, "space", along_y(k)) for k in (1, -1, 2)]
    pair = jnp.stack([cells, lax.ppermute(cells, "slab", [(i, i ^ 1) for i in range(2 * NX)])])
    pairs = [pair] + [lax.ppermute(pair, "slab", along_x(k)) for k in (1, -1, 2)]
    me = (lax.axis_index("space") // NZ).astype(I32).reshape(1)
    place = lax.axis_index("slab").astype(I32).reshape(1)
    tall, tab = call(
        prep_kernel,
        (((NY * NB, 4, PL), F32), ((16, 2 * PL), I32)),
        [sspec()] + [vspec()] * 4,
        [vspec(), sspec()],
        "prep",
        8,
        [pltpu.VMEM((16, 2 * PL), I32), pltpu.SemaphoreType.DMA],
    )(me, *tgts)
    window = window.reshape(NZ * NB, 4, PL)

    def near(first, tab):
        count = NY - 1 if first else 1
        return call(
            functools.partial(near_kernel, first),
            (((NB, 4, PL), F32),) * count,
            [sspec()] + [vspec()] * 2,
            [vspec()] * count,
            "near",
            24,
            [pltpu.VMEM((count * NB, 4, PL), F32)],
        )(tab, tall, window)

    sent = near(True, tab)
    back = [lax.ppermute(v, "space", along_y(-k)) for v, k in zip(sent, (1, -1, 2))]
    tab, sent = lax.optimization_barrier((tab, sent))
    (own,) = near(False, tab)
    *pairs, own = lax.optimization_barrier((*pairs, own))
    (far,) = call(
        far_kernel,
        (((3, NB, PL), F32),),
        [sspec()] + [vspec()] * 7,
        [vspec()],
        "far",
        16,
        [pltpu.VMEM((PL, PL), F32)],
    )(place, pos, cnt, cell_list[0].T, *pairs)
    (out,) = call(
        final_kernel,
        (((3, NB, PL), F32),),
        [vspec()] * 6,
        [vspec()],
        "final",
        8,
    )(cnt, far, own, *back)
    return jnp.transpose(out, (1, 0, 2))[None]


def solution(mesh):
    in_specs = (
        P("slab", "space", None, None),
        P("slab", "space", None),
        P("slab", "space", None),
        P("slab", "space"),
        P("slab", "space", None),
        P("slab", "space", None),
        P(None, "slab"),
        P("slab"),
    )
    return jax.shard_map(
        per_device,
        mesh=mesh,
        in_specs=in_specs,
        out_specs=P("slab", "space", None, None),
        check_vma=False,
    )
```

```python
import functools

import jax
import jax.numpy as jnp
from jax import lax
from jax.experimental import pallas as pl
from jax.experimental.pallas import tpu as pltpu
from jax.sharding import PartitionSpec as P

NB = 48
PL = 128
K = 4
LC = 32
NY = 4
NZ = 8
NX = 4
SOFT = 0.01
UNROLL = 8
MIB = 1 << 20
F32 = jnp.float32
I32 = jnp.int32
BF16 = jnp.bfloat16
VMEM = pltpu.VMEM
SMEM = pltpu.SMEM


def vspec():
    return pl.BlockSpec(memory_space=VMEM)


def sspec():
    return pl.BlockSpec(memory_space=SMEM)


def column_of(row, n):
    square = jnp.broadcast_to(row, (n, n))
    diag = lax.broadcasted_iota(I32, (n, n), 0) == lax.broadcasted_iota(I32, (n, n), 1)
    return jnp.sum(jnp.where(diag, square, jnp.zeros_like(square)), axis=1, keepdims=True)


def pack_kernel(*refs):
    ins, (src_ref, tgt_ref, cell_ref), holds, sem = refs[:7], refs[7:10], refs[10:17], refs[17]
    copies = [pltpu.make_async_copy(ins[i], holds[i], sem.at[i]) for i in range(7)]
    for copy in copies:
        copy.start()
    for copy in copies:
        copy.wait()
    pos_ref, mass_ref, cnt_ref, dest_ref, near_ref, ctr_ref, cm_ref = holds
    counts = cnt_ref[...]
    cnt = column_of(counts, NB)
    near = near_ref[...]
    off = (near >= NB).astype(I32) + (near >= 2 * NB).astype(I32)
    dev = (dest_ref[...] + off - 1) & (NY * NZ - 1)
    code = (dev >> 3) * 512 + (dev & (NZ - 1)) * NB + (near - off * NB)
    gap = jnp.zeros((4, 64 - NB), I32)
    info = jnp.concatenate([code, gap, jnp.broadcast_to(counts, (4, NB)), gap], axis=1)
    lane = lax.broadcasted_iota(I32, (NB, PL), 1)
    weight = jnp.where(lane < cnt, mass_ref[...], 0.0)
    for c in range(3):
        value = pos_ref[c]
        tgt_ref[0:NB, c, :] = value
        for z in range(NZ):
            src_ref[z, :, c, :] = value
    for z in range(NZ):
        src_ref[z, :, 3, :] = weight
    tgt_ref[0:NB, 3, :] = jnp.zeros((NB, PL), F32)
    tgt_ref[NB] = info.astype(F32)
    for j in range(16):
        part = slice(j * PL, (j + 1) * PL)
        cell_ref[j, 0:3, :] = ctr_ref[:, part]
        cell_ref[j, 3:4, :] = cm_ref[0:1, part]


def far_kernel(place_ref, pos_ref, cnt_ref, list_ref, c0, c1, c2, c3, out_ref, pad):
    xs, cs = place_ref[0] >> 1, place_ref[0] & 1
    lane = lax.broadcasted_iota(I32, (NB, PL), 1)
    cnt = column_of(cnt_ref[...], NB)
    live = lane < cnt
    total = jnp.maximum(cnt, 1).astype(F32)
    pos = [pos_ref[c] for c in range(3)]
    centre = [jnp.sum(jnp.where(live, v, 0.0), axis=1, keepdims=True) / total for v in pos]
    diag = lax.broadcasted_iota(I32, (NB, PL), 0) == (lane & 63)
    ctr = [jnp.sum(jnp.where(diag, v, 0.0), axis=0, keepdims=True) for v in centre]
    wide = jnp.concatenate([list_ref[...], jnp.zeros((LC, PL - NB), I32)], axis=1)
    twice = wide + pltpu.roll(wide, 64, 1)
    half = lax.broadcasted_iota(I32, (1, PL), 1) < 64
    ids = [jnp.where(half, twice[2 * j : 2 * j + 1], twice[2 * j + 1 : 2 * j + 2]) for j in range(LC // 2)]
    ids = jnp.concatenate(ids, axis=0)
    slab = ids >> 11
    dx = ((slab >> 1) - xs) & (NX - 1)
    order = jnp.where(dx == 3, 1, jnp.where(dx == 0, 0, dx + 1))
    rows = (order * 2 + ((slab & 1) ^ cs)) * 16 + ((ids >> 7) & 15)
    lanes = ids & (PL - 1)
    tables = []
    for c in range(4):
        whole = jnp.concatenate([ref[i, :, c, :] for ref in (c0, c1, c2, c3) for i in range(2)], axis=0)
        whole = whole.T
        high = whole.astype(BF16)
        low = (whole - high.astype(F32)).astype(BF16)
        tables.append(jnp.concatenate([high, low], axis=1))
    tables = jnp.concatenate(tables, axis=0)
    sub = lax.broadcasted_iota(I32, (PL, 2 * PL), 0)
    got = [[] for _ in range(4)]
    for j in range(0, LC // 2, 2):
        r2 = jnp.concatenate([rows[j : j + 1], rows[j + 1 : j + 2]], axis=1)
        l2 = jnp.concatenate([lanes[j : j + 1], lanes[j + 1 : j + 2]], axis=1)
        hot = jnp.where(sub == r2, 1.0, 0.0).astype(BF16)
        hot = jnp.concatenate([hot, hot], axis=0)
        found = jnp.dot(tables, hot, preferred_element_type=F32)
        pick = sub == l2
        for c in range(4):
            value = jnp.sum(jnp.where(pick, found[c * PL : (c + 1) * PL], 0.0), axis=0, keepdims=True)
            got[c] += [value[:, :PL], value[:, PL:]]
    cells = [jnp.concatenate(v, axis=0) for v in got]
    rel = [ctr[c] - cells[c] for c in range(3)]
    dist = rel[0] * rel[0] + rel[1] * rel[1] + rel[2] * rel[2] + 1.0
    inv = lax.rsqrt(dist)
    cube = cells[3] * (inv * inv * inv)
    fifth = 3.0 * cube * (inv * inv)
    terms = [-(cube * rel[c]) for c in range(3)]
    for a, b in ((0, 0), (1, 1), (2, 2), (0, 1), (0, 2), (1, 2)):
        value = fifth * rel[a] * rel[b]
        if a == b:
            value = value - cube
        terms.append(value)
    terms = [jnp.sum(v, axis=0, keepdims=True) for v in terms]
    pad[...] = jnp.zeros((PL, PL), F32)
    for i, v in enumerate(terms):
        pad[i : i + 1, :] = v + pltpu.roll(v, 64, 1)
    back = pad[...].T
    field = [back[0:NB, i : i + 1] for i in range(3)]
    tide = [back[0:NB, 3 + i : 4 + i] for i in range(6)]
    offset = [pos[c] - centre[c] for c in range(3)]
    for c, (i, j, k) in enumerate(((0, 3, 4), (3, 1, 5), (4, 5, 2))):
        out_ref[c] = field[c] + tide[i] * offset[0] + tide[j] * offset[1] + tide[k] * offset[2]


def split3(v):
    high = v.astype(BF16).astype(F32)
    rest = v - high
    mid = rest.astype(BF16).astype(F32)
    return high, mid, rest - mid


def prep_kernel(y_ref, t0, t1, t2, t3, tall, tab, hold, sem):
    me = y_ref[0]
    wide = 2 * PL
    tiles = []
    for i, t in enumerate((t0, t1, t2, t3)):
        tall[i * NB : (i + 1) * NB] = t[0:NB]
        tiles.append(t[NB])
    left = lax.broadcasted_iota(I32, (4, PL), 1) < 64
    code, cnt = [], []
    for a, b in ((tiles[0], tiles[1]), (tiles[2], tiles[3])):
        code.append(jnp.where(left, a, pltpu.roll(b, 64, 1)))
        cnt.append(jnp.where(left, pltpu.roll(a, 64, 1), b))
    code = jnp.concatenate(code, axis=1).astype(I32)
    cnt = jnp.concatenate(cnt, axis=1)[0:1]
    lane = lax.broadcasted_iota(I32, (1, wide), 1)
    valid = (lane & 63) < NB
    flag = [jnp.where(((code[k : k + 1] >> 9) == me) & valid, 1.0, 0.0) for k in range(K)]
    local = [(code[k : k + 1] & 511).astype(F32) for k in range(K)]
    count = (flag[0] + flag[1]) + (flag[2] + flag[3])
    full = jnp.where(count > 2.5, 1.0, 0.0)
    half = jnp.where((count > 0.5) & (count < 2.5), 1.0, 0.0)
    group = lane >> 6
    mine = group == 0
    lists = [jnp.where(mine, 0.0, v) for v in (full, half)] + [jnp.where(mine, v, 0.0) for v in (full, half)]
    marks = jnp.concatenate(lists + [jnp.zeros((12, wide), F32)], axis=0).astype(BF16)
    a = lax.broadcasted_iota(I32, (wide, wide), 0)
    b = lax.broadcasted_iota(I32, (wide, wide), 1)
    before = jnp.dot(marks, jnp.where(a < b, 1.0, 0.0).astype(BF16), preferred_element_type=F32)
    sizes = [jnp.sum(v, axis=1, keepdims=True) for v in lists]
    place, begin = jnp.full((1, wide), -1.0, F32), jnp.zeros((1, 1), F32)
    for i, v in enumerate(lists):
        place = jnp.where(v > 0.5, begin + before[i : i + 1], place)
        begin = begin + sizes[i]
    moved = jnp.where(a == place.astype(I32), 1.0, 0.0).astype(BF16)
    bucket = lane & 63
    home = jnp.where(mine, bucket, (group - 1) * NB + bucket)
    slot, ins, outs = [], jnp.zeros((1, wide), F32), jnp.zeros((1, wide), F32)
    for k in range(K):
        slot.append(jnp.where(flag[k] > 0.5, ins, count + outs))
        ins, outs = ins + flag[k], outs + (1.0 - flag[k])
    fields = []
    for j in range(K):
        pick = jnp.zeros((1, wide), F32)
        for k in range(K):
            pick = pick + jnp.where(slot[k] == float(j), local[k], 0.0)
        fields.append(pick)
    fields += [cnt, home.astype(F32), count, (group * NB + bucket).astype(F32)]
    load = jnp.concatenate(fields, axis=0)
    high = load.astype(BF16).astype(F32)
    both = jnp.concatenate([high, load - high], axis=0).astype(BF16)
    out = lax.dot_general(both, moved, (((1,), (1,)), ((), ())), preferred_element_type=F32)
    out = out[0:8] + out[8:16]
    sizes = jnp.concatenate([jnp.broadcast_to(v, (1, wide)) for v in sizes + [begin] * 4], axis=0)
    hold[...] = jnp.concatenate([out, sizes], axis=0).astype(I32)
    copy = pltpu.make_async_copy(hold, tab, sem)
    copy.start()
    copy.wait()


def near_kernel(first, tab, tall, src_ref, *refs):
    outs, out_ref = refs[:-1], refs[-1]
    out_ref[...] = jnp.zeros(out_ref.shape, F32)
    sub4 = lax.broadcasted_iota(I32, (4, PL), 0)
    lane4 = lax.broadcasted_iota(I32, (4, PL), 1)
    spatial = sub4 < 3
    one = jnp.ones((4, PL), F32)
    zero4 = jnp.zeros((4, PL), F32)
    zero8 = jnp.zeros((8, PL), F32)

    def square(v):
        return jnp.sum(jnp.where(spatial, v * v, 0.0), axis=0, keepdims=True)

    def mix(a, b):
        return jnp.where(spatial, a, b)

    def stack(*v):
        return jnp.concatenate(v, axis=0).astype(BF16)

    def job(e, width):
        n = tab[6, e]
        t = tall[tab[7, e]]
        th, tm, tl = split3(t)
        qh, qm, ql = split3(square(t))
        u = stack(mix(th, one), mix(th, one), mix(tm, one), mix(tm, qh), mix(th, qm), mix(tl, ql), zero8)
        vs, gs = [], []
        for k in range(width):
            s = src_ref[tab[k, e]]
            flag = (k < n).astype(F32)
            sh, sm, sl = split3(-2.0 * s)
            qh, qm, ql = split3(square(s) + SOFT)
            vs.append(stack(mix(sh, qh), mix(sm, qm), mix(sh, ql), mix(sm, one), mix(sl, one), mix(sh, one), zero8))
            w = s[3:4] * flag
            gs.append(stack(*split3(mix(s * w, w)), zero4))
        v = jnp.concatenate(vs, axis=1)
        g = jnp.concatenate(gs, axis=1)
        dist = lax.dot_general(v, u, (((0,), (0,)), ((), ())), preferred_element_type=F32)
        inv = lax.rsqrt(dist)
        f = inv * inv * inv
        high = f.astype(BF16)
        low = (f - high.astype(F32)).astype(BF16)
        o = jnp.dot(g, jnp.concatenate([high, low], axis=1), preferred_element_type=F32)
        o = o[:, :PL] + o[:, PL:]
        a = o[0:4] + o[4:8] + o[8:12]
        out_ref[tab[5, e]] = jnp.where(lane4 < tab[4, e], a - t * a[3:4], 0.0)

    sizes = [tab[8 + i, 0] for i in range(4)]

    def run(begin, size, width, step):
        def body(i, _):
            for j in range(step):
                job(begin + jnp.minimum(step * i + j, size - 1), width)

        lax.fori_loop(0, (size + step - 1) // step, body, None)

    begin = jnp.int32(0) if first else sizes[0] + sizes[1]
    n_full, n_half = (sizes[0], sizes[1]) if first else (sizes[2], sizes[3])
    run(begin, n_full, 4, UNROLL)
    run(begin + n_full, n_half, 2, UNROLL // 2)
    for i, o in enumerate(outs):
        o[...] = out_ref[i * NB : (i + 1) * NB]


def final_kernel(cnt_ref, far_ref, p0, p1, p2, p3, out_ref):
    live = lax.broadcasted_iota(I32, (NB, PL), 1) < column_of(cnt_ref[...], NB)
    for c in range(3):
        near = (p0[:, c, :] + p1[:, c, :]) + (p2[:, c, :] + p3[:, c, :])
        out_ref[c] = jnp.where(live, far_ref[c] + near, 0.0)


def along_y(k):
    return [(NZ * y + z, NZ * ((y + k) % NY) + z) for y in range(NY) for z in range(NZ)]


def along_x(k):
    return [(2 * x + c, 2 * ((x + k) % NX) + c) for x in range(NX) for c in range(2)]


def call(kernel, outs, in_specs, out_specs, name, mib, scratch=()):
    return pl.pallas_call(
        kernel,
        out_shape=[jax.ShapeDtypeStruct(shape, dtype) for shape, dtype in outs],
        in_specs=in_specs,
        out_specs=out_specs,
        scratch_shapes=scratch,
        compiler_params=pltpu.CompilerParams(vmem_limit_bytes=mib * MIB),
        name=name,
    )


def per_device(positions, masses, counts, dest_ids, near_list, cell_list, cell_centers, cell_mass):
    pos = jnp.transpose(positions[0], (1, 0, 2))
    cnt = counts[0]
    src, tgt, cells = call(
        pack_kernel,
        (((NZ, NB, 4, PL), F32), ((NB + 1, 4, PL), F32), ((16, 4, PL), F32)),
        [pl.BlockSpec(memory_space=pltpu.HBM)] * 7,
        [vspec()] * 3,
        "pack",
        60,
        [
            pltpu.VMEM((3, NB, PL), F32),
            pltpu.VMEM((NB, PL), F32),
            pltpu.VMEM((1, NB), I32),
            pltpu.VMEM((1, NB), I32),
            pltpu.VMEM((K, NB), I32),
            pltpu.VMEM((3, 2048), F32),
            pltpu.VMEM((1, 2048), F32),
            pltpu.SemaphoreType.DMA((7,)),
        ],
    )(pos, masses[0], cnt, dest_ids, near_list[0].T, cell_centers, cell_mass[None])
    z_rows = [[NZ * y + z for z in range(NZ)] for y in range(NY)]
    window = lax.all_to_all(src, "space", 0, 0, axis_index_groups=z_rows, tiled=True)
    tgts = [tgt] + [lax.ppermute(tgt, "space", along_y(k)) for k in (1, -1, 2)]
    pair = jnp.stack([cells, lax.ppermute(cells, "slab", [(i, i ^ 1) for i in range(2 * NX)])])
    pairs = [pair] + [lax.ppermute(pair, "slab", along_x(k)) for k in (1, -1, 2)]
    me = (lax.axis_index("space") // NZ).astype(I32).reshape(1)
    place = lax.axis_index("slab").astype(I32).reshape(1)
    tall, tab = call(
        prep_kernel,
        (((NY * NB, 4, PL), F32), ((16, 2 * PL), I32)),
        [sspec()] + [vspec()] * 4,
        [vspec(), sspec()],
        "prep",
        8,
        [pltpu.VMEM((16, 2 * PL), I32), pltpu.SemaphoreType.DMA],
    )(me, *tgts)
    (far,) = call(
        far_kernel,
        (((3, NB, PL), F32),),
        [sspec()] + [vspec()] * 7,
        [vspec()],
        "far",
        16,
        [pltpu.VMEM((PL, PL), F32)],
    )(place, pos, cnt, cell_list[0].T, *pairs)
    tall, tab, far = lax.optimization_barrier((tall, tab, far))
    window = window.reshape(NZ * NB, 4, PL)

    def near(first, tab):
        count = NY - 1 if first else 1
        return call(
            functools.partial(near_kernel, first),
            (((NB, 4, PL), F32),) * count,
            [sspec()] + [vspec()] * 2,
            [vspec()] * count,
            "near",
            24,
            [pltpu.VMEM((count * NB, 4, PL), F32)],
        )(tab, tall, window)

    sent = near(True, tab)
    back = [lax.ppermute(v, "space", along_y(-k)) for v, k in zip(sent, (1, -1, 2))]
    tab, sent = lax.optimization_barrier((tab, sent))
    (own,) = near(False, tab)
    (out,) = call(
        final_kernel,
        (((3, NB, PL), F32),),
        [vspec()] * 6,
        [vspec()],
        "final",
        8,
    )(cnt, far, own, *back)
    return jnp.transpose(out, (1, 0, 2))[None]


def solution(mesh):
    in_specs = (
        P("slab", "space", None, None),
        P("slab", "space", None),
        P("slab", "space", None),
        P("slab", "space"),
        P("slab", "space", None),
        P("slab", "space", None),
        P(None, "slab"),
        P("slab"),
    )
    return jax.shard_map(
        per_device,
        mesh=mesh,
        in_specs=in_specs,
        out_specs=P("slab", "space", None, None),
        check_vma=False,
    )
```

```python
import functools

import jax
import jax.numpy as jnp
from jax import lax
from jax.experimental import pallas as pl
from jax.experimental.pallas import tpu as pltpu
from jax.sharding import PartitionSpec as P

NB = 48
PL = 128
K = 4
LC = 32
NY = 4
NZ = 8
NX = 4
SOFT = 0.01
UNROLL = 8
MIB = 1 << 20
TILES = 36
F32 = jnp.float32
I32 = jnp.int32
BF16 = jnp.bfloat16
VMEM = pltpu.VMEM
SMEM = pltpu.SMEM


def vspec():
    return pl.BlockSpec(memory_space=VMEM)


def sspec():
    return pl.BlockSpec(memory_space=SMEM)


def column_of(row, n):
    square = jnp.broadcast_to(row, (n, n))
    diag = lax.broadcasted_iota(I32, (n, n), 0) == lax.broadcasted_iota(I32, (n, n), 1)
    return jnp.sum(jnp.where(diag, square, jnp.zeros_like(square)), axis=1, keepdims=True)


def pack_kernel(*refs):
    ins, (src_ref, tgt_ref, cell_ref), holds = refs[:7], refs[7:10], refs[10:18]
    full, sem = refs[18:]
    copies = [pltpu.make_async_copy(ins[i], holds[i], sem.at[i]) for i in range(7)]
    copies.append(pltpu.make_async_copy(ins[2], holds[7], sem.at[7]))
    for copy in copies:
        copy.start()
    for copy in copies:
        copy.wait()
    pos_ref, mass_ref, cnt_ref, dest_ref, near_ref, ctr_ref, cm_ref, cnt_smem = holds
    counts = cnt_ref[...]
    cnt = column_of(counts, NB)
    near = near_ref[...]
    off = (near >= NB).astype(I32) + (near >= 2 * NB).astype(I32)
    dev = (dest_ref[...] + off - 1) & (NY * NZ - 1)
    code = (dev >> 3) * 512 + (dev & (NZ - 1)) * 64 + (near - off * NB)
    gap = jnp.zeros((4, 64 - NB), I32)
    info = jnp.concatenate([code, gap, jnp.broadcast_to(counts, (4, NB)), gap], axis=1)
    lane = lax.broadcasted_iota(I32, (NB, PL), 1)
    weight = jnp.where(lane < cnt, mass_ref[...], 0.0)
    for c in range(3):
        value = pos_ref[c]
        tgt_ref[0:NB, c, :] = value
        full[:, c, :] = value
    full[:, 3, :] = weight
    lane4 = lax.broadcasted_iota(I32, (4, PL), 1)
    carry, begin = jnp.zeros((4, PL), F32), jnp.int32(0)
    for b in range(NB):
        shift, tile = begin & (PL - 1), begin >> 7
        turned = pltpu.roll(full[b], shift, 1)[0:4]
        merged = jnp.where(lane4 >= shift, turned, carry)
        src_ref[0, tile] = merged
        begin = begin + cnt_smem[0, b]
        carry = jnp.where((begin >> 7) != tile, turned, merged)
    square = (NB, NB)
    earlier = lax.broadcasted_iota(I32, square, 0) < lax.broadcasted_iota(I32, square, 1)
    starts = jnp.sum(jnp.where(earlier, cnt, 0), axis=0, keepdims=True)
    places = jnp.concatenate([starts, gap[0:1], counts, gap[0:1]], axis=1)
    src_ref[0, TILES] = jnp.broadcast_to(places, (4, PL)).astype(F32)
    for z in range(1, NZ):
        src_ref[z] = src_ref[0]
    tgt_ref[0:NB, 3, :] = jnp.zeros((NB, PL), F32)
    tgt_ref[NB] = info.astype(F32)
    for j in range(16):
        part = slice(j * PL, (j + 1) * PL)
        cell_ref[j, 0:3, :] = ctr_ref[:, part]
        cell_ref[j, 3:4, :] = cm_ref[0:1, part]


def far_kernel(place_ref, pos_ref, cnt_ref, list_ref, c0, c1, c2, c3, out_ref, pad):
    xs, cs = place_ref[0] >> 1, place_ref[0] & 1
    lane = lax.broadcasted_iota(I32, (NB, PL), 1)
    cnt = column_of(cnt_ref[...], NB)
    live = lane < cnt
    total = jnp.maximum(cnt, 1).astype(F32)
    pos = [pos_ref[c] for c in range(3)]
    centre = [jnp.sum(jnp.where(live, v, 0.0), axis=1, keepdims=True) / total for v in pos]
    diag = lax.broadcasted_iota(I32, (NB, PL), 0) == (lane & 63)
    ctr = [jnp.sum(jnp.where(diag, v, 0.0), axis=0, keepdims=True) for v in centre]
    wide = jnp.concatenate([list_ref[...], jnp.zeros((LC, PL - NB), I32)], axis=1)
    twice = wide + pltpu.roll(wide, 64, 1)
    half = lax.broadcasted_iota(I32, (1, PL), 1) < 64
    ids = [jnp.where(half, twice[2 * j : 2 * j + 1], twice[2 * j + 1 : 2 * j + 2]) for j in range(LC // 2)]
    ids = jnp.concatenate(ids, axis=0)
    slab = ids >> 11
    dx = ((slab >> 1) - xs) & (NX - 1)
    order = jnp.where(dx == 3, 1, jnp.where(dx == 0, 0, dx + 1))
    rows = (order * 2 + ((slab & 1) ^ cs)) * 16 + ((ids >> 7) & 15)
    lanes = ids & (PL - 1)
    tables = []
    for c in range(4):
        whole = jnp.concatenate([ref[i, :, c, :] for ref in (c0, c1, c2, c3) for i in range(2)], axis=0)
        whole = whole.T
        high = whole.astype(BF16)
        low = (whole - high.astype(F32)).astype(BF16)
        tables.append(jnp.concatenate([high, low], axis=1))
    tables = jnp.concatenate(tables, axis=0)
    sub = lax.broadcasted_iota(I32, (PL, 2 * PL), 0)
    got = [[] for _ in range(4)]
    for j in range(0, LC // 2, 2):
        r2 = jnp.concatenate([rows[j : j + 1], rows[j + 1 : j + 2]], axis=1)
        l2 = jnp.concatenate([lanes[j : j + 1], lanes[j + 1 : j + 2]], axis=1)
        hot = jnp.where(sub == r2, 1.0, 0.0).astype(BF16)
        hot = jnp.concatenate([hot, hot], axis=0)
        found = jnp.dot(tables, hot, preferred_element_type=F32)
        pick = sub == l2
        for c in range(4):
            value = jnp.sum(jnp.where(pick, found[c * PL : (c + 1) * PL], 0.0), axis=0, keepdims=True)
            got[c] += [value[:, :PL], value[:, PL:]]
    cells = [jnp.concatenate(v, axis=0) for v in got]
    rel = [ctr[c] - cells[c] for c in range(3)]
    dist = rel[0] * rel[0] + rel[1] * rel[1] + rel[2] * rel[2] + 1.0
    inv = lax.rsqrt(dist)
    cube = cells[3] * (inv * inv * inv)
    fifth = 3.0 * cube * (inv * inv)
    terms = [-(cube * rel[c]) for c in range(3)]
    for a, b in ((0, 0), (1, 1), (2, 2), (0, 1), (0, 2), (1, 2)):
        value = fifth * rel[a] * rel[b]
        if a == b:
            value = value - cube
        terms.append(value)
    terms = [jnp.sum(v, axis=0, keepdims=True) for v in terms]
    pad[...] = jnp.zeros((PL, PL), F32)
    for i, v in enumerate(terms):
        pad[i : i + 1, :] = v + pltpu.roll(v, 64, 1)
    back = pad[...].T
    field = [back[0:NB, i : i + 1] for i in range(3)]
    tide = [back[0:NB, 3 + i : 4 + i] for i in range(6)]
    offset = [pos[c] - centre[c] for c in range(3)]
    for c, (i, j, k) in enumerate(((0, 3, 4), (3, 1, 5), (4, 5, 2))):
        out_ref[c] = field[c] + tide[i] * offset[0] + tide[j] * offset[1] + tide[k] * offset[2]


def split3(v):
    high = v.astype(BF16).astype(F32)
    rest = v - high
    mid = rest.astype(BF16).astype(F32)
    return high, mid, rest - mid


def prep_kernel(y_ref, t0, t1, t2, t3, tall, tab, hold, sem):
    me = y_ref[0]
    wide = 2 * PL
    tiles = []
    for i, t in enumerate((t0, t1, t2, t3)):
        tall[i * NB : (i + 1) * NB] = t[0:NB]
        tiles.append(t[NB])
    left = lax.broadcasted_iota(I32, (4, PL), 1) < 64
    code, cnt = [], []
    for a, b in ((tiles[0], tiles[1]), (tiles[2], tiles[3])):
        code.append(jnp.where(left, a, pltpu.roll(b, 64, 1)))
        cnt.append(jnp.where(left, pltpu.roll(a, 64, 1), b))
    code = jnp.concatenate(code, axis=1).astype(I32)
    cnt = jnp.concatenate(cnt, axis=1)[0:1]
    lane = lax.broadcasted_iota(I32, (1, wide), 1)
    valid = (lane & 63) < NB
    flag = [jnp.where(((code[k : k + 1] >> 9) == me) & valid, 1.0, 0.0) for k in range(K)]
    local = [(code[k : k + 1] & 511).astype(F32) for k in range(K)]
    count = (flag[0] + flag[1]) + (flag[2] + flag[3])
    full = jnp.where(count > 2.5, 1.0, 0.0)
    half = jnp.where((count > 0.5) & (count < 2.5), 1.0, 0.0)
    group = lane >> 6
    mine = group == 0
    lists = [jnp.where(mine, 0.0, v) for v in (full, half)] + [jnp.where(mine, v, 0.0) for v in (full, half)]
    marks = jnp.concatenate(lists + [jnp.zeros((12, wide), F32)], axis=0).astype(BF16)
    a = lax.broadcasted_iota(I32, (wide, wide), 0)
    b = lax.broadcasted_iota(I32, (wide, wide), 1)
    before = jnp.dot(marks, jnp.where(a < b, 1.0, 0.0).astype(BF16), preferred_element_type=F32)
    sizes = [jnp.sum(v, axis=1, keepdims=True) for v in lists]
    place, begin = jnp.full((1, wide), -1.0, F32), jnp.zeros((1, 1), F32)
    for i, v in enumerate(lists):
        place = jnp.where(v > 0.5, begin + before[i : i + 1], place)
        begin = begin + sizes[i]
    moved = jnp.where(a == place.astype(I32), 1.0, 0.0).astype(BF16)
    bucket = lane & 63
    home = jnp.where(mine, bucket, (group - 1) * NB + bucket)
    slot, ins, outs = [], jnp.zeros((1, wide), F32), jnp.zeros((1, wide), F32)
    for k in range(K):
        slot.append(jnp.where(flag[k] > 0.5, ins, count + outs))
        ins, outs = ins + flag[k], outs + (1.0 - flag[k])
    fields = []
    for j in range(K):
        pick = jnp.zeros((1, wide), F32)
        for k in range(K):
            pick = pick + jnp.where(slot[k] == float(j), local[k], 0.0)
        fields.append(pick)
    fields += [cnt, home.astype(F32), count, (group * NB + bucket).astype(F32)]
    load = jnp.concatenate(fields, axis=0)
    high = load.astype(BF16).astype(F32)
    both = jnp.concatenate([high, load - high], axis=0).astype(BF16)
    out = lax.dot_general(both, moved, (((1,), (1,)), ((), ())), preferred_element_type=F32)
    out = out[0:8] + out[8:16]
    sizes = jnp.concatenate([jnp.broadcast_to(v, (1, wide)) for v in sizes + [begin] * 4], axis=0)
    hold[...] = jnp.concatenate([out, sizes], axis=0).astype(I32)
    copy = pltpu.make_async_copy(hold, tab, sem)
    copy.start()
    copy.wait()


def near_kernel(first, tab, tall, src_ref, *refs):
    outs, (out_ref, hold, spots, sem) = refs[:-4], refs[-4:]
    for z in range(NZ):
        hold[z : z + 1, :] = src_ref[z * (TILES + 1) + TILES][0:1].astype(I32)
    copy = pltpu.make_async_copy(hold, spots, sem)
    copy.start()
    out_ref[...] = jnp.zeros(out_ref.shape, F32)
    copy.wait()
    lane1 = lax.broadcasted_iota(I32, (1, PL), 1)
    sub4 = lax.broadcasted_iota(I32, (4, PL), 0)
    lane4 = lax.broadcasted_iota(I32, (4, PL), 1)
    spatial = sub4 < 3
    one = jnp.ones((4, PL), F32)
    zero4 = jnp.zeros((4, PL), F32)
    zero8 = jnp.zeros((8, PL), F32)

    def square(v):
        return jnp.sum(jnp.where(spatial, v * v, 0.0), axis=0, keepdims=True)

    def mix(a, b):
        return jnp.where(spatial, a, b)

    def stack(*v):
        return jnp.concatenate(v, axis=0).astype(BF16)

    def job(e, width):
        n = tab[6, e]
        t = tall[tab[7, e]]
        th, tm, tl = split3(t)
        qh, qm, ql = split3(square(t))
        u = stack(mix(th, one), mix(th, one), mix(tm, one), mix(tm, qh), mix(th, qm), mix(tl, ql), zero8)
        vs, gs = [], []
        for k in range(width):
            z, bucket = tab[k, e] >> 6, tab[k, e] & 63
            begin = spots[z, bucket]
            shift = begin & (PL - 1)
            tile = z * (TILES + 1) + (begin >> 7)
            s = jnp.concatenate([src_ref[tile], src_ref[tile + 1]], axis=0)
            s = pltpu.roll(s, (PL - shift) & (PL - 1), 1)
            s = jnp.where(lane4 < PL - shift, s[0:4], s[4:8])
            live = jnp.where(k < n, spots[z, 64 + bucket], 0)
            sh, sm, sl = split3(-2.0 * s)
            qh, qm, ql = split3(square(s) + SOFT)
            vs.append(stack(mix(sh, qh), mix(sm, qm), mix(sh, ql), mix(sm, one), mix(sl, one), mix(sh, one), zero8))
            w = jnp.where(lane1 < live, s[3:4], 0.0)
            gs.append(stack(*split3(mix(s * w, w)), zero4))
        v = jnp.concatenate(vs, axis=1)
        g = jnp.concatenate(gs, axis=1)
        dist = lax.dot_general(v, u, (((0,), (0,)), ((), ())), preferred_element_type=F32)
        inv = lax.rsqrt(dist)
        f = inv * inv * inv
        high = f.astype(BF16)
        low = (f - high.astype(F32)).astype(BF16)
        o = jnp.dot(g, jnp.concatenate([high, low], axis=1), preferred_element_type=F32)
        o = o[:, :PL] + o[:, PL:]
        a = o[0:4] + o[4:8] + o[8:12]
        out_ref[tab[5, e]] = jnp.where(lane4 < tab[4, e], a - t * a[3:4], 0.0)

    sizes = [tab[8 + i, 0] for i in range(4)]

    def run(begin, size, width, step):
        def body(i, _):
            for j in range(step):
                job(begin + jnp.minimum(step * i + j, size - 1), width)

        lax.fori_loop(0, (size + step - 1) // step, body, None)

    begin = jnp.int32(0) if first else sizes[0] + sizes[1]
    n_full, n_half = (sizes[0], sizes[1]) if first else (sizes[2], sizes[3])
    run(begin, n_full, 4, UNROLL)
    run(begin + n_full, n_half, 2, UNROLL // 2)
    for i, o in enumerate(outs):
        for c in range(3):
            o[c] = out_ref[i * NB : (i + 1) * NB, c, :]


def final_kernel(cnt_ref, far_ref, p0, p1, p2, p3, out_ref):
    live = lax.broadcasted_iota(I32, (NB, PL), 1) < column_of(cnt_ref[...], NB)
    for c in range(3):
        near = (p0[c] + p1[c]) + (p2[c] + p3[c])
        out_ref[c] = jnp.where(live, far_ref[c] + near, 0.0)


def along_y(k):
    return [(NZ * y + z, NZ * ((y + k) % NY) + z) for y in range(NY) for z in range(NZ)]


def along_x(k):
    return [(2 * x + c, 2 * ((x + k) % NX) + c) for x in range(NX) for c in range(2)]


def call(kernel, outs, in_specs, out_specs, name, mib, scratch=()):
    return pl.pallas_call(
        kernel,
        out_shape=[jax.ShapeDtypeStruct(shape, dtype) for shape, dtype in outs],
        in_specs=in_specs,
        out_specs=out_specs,
        scratch_shapes=scratch,
        compiler_params=pltpu.CompilerParams(vmem_limit_bytes=mib * MIB),
        name=name,
    )


def per_device(positions, masses, counts, dest_ids, near_list, cell_list, cell_centers, cell_mass):
    pos = jnp.transpose(positions[0], (1, 0, 2))
    cnt = counts[0]
    src, tgt, cells = call(
        pack_kernel,
        (((NZ, TILES + 1, 4, PL), F32), ((NB + 1, 4, PL), F32), ((16, 4, PL), F32)),
        [pl.BlockSpec(memory_space=pltpu.HBM)] * 7,
        [vspec()] * 3,
        "pack",
        60,
        [
            pltpu.VMEM((3, NB, PL), F32),
            pltpu.VMEM((NB, PL), F32),
            pltpu.VMEM((1, NB), I32),
            pltpu.VMEM((1, NB), I32),
            pltpu.VMEM((K, NB), I32),
            pltpu.VMEM((3, 2048), F32),
            pltpu.VMEM((1, 2048), F32),
            pltpu.SMEM((1, NB), I32),
            pltpu.VMEM((NB, 8, PL), F32),
            pltpu.SemaphoreType.DMA((8,)),
        ],
    )(pos, masses[0], cnt, dest_ids, near_list[0].T, cell_centers, cell_mass[None])
    z_rows = [[NZ * y + z for z in range(NZ)] for y in range(NY)]
    window = lax.all_to_all(src, "space", 0, 0, axis_index_groups=z_rows, tiled=True)
    tgts = [tgt] + [lax.ppermute(tgt, "space", along_y(k)) for k in (1, -1, 2)]
    pair = jnp.stack([cells, lax.ppermute(cells, "slab", [(i, i ^ 1) for i in range(2 * NX)])])
    pairs = [pair] + [lax.ppermute(pair, "slab", along_x(k)) for k in (1, -1, 2)]
    me = (lax.axis_index("space") // NZ).astype(I32).reshape(1)
    place = lax.axis_index("slab").astype(I32).reshape(1)
    tall, tab = call(
        prep_kernel,
        (((NY * NB, 4, PL), F32), ((16, 2 * PL), I32)),
        [sspec()] + [vspec()] * 4,
        [vspec(), sspec()],
        "prep",
        8,
        [pltpu.VMEM((16, 2 * PL), I32), pltpu.SemaphoreType.DMA],
    )(me, *tgts)
    (far,) = call(
        far_kernel,
        (((3, NB, PL), F32),),
        [sspec()] + [vspec()] * 7,
        [vspec()],
        "far",
        16,
        [pltpu.VMEM((PL, PL), F32)],
    )(place, pos, cnt, cell_list[0].T, *pairs)
    tall, tab, far = lax.optimization_barrier((tall, tab, far))
    window = window.reshape(NZ * (TILES + 1), 4, PL)

    def near(first, tab):
        count = NY - 1 if first else 1
        return call(
            functools.partial(near_kernel, first),
            (((3, NB, PL), F32),) * count,
            [sspec()] + [vspec()] * 2,
            [vspec()] * count,
            "near",
            24,
            [
                pltpu.VMEM((count * NB, 4, PL), F32),
                pltpu.VMEM((NZ, PL), I32),
                pltpu.SMEM((NZ, PL), I32),
                pltpu.SemaphoreType.DMA,
            ],
        )(tab, tall, window)

    sent = near(True, tab)
    back = [lax.ppermute(v, "space", along_y(-k)) for v, k in zip(sent, (1, -1, 2))]
    tab, sent = lax.optimization_barrier((tab, sent))
    (own,) = near(False, tab)
    (out,) = call(
        final_kernel,
        (((3, NB, PL), F32),),
        [vspec()] * 6,
        [vspec()],
        "final",
        8,
    )(cnt, far, own, *back)
    return jnp.transpose(out, (1, 0, 2))[None]


def solution(mesh):
    in_specs = (
        P("slab", "space", None, None),
        P("slab", "space", None),
        P("slab", "space", None),
        P("slab", "space"),
        P("slab", "space", None),
        P("slab", "space", None),
        P(None, "slab"),
        P("slab"),
    )
    return jax.shard_map(
        per_device,
        mesh=mesh,
        in_specs=in_specs,
        out_specs=P("slab", "space", None, None),
        check_vma=False,
    )
```

```python
import functools

import jax
import jax.numpy as jnp
from jax import lax
from jax.experimental import pallas as pl
from jax.experimental.pallas import tpu as pltpu
from jax.sharding import PartitionSpec as P

NB = 48
PL = 128
K = 4
LC = 32
NY = 4
NZ = 8
NX = 4
SOFT = 0.01
UNROLL = (14, 12)
UNROLL_OWN = (14, 4)
MIB = 1 << 20
TILES = 36
F32 = jnp.float32
I32 = jnp.int32
BF16 = jnp.bfloat16
VMEM = pltpu.VMEM
SMEM = pltpu.SMEM


def vspec():
    return pl.BlockSpec(memory_space=VMEM)


def sspec():
    return pl.BlockSpec(memory_space=SMEM)


def column_of(row, n):
    square = jnp.broadcast_to(row, (n, n))
    diag = lax.broadcasted_iota(I32, (n, n), 0) == lax.broadcasted_iota(I32, (n, n), 1)
    return jnp.sum(jnp.where(diag, square, jnp.zeros_like(square)), axis=1, keepdims=True)


def pack_kernel(*refs):
    ins, (src_ref, tgt_ref, cell_ref), holds = refs[:7], refs[7:10], refs[10:18]
    full, sem = refs[18:]
    copies = [pltpu.make_async_copy(ins[i], holds[i], sem.at[i]) for i in range(7)]
    copies.append(pltpu.make_async_copy(ins[2], holds[7], sem.at[7]))
    for copy in copies:
        copy.start()
    for copy in copies:
        copy.wait()
    pos_ref, mass_ref, cnt_ref, dest_ref, near_ref, ctr_ref, cm_ref, cnt_smem = holds
    counts = cnt_ref[...]
    cnt = column_of(counts, NB)
    near = near_ref[...]
    off = (near >= NB).astype(I32) + (near >= 2 * NB).astype(I32)
    dev = (dest_ref[...] + off - 1) & (NY * NZ - 1)
    code = (dev >> 3) * 512 + (dev & (NZ - 1)) * 64 + (near - off * NB)
    gap = jnp.zeros((4, 64 - NB), I32)
    info = jnp.concatenate([code, gap, jnp.broadcast_to(counts, (4, NB)), gap], axis=1)
    lane = lax.broadcasted_iota(I32, (NB, PL), 1)
    weight = jnp.where(lane < cnt, mass_ref[...], 0.0)
    for c in range(3):
        value = pos_ref[c]
        tgt_ref[0:NB, c, :] = value
        full[:, c, :] = value
    full[:, 3, :] = weight
    lane4 = lax.broadcasted_iota(I32, (4, PL), 1)
    carry, begin = jnp.zeros((4, PL), F32), jnp.int32(0)
    for b in range(NB):
        shift, tile = begin & (PL - 1), begin >> 7
        turned = pltpu.roll(full[b], shift, 1)[0:4]
        merged = jnp.where(lane4 >= shift, turned, carry)
        src_ref[0, tile] = merged
        begin = begin + cnt_smem[0, b]
        carry = jnp.where((begin >> 7) != tile, turned, merged)
    square = (NB, NB)
    earlier = lax.broadcasted_iota(I32, square, 0) < lax.broadcasted_iota(I32, square, 1)
    starts = jnp.sum(jnp.where(earlier, cnt, 0), axis=0, keepdims=True)
    places = jnp.concatenate([starts, gap[0:1], counts, gap[0:1]], axis=1)
    src_ref[0, TILES] = jnp.broadcast_to(places, (4, PL)).astype(F32)
    for z in range(1, NZ):
        src_ref[z] = src_ref[0]
    tgt_ref[0:NB, 3, :] = jnp.zeros((NB, PL), F32)
    tgt_ref[NB] = info.astype(F32)
    for j in range(16):
        part = slice(j * PL, (j + 1) * PL)
        cell_ref[j, 0:3, :] = ctr_ref[:, part]
        cell_ref[j, 3:4, :] = cm_ref[0:1, part]


def far_kernel(place_ref, pos_ref, cnt_ref, list_ref, c0, c1, c2, c3, out_ref, pad):
    xs, cs = place_ref[0] >> 1, place_ref[0] & 1
    lane = lax.broadcasted_iota(I32, (NB, PL), 1)
    cnt = column_of(cnt_ref[...], NB)
    live = lane < cnt
    total = jnp.maximum(cnt, 1).astype(F32)
    pos = [pos_ref[c] for c in range(3)]
    centre = [jnp.sum(jnp.where(live, v, 0.0), axis=1, keepdims=True) / total for v in pos]
    diag = lax.broadcasted_iota(I32, (NB, PL), 0) == (lane & 63)
    ctr = [jnp.sum(jnp.where(diag, v, 0.0), axis=0, keepdims=True) for v in centre]
    wide = jnp.concatenate([list_ref[...], jnp.zeros((LC, PL - NB), I32)], axis=1)
    twice = wide + pltpu.roll(wide, 64, 1)
    half = lax.broadcasted_iota(I32, (1, PL), 1) < 64
    ids = [jnp.where(half, twice[2 * j : 2 * j + 1], twice[2 * j + 1 : 2 * j + 2]) for j in range(LC // 2)]
    ids = jnp.concatenate(ids, axis=0)
    slab = ids >> 11
    dx = ((slab >> 1) - xs) & (NX - 1)
    order = jnp.where(dx == 3, 1, jnp.where(dx == 0, 0, dx + 1))
    rows = (order * 2 + ((slab & 1) ^ cs)) * 16 + ((ids >> 7) & 15)
    lanes = ids & (PL - 1)
    tables = []
    for c in range(4):
        whole = jnp.concatenate([ref[i, :, c, :] for ref in (c0, c1, c2, c3) for i in range(2)], axis=0)
        whole = whole.T
        high = whole.astype(BF16)
        low = (whole - high.astype(F32)).astype(BF16)
        tables.append(jnp.concatenate([high, low], axis=1))
    tables = jnp.concatenate(tables, axis=0)
    sub = lax.broadcasted_iota(I32, (PL, 2 * PL), 0)
    got = [[] for _ in range(4)]
    for j in range(0, LC // 2, 2):
        r2 = jnp.concatenate([rows[j : j + 1], rows[j + 1 : j + 2]], axis=1)
        l2 = jnp.concatenate([lanes[j : j + 1], lanes[j + 1 : j + 2]], axis=1)
        hot = jnp.where(sub == r2, 1.0, 0.0).astype(BF16)
        hot = jnp.concatenate([hot, hot], axis=0)
        found = jnp.dot(tables, hot, preferred_element_type=F32)
        pick = sub == l2
        for c in range(4):
            value = jnp.sum(jnp.where(pick, found[c * PL : (c + 1) * PL], 0.0), axis=0, keepdims=True)
            got[c] += [value[:, :PL], value[:, PL:]]
    cells = [jnp.concatenate(v, axis=0) for v in got]
    rel = [ctr[c] - cells[c] for c in range(3)]
    dist = rel[0] * rel[0] + rel[1] * rel[1] + rel[2] * rel[2] + 1.0
    inv = lax.rsqrt(dist)
    cube = cells[3] * (inv * inv * inv)
    fifth = 3.0 * cube * (inv * inv)
    terms = [-(cube * rel[c]) for c in range(3)]
    for a, b in ((0, 0), (1, 1), (2, 2), (0, 1), (0, 2), (1, 2)):
        value = fifth * rel[a] * rel[b]
        if a == b:
            value = value - cube
        terms.append(value)
    terms = [jnp.sum(v, axis=0, keepdims=True) for v in terms]
    pad[...] = jnp.zeros((PL, PL), F32)
    for i, v in enumerate(terms):
        pad[i : i + 1, :] = v + pltpu.roll(v, 64, 1)
    back = pad[...].T
    field = [back[0:NB, i : i + 1] for i in range(3)]
    tide = [back[0:NB, 3 + i : 4 + i] for i in range(6)]
    offset = [pos[c] - centre[c] for c in range(3)]
    for c, (i, j, k) in enumerate(((0, 3, 4), (3, 1, 5), (4, 5, 2))):
        out_ref[c] = field[c] + tide[i] * offset[0] + tide[j] * offset[1] + tide[k] * offset[2]


def split3(v):
    high = v.astype(BF16).astype(F32)
    rest = v - high
    mid = rest.astype(BF16).astype(F32)
    return high, mid, rest - mid


def prep_kernel(y_ref, t0, t1, t2, t3, tall, tab):
    me = y_ref[0]
    wide = 2 * PL
    tiles = []
    for i, t in enumerate((t0, t1, t2, t3)):
        tall[i * NB : (i + 1) * NB] = t[0:NB]
        tiles.append(t[NB])
    left = lax.broadcasted_iota(I32, (4, PL), 1) < 64
    code, cnt = [], []
    for a, b in ((tiles[0], tiles[1]), (tiles[2], tiles[3])):
        code.append(jnp.where(left, a, pltpu.roll(b, 64, 1)))
        cnt.append(jnp.where(left, pltpu.roll(a, 64, 1), b))
    code = jnp.concatenate(code, axis=1).astype(I32)
    cnt = jnp.concatenate(cnt, axis=1)[0:1]
    lane = lax.broadcasted_iota(I32, (1, wide), 1)
    valid = (lane & 63) < NB
    flag = [jnp.where(((code[k : k + 1] >> 9) == me) & valid, 1.0, 0.0) for k in range(K)]
    local = [(code[k : k + 1] & 511).astype(F32) for k in range(K)]
    count = (flag[0] + flag[1]) + (flag[2] + flag[3])
    full = jnp.where(count > 2.5, 1.0, 0.0)
    half = jnp.where((count > 0.5) & (count < 2.5), 1.0, 0.0)
    group = lane >> 6
    mine = group == 0
    lists = [jnp.where(mine, 0.0, v) for v in (full, half)] + [jnp.where(mine, v, 0.0) for v in (full, half)]
    marks = jnp.concatenate(lists + [jnp.zeros((12, wide), F32)], axis=0).astype(BF16)
    a = lax.broadcasted_iota(I32, (wide, wide), 0)
    b = lax.broadcasted_iota(I32, (wide, wide), 1)
    before = jnp.dot(marks, jnp.where(a < b, 1.0, 0.0).astype(BF16), preferred_element_type=F32)
    sizes = [jnp.sum(v, axis=1, keepdims=True) for v in lists]
    place, begin = jnp.full((1, wide), -1.0, F32), jnp.zeros((1, 1), F32)
    for i, v in enumerate(lists):
        place = jnp.where(v > 0.5, begin + before[i : i + 1], place)
        begin = begin + sizes[i]
    moved = jnp.where(a == place.astype(I32), 1.0, 0.0).astype(BF16)
    bucket = lane & 63
    home = jnp.where(mine, bucket, (group - 1) * NB + bucket)
    slot, ins, outs = [], jnp.zeros((1, wide), F32), jnp.zeros((1, wide), F32)
    for k in range(K):
        slot.append(jnp.where(flag[k] > 0.5, ins, count + outs))
        ins, outs = ins + flag[k], outs + (1.0 - flag[k])
    fields = []
    for j in range(K):
        pick = jnp.zeros((1, wide), F32)
        for k in range(K):
            pick = pick + jnp.where(slot[k] == float(j), local[k], 0.0)
        fields.append(pick)
    fields += [cnt, home.astype(F32), count, (group * NB + bucket).astype(F32)]
    load = jnp.concatenate(fields, axis=0)
    high = load.astype(BF16).astype(F32)
    both = jnp.concatenate([high, load - high], axis=0).astype(BF16)
    out = lax.dot_general(both, moved, (((1,), (1,)), ((), ())), preferred_element_type=F32)
    out = out[0:8] + out[8:16]
    sizes = jnp.concatenate([jnp.broadcast_to(v, (1, wide)) for v in sizes + [begin] * 4], axis=0)
    tab[...] = jnp.concatenate([out, sizes], axis=0).astype(I32)


def near_kernel(first, table, tall, src_ref, *refs):
    outs, (out_ref, hold, spots, tab, sem) = refs[:-5], refs[-5:]
    copies = [pltpu.make_async_copy(table, tab, sem.at[0]), pltpu.make_async_copy(hold, spots, sem.at[1])]
    copies[0].start()
    for z in range(NZ):
        hold[z : z + 1, :] = src_ref[z * (TILES + 1) + TILES][0:1].astype(I32)
    copies[1].start()
    out_ref[...] = jnp.zeros(out_ref.shape, F32)
    for copy in copies:
        copy.wait()
    lane1 = lax.broadcasted_iota(I32, (1, PL), 1)
    sub4 = lax.broadcasted_iota(I32, (4, PL), 0)
    lane4 = lax.broadcasted_iota(I32, (4, PL), 1)
    spatial = sub4 < 3
    one = jnp.ones((4, PL), F32)
    zero4 = jnp.zeros((4, PL), F32)
    zero8 = jnp.zeros((8, PL), F32)

    def square(v):
        return jnp.sum(jnp.where(spatial, v * v, 0.0), axis=0, keepdims=True)

    def mix(a, b):
        return jnp.where(spatial, a, b)

    def stack(*v):
        return jnp.concatenate(v, axis=0).astype(BF16)

    def job(e, width):
        n = tab[6, e]
        t = tall[tab[7, e]]
        th, tm, tl = split3(t)
        qh, qm, ql = split3(square(t))
        u = stack(mix(th, one), mix(th, one), mix(tm, one), mix(tm, qh), mix(th, qm), mix(tl, ql), zero8)
        vs, gs = [], []
        for k in range(width):
            z, bucket = tab[k, e] >> 6, tab[k, e] & 63
            begin = spots[z, bucket]
            shift = begin & (PL - 1)
            tile = z * (TILES + 1) + (begin >> 7)
            s = jnp.concatenate([src_ref[tile], src_ref[tile + 1]], axis=0)
            s = pltpu.roll(s, (PL - shift) & (PL - 1), 1)
            s = jnp.where(lane4 < PL - shift, s[0:4], s[4:8])
            live = jnp.where(k < n, spots[z, 64 + bucket], 0)
            sh, sm, sl = split3(-2.0 * s)
            qh, qm, ql = split3(square(s) + SOFT)
            vs.append(stack(mix(sh, qh), mix(sm, qm), mix(sh, ql), mix(sm, one), mix(sl, one), mix(sh, one), zero8))
            w = jnp.where(lane1 < live, s[3:4], 0.0)
            gs.append(stack(*split3(mix(s * w, w)), zero4))
        v = jnp.concatenate(vs, axis=1)
        g = jnp.concatenate(gs, axis=1)
        dist = lax.dot_general(v, u, (((0,), (0,)), ((), ())), preferred_element_type=F32)
        inv = lax.rsqrt(dist)
        f = inv * inv * inv
        high = f.astype(BF16)
        low = (f - high.astype(F32)).astype(BF16)
        o = jnp.dot(g, jnp.concatenate([high, low], axis=1), preferred_element_type=F32)
        o = o[:, :PL] + o[:, PL:]
        a = o[0:4] + o[4:8] + o[8:12]
        out_ref[tab[5, e]] = jnp.where(lane4 < tab[4, e], a - t * a[3:4], 0.0)

    sizes = [tab[8 + i, 0] for i in range(4)]

    def run(begin, size, width, step):
        def body(i, _):
            for j in range(step):
                job(begin + jnp.minimum(step * i + j, size - 1), width)

        lax.fori_loop(0, (size + step - 1) // step, body, None)

    begin = jnp.int32(0) if first else sizes[0] + sizes[1]
    n_full, n_half = (sizes[0], sizes[1]) if first else (sizes[2], sizes[3])
    steps = UNROLL if first else UNROLL_OWN
    run(begin, n_full, 4, steps[0])
    run(begin + n_full, n_half, 2, steps[1])
    for i, o in enumerate(outs):
        for c in range(3):
            o[c] = out_ref[i * NB : (i + 1) * NB, c, :]


def final_kernel(cnt_ref, far_ref, p0, p1, p2, p3, out_ref):
    live = lax.broadcasted_iota(I32, (NB, PL), 1) < column_of(cnt_ref[...], NB)
    for c in range(3):
        near = (p0[c] + p1[c]) + (p2[c] + p3[c])
        out_ref[c] = jnp.where(live, far_ref[c] + near, 0.0)


def along_y(k):
    return [(NZ * y + z, NZ * ((y + k) % NY) + z) for y in range(NY) for z in range(NZ)]


def along_x(k):
    return [(2 * x + c, 2 * ((x + k) % NX) + c) for x in range(NX) for c in range(2)]


def call(kernel, outs, in_specs, out_specs, name, mib, scratch=()):
    return pl.pallas_call(
        kernel,
        out_shape=[jax.ShapeDtypeStruct(shape, dtype) for shape, dtype in outs],
        in_specs=in_specs,
        out_specs=out_specs,
        scratch_shapes=scratch,
        compiler_params=pltpu.CompilerParams(vmem_limit_bytes=mib * MIB),
        name=name,
    )


def per_device(positions, masses, counts, dest_ids, near_list, cell_list, cell_centers, cell_mass):
    pos = jnp.transpose(positions[0], (1, 0, 2))
    cnt = counts[0]
    src, tgt, cells = call(
        pack_kernel,
        (((NZ, TILES + 1, 4, PL), F32), ((NB + 1, 4, PL), F32), ((16, 4, PL), F32)),
        [pl.BlockSpec(memory_space=pltpu.HBM)] * 7,
        [vspec()] * 3,
        "pack",
        60,
        [
            pltpu.VMEM((3, NB, PL), F32),
            pltpu.VMEM((NB, PL), F32),
            pltpu.VMEM((1, NB), I32),
            pltpu.VMEM((1, NB), I32),
            pltpu.VMEM((K, NB), I32),
            pltpu.VMEM((3, 2048), F32),
            pltpu.VMEM((1, 2048), F32),
            pltpu.SMEM((1, NB), I32),
            pltpu.VMEM((NB, 8, PL), F32),
            pltpu.SemaphoreType.DMA((8,)),
        ],
    )(pos, masses[0], cnt, dest_ids, near_list[0].T, cell_centers, cell_mass[None])
    z_rows = [[NZ * y + z for z in range(NZ)] for y in range(NY)]
    window = lax.all_to_all(src, "space", 0, 0, axis_index_groups=z_rows, tiled=True)
    tgts = [tgt] + [lax.ppermute(tgt, "space", along_y(k)) for k in (1, -1, 2)]
    pair = jnp.stack([cells, lax.ppermute(cells, "slab", [(i, i ^ 1) for i in range(2 * NX)])])
    pairs = [pair] + [lax.ppermute(pair, "slab", along_x(k)) for k in (1, -1, 2)]
    me = (lax.axis_index("space") // NZ).astype(I32).reshape(1)
    place = lax.axis_index("slab").astype(I32).reshape(1)
    tall, tab = call(
        prep_kernel,
        (((NY * NB, 4, PL), F32), ((16, 2 * PL), I32)),
        [sspec()] + [vspec()] * 4,
        [vspec(), vspec()],
        "prep",
        8,
    )(me, *tgts)
    (far,) = call(
        far_kernel,
        (((3, NB, PL), F32),),
        [sspec()] + [vspec()] * 7,
        [vspec()],
        "far",
        16,
        [pltpu.VMEM((PL, PL), F32)],
    )(place, pos, cnt, cell_list[0].T, *pairs)
    tall, tab, far = lax.optimization_barrier((tall, tab, far))
    window = window.reshape(NZ * (TILES + 1), 4, PL)

    def near(first, tab):
        count = NY - 1 if first else 1
        return call(
            functools.partial(near_kernel, first),
            (((3, NB, PL), F32),) * count,
            [vspec()] * 3,
            [vspec()] * count,
            "near",
            24,
            [
                pltpu.VMEM((count * NB, 4, PL), F32),
                pltpu.VMEM((NZ, PL), I32),
                pltpu.SMEM((NZ, PL), I32),
                pltpu.SMEM((16, 2 * PL), I32),
                pltpu.SemaphoreType.DMA((2,)),
            ],
        )(tab, tall, window)

    sent = near(True, tab)
    back = [lax.ppermute(v, "space", along_y(-k)) for v, k in zip(sent, (1, -1, 2))]
    tab, sent = lax.optimization_barrier((tab, sent))
    (own,) = near(False, tab)
    (out,) = call(
        final_kernel,
        (((3, NB, PL), F32),),
        [vspec()] * 6,
        [vspec()],
        "final",
        8,
    )(cnt, far, own, *back)
    return jnp.transpose(out, (1, 0, 2))[None]


def solution(mesh):
    in_specs = (
        P("slab", "space", None, None),
        P("slab", "space", None),
        P("slab", "space", None),
        P("slab", "space"),
        P("slab", "space", None),
        P("slab", "space", None),
        P(None, "slab"),
        P("slab"),
    )
    return jax.shard_map(
        per_device,
        mesh=mesh,
        in_specs=in_specs,
        out_specs=P("slab", "space", None, None),
        check_vma=False,
    )
```

```python
import functools

import jax
import jax.numpy as jnp
from jax import lax
from jax.experimental import pallas as pl
from jax.experimental.pallas import tpu as pltpu
from jax.sharding import PartitionSpec as P

NB = 48
PL = 128
K = 4
LC = 32
NY = 4
NZ = 8
NX = 4
SOFT = 0.01
UNROLL = (18, 16)
UNROLL_OWN = (18, 6)
MIB = 1 << 20
TILES = 36
F32 = jnp.float32
I32 = jnp.int32
BF16 = jnp.bfloat16
VMEM = pltpu.VMEM
SMEM = pltpu.SMEM


def vspec():
    return pl.BlockSpec(memory_space=VMEM)


def sspec():
    return pl.BlockSpec(memory_space=SMEM)


def column_of(row, n):
    square = jnp.broadcast_to(row, (n, n))
    diag = lax.broadcasted_iota(I32, (n, n), 0) == lax.broadcasted_iota(I32, (n, n), 1)
    return jnp.sum(jnp.where(diag, square, jnp.zeros_like(square)), axis=1, keepdims=True)


def pack_kernel(*refs):
    ins, (src_ref, tgt_ref, cell_ref), holds = refs[:7], refs[7:10], refs[10:18]
    full, sem = refs[18:]
    copies = [pltpu.make_async_copy(ins[i], holds[i], sem.at[i]) for i in range(7)]
    copies.append(pltpu.make_async_copy(ins[2], holds[7], sem.at[7]))
    for copy in copies:
        copy.start()
    for copy in copies:
        copy.wait()
    pos_ref, mass_ref, cnt_ref, dest_ref, near_ref, ctr_ref, cm_ref, cnt_smem = holds
    counts = cnt_ref[...]
    cnt = column_of(counts, NB)
    near = near_ref[...]
    off = (near >= NB).astype(I32) + (near >= 2 * NB).astype(I32)
    dev = (dest_ref[...] + off - 1) & (NY * NZ - 1)
    code = (dev >> 3) * 512 + (dev & (NZ - 1)) * 64 + (near - off * NB)
    gap = jnp.zeros((4, 64 - NB), I32)
    info = jnp.concatenate([code, gap, jnp.broadcast_to(counts, (4, NB)), gap], axis=1)
    lane = lax.broadcasted_iota(I32, (NB, PL), 1)
    weight = jnp.where(lane < cnt, mass_ref[...], 0.0)
    for c in range(3):
        value = pos_ref[c]
        tgt_ref[0:NB, c, :] = value
        full[:, c, :] = value
    full[:, 3, :] = weight
    lane4 = lax.broadcasted_iota(I32, (4, PL), 1)
    carry, begin = jnp.zeros((4, PL), F32), jnp.int32(0)
    for b in range(NB):
        shift, tile = begin & (PL - 1), begin >> 7
        turned = pltpu.roll(full[b], shift, 1)[0:4]
        merged = jnp.where(lane4 >= shift, turned, carry)
        src_ref[0, tile] = merged
        begin = begin + cnt_smem[0, b]
        carry = jnp.where((begin >> 7) != tile, turned, merged)
    square = (NB, NB)
    earlier = lax.broadcasted_iota(I32, square, 0) < lax.broadcasted_iota(I32, square, 1)
    starts = jnp.sum(jnp.where(earlier, cnt, 0), axis=0, keepdims=True)
    places = jnp.concatenate([starts, gap[0:1], counts, gap[0:1]], axis=1)
    src_ref[0, TILES] = jnp.broadcast_to(places, (4, PL)).astype(F32)
    for z in range(1, NZ):
        src_ref[z] = src_ref[0]
    tgt_ref[0:NB, 3, :] = jnp.zeros((NB, PL), F32)
    tgt_ref[NB] = info.astype(F32)
    for j in range(16):
        part = slice(j * PL, (j + 1) * PL)
        cell_ref[j, 0:3, :] = ctr_ref[:, part]
        cell_ref[j, 3:4, :] = cm_ref[0:1, part]


def far_kernel(place_ref, pos_ref, cnt_ref, list_ref, c0, c1, c2, c3, out_ref, pad):
    xs, cs = place_ref[0] >> 1, place_ref[0] & 1
    lane = lax.broadcasted_iota(I32, (NB, PL), 1)
    cnt = column_of(cnt_ref[...], NB)
    live = lane < cnt
    total = jnp.maximum(cnt, 1).astype(F32)
    pos = [pos_ref[c] for c in range(3)]
    centre = [jnp.sum(jnp.where(live, v, 0.0), axis=1, keepdims=True) / total for v in pos]
    diag = lax.broadcasted_iota(I32, (NB, PL), 0) == (lane & 63)
    ctr = [jnp.sum(jnp.where(diag, v, 0.0), axis=0, keepdims=True) for v in centre]
    wide = jnp.concatenate([list_ref[...], jnp.zeros((LC, PL - NB), I32)], axis=1)
    twice = wide + pltpu.roll(wide, 64, 1)
    half = lax.broadcasted_iota(I32, (1, PL), 1) < 64
    ids = [jnp.where(half, twice[2 * j : 2 * j + 1], twice[2 * j + 1 : 2 * j + 2]) for j in range(LC // 2)]
    ids = jnp.concatenate(ids, axis=0)
    slab = ids >> 11
    dx = ((slab >> 1) - xs) & (NX - 1)
    order = jnp.where(dx == 3, 1, jnp.where(dx == 0, 0, dx + 1))
    rows = (order * 2 + ((slab & 1) ^ cs)) * 16 + ((ids >> 7) & 15)
    lanes = ids & (PL - 1)
    tables = []
    for c in range(4):
        whole = jnp.concatenate([ref[i, :, c, :] for ref in (c0, c1, c2, c3) for i in range(2)], axis=0)
        whole = whole.T
        high = whole.astype(BF16)
        low = (whole - high.astype(F32)).astype(BF16)
        tables.append(jnp.concatenate([high, low], axis=1))
    tables = jnp.concatenate(tables, axis=0)
    sub = lax.broadcasted_iota(I32, (PL, 2 * PL), 0)
    got = [[] for _ in range(4)]
    for j in range(0, LC // 2, 2):
        r2 = jnp.concatenate([rows[j : j + 1], rows[j + 1 : j + 2]], axis=1)
        l2 = jnp.concatenate([lanes[j : j + 1], lanes[j + 1 : j + 2]], axis=1)
        hot = jnp.where(sub == r2, 1.0, 0.0).astype(BF16)
        hot = jnp.concatenate([hot, hot], axis=0)
        found = jnp.dot(tables, hot, preferred_element_type=F32)
        pick = sub == l2
        for c in range(4):
            value = jnp.sum(jnp.where(pick, found[c * PL : (c + 1) * PL], 0.0), axis=0, keepdims=True)
            got[c] += [value[:, :PL], value[:, PL:]]
    cells = [jnp.concatenate(v, axis=0) for v in got]
    rel = [ctr[c] - cells[c] for c in range(3)]
    dist = rel[0] * rel[0] + rel[1] * rel[1] + rel[2] * rel[2] + 1.0
    inv = lax.rsqrt(dist)
    cube = cells[3] * (inv * inv * inv)
    fifth = 3.0 * cube * (inv * inv)
    terms = [-(cube * rel[c]) for c in range(3)]
    for a, b in ((0, 0), (1, 1), (2, 2), (0, 1), (0, 2), (1, 2)):
        value = fifth * rel[a] * rel[b]
        if a == b:
            value = value - cube
        terms.append(value)
    terms = [jnp.sum(v, axis=0, keepdims=True) for v in terms]
    pad[...] = jnp.zeros((PL, PL), F32)
    for i, v in enumerate(terms):
        pad[i : i + 1, :] = v + pltpu.roll(v, 64, 1)
    back = pad[...].T
    field = [back[0:NB, i : i + 1] for i in range(3)]
    tide = [back[0:NB, 3 + i : 4 + i] for i in range(6)]
    offset = [pos[c] - centre[c] for c in range(3)]
    for c, (i, j, k) in enumerate(((0, 3, 4), (3, 1, 5), (4, 5, 2))):
        out_ref[c] = field[c] + tide[i] * offset[0] + tide[j] * offset[1] + tide[k] * offset[2]


def split3(v):
    high = v.astype(BF16).astype(F32)
    rest = v - high
    mid = rest.astype(BF16).astype(F32)
    return high, mid, rest - mid


def prep_kernel(y_ref, t0, t1, t2, t3, tall, tab):
    me = y_ref[0]
    wide = 2 * PL
    tiles = []
    for i, t in enumerate((t0, t1, t2, t3)):
        tall[i * NB : (i + 1) * NB] = t[0:NB]
        tiles.append(t[NB])
    left = lax.broadcasted_iota(I32, (4, PL), 1) < 64
    code, cnt = [], []
    for a, b in ((tiles[0], tiles[1]), (tiles[2], tiles[3])):
        code.append(jnp.where(left, a, pltpu.roll(b, 64, 1)))
        cnt.append(jnp.where(left, pltpu.roll(a, 64, 1), b))
    code = jnp.concatenate(code, axis=1).astype(I32)
    cnt = jnp.concatenate(cnt, axis=1)[0:1]
    lane = lax.broadcasted_iota(I32, (1, wide), 1)
    valid = (lane & 63) < NB
    flag = [jnp.where(((code[k : k + 1] >> 9) == me) & valid, 1.0, 0.0) for k in range(K)]
    local = [(code[k : k + 1] & 511).astype(F32) for k in range(K)]
    count = (flag[0] + flag[1]) + (flag[2] + flag[3])
    full = jnp.where(count > 2.5, 1.0, 0.0)
    half = jnp.where((count > 0.5) & (count < 2.5), 1.0, 0.0)
    group = lane >> 6
    mine = group == 0
    lists = [jnp.where(mine, 0.0, v) for v in (full, half)] + [jnp.where(mine, v, 0.0) for v in (full, half)]
    marks = jnp.concatenate(lists + [jnp.zeros((12, wide), F32)], axis=0).astype(BF16)
    a = lax.broadcasted_iota(I32, (wide, wide), 0)
    b = lax.broadcasted_iota(I32, (wide, wide), 1)
    before = jnp.dot(marks, jnp.where(a < b, 1.0, 0.0).astype(BF16), preferred_element_type=F32)
    sizes = [jnp.sum(v, axis=1, keepdims=True) for v in lists]
    place, begin = jnp.full((1, wide), -1.0, F32), jnp.zeros((1, 1), F32)
    for i, v in enumerate(lists):
        place = jnp.where(v > 0.5, begin + before[i : i + 1], place)
        begin = begin + sizes[i]
    moved = jnp.where(a == place.astype(I32), 1.0, 0.0).astype(BF16)
    bucket = lane & 63
    home = jnp.where(mine, bucket, (group - 1) * NB + bucket)
    slot, ins, outs = [], jnp.zeros((1, wide), F32), jnp.zeros((1, wide), F32)
    for k in range(K):
        slot.append(jnp.where(flag[k] > 0.5, ins, count + outs))
        ins, outs = ins + flag[k], outs + (1.0 - flag[k])
    fields = []
    for j in range(K):
        pick = jnp.zeros((1, wide), F32)
        for k in range(K):
            pick = pick + jnp.where(slot[k] == float(j), local[k], 0.0)
        fields.append(pick)
    fields += [cnt, home.astype(F32), count, (group * NB + bucket).astype(F32)]
    load = jnp.concatenate(fields, axis=0)
    high = load.astype(BF16).astype(F32)
    both = jnp.concatenate([high, load - high], axis=0).astype(BF16)
    out = lax.dot_general(both, moved, (((1,), (1,)), ((), ())), preferred_element_type=F32)
    out = out[0:8] + out[8:16]
    sizes = jnp.concatenate([jnp.broadcast_to(v, (1, wide)) for v in sizes + [begin] * 4], axis=0)
    tab[...] = jnp.concatenate([out, sizes], axis=0).astype(I32)


def near_kernel(first, table, tall, src_ref, *refs):
    outs, (out_ref, hold, spots, tab, sem) = refs[:-5], refs[-5:]
    copies = [pltpu.make_async_copy(table, tab, sem.at[0]), pltpu.make_async_copy(hold, spots, sem.at[1])]
    copies[0].start()
    for z in range(NZ):
        hold[z : z + 1, :] = src_ref[z * (TILES + 1) + TILES][0:1].astype(I32)
    copies[1].start()
    out_ref[...] = jnp.zeros(out_ref.shape, F32)
    for copy in copies:
        copy.wait()
    lane1 = lax.broadcasted_iota(I32, (1, PL), 1)
    sub4 = lax.broadcasted_iota(I32, (4, PL), 0)
    lane4 = lax.broadcasted_iota(I32, (4, PL), 1)
    spatial = sub4 < 3
    one = jnp.ones((4, PL), F32)
    zero4 = jnp.zeros((4, PL), F32)
    zero8 = jnp.zeros((8, PL), F32)

    def square(v):
        return jnp.sum(jnp.where(spatial, v * v, 0.0), axis=0, keepdims=True)

    def mix(a, b):
        return jnp.where(spatial, a, b)

    def stack(*v):
        return jnp.concatenate(v, axis=0).astype(BF16)

    def job(e, width):
        n = tab[6, e]
        t = tall[tab[7, e]]
        th, tm, tl = split3(t)
        qh, qm, ql = split3(square(t))
        u = stack(mix(th, one), mix(th, one), mix(tm, one), mix(tm, qh), mix(th, qm), mix(tl, ql), zero8)
        vs, gs = [], []
        for k in range(width):
            z, bucket = tab[k, e] >> 6, tab[k, e] & 63
            begin = spots[z, bucket]
            shift = begin & (PL - 1)
            tile = z * (TILES + 1) + (begin >> 7)
            s = jnp.concatenate([src_ref[tile], src_ref[tile + 1]], axis=0)
            s = pltpu.roll(s, (PL - shift) & (PL - 1), 1)
            s = jnp.where(lane4 < PL - shift, s[0:4], s[4:8])
            live = jnp.where(k < n, spots[z, 64 + bucket], 0)
            sh, sm, sl = split3(-2.0 * s)
            qh, qm, ql = split3(square(s) + SOFT)
            vs.append(stack(mix(sh, qh), mix(sm, qm), mix(sh, ql), mix(sm, one), mix(sl, one), mix(sh, one), zero8))
            w = jnp.where(lane1 < live, s[3:4], 0.0)
            gs.append(stack(*split3(mix(s * w, w)), zero4))
        v = jnp.concatenate(vs, axis=1)
        g = jnp.concatenate(gs, axis=1)
        dist = lax.dot_general(v, u, (((0,), (0,)), ((), ())), preferred_element_type=F32)
        inv = lax.rsqrt(dist)
        f = inv * inv * inv
        high = f.astype(BF16)
        low = (f - high.astype(F32)).astype(BF16)
        o = jnp.dot(g, jnp.concatenate([high, low], axis=1), preferred_element_type=F32)
        o = o[:, :PL] + o[:, PL:]
        a = o[0:4] + o[4:8] + o[8:12]
        out_ref[tab[5, e]] = jnp.where(lane4 < tab[4, e], a - t * a[3:4], 0.0)

    sizes = [tab[8 + i, 0] for i in range(4)]

    def run(begin, size, width, step):
        def body(i, _):
            for j in range(step):
                job(begin + jnp.minimum(step * i + j, size - 1), width)

        lax.fori_loop(0, (size + step - 1) // step, body, None)

    begin = jnp.int32(0) if first else sizes[0] + sizes[1]
    n_full, n_half = (sizes[0], sizes[1]) if first else (sizes[2], sizes[3])
    steps = UNROLL if first else UNROLL_OWN
    run(begin, n_full, 4, steps[0])
    run(begin + n_full, n_half, 2, steps[1])
    for i, o in enumerate(outs):
        for c in range(3):
            o[c] = out_ref[i * NB : (i + 1) * NB, c, :]


def final_kernel(cnt_ref, far_ref, p0, p1, p2, p3, out_ref):
    live = lax.broadcasted_iota(I32, (NB, PL), 1) < column_of(cnt_ref[...], NB)
    for c in range(3):
        near = (p0[c] + p1[c]) + (p2[c] + p3[c])
        out_ref[c] = jnp.where(live, far_ref[c] + near, 0.0)


def along_y(k):
    return [(NZ * y + z, NZ * ((y + k) % NY) + z) for y in range(NY) for z in range(NZ)]


def along_x(k):
    return [(2 * x + c, 2 * ((x + k) % NX) + c) for x in range(NX) for c in range(2)]


def call(kernel, outs, in_specs, out_specs, name, mib, scratch=()):
    return pl.pallas_call(
        kernel,
        out_shape=[jax.ShapeDtypeStruct(shape, dtype) for shape, dtype in outs],
        in_specs=in_specs,
        out_specs=out_specs,
        scratch_shapes=scratch,
        compiler_params=pltpu.CompilerParams(vmem_limit_bytes=mib * MIB),
        name=name,
    )


def per_device(positions, masses, counts, dest_ids, near_list, cell_list, cell_centers, cell_mass):
    pos = jnp.transpose(positions[0], (1, 0, 2))
    cnt = counts[0]
    src, tgt, cells = call(
        pack_kernel,
        (((NZ, TILES + 1, 4, PL), F32), ((NB + 1, 4, PL), F32), ((16, 4, PL), F32)),
        [pl.BlockSpec(memory_space=pltpu.HBM)] * 7,
        [vspec()] * 3,
        "pack",
        8,
        [
            pltpu.VMEM((3, NB, PL), F32),
            pltpu.VMEM((NB, PL), F32),
            pltpu.VMEM((1, NB), I32),
            pltpu.VMEM((1, NB), I32),
            pltpu.VMEM((K, NB), I32),
            pltpu.VMEM((3, 2048), F32),
            pltpu.VMEM((1, 2048), F32),
            pltpu.SMEM((1, NB), I32),
            pltpu.VMEM((NB, 8, PL), F32),
            pltpu.SemaphoreType.DMA((8,)),
        ],
    )(
        *[
            pltpu.with_memory_space_constraint(v, pltpu.HBM)
            for v in (pos, masses[0], cnt, dest_ids, near_list[0].T, cell_centers, cell_mass[None])
        ]
    )
    z_rows = [[NZ * y + z for z in range(NZ)] for y in range(NY)]
    window = lax.all_to_all(src, "space", 0, 0, axis_index_groups=z_rows, tiled=True)
    tgts = [tgt] + [lax.ppermute(tgt, "space", along_y(k)) for k in (1, -1, 2)]
    pair = jnp.stack([cells, lax.ppermute(cells, "slab", [(i, i ^ 1) for i in range(2 * NX)])])
    pairs = [pair] + [lax.ppermute(pair, "slab", along_x(k)) for k in (1, -1, 2)]
    me = (lax.axis_index("space") // NZ).astype(I32).reshape(1)
    place = lax.axis_index("slab").astype(I32).reshape(1)
    tall, tab = call(
        prep_kernel,
        (((NY * NB, 4, PL), F32), ((16, 2 * PL), I32)),
        [sspec()] + [vspec()] * 4,
        [vspec(), vspec()],
        "prep",
        8,
    )(me, *tgts)
    (far,) = call(
        far_kernel,
        (((3, NB, PL), F32),),
        [sspec()] + [vspec()] * 7,
        [vspec()],
        "far",
        16,
        [pltpu.VMEM((PL, PL), F32)],
    )(place, pos, cnt, cell_list[0].T, *pairs)
    tall, tab, far = lax.optimization_barrier((tall, tab, far))
    window = window.reshape(NZ * (TILES + 1), 4, PL)

    def near(first, tab):
        count = NY - 1 if first else 1
        return call(
            functools.partial(near_kernel, first),
            (((3, NB, PL), F32),) * count,
            [vspec()] * 3,
            [vspec()] * count,
            "near",
            24,
            [
                pltpu.VMEM((count * NB, 4, PL), F32),
                pltpu.VMEM((NZ, PL), I32),
                pltpu.SMEM((NZ, PL), I32),
                pltpu.SMEM((16, 2 * PL), I32),
                pltpu.SemaphoreType.DMA((2,)),
            ],
        )(tab, tall, window)

    sent = near(True, tab)
    back = [lax.ppermute(v, "space", along_y(-k)) for v, k in zip(sent, (1, -1, 2))]
    tab, sent = lax.optimization_barrier((tab, sent))
    (own,) = near(False, tab)
    (out,) = call(
        final_kernel,
        (((3, NB, PL), F32),),
        [vspec()] * 6,
        [vspec()],
        "final",
        8,
    )(cnt, far, own, *back)
    return jnp.transpose(out, (1, 0, 2))[None]


def solution(mesh):
    in_specs = (
        P("slab", "space", None, None),
        P("slab", "space", None),
        P("slab", "space", None),
        P("slab", "space"),
        P("slab", "space", None),
        P("slab", "space", None),
        P(None, "slab"),
        P("slab"),
    )
    return jax.shard_map(
        per_device,
        mesh=mesh,
        in_specs=in_specs,
        out_specs=P("slab", "space", None, None),
        check_vma=False,
    )
```

```python
import functools

import jax
import jax.numpy as jnp
from jax import lax
from jax.experimental import pallas as pl
from jax.experimental.pallas import tpu as pltpu
from jax.sharding import PartitionSpec as P

NB = 48
PL = 128
K = 4
LC = 32
NY = 4
NZ = 8
NX = 4
SOFT = 0.01
UNROLL = (18, 16)
UNROLL_OWN = (12, 8)
FULL_SLOTS = 54
MIB = 1 << 20
TILES = 36
F32 = jnp.float32
I32 = jnp.int32
BF16 = jnp.bfloat16
VMEM = pltpu.VMEM
SMEM = pltpu.SMEM


def vspec():
    return pl.BlockSpec(memory_space=VMEM)


def sspec():
    return pl.BlockSpec(memory_space=SMEM)


def column_of(row, n):
    square = jnp.broadcast_to(row, (n, n))
    diag = lax.broadcasted_iota(I32, (n, n), 0) == lax.broadcasted_iota(I32, (n, n), 1)
    return jnp.sum(jnp.where(diag, square, jnp.zeros_like(square)), axis=1, keepdims=True)


def pack_kernel(*refs):
    ins, (src_ref, tgt_ref, cell_ref), holds = refs[:7], refs[7:10], refs[10:18]
    full, sem = refs[18:]
    copies = [pltpu.make_async_copy(ins[i], holds[i], sem.at[i]) for i in range(7)]
    copies.append(pltpu.make_async_copy(ins[2], holds[7], sem.at[7]))
    for copy in copies:
        copy.start()
    for copy in copies:
        copy.wait()
    pos_ref, mass_ref, cnt_ref, dest_ref, near_ref, ctr_ref, cm_ref, cnt_smem = holds
    counts = cnt_ref[...]
    cnt = column_of(counts, NB)
    near = near_ref[...]
    off = (near >= NB).astype(I32) + (near >= 2 * NB).astype(I32)
    dev = (dest_ref[...] + off - 1) & (NY * NZ - 1)
    code = (dev >> 3) * 512 + (dev & (NZ - 1)) * 64 + (near - off * NB)
    gap = jnp.zeros((4, 64 - NB), I32)
    info = jnp.concatenate([code, gap, jnp.broadcast_to(counts, (4, NB)), gap], axis=1)
    lane = lax.broadcasted_iota(I32, (NB, PL), 1)
    weight = jnp.where(lane < cnt, mass_ref[...], 0.0)
    for c in range(3):
        value = pos_ref[c]
        tgt_ref[0:NB, c, :] = value
        full[:, c, :] = value
    full[:, 3, :] = weight
    lane4 = lax.broadcasted_iota(I32, (4, PL), 1)
    carry, begin = jnp.zeros((4, PL), F32), jnp.int32(0)
    for b in range(NB):
        shift, tile = begin & (PL - 1), begin >> 7
        turned = pltpu.roll(full[b], shift, 1)[0:4]
        merged = jnp.where(lane4 >= shift, turned, carry)
        src_ref[0, tile] = merged
        begin = begin + cnt_smem[0, b]
        carry = jnp.where((begin >> 7) != tile, turned, merged)
    square = (NB, NB)
    earlier = lax.broadcasted_iota(I32, square, 0) < lax.broadcasted_iota(I32, square, 1)
    starts = jnp.sum(jnp.where(earlier, cnt, 0), axis=0, keepdims=True)
    places = jnp.concatenate([starts, gap[0:1], counts, gap[0:1]], axis=1)
    src_ref[0, TILES] = jnp.broadcast_to(places, (4, PL)).astype(F32)
    for z in range(1, NZ):
        src_ref[z] = src_ref[0]
    tgt_ref[0:NB, 3, :] = jnp.zeros((NB, PL), F32)
    tgt_ref[NB] = info.astype(F32)
    for j in range(16):
        part = slice(j * PL, (j + 1) * PL)
        cell_ref[j, 0:3, :] = ctr_ref[:, part]
        cell_ref[j, 3:4, :] = cm_ref[0:1, part]


def far_kernel(place_ref, pos_ref, cnt_ref, list_ref, c0, c1, c2, c3, out_ref, pad):
    xs, cs = place_ref[0] >> 1, place_ref[0] & 1
    lane = lax.broadcasted_iota(I32, (NB, PL), 1)
    cnt = column_of(cnt_ref[...], NB)
    live = lane < cnt
    total = jnp.maximum(cnt, 1).astype(F32)
    pos = [pos_ref[c] for c in range(3)]
    centre = [jnp.sum(jnp.where(live, v, 0.0), axis=1, keepdims=True) / total for v in pos]
    diag = lax.broadcasted_iota(I32, (NB, PL), 0) == (lane & 63)
    ctr = [jnp.sum(jnp.where(diag, v, 0.0), axis=0, keepdims=True) for v in centre]
    wide = jnp.concatenate([list_ref[...], jnp.zeros((LC, PL - NB), I32)], axis=1)
    twice = wide + pltpu.roll(wide, 64, 1)
    half = lax.broadcasted_iota(I32, (1, PL), 1) < 64
    ids = [jnp.where(half, twice[2 * j : 2 * j + 1], twice[2 * j + 1 : 2 * j + 2]) for j in range(LC // 2)]
    ids = jnp.concatenate(ids, axis=0)
    slab = ids >> 11
    dx = ((slab >> 1) - xs) & (NX - 1)
    order = jnp.where(dx == 3, 1, jnp.where(dx == 0, 0, dx + 1))
    rows = (order * 2 + ((slab & 1) ^ cs)) * 16 + ((ids >> 7) & 15)
    lanes = ids & (PL - 1)
    tables = []
    for c in range(4):
        whole = jnp.concatenate([ref[i, :, c, :] for ref in (c0, c1, c2, c3) for i in range(2)], axis=0)
        whole = whole.T
        high = whole.astype(BF16)
        low = (whole - high.astype(F32)).astype(BF16)
        tables.append(jnp.concatenate([high, low], axis=1))
    tables = jnp.concatenate(tables, axis=0)
    sub = lax.broadcasted_iota(I32, (PL, 2 * PL), 0)
    got = [[] for _ in range(4)]
    for j in range(0, LC // 2, 2):
        r2 = jnp.concatenate([rows[j : j + 1], rows[j + 1 : j + 2]], axis=1)
        l2 = jnp.concatenate([lanes[j : j + 1], lanes[j + 1 : j + 2]], axis=1)
        hot = jnp.where(sub == r2, 1.0, 0.0).astype(BF16)
        hot = jnp.concatenate([hot, hot], axis=0)
        found = jnp.dot(tables, hot, preferred_element_type=F32)
        pick = sub == l2
        for c in range(4):
            value = jnp.sum(jnp.where(pick, found[c * PL : (c + 1) * PL], 0.0), axis=0, keepdims=True)
            got[c] += [value[:, :PL], value[:, PL:]]
    cells = [jnp.concatenate(v, axis=0) for v in got]
    rel = [ctr[c] - cells[c] for c in range(3)]
    dist = rel[0] * rel[0] + rel[1] * rel[1] + rel[2] * rel[2] + 1.0
    inv = lax.rsqrt(dist)
    cube = cells[3] * (inv * inv * inv)
    fifth = 3.0 * cube * (inv * inv)
    terms = [-(cube * rel[c]) for c in range(3)]
    for a, b in ((0, 0), (1, 1), (2, 2), (0, 1), (0, 2), (1, 2)):
        value = fifth * rel[a] * rel[b]
        if a == b:
            value = value - cube
        terms.append(value)
    terms = [jnp.sum(v, axis=0, keepdims=True) for v in terms]
    pad[...] = jnp.zeros((PL, PL), F32)
    for i, v in enumerate(terms):
        pad[i : i + 1, :] = v + pltpu.roll(v, 64, 1)
    back = pad[...].T
    field = [back[0:NB, i : i + 1] for i in range(3)]
    tide = [back[0:NB, 3 + i : 4 + i] for i in range(6)]
    offset = [pos[c] - centre[c] for c in range(3)]
    for c, (i, j, k) in enumerate(((0, 3, 4), (3, 1, 5), (4, 5, 2))):
        out_ref[c] = field[c] + tide[i] * offset[0] + tide[j] * offset[1] + tide[k] * offset[2]


def split3(v):
    high = v.astype(BF16).astype(F32)
    rest = v - high
    mid = rest.astype(BF16).astype(F32)
    return high, mid, rest - mid


def prep_kernel(y_ref, t0, t1, t2, t3, tall, tab):
    me = y_ref[0]
    wide = 2 * PL
    tiles = []
    for i, t in enumerate((t0, t1, t2, t3)):
        tall[i * NB : (i + 1) * NB] = t[0:NB]
        tiles.append(t[NB])
    left = lax.broadcasted_iota(I32, (4, PL), 1) < 64
    code, cnt = [], []
    for a, b in ((tiles[0], tiles[1]), (tiles[2], tiles[3])):
        code.append(jnp.where(left, a, pltpu.roll(b, 64, 1)))
        cnt.append(jnp.where(left, pltpu.roll(a, 64, 1), b))
    code = jnp.concatenate(code, axis=1).astype(I32)
    cnt = jnp.concatenate(cnt, axis=1)[0:1]
    lane = lax.broadcasted_iota(I32, (1, wide), 1)
    valid = (lane & 63) < NB
    flag = [jnp.where(((code[k : k + 1] >> 9) == me) & valid, 1.0, 0.0) for k in range(K)]
    local = [(code[k : k + 1] & 511).astype(F32) for k in range(K)]
    count = (flag[0] + flag[1]) + (flag[2] + flag[3])
    full = jnp.where(count > 2.5, 1.0, 0.0)
    half = jnp.where((count > 0.5) & (count < 2.5), 1.0, 0.0)
    group = lane >> 6
    mine = group == 0
    lists = [jnp.where(m, v, 0.0) for v in (full, half) for m in (~mine, mine)]
    marks = jnp.concatenate(lists + [jnp.zeros((12, wide), F32)], axis=0).astype(BF16)
    a = lax.broadcasted_iota(I32, (wide, wide), 0)
    b = lax.broadcasted_iota(I32, (wide, wide), 1)
    before = jnp.dot(marks, jnp.where(a < b, 1.0, 0.0).astype(BF16), preferred_element_type=F32)
    sizes = [jnp.sum(v, axis=1, keepdims=True) for v in lists]
    place, begin = jnp.full((1, wide), -1.0, F32), jnp.zeros((1, 1), F32)
    for i, v in enumerate(lists):
        place = jnp.where(v > 0.5, begin + before[i : i + 1], place)
        begin = begin + sizes[i]
    moved = jnp.where(a == place.astype(I32), 1.0, 0.0).astype(BF16)
    bucket = lane & 63
    home = ((group - 1) & (NY - 1)) * NB + bucket
    slot, ins, outs = [], jnp.zeros((1, wide), F32), jnp.zeros((1, wide), F32)
    for k in range(K):
        slot.append(jnp.where(flag[k] > 0.5, ins, count + outs))
        ins, outs = ins + flag[k], outs + (1.0 - flag[k])
    fields = []
    for j in range(K):
        pick = jnp.zeros((1, wide), F32)
        for k in range(K):
            pick = pick + jnp.where(slot[k] == float(j), local[k], 0.0)
        fields.append(pick)
    fields += [cnt, home.astype(F32), count, (group * NB + bucket).astype(F32)]
    load = jnp.concatenate(fields, axis=0)
    high = load.astype(BF16).astype(F32)
    both = jnp.concatenate([high, load - high], axis=0).astype(BF16)
    out = lax.dot_general(both, moved, (((1,), (1,)), ((), ())), preferred_element_type=F32)
    out = out[0:8] + out[8:16]
    sizes = jnp.concatenate([jnp.broadcast_to(v, (1, wide)) for v in sizes + [begin] * 4], axis=0)
    tab[...] = jnp.concatenate([out, sizes], axis=0).astype(I32)


def near_kernel(first, *refs):
    (table, tall, src_ref), refs = refs[:3], refs[3:]
    outs, (out_ref, hold, spots, tab, sem) = refs[:-5], refs[-5:]
    if not first:
        kept, outs = outs[0], outs[1:]
    copies = [pltpu.make_async_copy(table, tab, sem.at[0]), pltpu.make_async_copy(hold, spots, sem.at[1])]
    copies[0].start()
    for z in range(NZ):
        hold[z : z + 1, :] = src_ref[z * (TILES + 1) + TILES][0:1].astype(I32)
    copies[1].start()
    out_ref[...] = jnp.zeros(out_ref.shape, F32) if first else kept[...]
    for copy in copies:
        copy.wait()
    lane1 = lax.broadcasted_iota(I32, (1, PL), 1)
    sub4 = lax.broadcasted_iota(I32, (4, PL), 0)
    lane4 = lax.broadcasted_iota(I32, (4, PL), 1)
    spatial = sub4 < 3
    one = jnp.ones((4, PL), F32)
    zero4 = jnp.zeros((4, PL), F32)
    zero8 = jnp.zeros((8, PL), F32)

    def square(v):
        return jnp.sum(jnp.where(spatial, v * v, 0.0), axis=0, keepdims=True)

    def mix(a, b):
        return jnp.where(spatial, a, b)

    def stack(*v):
        return jnp.concatenate(v, axis=0).astype(BF16)

    row_base = 0 if first else (NY - 1) * NB

    def job(e, width):
        n = tab[6, e]
        t = tall[tab[7, e]]
        th, tm, tl = split3(t)
        qh, qm, ql = split3(square(t))
        u = stack(mix(th, one), mix(th, one), mix(tm, one), mix(tm, qh), mix(th, qm), mix(tl, ql), zero8)
        vs, gs = [], []
        for k in range(width):
            z, bucket = tab[k, e] >> 6, tab[k, e] & 63
            begin = spots[z, bucket]
            shift = begin & (PL - 1)
            tile = z * (TILES + 1) + (begin >> 7)
            s = jnp.concatenate([src_ref[tile], src_ref[tile + 1]], axis=0)
            s = pltpu.roll(s, (PL - shift) & (PL - 1), 1)
            s = jnp.where(lane4 < PL - shift, s[0:4], s[4:8])
            live = jnp.where(k < n, spots[z, 64 + bucket], 0)
            sh, sm, sl = split3(-2.0 * s)
            qh, qm, ql = split3(square(s) + SOFT)
            vs.append(stack(mix(sh, qh), mix(sm, qm), mix(sh, ql), mix(sm, one), mix(sl, one), mix(sh, one), zero8))
            w = jnp.where(lane1 < live, s[3:4], 0.0)
            gs.append(stack(*split3(mix(s * w, w)), zero4))
        v = jnp.concatenate(vs, axis=1)
        g = jnp.concatenate(gs, axis=1)
        dist = lax.dot_general(v, u, (((0,), (0,)), ((), ())), preferred_element_type=F32)
        inv = lax.rsqrt(dist)
        f = inv * inv * inv
        high = f.astype(BF16)
        low = (f - high.astype(F32)).astype(BF16)
        o = jnp.dot(g, jnp.concatenate([high, low], axis=1), preferred_element_type=F32)
        o = o[:, :PL] + o[:, PL:]
        a = o[0:4] + o[4:8] + o[8:12]
        out_ref[tab[5, e] - row_base] = jnp.where(lane4 < tab[4, e], a - t * a[3:4], 0.0)

    sizes = [tab[8 + i, 0] for i in range(4)]

    def run(begin, size, width, step):
        def body(i, _):
            for j in range(step):
                job(begin + jnp.minimum(step * i + j, size - 1), width)

        lax.fori_loop(0, (size + step - 1) // step, body, None)

    def whole_steps(size, step):
        return (size + step - 1) // step * step

    n_full, n_half = sizes[0] + sizes[1], sizes[2] + sizes[3]
    early_full = jnp.minimum(n_full, jnp.maximum(whole_steps(sizes[0], UNROLL[0]), FULL_SLOTS))
    early_half = jnp.minimum(n_half, whole_steps(sizes[2], UNROLL[1]))
    if first:
        run(jnp.int32(0), early_full, 4, UNROLL[0])
        run(n_full, early_half, 2, UNROLL[1])
    else:
        run(early_full, n_full - early_full, 4, UNROLL_OWN[0])
        run(n_full + early_half, n_half - early_half, 2, UNROLL_OWN[1])
    if first:
        outs[-1][...] = out_ref[(NY - 1) * NB : NY * NB]
        outs = outs[:-1]
    for i, o in enumerate(outs):
        for c in range(3):
            o[c] = out_ref[i * NB : (i + 1) * NB, c, :]


def final_kernel(cnt_ref, far_ref, p0, p1, p2, p3, out_ref):
    live = lax.broadcasted_iota(I32, (NB, PL), 1) < column_of(cnt_ref[...], NB)
    for c in range(3):
        near = (p0[c] + p1[c]) + (p2[c] + p3[c])
        out_ref[c] = jnp.where(live, far_ref[c] + near, 0.0)


def along_y(k):
    return [(NZ * y + z, NZ * ((y + k) % NY) + z) for y in range(NY) for z in range(NZ)]


def along_x(k):
    return [(2 * x + c, 2 * ((x + k) % NX) + c) for x in range(NX) for c in range(2)]


def call(kernel, outs, in_specs, out_specs, name, mib, scratch=()):
    return pl.pallas_call(
        kernel,
        out_shape=[jax.ShapeDtypeStruct(shape, dtype) for shape, dtype in outs],
        in_specs=in_specs,
        out_specs=out_specs,
        scratch_shapes=scratch,
        compiler_params=pltpu.CompilerParams(vmem_limit_bytes=mib * MIB),
        name=name,
    )


def per_device(positions, masses, counts, dest_ids, near_list, cell_list, cell_centers, cell_mass):
    pos = jnp.transpose(positions[0], (1, 0, 2))
    cnt = counts[0]
    src, tgt, cells = call(
        pack_kernel,
        (((NZ, TILES + 1, 4, PL), F32), ((NB + 1, 4, PL), F32), ((16, 4, PL), F32)),
        [pl.BlockSpec(memory_space=pltpu.HBM)] * 7,
        [vspec()] * 3,
        "pack",
        8,
        [
            pltpu.VMEM((3, NB, PL), F32),
            pltpu.VMEM((NB, PL), F32),
            pltpu.VMEM((1, NB), I32),
            pltpu.VMEM((1, NB), I32),
            pltpu.VMEM((K, NB), I32),
            pltpu.VMEM((3, 2048), F32),
            pltpu.VMEM((1, 2048), F32),
            pltpu.SMEM((1, NB), I32),
            pltpu.VMEM((NB, 8, PL), F32),
            pltpu.SemaphoreType.DMA((8,)),
        ],
    )(
        *[
            pltpu.with_memory_space_constraint(v, pltpu.HBM)
            for v in (pos, masses[0], cnt, dest_ids, near_list[0].T, cell_centers, cell_mass[None])
        ]
    )
    z_rows = [[NZ * y + z for z in range(NZ)] for y in range(NY)]
    window = lax.all_to_all(src, "space", 0, 0, axis_index_groups=z_rows, tiled=True)
    tgts = [tgt] + [lax.ppermute(tgt, "space", along_y(k)) for k in (1, -1, 2)]
    pair = jnp.stack([cells, lax.ppermute(cells, "slab", [(i, i ^ 1) for i in range(2 * NX)])])
    pairs = [pair] + [lax.ppermute(pair, "slab", along_x(k)) for k in (1, -1, 2)]
    me = (lax.axis_index("space") // NZ).astype(I32).reshape(1)
    place = lax.axis_index("slab").astype(I32).reshape(1)
    tall, tab = call(
        prep_kernel,
        (((NY * NB, 4, PL), F32), ((16, 2 * PL), I32)),
        [sspec()] + [vspec()] * 4,
        [vspec(), vspec()],
        "prep",
        8,
    )(me, *tgts)
    (far,) = call(
        far_kernel,
        (((3, NB, PL), F32),),
        [sspec()] + [vspec()] * 7,
        [vspec()],
        "far",
        16,
        [pltpu.VMEM((PL, PL), F32)],
    )(place, pos, cnt, cell_list[0].T, *pairs)
    tall, tab, far = lax.optimization_barrier((tall, tab, far))
    window = window.reshape(NZ * (TILES + 1), 4, PL)

    def near(first, *arrays):
        partial = ((3, NB, PL), F32)
        kept = ((NB, 4, PL), F32)
        outs = (partial,) * (NY - 1) + (kept,) if first else (partial,)
        return call(
            functools.partial(near_kernel, first),
            outs,
            [vspec()] * len(arrays),
            [vspec()] * len(outs),
            "near",
            32,
            [
                pltpu.VMEM(((NY if first else 1) * NB, 4, PL), F32),
                pltpu.VMEM((NZ, PL), I32),
                pltpu.SMEM((NZ, PL), I32),
                pltpu.SMEM((16, 2 * PL), I32),
                pltpu.SemaphoreType.DMA((2,)),
            ],
        )(*arrays)

    *sent, kept = near(True, tab, tall, window)
    back = [lax.ppermute(v, "space", along_y(-k)) for v, k in zip(sent, (1, -1, 2))]
    (own,) = near(False, tab, tall, window, kept)
    (out,) = call(
        final_kernel,
        (((3, NB, PL), F32),),
        [vspec()] * 6,
        [vspec()],
        "final",
        8,
    )(cnt, far, own, *back)
    return jnp.transpose(out, (1, 0, 2))[None]


def solution(mesh):
    in_specs = (
        P("slab", "space", None, None),
        P("slab", "space", None),
        P("slab", "space", None),
        P("slab", "space"),
        P("slab", "space", None),
        P("slab", "space", None),
        P(None, "slab"),
        P("slab"),
    )
    return jax.shard_map(
        per_device,
        mesh=mesh,
        in_specs=in_specs,
        out_specs=P("slab", "space", None, None),
        check_vma=False,
    )
```

```python
import functools

import jax
import jax.numpy as jnp
from jax import lax
from jax.experimental import pallas as pl
from jax.experimental.pallas import tpu as pltpu
from jax.sharding import PartitionSpec as P

NB = 48
PL = 128
K = 4
LC = 32
NY = 4
NZ = 8
NX = 4
SOFT = 0.01
UNROLL = (18, 16)
UNROLL_OWN = (12, 8)
MIB = 1 << 20
TILES = 36
F32 = jnp.float32
I32 = jnp.int32
BF16 = jnp.bfloat16
VMEM = pltpu.VMEM
SMEM = pltpu.SMEM


def vspec():
    return pl.BlockSpec(memory_space=VMEM)


def sspec():
    return pl.BlockSpec(memory_space=SMEM)


def column_of(row, n):
    square = jnp.broadcast_to(row, (n, n))
    diag = lax.broadcasted_iota(I32, (n, n), 0) == lax.broadcasted_iota(I32, (n, n), 1)
    return jnp.sum(jnp.where(diag, square, jnp.zeros_like(square)), axis=1, keepdims=True)


def pack_kernel(*refs):
    ins, (src_ref, tgt_ref, cell_ref), holds = refs[:7], refs[7:10], refs[10:18]
    full, sem = refs[18:]
    copies = [pltpu.make_async_copy(ins[i], holds[i], sem.at[i]) for i in range(7)]
    copies.append(pltpu.make_async_copy(ins[2], holds[7], sem.at[7]))
    for copy in copies:
        copy.start()
    for copy in copies:
        copy.wait()
    pos_ref, mass_ref, cnt_ref, dest_ref, near_ref, ctr_ref, cm_ref, cnt_smem = holds
    counts = cnt_ref[...]
    cnt = column_of(counts, NB)
    near = near_ref[...]
    off = (near >= NB).astype(I32) + (near >= 2 * NB).astype(I32)
    dev = (dest_ref[...] + off - 1) & (NY * NZ - 1)
    code = (dev >> 3) * 512 + (dev & (NZ - 1)) * 64 + (near - off * NB)
    gap = jnp.zeros((4, 64 - NB), I32)
    info = jnp.concatenate([code, gap, jnp.broadcast_to(counts, (4, NB)), gap], axis=1)
    lane = lax.broadcasted_iota(I32, (NB, PL), 1)
    weight = jnp.where(lane < cnt, mass_ref[...], 0.0)
    for c in range(3):
        value = pos_ref[c]
        tgt_ref[0:NB, c, :] = value
        full[:, c, :] = value
    full[:, 3, :] = weight
    lane4 = lax.broadcasted_iota(I32, (4, PL), 1)
    carry, begin = jnp.zeros((4, PL), F32), jnp.int32(0)
    for b in range(NB):
        shift, tile = begin & (PL - 1), begin >> 7
        turned = pltpu.roll(full[b], shift, 1)[0:4]
        merged = jnp.where(lane4 >= shift, turned, carry)
        src_ref[0, tile] = merged
        begin = begin + cnt_smem[0, b]
        carry = jnp.where((begin >> 7) != tile, turned, merged)
    square = (NB, NB)
    earlier = lax.broadcasted_iota(I32, square, 0) < lax.broadcasted_iota(I32, square, 1)
    starts = jnp.sum(jnp.where(earlier, cnt, 0), axis=0, keepdims=True)
    places = jnp.concatenate([starts, gap[0:1], counts, gap[0:1]], axis=1)
    src_ref[0, TILES] = jnp.broadcast_to(places, (4, PL)).astype(F32)
    for z in range(1, NZ):
        src_ref[z] = src_ref[0]
    tgt_ref[0:NB, 3, :] = jnp.zeros((NB, PL), F32)
    tgt_ref[NB] = info.astype(F32)
    for j in range(16):
        part = slice(j * PL, (j + 1) * PL)
        cell_ref[j, 0:3, :] = ctr_ref[:, part]
        cell_ref[j, 3:4, :] = cm_ref[0:1, part]


def far_kernel(place_ref, pos_ref, cnt_ref, list_ref, c0, c1, c2, c3, out_ref, pad):
    xs, cs = place_ref[0] >> 1, place_ref[0] & 1
    lane = lax.broadcasted_iota(I32, (NB, PL), 1)
    cnt = column_of(cnt_ref[...], NB)
    live = lane < cnt
    total = jnp.maximum(cnt, 1).astype(F32)
    pos = [pos_ref[c] for c in range(3)]
    centre = [jnp.sum(jnp.where(live, v, 0.0), axis=1, keepdims=True) / total for v in pos]
    diag = lax.broadcasted_iota(I32, (NB, PL), 0) == (lane & 63)
    ctr = [jnp.sum(jnp.where(diag, v, 0.0), axis=0, keepdims=True) for v in centre]
    wide = jnp.concatenate([list_ref[...], jnp.zeros((LC, PL - NB), I32)], axis=1)
    twice = wide + pltpu.roll(wide, 64, 1)
    half = lax.broadcasted_iota(I32, (1, PL), 1) < 64
    ids = [jnp.where(half, twice[2 * j : 2 * j + 1], twice[2 * j + 1 : 2 * j + 2]) for j in range(LC // 2)]
    ids = jnp.concatenate(ids, axis=0)
    slab = ids >> 11
    dx = ((slab >> 1) - xs) & (NX - 1)
    order = jnp.where(dx == 3, 1, jnp.where(dx == 0, 0, dx + 1))
    rows = (order * 2 + ((slab & 1) ^ cs)) * 16 + ((ids >> 7) & 15)
    lanes = ids & (PL - 1)
    tables = []
    for c in range(4):
        whole = jnp.concatenate([ref[i, :, c, :] for ref in (c0, c1, c2, c3) for i in range(2)], axis=0)
        whole = whole.T
        high = whole.astype(BF16)
        low = (whole - high.astype(F32)).astype(BF16)
        tables.append(jnp.concatenate([high, low], axis=1))
    tables = jnp.concatenate(tables, axis=0)
    sub = lax.broadcasted_iota(I32, (PL, 2 * PL), 0)
    got = [[] for _ in range(4)]
    for j in range(0, LC // 2, 2):
        r2 = jnp.concatenate([rows[j : j + 1], rows[j + 1 : j + 2]], axis=1)
        l2 = jnp.concatenate([lanes[j : j + 1], lanes[j + 1 : j + 2]], axis=1)
        hot = jnp.where(sub == r2, 1.0, 0.0).astype(BF16)
        hot = jnp.concatenate([hot, hot], axis=0)
        found = jnp.dot(tables, hot, preferred_element_type=F32)
        pick = sub == l2
        for c in range(4):
            value = jnp.sum(jnp.where(pick, found[c * PL : (c + 1) * PL], 0.0), axis=0, keepdims=True)
            got[c] += [value[:, :PL], value[:, PL:]]
    cells = [jnp.concatenate(v, axis=0) for v in got]
    rel = [ctr[c] - cells[c] for c in range(3)]
    dist = rel[0] * rel[0] + rel[1] * rel[1] + rel[2] * rel[2] + 1.0
    inv = lax.rsqrt(dist)
    cube = cells[3] * (inv * inv * inv)
    fifth = 3.0 * cube * (inv * inv)
    terms = [-(cube * rel[c]) for c in range(3)]
    for a, b in ((0, 0), (1, 1), (2, 2), (0, 1), (0, 2), (1, 2)):
        value = fifth * rel[a] * rel[b]
        if a == b:
            value = value - cube
        terms.append(value)
    terms = [jnp.sum(v, axis=0, keepdims=True) for v in terms]
    pad[...] = jnp.zeros((PL, PL), F32)
    for i, v in enumerate(terms):
        pad[i : i + 1, :] = v + pltpu.roll(v, 64, 1)
    back = pad[...].T
    field = [back[0:NB, i : i + 1] for i in range(3)]
    tide = [back[0:NB, 3 + i : 4 + i] for i in range(6)]
    offset = [pos[c] - centre[c] for c in range(3)]
    for c, (i, j, k) in enumerate(((0, 3, 4), (3, 1, 5), (4, 5, 2))):
        out_ref[c] = field[c] + tide[i] * offset[0] + tide[j] * offset[1] + tide[k] * offset[2]


def split3(v):
    high = v.astype(BF16).astype(F32)
    rest = v - high
    mid = rest.astype(BF16).astype(F32)
    return high, mid, rest - mid


def prep_kernel(y_ref, t0, t1, t2, t3, tall, tab):
    me = y_ref[0]
    wide = 2 * PL
    tiles = []
    for i, t in enumerate((t0, t1, t2, t3)):
        tall[i * NB : (i + 1) * NB] = t[0:NB]
        tiles.append(t[NB])
    left = lax.broadcasted_iota(I32, (4, PL), 1) < 64
    code, cnt = [], []
    for a, b in ((tiles[0], tiles[1]), (tiles[2], tiles[3])):
        code.append(jnp.where(left, a, pltpu.roll(b, 64, 1)))
        cnt.append(jnp.where(left, pltpu.roll(a, 64, 1), b))
    code = jnp.concatenate(code, axis=1).astype(I32)
    cnt = jnp.concatenate(cnt, axis=1)[0:1]
    lane = lax.broadcasted_iota(I32, (1, wide), 1)
    valid = (lane & 63) < NB
    flag = [jnp.where(((code[k : k + 1] >> 9) == me) & valid, 1.0, 0.0) for k in range(K)]
    local = [(code[k : k + 1] & 511).astype(F32) for k in range(K)]
    count = (flag[0] + flag[1]) + (flag[2] + flag[3])
    full = jnp.where(count > 2.5, 1.0, 0.0)
    half = jnp.where((count > 0.5) & (count < 2.5), 1.0, 0.0)
    group = lane >> 6
    mine = group == 0
    lists = [jnp.where(m, v, 0.0) for v in (full, half) for m in (~mine, mine)]
    marks = jnp.concatenate(lists + [jnp.zeros((12, wide), F32)], axis=0).astype(BF16)
    a = lax.broadcasted_iota(I32, (wide, wide), 0)
    b = lax.broadcasted_iota(I32, (wide, wide), 1)
    before = jnp.dot(marks, jnp.where(a < b, 1.0, 0.0).astype(BF16), preferred_element_type=F32)
    sizes = [jnp.sum(v, axis=1, keepdims=True) for v in lists]
    place, begin = jnp.full((1, wide), -1.0, F32), jnp.zeros((1, 1), F32)
    for i, v in enumerate(lists):
        place = jnp.where(v > 0.5, begin + before[i : i + 1], place)
        begin = begin + sizes[i]
    moved = jnp.where(a == place.astype(I32), 1.0, 0.0).astype(BF16)
    bucket = lane & 63
    step = jnp.where(group == 2, -1, jnp.where(group == 3, 2, group))
    home = ((me - step) & (NY - 1)) * NB + bucket
    slot, ins, outs = [], jnp.zeros((1, wide), F32), jnp.zeros((1, wide), F32)
    for k in range(K):
        slot.append(jnp.where(flag[k] > 0.5, ins, count + outs))
        ins, outs = ins + flag[k], outs + (1.0 - flag[k])
    fields = []
    for j in range(K):
        pick = jnp.zeros((1, wide), F32)
        for k in range(K):
            pick = pick + jnp.where(slot[k] == float(j), local[k], 0.0)
        fields.append(pick)
    fields += [cnt, home.astype(F32), count, (group * NB + bucket).astype(F32)]
    load = jnp.concatenate(fields, axis=0)
    high = load.astype(BF16).astype(F32)
    both = jnp.concatenate([high, load - high], axis=0).astype(BF16)
    out = lax.dot_general(both, moved, (((1,), (1,)), ((), ())), preferred_element_type=F32)
    out = out[0:8] + out[8:16]
    sizes = jnp.concatenate([jnp.broadcast_to(v, (1, wide)) for v in sizes + [begin] * 4], axis=0)
    tab[...] = jnp.concatenate([out, sizes], axis=0).astype(I32)


def near_kernel(first, *refs):
    (table, tall, src_ref), refs = refs[:3], refs[3:]
    sums, out_ref, hold, spots, tab, sem = refs
    copies = [pltpu.make_async_copy(table, tab, sem.at[0]), pltpu.make_async_copy(hold, spots, sem.at[1])]
    copies[0].start()
    for z in range(NZ):
        hold[z : z + 1, :] = src_ref[z * (TILES + 1) + TILES][0:1].astype(I32)
    copies[1].start()
    out_ref[...] = jnp.zeros(out_ref.shape, F32)
    for copy in copies:
        copy.wait()
    lane1 = lax.broadcasted_iota(I32, (1, PL), 1)
    sub4 = lax.broadcasted_iota(I32, (4, PL), 0)
    lane4 = lax.broadcasted_iota(I32, (4, PL), 1)
    spatial = sub4 < 3
    one = jnp.ones((4, PL), F32)
    zero4 = jnp.zeros((4, PL), F32)
    zero8 = jnp.zeros((8, PL), F32)

    def square(v):
        return jnp.sum(jnp.where(spatial, v * v, 0.0), axis=0, keepdims=True)

    def mix(a, b):
        return jnp.where(spatial, a, b)

    def stack(*v):
        return jnp.concatenate(v, axis=0).astype(BF16)

    row_field = 5 if first else 7

    def job(e, width):
        n = tab[6, e]
        t = tall[tab[7, e]]
        th, tm, tl = split3(t)
        qh, qm, ql = split3(square(t))
        u = stack(mix(th, one), mix(th, one), mix(tm, one), mix(tm, qh), mix(th, qm), mix(tl, ql), zero8)
        vs, gs = [], []
        for k in range(width):
            z, bucket = tab[k, e] >> 6, tab[k, e] & 63
            begin = spots[z, bucket]
            shift = begin & (PL - 1)
            tile = z * (TILES + 1) + (begin >> 7)
            s = jnp.concatenate([src_ref[tile], src_ref[tile + 1]], axis=0)
            s = pltpu.roll(s, (PL - shift) & (PL - 1), 1)
            s = jnp.where(lane4 < PL - shift, s[0:4], s[4:8])
            live = jnp.where(k < n, spots[z, 64 + bucket], 0)
            sh, sm, sl = split3(-2.0 * s)
            qh, qm, ql = split3(square(s) + SOFT)
            vs.append(stack(mix(sh, qh), mix(sm, qm), mix(sh, ql), mix(sm, one), mix(sl, one), mix(sh, one), zero8))
            w = jnp.where(lane1 < live, s[3:4], 0.0)
            gs.append(stack(*split3(mix(s * w, w)), zero4))
        v = jnp.concatenate(vs, axis=1)
        g = jnp.concatenate(gs, axis=1)
        dist = lax.dot_general(v, u, (((0,), (0,)), ((), ())), preferred_element_type=F32)
        inv = lax.rsqrt(dist)
        f = inv * inv * inv
        high = f.astype(BF16)
        low = (f - high.astype(F32)).astype(BF16)
        o = jnp.dot(g, jnp.concatenate([high, low], axis=1), preferred_element_type=F32)
        o = o[:, :PL] + o[:, PL:]
        a = o[0:4] + o[4:8] + o[8:12]
        out_ref[tab[row_field, e]] = jnp.where(lane4 < tab[4, e], a - t * a[3:4], 0.0)

    sizes = [tab[8 + i, 0] for i in range(4)]

    def run(begin, size, width, step):
        def body(i, _):
            for j in range(step):
                job(begin + jnp.minimum(step * i + j, size - 1), width)

        lax.fori_loop(0, (size + step - 1) // step, body, None)

    def whole_steps(size, step):
        return (size + step - 1) // step * step

    n_full, n_half = sizes[0] + sizes[1], sizes[2] + sizes[3]
    early_full = jnp.minimum(n_full, whole_steps(sizes[0], UNROLL[0]))
    early_half = jnp.minimum(n_half, whole_steps(sizes[2], UNROLL[1]))
    if first:
        run(jnp.int32(0), early_full, 4, UNROLL[0])
        run(n_full, early_half, 2, UNROLL[1])
    else:
        run(early_full, n_full - early_full, 4, UNROLL_OWN[0])
        run(n_full + early_half, n_half - early_half, 2, UNROLL_OWN[1])
    for i in range(sums.shape[0]):
        for c in range(3):
            sums[i, c] = out_ref[i * NB : (i + 1) * NB, c, :]


def final_kernel(cnt_ref, far_ref, own_ref, back_ref, out_ref):
    live = lax.broadcasted_iota(I32, (NB, PL), 1) < column_of(cnt_ref[...], NB)
    for c in range(3):
        near = (back_ref[0, c] + back_ref[1, c]) + (back_ref[2, c] + back_ref[3, c])
        out_ref[c] = jnp.where(live, far_ref[c] + (near + own_ref[0, c]), 0.0)


def along_y(k):
    return [(NZ * y + z, NZ * ((y + k) % NY) + z) for y in range(NY) for z in range(NZ)]


def along_x(k):
    return [(2 * x + c, 2 * ((x + k) % NX) + c) for x in range(NX) for c in range(2)]


def call(kernel, outs, in_specs, out_specs, name, mib, scratch=()):
    return pl.pallas_call(
        kernel,
        out_shape=[jax.ShapeDtypeStruct(shape, dtype) for shape, dtype in outs],
        in_specs=in_specs,
        out_specs=out_specs,
        scratch_shapes=scratch,
        compiler_params=pltpu.CompilerParams(vmem_limit_bytes=mib * MIB),
        name=name,
    )


def per_device(positions, masses, counts, dest_ids, near_list, cell_list, cell_centers, cell_mass):
    pos = jnp.transpose(positions[0], (1, 0, 2))
    cnt = counts[0]
    src, tgt, cells = call(
        pack_kernel,
        (((NZ, TILES + 1, 4, PL), F32), ((NB + 1, 4, PL), F32), ((16, 4, PL), F32)),
        [pl.BlockSpec(memory_space=pltpu.HBM)] * 7,
        [vspec()] * 3,
        "pack",
        8,
        [
            pltpu.VMEM((3, NB, PL), F32),
            pltpu.VMEM((NB, PL), F32),
            pltpu.VMEM((1, NB), I32),
            pltpu.VMEM((1, NB), I32),
            pltpu.VMEM((K, NB), I32),
            pltpu.VMEM((3, 2048), F32),
            pltpu.VMEM((1, 2048), F32),
            pltpu.SMEM((1, NB), I32),
            pltpu.VMEM((NB, 8, PL), F32),
            pltpu.SemaphoreType.DMA((8,)),
        ],
    )(
        *[
            pltpu.with_memory_space_constraint(v, pltpu.HBM)
            for v in (pos, masses[0], cnt, dest_ids, near_list[0].T, cell_centers, cell_mass[None])
        ]
    )
    z_rows = [[NZ * y + z for z in range(NZ)] for y in range(NY)]
    window = lax.all_to_all(src, "space", 0, 0, axis_index_groups=z_rows, tiled=True)
    tgts = [tgt] + [lax.ppermute(tgt, "space", along_y(k)) for k in (1, -1, 2)]
    pair = jnp.stack([cells, lax.ppermute(cells, "slab", [(i, i ^ 1) for i in range(2 * NX)])])
    pairs = [pair] + [lax.ppermute(pair, "slab", along_x(k)) for k in (1, -1, 2)]
    me = (lax.axis_index("space") // NZ).astype(I32).reshape(1)
    place = lax.axis_index("slab").astype(I32).reshape(1)
    tall, tab = call(
        prep_kernel,
        (((NY * NB, 4, PL), F32), ((16, 2 * PL), I32)),
        [sspec()] + [vspec()] * 4,
        [vspec(), vspec()],
        "prep",
        8,
    )(me, *tgts)
    (far,) = call(
        far_kernel,
        (((3, NB, PL), F32),),
        [sspec()] + [vspec()] * 7,
        [vspec()],
        "far",
        16,
        [pltpu.VMEM((PL, PL), F32)],
    )(place, pos, cnt, cell_list[0].T, *pairs)
    tall, tab, far = lax.optimization_barrier((tall, tab, far))
    window = window.reshape(NZ * (TILES + 1), 4, PL)

    def near(first, tab):
        count = NY if first else 1
        return call(
            functools.partial(near_kernel, first),
            (((count, 3, NB, PL), F32),),
            [vspec()] * 3,
            [vspec()],
            "near",
            32,
            [
                pltpu.VMEM((count * NB, 4, PL), F32),
                pltpu.VMEM((NZ, PL), I32),
                pltpu.SMEM((NZ, PL), I32),
                pltpu.SMEM((16, 2 * PL), I32),
                pltpu.SemaphoreType.DMA((2,)),
            ],
        )(tab, tall, window)[0]

    sums = near(True, tab)
    y_rows = [[NZ * y + z for y in range(NY)] for z in range(NZ)]
    back = lax.all_to_all(sums, "space", 0, 0, axis_index_groups=y_rows, tiled=True)
    tab, sums = lax.optimization_barrier((tab, sums))
    own = near(False, tab)
    (out,) = call(
        final_kernel,
        (((3, NB, PL), F32),),
        [vspec()] * 4,
        [vspec()],
        "final",
        8,
    )(cnt, far, own, back)
    return jnp.transpose(out, (1, 0, 2))[None]


def solution(mesh):
    in_specs = (
        P("slab", "space", None, None),
        P("slab", "space", None),
        P("slab", "space", None),
        P("slab", "space"),
        P("slab", "space", None),
        P("slab", "space", None),
        P(None, "slab"),
        P("slab"),
    )
    return jax.shard_map(
        per_device,
        mesh=mesh,
        in_specs=in_specs,
        out_specs=P("slab", "space", None, None),
        check_vma=False,
    )
```

```python
import functools

import jax
import jax.numpy as jnp
from jax import lax
from jax.experimental import pallas as pl
from jax.experimental.pallas import tpu as pltpu
from jax.sharding import PartitionSpec as P

NB = 48
PL = 128
K = 4
LC = 32
NY = 4
NZ = 8
NX = 4
SOFT = 0.01
UNROLL = (18, 20)
UNROLL_OWN = (12, 8)
MIB = 1 << 20
TILES = 36
F32 = jnp.float32
I32 = jnp.int32
BF16 = jnp.bfloat16
VMEM = pltpu.VMEM
SMEM = pltpu.SMEM


def vspec():
    return pl.BlockSpec(memory_space=VMEM)


def sspec():
    return pl.BlockSpec(memory_space=SMEM)


def column_of(row, n):
    square = jnp.broadcast_to(row, (n, n))
    diag = lax.broadcasted_iota(I32, (n, n), 0) == lax.broadcasted_iota(I32, (n, n), 1)
    return jnp.sum(jnp.where(diag, square, jnp.zeros_like(square)), axis=1, keepdims=True)


def pack_kernel(*refs):
    ins, (src_ref, tgt_ref, cell_ref), holds = refs[:7], refs[7:10], refs[10:18]
    full, sem = refs[18:]
    copies = [pltpu.make_async_copy(ins[i], holds[i], sem.at[i]) for i in range(7)]
    copies.append(pltpu.make_async_copy(ins[2], holds[7], sem.at[7]))
    for copy in copies:
        copy.start()
    for copy in copies:
        copy.wait()
    pos_ref, mass_ref, cnt_ref, dest_ref, near_ref, ctr_ref, cm_ref, cnt_smem = holds
    counts = cnt_ref[...]
    cnt = column_of(counts, NB)
    near = near_ref[...]
    off = (near >= NB).astype(I32) + (near >= 2 * NB).astype(I32)
    dev = (dest_ref[...] + off - 1) & (NY * NZ - 1)
    code = (dev >> 3) * 512 + (dev & (NZ - 1)) * 64 + (near - off * NB)
    gap = jnp.zeros((4, 64 - NB), I32)
    info = jnp.concatenate([code, gap, jnp.broadcast_to(counts, (4, NB)), gap], axis=1)
    lane = lax.broadcasted_iota(I32, (NB, PL), 1)
    weight = jnp.where(lane < cnt, mass_ref[...], 0.0)
    for c in range(3):
        value = pos_ref[c]
        tgt_ref[0:NB, c, :] = value
        full[:, c, :] = value
    full[:, 3, :] = weight
    lane4 = lax.broadcasted_iota(I32, (4, PL), 1)
    carry, begin = jnp.zeros((4, PL), F32), jnp.int32(0)
    for b in range(NB):
        shift, tile = begin & (PL - 1), begin >> 7
        turned = pltpu.roll(full[b], shift, 1)[0:4]
        merged = jnp.where(lane4 >= shift, turned, carry)
        src_ref[0, tile] = merged
        begin = begin + cnt_smem[0, b]
        carry = jnp.where((begin >> 7) != tile, turned, merged)
    square = (NB, NB)
    earlier = lax.broadcasted_iota(I32, square, 0) < lax.broadcasted_iota(I32, square, 1)
    starts = jnp.sum(jnp.where(earlier, cnt, 0), axis=0, keepdims=True)
    places = jnp.concatenate([starts, gap[0:1], counts, gap[0:1]], axis=1)
    src_ref[0, TILES] = jnp.broadcast_to(places, (4, PL)).astype(F32)
    for z in range(1, NZ):
        src_ref[z] = src_ref[0]
    tgt_ref[0:NB, 3, :] = jnp.zeros((NB, PL), F32)
    tgt_ref[NB] = info.astype(F32)
    for j in range(16):
        part = slice(j * PL, (j + 1) * PL)
        cell_ref[j, 0:3, :] = ctr_ref[:, part]
        cell_ref[j, 3:4, :] = cm_ref[0:1, part]


def far_kernel(place_ref, pos_ref, cnt_ref, list_ref, c0, c1, c2, c3, out_ref, pad):
    xs, cs = place_ref[0] >> 1, place_ref[0] & 1
    lane = lax.broadcasted_iota(I32, (NB, PL), 1)
    cnt = column_of(cnt_ref[...], NB)
    live = lane < cnt
    total = jnp.maximum(cnt, 1).astype(F32)
    pos = [pos_ref[c] for c in range(3)]
    centre = [jnp.sum(jnp.where(live, v, 0.0), axis=1, keepdims=True) / total for v in pos]
    diag = lax.broadcasted_iota(I32, (NB, PL), 0) == (lane & 63)
    ctr = [jnp.sum(jnp.where(diag, v, 0.0), axis=0, keepdims=True) for v in centre]
    wide = jnp.concatenate([list_ref[...], jnp.zeros((LC, PL - NB), I32)], axis=1)
    twice = wide + pltpu.roll(wide, 64, 1)
    half = lax.broadcasted_iota(I32, (1, PL), 1) < 64
    ids = [jnp.where(half, twice[2 * j : 2 * j + 1], twice[2 * j + 1 : 2 * j + 2]) for j in range(LC // 2)]
    ids = jnp.concatenate(ids, axis=0)
    slab = ids >> 11
    dx = ((slab >> 1) - xs) & (NX - 1)
    order = jnp.where(dx == 3, 1, jnp.where(dx == 0, 0, dx + 1))
    rows = (order * 2 + ((slab & 1) ^ cs)) * 16 + ((ids >> 7) & 15)
    lanes = ids & (PL - 1)
    tables = []
    for c in range(4):
        whole = jnp.concatenate([ref[i, :, c, :] for ref in (c0, c1, c2, c3) for i in range(2)], axis=0)
        whole = whole.T
        high = whole.astype(BF16)
        low = (whole - high.astype(F32)).astype(BF16)
        tables.append(jnp.concatenate([high, low], axis=1))
    tables = jnp.concatenate(tables, axis=0)
    sub = lax.broadcasted_iota(I32, (PL, 2 * PL), 0)
    got = [[] for _ in range(4)]
    for j in range(0, LC // 2, 2):
        r2 = jnp.concatenate([rows[j : j + 1], rows[j + 1 : j + 2]], axis=1)
        l2 = jnp.concatenate([lanes[j : j + 1], lanes[j + 1 : j + 2]], axis=1)
        hot = jnp.where(sub == r2, 1.0, 0.0).astype(BF16)
        hot = jnp.concatenate([hot, hot], axis=0)
        found = jnp.dot(tables, hot, preferred_element_type=F32)
        pick = sub == l2
        for c in range(4):
            value = jnp.sum(jnp.where(pick, found[c * PL : (c + 1) * PL], 0.0), axis=0, keepdims=True)
            got[c] += [value[:, :PL], value[:, PL:]]
    cells = [jnp.concatenate(v, axis=0) for v in got]
    rel = [ctr[c] - cells[c] for c in range(3)]
    dist = rel[0] * rel[0] + rel[1] * rel[1] + rel[2] * rel[2] + 1.0
    inv = lax.rsqrt(dist)
    cube = cells[3] * (inv * inv * inv)
    fifth = 3.0 * cube * (inv * inv)
    terms = [-(cube * rel[c]) for c in range(3)]
    for a, b in ((0, 0), (1, 1), (2, 2), (0, 1), (0, 2), (1, 2)):
        value = fifth * rel[a] * rel[b]
        if a == b:
            value = value - cube
        terms.append(value)
    terms = [jnp.sum(v, axis=0, keepdims=True) for v in terms]
    pad[...] = jnp.zeros((PL, PL), F32)
    for i, v in enumerate(terms):
        pad[i : i + 1, :] = v + pltpu.roll(v, 64, 1)
    back = pad[...].T
    field = [back[0:NB, i : i + 1] for i in range(3)]
    tide = [back[0:NB, 3 + i : 4 + i] for i in range(6)]
    offset = [pos[c] - centre[c] for c in range(3)]
    for c, (i, j, k) in enumerate(((0, 3, 4), (3, 1, 5), (4, 5, 2))):
        out_ref[c] = field[c] + tide[i] * offset[0] + tide[j] * offset[1] + tide[k] * offset[2]


def split3(v):
    high = v.astype(BF16).astype(F32)
    rest = v - high
    mid = rest.astype(BF16).astype(F32)
    return high, mid, rest - mid


def prep_kernel(y_ref, t0, t1, t2, t3, tall, tab):
    me = y_ref[0]
    wide = 2 * PL
    tiles = []
    for i, t in enumerate((t0, t1, t2, t3)):
        tall[i * NB : (i + 1) * NB] = t[0:NB]
        tiles.append(t[NB])
    left = lax.broadcasted_iota(I32, (4, PL), 1) < 64
    code, cnt = [], []
    for a, b in ((tiles[0], tiles[1]), (tiles[2], tiles[3])):
        code.append(jnp.where(left, a, pltpu.roll(b, 64, 1)))
        cnt.append(jnp.where(left, pltpu.roll(a, 64, 1), b))
    code = jnp.concatenate(code, axis=1).astype(I32)
    cnt = jnp.concatenate(cnt, axis=1)[0:1]
    lane = lax.broadcasted_iota(I32, (1, wide), 1)
    valid = (lane & 63) < NB
    flag = [jnp.where(((code[k : k + 1] >> 9) == me) & valid, 1.0, 0.0) for k in range(K)]
    local = [(code[k : k + 1] & 511).astype(F32) for k in range(K)]
    count = (flag[0] + flag[1]) + (flag[2] + flag[3])
    full = jnp.where(count > 2.5, 1.0, 0.0)
    half = jnp.where((count > 0.5) & (count < 2.5), 1.0, 0.0)
    group = lane >> 6
    mine = group == 0
    lists = [jnp.where(m, v, 0.0) for v in (full, half) for m in (~mine, mine)]
    marks = jnp.concatenate(lists + [jnp.zeros((12, wide), F32)], axis=0).astype(BF16)
    a = lax.broadcasted_iota(I32, (wide, wide), 0)
    b = lax.broadcasted_iota(I32, (wide, wide), 1)
    before = jnp.dot(marks, jnp.where(a < b, 1.0, 0.0).astype(BF16), preferred_element_type=F32)
    sizes = [jnp.sum(v, axis=1, keepdims=True) for v in lists]
    place, begin = jnp.full((1, wide), -1.0, F32), jnp.zeros((1, 1), F32)
    for i, v in enumerate(lists):
        place = jnp.where(v > 0.5, begin + before[i : i + 1], place)
        begin = begin + sizes[i]
    moved = jnp.where(a == place.astype(I32), 1.0, 0.0).astype(BF16)
    bucket = lane & 63
    home = ((group - 1) & (NY - 1)) * NB + bucket
    slot, ins, outs = [], jnp.zeros((1, wide), F32), jnp.zeros((1, wide), F32)
    for k in range(K):
        slot.append(jnp.where(flag[k] > 0.5, ins, count + outs))
        ins, outs = ins + flag[k], outs + (1.0 - flag[k])
    fields = []
    for j in range(K):
        pick = jnp.zeros((1, wide), F32)
        for k in range(K):
            pick = pick + jnp.where(slot[k] == float(j), local[k], 0.0)
        fields.append(pick)
    fields += [cnt, home.astype(F32), count, (group * NB + bucket).astype(F32)]
    load = jnp.concatenate(fields, axis=0)
    high = load.astype(BF16).astype(F32)
    both = jnp.concatenate([high, load - high], axis=0).astype(BF16)
    out = lax.dot_general(both, moved, (((1,), (1,)), ((), ())), preferred_element_type=F32)
    out = out[0:8] + out[8:16]
    sizes = jnp.concatenate([jnp.broadcast_to(v, (1, wide)) for v in sizes + [begin] * 4], axis=0)
    tab[...] = jnp.concatenate([out, sizes], axis=0).astype(I32)


def near_kernel(first, *refs):
    (table, tall, src_ref), refs = refs[:3], refs[3:]
    outs, (out_ref, hold, spots, tab, sem) = refs[:-5], refs[-5:]
    if not first:
        kept, outs = outs[0], outs[1:]
    copies = [pltpu.make_async_copy(table, tab, sem.at[0]), pltpu.make_async_copy(hold, spots, sem.at[1])]
    copies[0].start()
    for z in range(NZ):
        hold[z : z + 1, :] = src_ref[z * (TILES + 1) + TILES][0:1].astype(I32)
    copies[1].start()
    out_ref[...] = jnp.zeros(out_ref.shape, F32) if first else kept[...]
    for copy in copies:
        copy.wait()
    lane1 = lax.broadcasted_iota(I32, (1, PL), 1)
    sub4 = lax.broadcasted_iota(I32, (4, PL), 0)
    lane4 = lax.broadcasted_iota(I32, (4, PL), 1)
    spatial = sub4 < 3
    one = jnp.ones((4, PL), F32)
    zero4 = jnp.zeros((4, PL), F32)
    zero8 = jnp.zeros((8, PL), F32)

    def square(v):
        return jnp.sum(jnp.where(spatial, v * v, 0.0), axis=0, keepdims=True)

    def mix(a, b):
        return jnp.where(spatial, a, b)

    def stack(*v):
        return jnp.concatenate(v, axis=0).astype(BF16)

    row_base = 0 if first else (NY - 1) * NB

    def job(e, width):
        n = tab[6, e]
        t = tall[tab[7, e]]
        th, tm, tl = split3(t)
        qh, qm, ql = split3(square(t))
        u = stack(mix(th, one), mix(th, one), mix(tm, one), mix(tm, qh), mix(th, qm), mix(tl, ql), zero8)
        vs, gs = [], []
        for k in range(width):
            z, bucket = tab[k, e] >> 6, tab[k, e] & 63
            begin = spots[z, bucket]
            shift = begin & (PL - 1)
            tile = z * (TILES + 1) + (begin >> 7)
            s = jnp.concatenate([src_ref[tile], src_ref[tile + 1]], axis=0)
            s = pltpu.roll(s, (PL - shift) & (PL - 1), 1)
            s = jnp.where(lane4 < PL - shift, s[0:4], s[4:8])
            live = jnp.where(k < n, spots[z, 64 + bucket], 0)
            sh, sm, sl = split3(-2.0 * s)
            qh, qm, ql = split3(square(s) + SOFT)
            vs.append(stack(mix(sh, qh), mix(sm, qm), mix(sh, ql), mix(sm, one), mix(sl, one), mix(sh, one), zero8))
            w = jnp.where(lane1 < live, s[3:4], 0.0)
            gs.append(stack(*split3(mix(s * w, w)), zero4))
        v = jnp.concatenate(vs, axis=1)
        g = jnp.concatenate(gs, axis=1)
        dist = lax.dot_general(v, u, (((0,), (0,)), ((), ())), preferred_element_type=F32)
        inv = lax.rsqrt(dist)
        f = inv * inv * inv
        high = f.astype(BF16)
        low = (f - high.astype(F32)).astype(BF16)
        o = jnp.dot(g, jnp.concatenate([high, low], axis=1), preferred_element_type=F32)
        o = o[:, :PL] + o[:, PL:]
        a = o[0:4] + o[4:8] + o[8:12]
        out_ref[tab[5, e] - row_base] = jnp.where(lane4 < tab[4, e], a - t * a[3:4], 0.0)

    sizes = [tab[8 + i, 0] for i in range(4)]

    def run(begin, size, width, step):
        def body(i, _):
            for j in range(step):
                job(begin + jnp.minimum(step * i + j, size - 1), width)

        lax.fori_loop(0, (size + step - 1) // step, body, None)

    def whole_steps(size, step):
        return (size + step - 1) // step * step

    n_full, n_half = sizes[0] + sizes[1], sizes[2] + sizes[3]
    early_full = jnp.minimum(n_full, whole_steps(sizes[0], UNROLL[0]))
    early_half = jnp.minimum(n_half, whole_steps(sizes[2], UNROLL[1]))
    if first:
        run(jnp.int32(0), early_full, 4, UNROLL[0])
        run(n_full, early_half, 2, UNROLL[1])
    else:
        run(early_full, n_full - early_full, 4, UNROLL_OWN[0])
        run(n_full + early_half, n_half - early_half, 2, UNROLL_OWN[1])
    if first:
        outs[-1][...] = out_ref[(NY - 1) * NB : NY * NB]
        outs = outs[:-1]
    for i, o in enumerate(outs):
        for c in range(3):
            o[c] = out_ref[i * NB : (i + 1) * NB, c, :]


def final_kernel(cnt_ref, far_ref, p0, p1, p2, p3, out_ref):
    live = lax.broadcasted_iota(I32, (NB, PL), 1) < column_of(cnt_ref[...], NB)
    for c in range(3):
        near = (p0[c] + p1[c]) + (p2[c] + p3[c])
        out_ref[c] = jnp.where(live, far_ref[c] + near, 0.0)


def along_y(k):
    return [(NZ * y + z, NZ * ((y + k) % NY) + z) for y in range(NY) for z in range(NZ)]


def along_x(k):
    return [(2 * x + c, 2 * ((x + k) % NX) + c) for x in range(NX) for c in range(2)]


def call(kernel, outs, in_specs, out_specs, name, mib, scratch=()):
    return pl.pallas_call(
        kernel,
        out_shape=[jax.ShapeDtypeStruct(shape, dtype) for shape, dtype in outs],
        in_specs=in_specs,
        out_specs=out_specs,
        scratch_shapes=scratch,
        compiler_params=pltpu.CompilerParams(vmem_limit_bytes=mib * MIB),
        name=name,
    )


def per_device(positions, masses, counts, dest_ids, near_list, cell_list, cell_centers, cell_mass):
    pos = jnp.transpose(positions[0], (1, 0, 2))
    cnt = counts[0]
    src, tgt, cells = call(
        pack_kernel,
        (((NZ, TILES + 1, 4, PL), F32), ((NB + 1, 4, PL), F32), ((16, 4, PL), F32)),
        [pl.BlockSpec(memory_space=pltpu.HBM)] * 7,
        [vspec()] * 3,
        "pack",
        8,
        [
            pltpu.VMEM((3, NB, PL), F32),
            pltpu.VMEM((NB, PL), F32),
            pltpu.VMEM((1, NB), I32),
            pltpu.VMEM((1, NB), I32),
            pltpu.VMEM((K, NB), I32),
            pltpu.VMEM((3, 2048), F32),
            pltpu.VMEM((1, 2048), F32),
            pltpu.SMEM((1, NB), I32),
            pltpu.VMEM((NB, 8, PL), F32),
            pltpu.SemaphoreType.DMA((8,)),
        ],
    )(
        *[
            pltpu.with_memory_space_constraint(v, pltpu.HBM)
            for v in (pos, masses[0], cnt, dest_ids, near_list[0].T, cell_centers, cell_mass[None])
        ]
    )
    z_rows = [[NZ * y + z for z in range(NZ)] for y in range(NY)]
    window = lax.all_to_all(src, "space", 0, 0, axis_index_groups=z_rows, tiled=True)
    tgts = [tgt] + [lax.ppermute(tgt, "space", along_y(k)) for k in (1, -1, 2)]
    pair = jnp.stack([cells, lax.ppermute(cells, "slab", [(i, i ^ 1) for i in range(2 * NX)])])
    pairs = [pair] + [lax.ppermute(pair, "slab", along_x(k)) for k in (1, -1, 2)]
    me = (lax.axis_index("space") // NZ).astype(I32).reshape(1)
    place = lax.axis_index("slab").astype(I32).reshape(1)
    tall, tab = call(
        prep_kernel,
        (((NY * NB, 4, PL), F32), ((16, 2 * PL), I32)),
        [sspec()] + [vspec()] * 4,
        [vspec(), vspec()],
        "prep",
        8,
    )(me, *tgts)
    (far,) = call(
        far_kernel,
        (((3, NB, PL), F32),),
        [sspec()] + [vspec()] * 7,
        [vspec()],
        "far",
        16,
        [pltpu.VMEM((PL, PL), F32)],
    )(place, pos, cnt, cell_list[0].T, *pairs)
    tall, tab, far = lax.optimization_barrier((tall, tab, far))
    window = window.reshape(NZ * (TILES + 1), 4, PL)

    def near(first, *arrays):
        partial = ((3, NB, PL), F32)
        kept = ((NB, 4, PL), F32)
        outs = (partial,) * (NY - 1) + (kept,) if first else (partial,)
        return call(
            functools.partial(near_kernel, first),
            outs,
            [vspec()] * len(arrays),
            [vspec()] * len(outs),
            "near",
            32,
            [
                pltpu.VMEM(((NY if first else 1) * NB, 4, PL), F32),
                pltpu.VMEM((NZ, PL), I32),
                pltpu.SMEM((NZ, PL), I32),
                pltpu.SMEM((16, 2 * PL), I32),
                pltpu.SemaphoreType.DMA((2,)),
            ],
        )(*arrays)

    *sent, kept = near(True, tab, tall, window)
    back = [lax.ppermute(sent[i], "space", along_y(-k)) for i, k in ((2, 2), (0, 1), (1, -1))]
    (own,) = near(False, tab, tall, window, kept)
    (out,) = call(
        final_kernel,
        (((3, NB, PL), F32),),
        [vspec()] * 6,
        [vspec()],
        "final",
        8,
    )(cnt, far, own, *back)
    return jnp.transpose(out, (1, 0, 2))[None]


def solution(mesh):
    in_specs = (
        P("slab", "space", None, None),
        P("slab", "space", None),
        P("slab", "space", None),
        P("slab", "space"),
        P("slab", "space", None),
        P("slab", "space", None),
        P(None, "slab"),
        P("slab"),
    )
    return jax.shard_map(
        per_device,
        mesh=mesh,
        in_specs=in_specs,
        out_specs=P("slab", "space", None, None),
        check_vma=False,
    )
```

```python
import functools

import jax
import jax.numpy as jnp
from jax import lax
from jax.experimental import pallas as pl
from jax.experimental.pallas import tpu as pltpu
from jax.sharding import PartitionSpec as P

NB = 48
PL = 128
K = 4
LC = 32
NY = 4
NZ = 8
NX = 4
SOFT = 0.01
UNROLL = (18, 20)
UNROLL_OWN = (12, 8)
MIB = 1 << 20
TILES = 36
F32 = jnp.float32
I32 = jnp.int32
BF16 = jnp.bfloat16
VMEM = pltpu.VMEM
SMEM = pltpu.SMEM


def vspec():
    return pl.BlockSpec(memory_space=VMEM)


def sspec():
    return pl.BlockSpec(memory_space=SMEM)


def column_of(row, n):
    square = jnp.broadcast_to(row, (n, n))
    diag = lax.broadcasted_iota(I32, (n, n), 0) == lax.broadcasted_iota(I32, (n, n), 1)
    return jnp.sum(jnp.where(diag, square, jnp.zeros_like(square)), axis=1, keepdims=True)


def pack_kernel(*refs):
    ins, (src_ref, tgt_ref, cell_ref), holds = refs[:7], refs[7:10], refs[10:18]
    full, sem = refs[18:]
    copies = [pltpu.make_async_copy(ins[i], holds[i], sem.at[i]) for i in range(7)]
    copies.append(pltpu.make_async_copy(ins[2], holds[7], sem.at[7]))
    for copy in copies:
        copy.start()
    for copy in copies:
        copy.wait()
    pos_ref, mass_ref, cnt_ref, dest_ref, near_ref, ctr_ref, cm_ref, cnt_smem = holds
    counts = cnt_ref[...]
    cnt = column_of(counts, NB)
    near = near_ref[...]
    off = (near >= NB).astype(I32) + (near >= 2 * NB).astype(I32)
    dev = (dest_ref[...] + off - 1) & (NY * NZ - 1)
    code = (dev >> 3) * 512 + ((NZ - 1) - (dev & (NZ - 1))) * 64 + (near - off * NB)
    gap = jnp.zeros((4, 64 - NB), I32)
    info = jnp.concatenate([code, gap, jnp.broadcast_to(counts, (4, NB)), gap], axis=1)
    lane = lax.broadcasted_iota(I32, (NB, PL), 1)
    weight = jnp.where(lane < cnt, mass_ref[...], 0.0)
    for c in range(3):
        value = pos_ref[c]
        tgt_ref[0:NB, c, :] = value
        full[:, c, :] = value
    full[:, 3, :] = weight
    lane4 = lax.broadcasted_iota(I32, (4, PL), 1)
    carry, begin = jnp.zeros((4, PL), F32), jnp.int32(0)
    for b in range(NB):
        shift, tile = begin & (PL - 1), begin >> 7
        turned = pltpu.roll(full[b], shift, 1)[0:4]
        merged = jnp.where(lane4 >= shift, turned, carry)
        src_ref[0, tile] = merged
        begin = begin + cnt_smem[0, b]
        carry = jnp.where((begin >> 7) != tile, turned, merged)
    square = (NB, NB)
    earlier = lax.broadcasted_iota(I32, square, 0) < lax.broadcasted_iota(I32, square, 1)
    starts = jnp.sum(jnp.where(earlier, cnt, 0), axis=0, keepdims=True)
    places = jnp.concatenate([starts, gap[0:1], counts, gap[0:1]], axis=1)
    src_ref[0, TILES] = jnp.broadcast_to(places, (4, PL)).astype(F32)
    for z in range(1, NZ):
        src_ref[z] = src_ref[0]
    tgt_ref[0:NB, 3, :] = jnp.zeros((NB, PL), F32)
    tgt_ref[NB] = info.astype(F32)
    for j in range(16):
        part = slice(j * PL, (j + 1) * PL)
        cell_ref[j, 0:3, :] = ctr_ref[:, part]
        cell_ref[j, 3:4, :] = cm_ref[0:1, part]


def far_kernel(place_ref, pos_ref, cnt_ref, list_ref, c0, c1, c2, c3, out_ref, pad):
    xs, cs = place_ref[0] >> 1, place_ref[0] & 1
    lane = lax.broadcasted_iota(I32, (NB, PL), 1)
    cnt = column_of(cnt_ref[...], NB)
    live = lane < cnt
    total = jnp.maximum(cnt, 1).astype(F32)
    pos = [pos_ref[c] for c in range(3)]
    centre = [jnp.sum(jnp.where(live, v, 0.0), axis=1, keepdims=True) / total for v in pos]
    diag = lax.broadcasted_iota(I32, (NB, PL), 0) == (lane & 63)
    ctr = [jnp.sum(jnp.where(diag, v, 0.0), axis=0, keepdims=True) for v in centre]
    wide = jnp.concatenate([list_ref[...], jnp.zeros((LC, PL - NB), I32)], axis=1)
    twice = wide + pltpu.roll(wide, 64, 1)
    half = lax.broadcasted_iota(I32, (1, PL), 1) < 64
    ids = [jnp.where(half, twice[2 * j : 2 * j + 1], twice[2 * j + 1 : 2 * j + 2]) for j in range(LC // 2)]
    ids = jnp.concatenate(ids, axis=0)
    slab = ids >> 11
    dx = ((slab >> 1) - xs) & (NX - 1)
    order = jnp.where(dx == 3, 1, jnp.where(dx == 0, 0, dx + 1))
    rows = (order * 2 + ((slab & 1) ^ cs)) * 16 + ((ids >> 7) & 15)
    lanes = ids & (PL - 1)
    tables = []
    for c in range(4):
        whole = jnp.concatenate([ref[i, :, c, :] for ref in (c0, c1, c2, c3) for i in range(2)], axis=0)
        whole = whole.T
        high = whole.astype(BF16)
        low = (whole - high.astype(F32)).astype(BF16)
        tables.append(jnp.concatenate([high, low], axis=1))
    tables = jnp.concatenate(tables, axis=0)
    sub = lax.broadcasted_iota(I32, (PL, 2 * PL), 0)
    got = [[] for _ in range(4)]
    for j in range(0, LC // 2, 2):
        r2 = jnp.concatenate([rows[j : j + 1], rows[j + 1 : j + 2]], axis=1)
        l2 = jnp.concatenate([lanes[j : j + 1], lanes[j + 1 : j + 2]], axis=1)
        hot = jnp.where(sub == r2, 1.0, 0.0).astype(BF16)
        hot = jnp.concatenate([hot, hot], axis=0)
        found = jnp.dot(tables, hot, preferred_element_type=F32)
        pick = sub == l2
        for c in range(4):
            value = jnp.sum(jnp.where(pick, found[c * PL : (c + 1) * PL], 0.0), axis=0, keepdims=True)
            got[c] += [value[:, :PL], value[:, PL:]]
    cells = [jnp.concatenate(v, axis=0) for v in got]
    rel = [ctr[c] - cells[c] for c in range(3)]
    dist = rel[0] * rel[0] + rel[1] * rel[1] + rel[2] * rel[2] + 1.0
    inv = lax.rsqrt(dist)
    cube = cells[3] * (inv * inv * inv)
    fifth = 3.0 * cube * (inv * inv)
    terms = [-(cube * rel[c]) for c in range(3)]
    for a, b in ((0, 0), (1, 1), (2, 2), (0, 1), (0, 2), (1, 2)):
        value = fifth * rel[a] * rel[b]
        if a == b:
            value = value - cube
        terms.append(value)
    terms = [jnp.sum(v, axis=0, keepdims=True) for v in terms]
    pad[...] = jnp.zeros((PL, PL), F32)
    for i, v in enumerate(terms):
        pad[i : i + 1, :] = v + pltpu.roll(v, 64, 1)
    back = pad[...].T
    field = [back[0:NB, i : i + 1] for i in range(3)]
    tide = [back[0:NB, 3 + i : 4 + i] for i in range(6)]
    offset = [pos[c] - centre[c] for c in range(3)]
    for c, (i, j, k) in enumerate(((0, 3, 4), (3, 1, 5), (4, 5, 2))):
        out_ref[c] = field[c] + tide[i] * offset[0] + tide[j] * offset[1] + tide[k] * offset[2]


def split3(v):
    high = v.astype(BF16).astype(F32)
    rest = v - high
    mid = rest.astype(BF16).astype(F32)
    return high, mid, rest - mid


def prep_kernel(y_ref, t0, t1, t2, t3, tall, tab):
    me = y_ref[0]
    wide = 2 * PL
    tiles = []
    for i, t in enumerate((t0, t1, t2, t3)):
        tall[i * NB : (i + 1) * NB] = t[0:NB]
        tiles.append(t[NB])
    left = lax.broadcasted_iota(I32, (4, PL), 1) < 64
    code, cnt = [], []
    for a, b in ((tiles[0], tiles[1]), (tiles[2], tiles[3])):
        code.append(jnp.where(left, a, pltpu.roll(b, 64, 1)))
        cnt.append(jnp.where(left, pltpu.roll(a, 64, 1), b))
    code = jnp.concatenate(code, axis=1).astype(I32)
    cnt = jnp.concatenate(cnt, axis=1)[0:1]
    lane = lax.broadcasted_iota(I32, (1, wide), 1)
    valid = (lane & 63) < NB
    flag = [jnp.where(((code[k : k + 1] >> 9) == me) & valid, 1.0, 0.0) for k in range(K)]
    local = [(code[k : k + 1] & 511).astype(F32) for k in range(K)]
    count = (flag[0] + flag[1]) + (flag[2] + flag[3])
    full = jnp.where(count > 2.5, 1.0, 0.0)
    half = jnp.where((count > 0.5) & (count < 2.5), 1.0, 0.0)
    group = lane >> 6
    mine = group == 0
    lists = [jnp.where(m, v, 0.0) for v in (full, half) for m in (~mine, mine)]
    marks = jnp.concatenate(lists + [jnp.zeros((12, wide), F32)], axis=0).astype(BF16)
    a = lax.broadcasted_iota(I32, (wide, wide), 0)
    b = lax.broadcasted_iota(I32, (wide, wide), 1)
    before = jnp.dot(marks, jnp.where(a < b, 1.0, 0.0).astype(BF16), preferred_element_type=F32)
    sizes = [jnp.sum(v, axis=1, keepdims=True) for v in lists]
    place, begin = jnp.full((1, wide), -1.0, F32), jnp.zeros((1, 1), F32)
    for i, v in enumerate(lists):
        place = jnp.where(v > 0.5, begin + before[i : i + 1], place)
        begin = begin + sizes[i]
    moved = jnp.where(a == place.astype(I32), 1.0, 0.0).astype(BF16)
    bucket = lane & 63
    home = ((group - 1) & (NY - 1)) * NB + bucket
    slot, ins, outs = [], jnp.zeros((1, wide), F32), jnp.zeros((1, wide), F32)
    for k in range(K):
        slot.append(jnp.where(flag[k] > 0.5, ins, count + outs))
        ins, outs = ins + flag[k], outs + (1.0 - flag[k])
    fields = []
    for j in range(K):
        pick = jnp.zeros((1, wide), F32)
        for k in range(K):
            pick = pick + jnp.where(slot[k] == float(j), local[k], 0.0)
        fields.append(pick)
    fields += [cnt, home.astype(F32), count, (group * NB + bucket).astype(F32)]
    load = jnp.concatenate(fields, axis=0)
    high = load.astype(BF16).astype(F32)
    both = jnp.concatenate([high, load - high], axis=0).astype(BF16)
    out = lax.dot_general(both, moved, (((1,), (1,)), ((), ())), preferred_element_type=F32)
    out = out[0:8] + out[8:16]
    sizes = jnp.concatenate([jnp.broadcast_to(v, (1, wide)) for v in sizes + [begin] * 4], axis=0)
    tab[...] = jnp.concatenate([out, sizes], axis=0).astype(I32)


def near_kernel(first, *refs):
    (table, tall, src_ref), refs = refs[:3], refs[3:]
    outs, (out_ref, hold, spots, tab, sem) = refs[:-5], refs[-5:]
    if not first:
        kept, outs = outs[0], outs[1:]
    copies = [pltpu.make_async_copy(table, tab, sem.at[0]), pltpu.make_async_copy(hold, spots, sem.at[1])]
    copies[0].start()
    for z in range(NZ):
        hold[z : z + 1, :] = src_ref[z * (TILES + 1) + TILES][0:1].astype(I32)
    copies[1].start()
    out_ref[...] = jnp.zeros(out_ref.shape, F32) if first else kept[...]
    for copy in copies:
        copy.wait()
    lane1 = lax.broadcasted_iota(I32, (1, PL), 1)
    sub4 = lax.broadcasted_iota(I32, (4, PL), 0)
    lane4 = lax.broadcasted_iota(I32, (4, PL), 1)
    spatial = sub4 < 3
    one = jnp.ones((4, PL), F32)
    zero4 = jnp.zeros((4, PL), F32)
    zero8 = jnp.zeros((8, PL), F32)

    def square(v):
        return jnp.sum(jnp.where(spatial, v * v, 0.0), axis=0, keepdims=True)

    def mix(a, b):
        return jnp.where(spatial, a, b)

    def stack(*v):
        return jnp.concatenate(v, axis=0).astype(BF16)

    row_base = 0 if first else (NY - 1) * NB

    def job(e, width):
        n = tab[6, e]
        t = tall[tab[7, e]]
        th, tm, tl = split3(t)
        qh, qm, ql = split3(square(t))
        u = stack(mix(th, one), mix(th, one), mix(tm, one), mix(tm, qh), mix(th, qm), mix(tl, ql), zero8)
        vs, gs = [], []
        for k in range(width):
            z, bucket = tab[k, e] >> 6, tab[k, e] & 63
            begin = spots[z, bucket]
            shift = begin & (PL - 1)
            tile = z * (TILES + 1) + (begin >> 7)
            s = jnp.concatenate([src_ref[tile], src_ref[tile + 1]], axis=0)
            s = pltpu.roll(s, (PL - shift) & (PL - 1), 1)
            s = jnp.where(lane4 < PL - shift, s[0:4], s[4:8])
            live = jnp.where(k < n, spots[z, 64 + bucket], 0)
            sh, sm, sl = split3(-2.0 * s)
            qh, qm, ql = split3(square(s) + SOFT)
            vs.append(stack(mix(sh, qh), mix(sm, qm), mix(sh, ql), mix(sm, one), mix(sl, one), mix(sh, one), zero8))
            w = jnp.where(lane1 < live, s[3:4], 0.0)
            gs.append(stack(*split3(mix(s * w, w)), zero4))
        v = jnp.concatenate(vs, axis=1)
        g = jnp.concatenate(gs, axis=1)
        dist = lax.dot_general(v, u, (((0,), (0,)), ((), ())), preferred_element_type=F32)
        inv = lax.rsqrt(dist)
        f = inv * inv * inv
        high = f.astype(BF16)
        low = (f - high.astype(F32)).astype(BF16)
        o = jnp.dot(g, jnp.concatenate([high, low], axis=1), preferred_element_type=F32)
        o = o[:, :PL] + o[:, PL:]
        a = o[0:4] + o[4:8] + o[8:12]
        out_ref[tab[5, e] - row_base] = jnp.where(lane4 < tab[4, e], a - t * a[3:4], 0.0)

    sizes = [tab[8 + i, 0] for i in range(4)]

    def run(begin, size, width, step):
        def body(i, _):
            for j in range(step):
                job(begin + jnp.minimum(step * i + j, size - 1), width)

        lax.fori_loop(0, (size + step - 1) // step, body, None)

    def whole_steps(size, step):
        return (size + step - 1) // step * step

    n_full, n_half = sizes[0] + sizes[1], sizes[2] + sizes[3]
    early_full = jnp.minimum(n_full, whole_steps(sizes[0], UNROLL[0]))
    early_half = jnp.minimum(n_half, whole_steps(sizes[2], UNROLL[1]))
    if first:
        run(jnp.int32(0), early_full, 4, UNROLL[0])
        run(n_full, early_half, 2, UNROLL[1])
    else:
        run(early_full, n_full - early_full, 4, UNROLL_OWN[0])
        run(n_full + early_half, n_half - early_half, 2, UNROLL_OWN[1])
    if first:
        outs[-1][...] = out_ref[(NY - 1) * NB : NY * NB]
        outs = outs[:-1]
    for i, o in enumerate(outs):
        for c in range(3):
            o[c] = out_ref[i * NB : (i + 1) * NB, c, :]


def final_kernel(cnt_ref, far_ref, p0, p1, p2, p3, out_ref):
    live = lax.broadcasted_iota(I32, (NB, PL), 1) < column_of(cnt_ref[...], NB)
    for c in range(3):
        near = (p0[c] + p1[c]) + (p2[c] + p3[c])
        out_ref[c] = jnp.where(live, far_ref[c] + near, 0.0)


def along_y(k):
    return [(NZ * y + z, NZ * ((y + k) % NY) + z) for y in range(NY) for z in range(NZ)]


def along_x(k):
    return [(2 * x + c, 2 * ((x + k) % NX) + c) for x in range(NX) for c in range(2)]


def call(kernel, outs, in_specs, out_specs, name, mib, scratch=()):
    return pl.pallas_call(
        kernel,
        out_shape=[jax.ShapeDtypeStruct(shape, dtype) for shape, dtype in outs],
        in_specs=in_specs,
        out_specs=out_specs,
        scratch_shapes=scratch,
        compiler_params=pltpu.CompilerParams(vmem_limit_bytes=mib * MIB),
        name=name,
    )


def per_device(positions, masses, counts, dest_ids, near_list, cell_list, cell_centers, cell_mass):
    pos = jnp.transpose(positions[0], (1, 0, 2))
    cnt = counts[0]
    src, tgt, cells = call(
        pack_kernel,
        (((NZ, TILES + 1, 4, PL), F32), ((NB + 1, 4, PL), F32), ((16, 4, PL), F32)),
        [pl.BlockSpec(memory_space=pltpu.HBM)] * 7,
        [vspec()] * 3,
        "pack",
        8,
        [
            pltpu.VMEM((3, NB, PL), F32),
            pltpu.VMEM((NB, PL), F32),
            pltpu.VMEM((1, NB), I32),
            pltpu.VMEM((1, NB), I32),
            pltpu.VMEM((K, NB), I32),
            pltpu.VMEM((3, 2048), F32),
            pltpu.VMEM((1, 2048), F32),
            pltpu.SMEM((1, NB), I32),
            pltpu.VMEM((NB, 8, PL), F32),
            pltpu.SemaphoreType.DMA((8,)),
        ],
    )(
        *[
            pltpu.with_memory_space_constraint(v, pltpu.HBM)
            for v in (pos, masses[0], cnt, dest_ids, near_list[0].T, cell_centers, cell_mass[None])
        ]
    )
    z_rows = [[NZ * y + NZ - 1 - z for z in range(NZ)] for y in range(NY)]
    window = lax.all_to_all(src, "space", 0, 0, axis_index_groups=z_rows, tiled=True)
    tgts = [tgt] + [lax.ppermute(tgt, "space", along_y(k)) for k in (1, -1, 2)]
    pair = jnp.stack([cells, lax.ppermute(cells, "slab", [(i, i ^ 1) for i in range(2 * NX)])])
    pairs = [pair] + [lax.ppermute(pair, "slab", along_x(k)) for k in (1, -1, 2)]
    me = (lax.axis_index("space") // NZ).astype(I32).reshape(1)
    place = lax.axis_index("slab").astype(I32).reshape(1)
    tall, tab = call(
        prep_kernel,
        (((NY * NB, 4, PL), F32), ((16, 2 * PL), I32)),
        [sspec()] + [vspec()] * 4,
        [vspec(), vspec()],
        "prep",
        8,
    )(me, *tgts)
    (far,) = call(
        far_kernel,
        (((3, NB, PL), F32),),
        [sspec()] + [vspec()] * 7,
        [vspec()],
        "far",
        16,
        [pltpu.VMEM((PL, PL), F32)],
    )(place, pos, cnt, cell_list[0].T, *pairs)
    tall, tab, far = lax.optimization_barrier((tall, tab, far))
    window = window.reshape(NZ * (TILES + 1), 4, PL)

    def near(first, *arrays):
        partial = ((3, NB, PL), F32)
        kept = ((NB, 4, PL), F32)
        outs = (partial,) * (NY - 1) + (kept,) if first else (partial,)
        return call(
            functools.partial(near_kernel, first),
            outs,
            [vspec()] * len(arrays),
            [vspec()] * len(outs),
            "near",
            32,
            [
                pltpu.VMEM(((NY if first else 1) * NB, 4, PL), F32),
                pltpu.VMEM((NZ, PL), I32),
                pltpu.SMEM((NZ, PL), I32),
                pltpu.SMEM((16, 2 * PL), I32),
                pltpu.SemaphoreType.DMA((2,)),
            ],
        )(*arrays)

    *sent, kept = near(True, tab, tall, window)
    back = [lax.ppermute(sent[i], "space", along_y(-k)) for i, k in ((2, 2), (0, 1), (1, -1))]
    (own,) = near(False, tab, tall, window, kept)
    (out,) = call(
        final_kernel,
        (((3, NB, PL), F32),),
        [vspec()] * 6,
        [vspec()],
        "final",
        8,
    )(cnt, far, own, *back)
    return jnp.transpose(out, (1, 0, 2))[None]


def solution(mesh):
    in_specs = (
        P("slab", "space", None, None),
        P("slab", "space", None),
        P("slab", "space", None),
        P("slab", "space"),
        P("slab", "space", None),
        P("slab", "space", None),
        P(None, "slab"),
        P("slab"),
    )
    return jax.shard_map(
        per_device,
        mesh=mesh,
        in_specs=in_specs,
        out_specs=P("slab", "space", None, None),
        check_vma=False,
    )
```

```python
import functools

import jax
import jax.numpy as jnp
from jax import lax
from jax.experimental import pallas as pl
from jax.experimental.pallas import tpu as pltpu
from jax.sharding import PartitionSpec as P

NB = 48
PL = 128
K = 4
LC = 32
NY = 4
NZ = 8
NX = 4
SOFT = 0.01
UNROLL = (18, 20)
UNROLL_OWN = (12, 8)
MIB = 1 << 20
TILES = 36
F32 = jnp.float32
I32 = jnp.int32
BF16 = jnp.bfloat16
VMEM = pltpu.VMEM
SMEM = pltpu.SMEM


def vspec():
    return pl.BlockSpec(memory_space=VMEM)


def sspec():
    return pl.BlockSpec(memory_space=SMEM)


def column_of(row, n):
    square = jnp.broadcast_to(row, (n, n))
    diag = lax.broadcasted_iota(I32, (n, n), 0) == lax.broadcasted_iota(I32, (n, n), 1)
    return jnp.sum(jnp.where(diag, square, jnp.zeros_like(square)), axis=1, keepdims=True)


def pack_kernel(*refs):
    ins, (src_ref, tgt_ref, cell_ref), holds = refs[:7], refs[7:10], refs[10:18]
    full, sem = refs[18:]
    copies = [pltpu.make_async_copy(ins[i], holds[i], sem.at[i]) for i in range(7)]
    copies.append(pltpu.make_async_copy(ins[2], holds[7], sem.at[7]))
    for copy in copies:
        copy.start()
    for copy in copies:
        copy.wait()
    pos_ref, mass_ref, cnt_ref, dest_ref, near_ref, ctr_ref, cm_ref, cnt_smem = holds
    counts = cnt_ref[...]
    cnt = column_of(counts, NB)
    near = near_ref[...]
    off = (near >= NB).astype(I32) + (near >= 2 * NB).astype(I32)
    dev = (dest_ref[...] + off - 1) & (NY * NZ - 1)
    code = (dev >> 3) * 512 + ((NZ - 1) - (dev & (NZ - 1))) * 64 + (near - off * NB)
    gap = jnp.zeros((4, 64 - NB), I32)
    info = jnp.concatenate([code, gap, jnp.broadcast_to(counts, (4, NB)), gap], axis=1)
    lane = lax.broadcasted_iota(I32, (NB, PL), 1)
    weight = jnp.where(lane < cnt, mass_ref[...], 0.0)
    for c in range(3):
        value = pos_ref[c]
        tgt_ref[0:NB, c, :] = value
        full[:, c, :] = value
    full[:, 3, :] = weight
    lane4 = lax.broadcasted_iota(I32, (4, PL), 1)
    carry, begin = jnp.zeros((4, PL), F32), jnp.int32(0)
    for b in range(NB):
        shift, tile = begin & (PL - 1), begin >> 7
        turned = pltpu.roll(full[b], shift, 1)[0:4]
        merged = jnp.where(lane4 >= shift, turned, carry)
        src_ref[0, tile] = merged
        begin = begin + cnt_smem[0, b]
        carry = jnp.where((begin >> 7) != tile, turned, merged)
    square = (NB, NB)
    earlier = lax.broadcasted_iota(I32, square, 0) < lax.broadcasted_iota(I32, square, 1)
    starts = jnp.sum(jnp.where(earlier, cnt, 0), axis=0, keepdims=True)
    places = jnp.concatenate([starts, gap[0:1], counts, gap[0:1]], axis=1)
    src_ref[0, TILES] = jnp.broadcast_to(places, (4, PL)).astype(F32)
    for z in range(1, NZ):
        src_ref[z] = src_ref[0]
    tgt_ref[0:NB, 3, :] = jnp.zeros((NB, PL), F32)
    tgt_ref[NB] = info.astype(F32)
    for j in range(16):
        part = slice(j * PL, (j + 1) * PL)
        cell_ref[j, 0:3, :] = ctr_ref[:, part]
        cell_ref[j, 3:4, :] = cm_ref[0:1, part]


def far_kernel(place_ref, pos_ref, cnt_ref, list_ref, c0, c1, c2, c3, out_ref, pad):
    xs, cs = place_ref[0] >> 1, place_ref[0] & 1
    lane = lax.broadcasted_iota(I32, (NB, PL), 1)
    cnt = column_of(cnt_ref[...], NB)
    live = lane < cnt
    total = jnp.maximum(cnt, 1).astype(F32)
    pos = [pos_ref[c] for c in range(3)]
    centre = [jnp.sum(jnp.where(live, v, 0.0), axis=1, keepdims=True) / total for v in pos]
    diag = lax.broadcasted_iota(I32, (NB, PL), 0) == (lane & 63)
    ctr = [jnp.sum(jnp.where(diag, v, 0.0), axis=0, keepdims=True) for v in centre]
    wide = jnp.concatenate([list_ref[...], jnp.zeros((LC, PL - NB), I32)], axis=1)
    twice = wide + pltpu.roll(wide, 64, 1)
    half = lax.broadcasted_iota(I32, (1, PL), 1) < 64
    ids = [jnp.where(half, twice[2 * j : 2 * j + 1], twice[2 * j + 1 : 2 * j + 2]) for j in range(LC // 2)]
    ids = jnp.concatenate(ids, axis=0)
    slab = ids >> 11
    dx = ((slab >> 1) - xs) & (NX - 1)
    order = jnp.where(dx == 3, 1, jnp.where(dx == 0, 0, dx + 1))
    rows = (order * 2 + ((slab & 1) ^ cs)) * 16 + ((ids >> 7) & 15)
    lanes = ids & (PL - 1)
    tables = []
    for c in range(4):
        whole = jnp.concatenate([ref[i, :, c, :] for ref in (c0, c1, c2, c3) for i in range(2)], axis=0)
        whole = whole.T
        high = whole.astype(BF16)
        low = (whole - high.astype(F32)).astype(BF16)
        tables.append(jnp.concatenate([high, low], axis=1))
    tables = jnp.concatenate(tables, axis=0)
    sub = lax.broadcasted_iota(I32, (PL, 2 * PL), 0)
    got = [[] for _ in range(4)]
    for j in range(0, LC // 2, 2):
        r2 = jnp.concatenate([rows[j : j + 1], rows[j + 1 : j + 2]], axis=1)
        l2 = jnp.concatenate([lanes[j : j + 1], lanes[j + 1 : j + 2]], axis=1)
        hot = jnp.where(sub == r2, 1.0, 0.0).astype(BF16)
        hot = jnp.concatenate([hot, hot], axis=0)
        found = jnp.dot(tables, hot, preferred_element_type=F32)
        pick = sub == l2
        for c in range(4):
            value = jnp.sum(jnp.where(pick, found[c * PL : (c + 1) * PL], 0.0), axis=0, keepdims=True)
            got[c] += [value[:, :PL], value[:, PL:]]
    cells = [jnp.concatenate(v, axis=0) for v in got]
    rel = [ctr[c] - cells[c] for c in range(3)]
    dist = rel[0] * rel[0] + rel[1] * rel[1] + rel[2] * rel[2] + 1.0
    inv = lax.rsqrt(dist)
    cube = cells[3] * (inv * inv * inv)
    fifth = 3.0 * cube * (inv * inv)
    terms = [-(cube * rel[c]) for c in range(3)]
    for a, b in ((0, 0), (1, 1), (2, 2), (0, 1), (0, 2), (1, 2)):
        value = fifth * rel[a] * rel[b]
        if a == b:
            value = value - cube
        terms.append(value)
    terms = [jnp.sum(v, axis=0, keepdims=True) for v in terms]
    pad[...] = jnp.zeros((PL, PL), F32)
    for i, v in enumerate(terms):
        pad[i : i + 1, :] = v + pltpu.roll(v, 64, 1)
    back = pad[...].T
    field = [back[0:NB, i : i + 1] for i in range(3)]
    tide = [back[0:NB, 3 + i : 4 + i] for i in range(6)]
    offset = [pos[c] - centre[c] for c in range(3)]
    for c, (i, j, k) in enumerate(((0, 3, 4), (3, 1, 5), (4, 5, 2))):
        out_ref[c] = field[c] + tide[i] * offset[0] + tide[j] * offset[1] + tide[k] * offset[2]


def split3(v):
    high = v.astype(BF16).astype(F32)
    rest = v - high
    mid = rest.astype(BF16).astype(F32)
    return high, mid, rest - mid


def prep_kernel(y_ref, t0, t1, t2, t3, tall, tab):
    me = y_ref[0]
    wide = 2 * PL
    tiles = []
    for i, t in enumerate((t0, t1, t2, t3)):
        tall[i * NB : (i + 1) * NB] = t[0:NB]
        tiles.append(t[NB])
    left = lax.broadcasted_iota(I32, (4, PL), 1) < 64
    code, cnt = [], []
    for a, b in ((tiles[0], tiles[1]), (tiles[2], tiles[3])):
        code.append(jnp.where(left, a, pltpu.roll(b, 64, 1)))
        cnt.append(jnp.where(left, pltpu.roll(a, 64, 1), b))
    code = jnp.concatenate(code, axis=1).astype(I32)
    cnt = jnp.concatenate(cnt, axis=1)[0:1]
    lane = lax.broadcasted_iota(I32, (1, wide), 1)
    valid = (lane & 63) < NB
    flag = [jnp.where(((code[k : k + 1] >> 9) == me) & valid, 1.0, 0.0) for k in range(K)]
    local = [(code[k : k + 1] & 511).astype(F32) for k in range(K)]
    count = (flag[0] + flag[1]) + (flag[2] + flag[3])
    full = jnp.where(count > 2.5, 1.0, 0.0)
    half = jnp.where((count > 0.5) & (count < 2.5), 1.0, 0.0)
    group = lane >> 6
    mine = group == 0
    lists = [jnp.where(m, v, 0.0) for v in (full, half) for m in (~mine, mine)]
    marks = jnp.concatenate(lists + [jnp.zeros((12, wide), F32)], axis=0).astype(BF16)
    a = lax.broadcasted_iota(I32, (wide, wide), 0)
    b = lax.broadcasted_iota(I32, (wide, wide), 1)
    before = jnp.dot(marks, jnp.where(a < b, 1.0, 0.0).astype(BF16), preferred_element_type=F32)
    sizes = [jnp.sum(v, axis=1, keepdims=True) for v in lists]
    place, begin = jnp.full((1, wide), -1.0, F32), jnp.zeros((1, 1), F32)
    for i, v in enumerate(lists):
        place = jnp.where(v > 0.5, begin + before[i : i + 1], place)
        begin = begin + sizes[i]
    moved = jnp.where(a == place.astype(I32), 1.0, 0.0).astype(BF16)
    bucket = lane & 63
    home = ((group - 1) & (NY - 1)) * NB + bucket
    slot, ins, outs = [], jnp.zeros((1, wide), F32), jnp.zeros((1, wide), F32)
    for k in range(K):
        slot.append(jnp.where(flag[k] > 0.5, ins, count + outs))
        ins, outs = ins + flag[k], outs + (1.0 - flag[k])
    fields = []
    for j in range(K):
        pick = jnp.zeros((1, wide), F32)
        for k in range(K):
            pick = pick + jnp.where(slot[k] == float(j), local[k], 0.0)
        fields.append(pick)
    fields += [cnt, home.astype(F32), count, (group * NB + bucket).astype(F32)]
    load = jnp.concatenate(fields, axis=0)
    high = load.astype(BF16).astype(F32)
    both = jnp.concatenate([high, load - high], axis=0).astype(BF16)
    out = lax.dot_general(both, moved, (((1,), (1,)), ((), ())), preferred_element_type=F32)
    out = out[0:8] + out[8:16]
    sizes = jnp.concatenate([jnp.broadcast_to(v, (1, wide)) for v in sizes + [begin] * 4], axis=0)
    tab[...] = jnp.concatenate([out, sizes], axis=0).astype(I32)


def near_kernel(first, *refs):
    (table, tall, src_ref), refs = refs[:3], refs[3:]
    outs, (out_ref, hold, spots, tab, sem) = refs[:-5], refs[-5:]
    if not first:
        kept, outs = outs[0], outs[1:]
    copies = [pltpu.make_async_copy(table, tab, sem.at[0]), pltpu.make_async_copy(hold, spots, sem.at[1])]
    copies[0].start()
    for z in range(NZ):
        hold[z : z + 1, :] = src_ref[z * (TILES + 1) + TILES][0:1].astype(I32)
    copies[1].start()
    out_ref[...] = jnp.zeros(out_ref.shape, F32) if first else kept[...]
    for copy in copies:
        copy.wait()
    lane1 = lax.broadcasted_iota(I32, (1, PL), 1)
    sub4 = lax.broadcasted_iota(I32, (4, PL), 0)
    lane4 = lax.broadcasted_iota(I32, (4, PL), 1)
    spatial = sub4 < 3
    one = jnp.ones((4, PL), F32)
    zero4 = jnp.zeros((4, PL), F32)
    zero8 = jnp.zeros((8, PL), F32)

    def square(v):
        return jnp.sum(jnp.where(spatial, v * v, 0.0), axis=0, keepdims=True)

    def mix(a, b):
        return jnp.where(spatial, a, b)

    def stack(*v):
        return jnp.concatenate(v, axis=0).astype(BF16)

    row_base = 0 if first else (NY - 1) * NB

    def job(e, width):
        n = tab[6, e]
        t = tall[tab[7, e]]
        th, tm, tl = split3(t)
        qh, qm, ql = split3(square(t))
        u = stack(mix(th, one), mix(th, one), mix(tm, one), mix(tm, qh), mix(th, qm), mix(tl, ql), zero8)
        vs, gs = [], []
        for k in range(width):
            z, bucket = tab[k, e] >> 6, tab[k, e] & 63
            begin = spots[z, bucket]
            shift = begin & (PL - 1)
            tile = z * (TILES + 1) + (begin >> 7)
            s = jnp.concatenate([src_ref[tile], src_ref[tile + 1]], axis=0)
            s = pltpu.roll(s, (PL - shift) & (PL - 1), 1)
            s = jnp.where(lane4 < PL - shift, s[0:4], s[4:8])
            live = jnp.where(k < n, spots[z, 64 + bucket], 0)
            sh, sm, sl = split3(-2.0 * s)
            qh, qm, ql = split3(square(s) + SOFT)
            vs.append(stack(mix(sh, qh), mix(sm, qm), mix(sh, ql), mix(sm, one), mix(sl, one), mix(sh, one), zero8))
            w = jnp.where(lane1 < live, s[3:4], 0.0)
            gs.append(stack(*split3(mix(s * w, w)), zero4))
        v = jnp.concatenate(vs, axis=1)
        g = jnp.concatenate(gs, axis=1)
        dist = lax.dot_general(v, u, (((0,), (0,)), ((), ())), preferred_element_type=F32)
        inv = lax.rsqrt(dist)
        f = inv * inv * inv
        high = f.astype(BF16)
        low = (f - high.astype(F32)).astype(BF16)
        o = jnp.dot(g, jnp.concatenate([high, low], axis=1), preferred_element_type=F32)
        o = o[:, :PL] + o[:, PL:]
        a = o[0:4] + o[4:8] + o[8:12]
        out_ref[tab[5, e] - row_base] = jnp.where(lane4 < tab[4, e], a - t * a[3:4], 0.0)

    sizes = [tab[8 + i, 0] for i in range(4)]

    def run(begin, size, width, step):
        def body(i, _):
            for j in range(step):
                job(begin + jnp.minimum(step * i + j, size - 1), width)

        lax.fori_loop(0, (size + step - 1) // step, body, None)

    def whole_steps(size, step):
        return (size + step - 1) // step * step

    n_full, n_half = sizes[0] + sizes[1], sizes[2] + sizes[3]
    early_full = jnp.minimum(n_full, whole_steps(sizes[0], UNROLL[0]))
    early_half = jnp.minimum(n_half, whole_steps(sizes[2], UNROLL[1]))
    if first:
        run(jnp.int32(0), early_full, 4, UNROLL[0])
        run(n_full, early_half, 2, UNROLL[1])
    else:
        run(early_full, n_full - early_full, 4, UNROLL_OWN[0])
        run(n_full + early_half, n_half - early_half, 2, UNROLL_OWN[1])
    if first:
        outs[-1][...] = out_ref[(NY - 1) * NB : NY * NB]
        outs = outs[:-1]
    for i, o in enumerate(outs):
        for c in range(3):
            o[c] = out_ref[i * NB : (i + 1) * NB, c, :]


def final_kernel(cnt_ref, far_ref, p0, p1, p2, p3, out_ref):
    live = lax.broadcasted_iota(I32, (NB, PL), 1) < column_of(cnt_ref[...], NB)
    for c in range(3):
        near = (p0[c] + p1[c]) + (p2[c] + p3[c])
        out_ref[c] = jnp.where(live, far_ref[c] + near, 0.0)


def along_y(k):
    return [(NZ * y + z, NZ * ((y + k) % NY) + z) for y in range(NY) for z in range(NZ)]


def along_x(k):
    return [(2 * x + c, 2 * ((x + k) % NX) + c) for x in range(NX) for c in range(2)]


def call(kernel, outs, in_specs, out_specs, name, mib, scratch=()):
    return pl.pallas_call(
        kernel,
        out_shape=[jax.ShapeDtypeStruct(shape, dtype) for shape, dtype in outs],
        in_specs=in_specs,
        out_specs=out_specs,
        scratch_shapes=scratch,
        compiler_params=pltpu.CompilerParams(vmem_limit_bytes=mib * MIB),
        name=name,
    )


def per_device(positions, masses, counts, dest_ids, near_list, cell_list, cell_centers, cell_mass):
    pos = jnp.transpose(positions[0], (1, 0, 2))
    cnt = counts[0]
    src, tgt, cells = call(
        pack_kernel,
        (((NZ, TILES + 1, 4, PL), F32), ((NB + 1, 4, PL), F32), ((16, 4, PL), F32)),
        [pl.BlockSpec(memory_space=pltpu.HBM)] * 7,
        [vspec()] * 3,
        "pack",
        8,
        [
            pltpu.VMEM((3, NB, PL), F32),
            pltpu.VMEM((NB, PL), F32),
            pltpu.VMEM((1, NB), I32),
            pltpu.VMEM((1, NB), I32),
            pltpu.VMEM((K, NB), I32),
            pltpu.VMEM((3, 2048), F32),
            pltpu.VMEM((1, 2048), F32),
            pltpu.SMEM((1, NB), I32),
            pltpu.VMEM((NB, 8, PL), F32),
            pltpu.SemaphoreType.DMA((8,)),
        ],
    )(
        *[
            pltpu.with_memory_space_constraint(v, pltpu.HBM)
            for v in (pos, masses[0], cnt, dest_ids, near_list[0].T, cell_centers, cell_mass[None])
        ]
    )
    z_rows = [[NZ * y + NZ - 1 - z for z in range(NZ)] for y in range(NY)]
    window = lax.all_to_all(src, "space", 0, 0, axis_index_groups=z_rows, tiled=True)
    tgts = [tgt] + [lax.ppermute(tgt, "space", along_y(k)) for k in (1, -1)]
    tgts.append(lax.ppermute(tgts[1], "space", along_y(1)))
    pair = jnp.stack([cells, lax.ppermute(cells, "slab", [(i, i ^ 1) for i in range(2 * NX)])])
    pairs = [pair] + [lax.ppermute(pair, "slab", along_x(k)) for k in (1, -1)]
    pairs.append(lax.ppermute(pairs[1], "slab", along_x(1)))
    me = (lax.axis_index("space") // NZ).astype(I32).reshape(1)
    place = lax.axis_index("slab").astype(I32).reshape(1)
    tall, tab = call(
        prep_kernel,
        (((NY * NB, 4, PL), F32), ((16, 2 * PL), I32)),
        [sspec()] + [vspec()] * 4,
        [vspec(), vspec()],
        "prep",
        8,
    )(me, *tgts)
    tall, tab, *pairs = lax.optimization_barrier((tall, tab, *pairs))
    window = window.reshape(NZ * (TILES + 1), 4, PL)

    def near(first, *arrays):
        partial = ((3, NB, PL), F32)
        kept = ((NB, 4, PL), F32)
        outs = (partial,) * (NY - 1) + (kept,) if first else (partial,)
        return call(
            functools.partial(near_kernel, first),
            outs,
            [vspec()] * len(arrays),
            [vspec()] * len(outs),
            "near",
            32,
            [
                pltpu.VMEM(((NY if first else 1) * NB, 4, PL), F32),
                pltpu.VMEM((NZ, PL), I32),
                pltpu.SMEM((NZ, PL), I32),
                pltpu.SMEM((16, 2 * PL), I32),
                pltpu.SemaphoreType.DMA((2,)),
            ],
        )(*arrays)

    *sent, kept = near(True, tab, tall, window)
    back = [lax.ppermute(sent[i], "space", along_y(-k)) for i, k in ((2, 2), (0, 1), (1, -1))]
    *pairs, kept, sent[0] = lax.optimization_barrier((*pairs, kept, sent[0]))
    (far,) = call(
        far_kernel,
        (((3, NB, PL), F32),),
        [sspec()] + [vspec()] * 7,
        [vspec()],
        "far",
        16,
        [pltpu.VMEM((PL, PL), F32)],
    )(place, pos, cnt, cell_list[0].T, *pairs)
    (own,) = near(False, tab, tall, window, kept)
    (out,) = call(
        final_kernel,
        (((3, NB, PL), F32),),
        [vspec()] * 6,
        [vspec()],
        "final",
        8,
    )(cnt, far, own, *back)
    return jnp.transpose(out, (1, 0, 2))[None]


def solution(mesh):
    in_specs = (
        P("slab", "space", None, None),
        P("slab", "space", None),
        P("slab", "space", None),
        P("slab", "space"),
        P("slab", "space", None),
        P("slab", "space", None),
        P(None, "slab"),
        P("slab"),
    )
    return jax.shard_map(
        per_device,
        mesh=mesh,
        in_specs=in_specs,
        out_specs=P("slab", "space", None, None),
        check_vma=False,
    )
```

```python
import functools

import jax
import jax.numpy as jnp
from jax import lax
from jax.experimental import pallas as pl
from jax.experimental.pallas import tpu as pltpu
from jax.sharding import PartitionSpec as P

NB = 48
PL = 128
K = 4
LC = 32
NY = 4
NZ = 8
NX = 4
SOFT = 0.01
UNROLL = (18, 20)
UNROLL_OWN = (12, 8)
MIB = 1 << 20
TILES = 36
F32 = jnp.float32
I32 = jnp.int32
BF16 = jnp.bfloat16
VMEM = pltpu.VMEM
SMEM = pltpu.SMEM


def vspec():
    return pl.BlockSpec(memory_space=VMEM)


def sspec():
    return pl.BlockSpec(memory_space=SMEM)


def column_of(row, n):
    square = jnp.broadcast_to(row, (n, n))
    diag = lax.broadcasted_iota(I32, (n, n), 0) == lax.broadcasted_iota(I32, (n, n), 1)
    return jnp.sum(jnp.where(diag, square, jnp.zeros_like(square)), axis=1, keepdims=True)


def pack_kernel(*refs):
    ins, (src_ref, tgt_ref, cell_ref), holds = refs[:7], refs[7:10], refs[10:18]
    full, sem = refs[18:]
    copies = [pltpu.make_async_copy(ins[i], holds[i], sem.at[i]) for i in range(7)]
    copies.append(pltpu.make_async_copy(ins[2], holds[7], sem.at[7]))
    for copy in copies:
        copy.start()
    for copy in copies:
        copy.wait()
    pos_ref, mass_ref, cnt_ref, dest_ref, near_ref, ctr_ref, cm_ref, cnt_smem = holds
    counts = cnt_ref[...]
    cnt = column_of(counts, NB)
    near = near_ref[...]
    off = (near >= NB).astype(I32) + (near >= 2 * NB).astype(I32)
    dev = (dest_ref[...] + off - 1) & (NY * NZ - 1)
    code = (dev >> 3) * 512 + ((NZ - 1) - (dev & (NZ - 1))) * 64 + (near - off * NB)
    gap = jnp.zeros((4, 64 - NB), I32)
    info = jnp.concatenate([code, gap, jnp.broadcast_to(counts, (4, NB)), gap], axis=1)
    lane = lax.broadcasted_iota(I32, (NB, PL), 1)
    weight = jnp.where(lane < cnt, mass_ref[...], 0.0)
    for c in range(3):
        value = pos_ref[c]
        tgt_ref[0:NB, c, :] = value
        full[:, c, :] = value
    full[:, 3, :] = weight
    lane4 = lax.broadcasted_iota(I32, (4, PL), 1)
    carry, begin = jnp.zeros((4, PL), F32), jnp.int32(0)
    for b in range(NB):
        shift, tile = begin & (PL - 1), begin >> 7
        turned = pltpu.roll(full[b], shift, 1)[0:4]
        merged = jnp.where(lane4 >= shift, turned, carry)
        src_ref[0, tile] = merged
        begin = begin + cnt_smem[0, b]
        carry = jnp.where((begin >> 7) != tile, turned, merged)
    square = (NB, NB)
    earlier = lax.broadcasted_iota(I32, square, 0) < lax.broadcasted_iota(I32, square, 1)
    starts = jnp.sum(jnp.where(earlier, cnt, 0), axis=0, keepdims=True)
    places = jnp.concatenate([starts, gap[0:1], counts, gap[0:1]], axis=1)
    src_ref[0, TILES] = jnp.broadcast_to(places, (4, PL)).astype(F32)
    for z in range(1, NZ):
        src_ref[z] = src_ref[0]
    tgt_ref[0:NB, 3, :] = jnp.zeros((NB, PL), F32)
    tgt_ref[NB] = info.astype(F32)
    for j in range(16):
        part = slice(j * PL, (j + 1) * PL)
        cell_ref[j, 0:3, :] = ctr_ref[:, part]
        cell_ref[j, 3:4, :] = cm_ref[0:1, part]


def far_kernel(place_ref, pos_ref, cnt_ref, list_ref, c0, c1, c2, c3, out_ref, pad):
    xs, cs = place_ref[0] >> 1, place_ref[0] & 1
    lane = lax.broadcasted_iota(I32, (NB, PL), 1)
    cnt = column_of(cnt_ref[...], NB)
    live = lane < cnt
    total = jnp.maximum(cnt, 1).astype(F32)
    pos = [pos_ref[c] for c in range(3)]
    centre = [jnp.sum(jnp.where(live, v, 0.0), axis=1, keepdims=True) / total for v in pos]
    diag = lax.broadcasted_iota(I32, (NB, PL), 0) == (lane & 63)
    ctr = [jnp.sum(jnp.where(diag, v, 0.0), axis=0, keepdims=True) for v in centre]
    wide = jnp.concatenate([list_ref[...], jnp.zeros((LC, PL - NB), I32)], axis=1)
    twice = wide + pltpu.roll(wide, 64, 1)
    half = lax.broadcasted_iota(I32, (1, PL), 1) < 64
    ids = [jnp.where(half, twice[2 * j : 2 * j + 1], twice[2 * j + 1 : 2 * j + 2]) for j in range(LC // 2)]
    ids = jnp.concatenate(ids, axis=0)
    slab = ids >> 11
    dx = ((slab >> 1) - xs) & (NX - 1)
    order = jnp.where(dx == 3, 1, jnp.where(dx == 0, 0, dx + 1))
    rows = (order * 2 + ((slab & 1) ^ cs)) * 16 + ((ids >> 7) & 15)
    lanes = ids & (PL - 1)
    tables = []
    for c in range(4):
        whole = jnp.concatenate([ref[i, :, c, :] for ref in (c0, c1, c2, c3) for i in range(2)], axis=0)
        whole = whole.T
        high = whole.astype(BF16)
        low = (whole - high.astype(F32)).astype(BF16)
        tables.append(jnp.concatenate([high, low], axis=1))
    tables = jnp.concatenate(tables, axis=0)
    sub = lax.broadcasted_iota(I32, (PL, 2 * PL), 0)
    got = [[] for _ in range(4)]
    for j in range(0, LC // 2, 2):
        r2 = jnp.concatenate([rows[j : j + 1], rows[j + 1 : j + 2]], axis=1)
        l2 = jnp.concatenate([lanes[j : j + 1], lanes[j + 1 : j + 2]], axis=1)
        hot = jnp.where(sub == r2, 1.0, 0.0).astype(BF16)
        hot = jnp.concatenate([hot, hot], axis=0)
        found = jnp.dot(tables, hot, preferred_element_type=F32)
        pick = sub == l2
        for c in range(4):
            value = jnp.sum(jnp.where(pick, found[c * PL : (c + 1) * PL], 0.0), axis=0, keepdims=True)
            got[c] += [value[:, :PL], value[:, PL:]]
    cells = [jnp.concatenate(v, axis=0) for v in got]
    rel = [ctr[c] - cells[c] for c in range(3)]
    dist = rel[0] * rel[0] + rel[1] * rel[1] + rel[2] * rel[2] + 1.0
    inv = lax.rsqrt(dist)
    cube = cells[3] * (inv * inv * inv)
    fifth = 3.0 * cube * (inv * inv)
    terms = [-(cube * rel[c]) for c in range(3)]
    for a, b in ((0, 0), (1, 1), (2, 2), (0, 1), (0, 2), (1, 2)):
        value = fifth * rel[a] * rel[b]
        if a == b:
            value = value - cube
        terms.append(value)
    terms = [jnp.sum(v, axis=0, keepdims=True) for v in terms]
    pad[...] = jnp.zeros((PL, PL), F32)
    for i, v in enumerate(terms):
        pad[i : i + 1, :] = v + pltpu.roll(v, 64, 1)
    back = pad[...].T
    field = [back[0:NB, i : i + 1] for i in range(3)]
    tide = [back[0:NB, 3 + i : 4 + i] for i in range(6)]
    offset = [pos[c] - centre[c] for c in range(3)]
    for c, (i, j, k) in enumerate(((0, 3, 4), (3, 1, 5), (4, 5, 2))):
        out_ref[c] = field[c] + tide[i] * offset[0] + tide[j] * offset[1] + tide[k] * offset[2]


def split3(v):
    high = v.astype(BF16).astype(F32)
    rest = v - high
    mid = rest.astype(BF16).astype(F32)
    return high, mid, rest - mid


def prep_kernel(y_ref, t0, t1, t2, t3, tall, tab):
    me = y_ref[0]
    wide = 2 * PL
    tiles = []
    for i, t in enumerate((t0, t1, t2, t3)):
        tall[i * NB : (i + 1) * NB] = t[0:NB]
        tiles.append(t[NB])
    left = lax.broadcasted_iota(I32, (4, PL), 1) < 64
    code, cnt = [], []
    for a, b in ((tiles[0], tiles[1]), (tiles[2], tiles[3])):
        code.append(jnp.where(left, a, pltpu.roll(b, 64, 1)))
        cnt.append(jnp.where(left, pltpu.roll(a, 64, 1), b))
    code = jnp.concatenate(code, axis=1).astype(I32)
    cnt = jnp.concatenate(cnt, axis=1)[0:1]
    lane = lax.broadcasted_iota(I32, (1, wide), 1)
    valid = (lane & 63) < NB
    flag = [jnp.where(((code[k : k + 1] >> 9) == me) & valid, 1.0, 0.0) for k in range(K)]
    local = [(code[k : k + 1] & 511).astype(F32) for k in range(K)]
    count = (flag[0] + flag[1]) + (flag[2] + flag[3])
    full = jnp.where(count > 2.5, 1.0, 0.0)
    half = jnp.where((count > 0.5) & (count < 2.5), 1.0, 0.0)
    group = lane >> 6
    mine = group == 0
    lists = [jnp.where(m, v, 0.0) for v in (full, half) for m in (~mine, mine)]
    marks = jnp.concatenate(lists + [jnp.zeros((12, wide), F32)], axis=0).astype(BF16)
    a = lax.broadcasted_iota(I32, (wide, wide), 0)
    b = lax.broadcasted_iota(I32, (wide, wide), 1)
    before = jnp.dot(marks, jnp.where(a < b, 1.0, 0.0).astype(BF16), preferred_element_type=F32)
    sizes = [jnp.sum(v, axis=1, keepdims=True) for v in lists]
    place, begin = jnp.full((1, wide), -1.0, F32), jnp.zeros((1, 1), F32)
    for i, v in enumerate(lists):
        place = jnp.where(v > 0.5, begin + before[i : i + 1], place)
        begin = begin + sizes[i]
    moved = jnp.where(a == place.astype(I32), 1.0, 0.0).astype(BF16)
    bucket = lane & 63
    home = ((group - 1) & (NY - 1)) * NB + bucket
    slot, ins, outs = [], jnp.zeros((1, wide), F32), jnp.zeros((1, wide), F32)
    for k in range(K):
        slot.append(jnp.where(flag[k] > 0.5, ins, count + outs))
        ins, outs = ins + flag[k], outs + (1.0 - flag[k])
    fields = []
    for j in range(K):
        pick = jnp.zeros((1, wide), F32)
        for k in range(K):
            pick = pick + jnp.where(slot[k] == float(j), local[k], 0.0)
        fields.append(pick)
    fields += [cnt, home.astype(F32), count, (group * NB + bucket).astype(F32)]
    load = jnp.concatenate(fields, axis=0)
    high = load.astype(BF16).astype(F32)
    both = jnp.concatenate([high, load - high], axis=0).astype(BF16)
    out = lax.dot_general(both, moved, (((1,), (1,)), ((), ())), preferred_element_type=F32)
    out = out[0:8] + out[8:16]
    sizes = jnp.concatenate([jnp.broadcast_to(v, (1, wide)) for v in sizes + [begin] * 4], axis=0)
    tab[...] = jnp.concatenate([out, sizes], axis=0).astype(I32)


def near_kernel(first, *refs):
    (table, tall, src_ref), refs = refs[:3], refs[3:]
    outs, (out_ref, hold, spots, tab, sem) = refs[:-5], refs[-5:]
    if not first:
        kept, outs = outs[0], outs[1:]
    copies = [pltpu.make_async_copy(table, tab, sem.at[0]), pltpu.make_async_copy(hold, spots, sem.at[1])]
    copies[0].start()
    for z in range(NZ):
        hold[z : z + 1, :] = src_ref[z * (TILES + 1) + TILES][0:1].astype(I32)
    copies[1].start()
    out_ref[...] = jnp.zeros(out_ref.shape, F32) if first else kept[...]
    for copy in copies:
        copy.wait()
    lane1 = lax.broadcasted_iota(I32, (1, PL), 1)
    sub4 = lax.broadcasted_iota(I32, (4, PL), 0)
    lane4 = lax.broadcasted_iota(I32, (4, PL), 1)
    spatial = sub4 < 3
    one = jnp.ones((4, PL), F32)
    zero4 = jnp.zeros((4, PL), F32)
    zero8 = jnp.zeros((8, PL), F32)

    def square(v):
        return jnp.sum(jnp.where(spatial, v * v, 0.0), axis=0, keepdims=True)

    def mix(a, b):
        return jnp.where(spatial, a, b)

    def stack(*v):
        return jnp.concatenate(v, axis=0).astype(BF16)

    row_base = 0 if first else (NY - 1) * NB

    def job(e, width):
        n = tab[6, e]
        t = tall[tab[7, e]]
        th, tm, tl = split3(t)
        qh, qm, ql = split3(square(t))
        u = stack(mix(th, one), mix(th, one), mix(tm, one), mix(tm, qh), mix(th, qm), mix(tl, ql), zero8)
        vs, gs = [], []
        for k in range(width):
            z, bucket = tab[k, e] >> 6, tab[k, e] & 63
            begin = spots[z, bucket]
            shift = begin & (PL - 1)
            tile = z * (TILES + 1) + (begin >> 7)
            s = jnp.concatenate([src_ref[tile], src_ref[tile + 1]], axis=0)
            s = pltpu.roll(s, (PL - shift) & (PL - 1), 1)
            s = jnp.where(lane4 < PL - shift, s[0:4], s[4:8])
            live = jnp.where(k < n, spots[z, 64 + bucket], 0)
            sh, sm, sl = split3(-2.0 * s)
            qh, qm, ql = split3(square(s) + SOFT)
            vs.append(stack(mix(sh, qh), mix(sm, qm), mix(sh, ql), mix(sm, one), mix(sl, one), mix(sh, one), zero8))
            w = jnp.where(lane1 < live, s[3:4], 0.0)
            gs.append(stack(*split3(mix(s * w, w)), zero4))
        v = jnp.concatenate(vs, axis=1)
        g = jnp.concatenate(gs, axis=1)
        dist = lax.dot_general(v, u, (((0,), (0,)), ((), ())), preferred_element_type=F32)
        inv = lax.rsqrt(dist)
        f = inv * inv * inv
        high = f.astype(BF16)
        low = (f - high.astype(F32)).astype(BF16)
        o = jnp.dot(g, jnp.concatenate([high, low], axis=1), preferred_element_type=F32)
        o = o[:, :PL] + o[:, PL:]
        a = o[0:4] + o[4:8] + o[8:12]
        out_ref[tab[5, e] - row_base] = jnp.where(lane4 < tab[4, e], a - t * a[3:4], 0.0)

    sizes = [tab[8 + i, 0] for i in range(4)]

    def run(begin, size, width, step):
        def body(i, _):
            for j in range(step):
                job(begin + jnp.minimum(step * i + j, size - 1), width)

        lax.fori_loop(0, (size + step - 1) // step, body, None)

    def whole_steps(size, step):
        return (size + step - 1) // step * step

    n_full, n_half = sizes[0] + sizes[1], sizes[2] + sizes[3]
    early_full = jnp.minimum(n_full, whole_steps(sizes[0], UNROLL[0]))
    early_half = jnp.minimum(n_half, whole_steps(sizes[2], UNROLL[1]))
    if first:
        run(jnp.int32(0), early_full, 4, UNROLL[0])
        run(n_full, early_half, 2, UNROLL[1])
    else:
        run(early_full, n_full - early_full, 4, UNROLL_OWN[0])
        run(n_full + early_half, n_half - early_half, 2, UNROLL_OWN[1])
    if first:
        outs[-1][...] = out_ref[(NY - 1) * NB : NY * NB]
        outs = outs[:-1]
    for i, o in enumerate(outs):
        for c in range(3):
            o[c] = out_ref[i * NB : (i + 1) * NB, c, :]


def final_kernel(cnt_ref, far_ref, p0, p1, p2, p3, out_ref):
    live = lax.broadcasted_iota(I32, (NB, PL), 1) < column_of(cnt_ref[...], NB)
    for c in range(3):
        near = (p0[c] + p1[c]) + (p2[c] + p3[c])
        out_ref[c] = jnp.where(live, far_ref[c] + near, 0.0)


def along_y(k):
    return [(NZ * y + z, NZ * ((y + k) % NY) + z) for y in range(NY) for z in range(NZ)]


def along_x(k):
    return [(2 * x + c, 2 * ((x + k) % NX) + c) for x in range(NX) for c in range(2)]


def call(kernel, outs, in_specs, out_specs, name, mib, scratch=()):
    return pl.pallas_call(
        kernel,
        out_shape=[jax.ShapeDtypeStruct(shape, dtype) for shape, dtype in outs],
        in_specs=in_specs,
        out_specs=out_specs,
        scratch_shapes=scratch,
        compiler_params=pltpu.CompilerParams(vmem_limit_bytes=mib * MIB),
        name=name,
    )


def per_device(positions, masses, counts, dest_ids, near_list, cell_list, cell_centers, cell_mass):
    pos = jnp.transpose(positions[0], (1, 0, 2))
    cnt = counts[0]
    src, tgt, cells = call(
        pack_kernel,
        (((NZ, TILES + 1, 4, PL), F32), ((NB + 1, 4, PL), F32), ((16, 4, PL), F32)),
        [pl.BlockSpec(memory_space=pltpu.HBM)] * 7,
        [vspec()] * 3,
        "pack",
        8,
        [
            pltpu.VMEM((3, NB, PL), F32),
            pltpu.VMEM((NB, PL), F32),
            pltpu.VMEM((1, NB), I32),
            pltpu.VMEM((1, NB), I32),
            pltpu.VMEM((K, NB), I32),
            pltpu.VMEM((3, 2048), F32),
            pltpu.VMEM((1, 2048), F32),
            pltpu.SMEM((1, NB), I32),
            pltpu.VMEM((NB, 8, PL), F32),
            pltpu.SemaphoreType.DMA((8,)),
        ],
    )(
        *[
            pltpu.with_memory_space_constraint(v, pltpu.HBM)
            for v in (pos, masses[0], cnt, dest_ids, near_list[0].T, cell_centers, cell_mass[None])
        ]
    )
    z_rows = [[NZ * y + NZ - 1 - z for z in range(NZ)] for y in range(NY)]
    window = lax.all_to_all(src, "space", 0, 0, axis_index_groups=z_rows, tiled=True)
    tgts = [tgt] + [lax.ppermute(tgt, "space", along_y(k)) for k in (1, -1)]
    tgts.append(lax.ppermute(tgts[1], "space", along_y(1)))
    pair = jnp.stack([cells, lax.ppermute(cells, "slab", [(i, i ^ 1) for i in range(2 * NX)])])
    pairs = [pair] + [lax.ppermute(pair, "slab", along_x(k)) for k in (1, -1)]
    pairs.append(lax.ppermute(pairs[1], "slab", along_x(1)))
    me = (lax.axis_index("space") // NZ).astype(I32).reshape(1)
    place = lax.axis_index("slab").astype(I32).reshape(1)
    tall, tab = call(
        prep_kernel,
        (((NY * NB, 4, PL), F32), ((16, 2 * PL), I32)),
        [sspec()] + [vspec()] * 4,
        [vspec(), vspec()],
        "prep",
        8,
    )(me, *tgts)
    (far,) = call(
        far_kernel,
        (((3, NB, PL), F32),),
        [sspec()] + [vspec()] * 7,
        [vspec()],
        "far",
        16,
        [pltpu.VMEM((PL, PL), F32)],
    )(place, pos, cnt, cell_list[0].T, *pairs)
    tall, tab, far = lax.optimization_barrier((tall, tab, far))
    window = window.reshape(NZ * (TILES + 1), 4, PL)

    def near(first, *arrays):
        partial = ((3, NB, PL), F32)
        kept = ((NB, 4, PL), F32)
        outs = (partial,) * (NY - 1) + (kept,) if first else (partial,)
        return call(
            functools.partial(near_kernel, first),
            outs,
            [vspec()] * len(arrays),
            [vspec()] * len(outs),
            "near",
            32,
            [
                pltpu.VMEM(((NY if first else 1) * NB, 4, PL), F32),
                pltpu.VMEM((NZ, PL), I32),
                pltpu.SMEM((NZ, PL), I32),
                pltpu.SMEM((16, 2 * PL), I32),
                pltpu.SemaphoreType.DMA((2,)),
            ],
        )(*arrays)

    *sent, kept = near(True, tab, tall, window)
    back = [lax.ppermute(sent[i], "space", along_y(-k)) for i, k in ((2, 2), (0, 1), (1, -1))]
    (own,) = near(False, tab, tall, window, kept)
    (out,) = call(
        final_kernel,
        (((3, NB, PL), F32),),
        [vspec()] * 6,
        [vspec()],
        "final",
        8,
    )(cnt, far, own, *back)
    return jnp.transpose(out, (1, 0, 2))[None]


def solution(mesh):
    in_specs = (
        P("slab", "space", None, None),
        P("slab", "space", None),
        P("slab", "space", None),
        P("slab", "space"),
        P("slab", "space", None),
        P("slab", "space", None),
        P(None, "slab"),
        P("slab"),
    )
    return jax.shard_map(
        per_device,
        mesh=mesh,
        in_specs=in_specs,
        out_specs=P("slab", "space", None, None),
        check_vma=False,
    )
```

```python
import functools

import jax
import jax.numpy as jnp
from jax import lax
from jax.experimental import pallas as pl
from jax.experimental.pallas import tpu as pltpu
from jax.sharding import PartitionSpec as P

NB = 48
PL = 128
K = 4
LC = 32
NY = 4
NZ = 8
NX = 4
SOFT = 0.01
UNROLL = (18, 20)
UNROLL_OWN = (12, 8)
FULL_SLOTS = 54
MIB = 1 << 20
TILES = 36
F32 = jnp.float32
I32 = jnp.int32
BF16 = jnp.bfloat16
VMEM = pltpu.VMEM
SMEM = pltpu.SMEM


def vspec():
    return pl.BlockSpec(memory_space=VMEM)


def sspec():
    return pl.BlockSpec(memory_space=SMEM)


def column_of(row, n):
    square = jnp.broadcast_to(row, (n, n))
    diag = lax.broadcasted_iota(I32, (n, n), 0) == lax.broadcasted_iota(I32, (n, n), 1)
    return jnp.sum(jnp.where(diag, square, jnp.zeros_like(square)), axis=1, keepdims=True)


def pack_kernel(*refs):
    ins, (src_ref, tgt_ref, cell_ref), holds = refs[:7], refs[7:10], refs[10:18]
    full, sem = refs[18:]
    copies = [pltpu.make_async_copy(ins[i], holds[i], sem.at[i]) for i in range(7)]
    copies.append(pltpu.make_async_copy(ins[2], holds[7], sem.at[7]))
    for copy in copies:
        copy.start()
    for copy in copies:
        copy.wait()
    pos_ref, mass_ref, cnt_ref, dest_ref, near_ref, ctr_ref, cm_ref, cnt_smem = holds
    counts = cnt_ref[...]
    cnt = column_of(counts, NB)
    near = near_ref[...]
    off = (near >= NB).astype(I32) + (near >= 2 * NB).astype(I32)
    dev = (dest_ref[...] + off - 1) & (NY * NZ - 1)
    code = (dev >> 3) * 512 + ((NZ - 1) - (dev & (NZ - 1))) * 64 + (near - off * NB)
    gap = jnp.zeros((4, 64 - NB), I32)
    info = jnp.concatenate([code, gap, jnp.broadcast_to(counts, (4, NB)), gap], axis=1)
    lane = lax.broadcasted_iota(I32, (NB, PL), 1)
    weight = jnp.where(lane < cnt, mass_ref[...], 0.0)
    for c in range(3):
        value = pos_ref[c]
        tgt_ref[0:NB, c, :] = value
        full[:, c, :] = value
    full[:, 3, :] = weight
    lane4 = lax.broadcasted_iota(I32, (4, PL), 1)
    carry, begin = jnp.zeros((4, PL), F32), jnp.int32(0)
    for b in range(NB):
        shift, tile = begin & (PL - 1), begin >> 7
        turned = pltpu.roll(full[b], shift, 1)[0:4]
        merged = jnp.where(lane4 >= shift, turned, carry)
        src_ref[0, tile] = merged
        begin = begin + cnt_smem[0, b]
        carry = jnp.where((begin >> 7) != tile, turned, merged)
    square = (NB, NB)
    earlier = lax.broadcasted_iota(I32, square, 0) < lax.broadcasted_iota(I32, square, 1)
    starts = jnp.sum(jnp.where(earlier, cnt, 0), axis=0, keepdims=True)
    places = jnp.concatenate([starts, gap[0:1], counts, gap[0:1]], axis=1)
    src_ref[0, TILES] = jnp.broadcast_to(places, (4, PL)).astype(F32)
    for z in range(1, NZ):
        src_ref[z] = src_ref[0]
    tgt_ref[0:NB, 3, :] = jnp.zeros((NB, PL), F32)
    tgt_ref[NB] = info.astype(F32)
    for j in range(16):
        part = slice(j * PL, (j + 1) * PL)
        cell_ref[j, 0:3, :] = ctr_ref[:, part]
        cell_ref[j, 3:4, :] = cm_ref[0:1, part]


def far_kernel(place_ref, pos_ref, cnt_ref, list_ref, c0, c1, c2, c3, out_ref, pad):
    xs, cs = place_ref[0] >> 1, place_ref[0] & 1
    lane = lax.broadcasted_iota(I32, (NB, PL), 1)
    cnt = column_of(cnt_ref[...], NB)
    live = lane < cnt
    total = jnp.maximum(cnt, 1).astype(F32)
    pos = [pos_ref[c] for c in range(3)]
    centre = [jnp.sum(jnp.where(live, v, 0.0), axis=1, keepdims=True) / total for v in pos]
    diag = lax.broadcasted_iota(I32, (NB, PL), 0) == (lane & 63)
    ctr = [jnp.sum(jnp.where(diag, v, 0.0), axis=0, keepdims=True) for v in centre]
    wide = jnp.concatenate([list_ref[...], jnp.zeros((LC, PL - NB), I32)], axis=1)
    twice = wide + pltpu.roll(wide, 64, 1)
    half = lax.broadcasted_iota(I32, (1, PL), 1) < 64
    ids = [jnp.where(half, twice[2 * j : 2 * j + 1], twice[2 * j + 1 : 2 * j + 2]) for j in range(LC // 2)]
    ids = jnp.concatenate(ids, axis=0)
    slab = ids >> 11
    dx = ((slab >> 1) - xs) & (NX - 1)
    order = jnp.where(dx == 3, 1, jnp.where(dx == 0, 0, dx + 1))
    rows = (order * 2 + ((slab & 1) ^ cs)) * 16 + ((ids >> 7) & 15)
    lanes = ids & (PL - 1)
    tables = []
    for c in range(4):
        whole = jnp.concatenate([ref[i, :, c, :] for ref in (c0, c1, c2, c3) for i in range(2)], axis=0)
        whole = whole.T
        high = whole.astype(BF16)
        low = (whole - high.astype(F32)).astype(BF16)
        tables.append(jnp.concatenate([high, low], axis=1))
    tables = jnp.concatenate(tables, axis=0)
    sub = lax.broadcasted_iota(I32, (PL, 2 * PL), 0)
    got = [[] for _ in range(4)]
    for j in range(0, LC // 2, 2):
        r2 = jnp.concatenate([rows[j : j + 1], rows[j + 1 : j + 2]], axis=1)
        l2 = jnp.concatenate([lanes[j : j + 1], lanes[j + 1 : j + 2]], axis=1)
        hot = jnp.where(sub == r2, 1.0, 0.0).astype(BF16)
        hot = jnp.concatenate([hot, hot], axis=0)
        found = jnp.dot(tables, hot, preferred_element_type=F32)
        pick = sub == l2
        for c in range(4):
            value = jnp.sum(jnp.where(pick, found[c * PL : (c + 1) * PL], 0.0), axis=0, keepdims=True)
            got[c] += [value[:, :PL], value[:, PL:]]
    cells = [jnp.concatenate(v, axis=0) for v in got]
    rel = [ctr[c] - cells[c] for c in range(3)]
    dist = rel[0] * rel[0] + rel[1] * rel[1] + rel[2] * rel[2] + 1.0
    inv = lax.rsqrt(dist)
    cube = cells[3] * (inv * inv * inv)
    fifth = 3.0 * cube * (inv * inv)
    terms = [-(cube * rel[c]) for c in range(3)]
    for a, b in ((0, 0), (1, 1), (2, 2), (0, 1), (0, 2), (1, 2)):
        value = fifth * rel[a] * rel[b]
        if a == b:
            value = value - cube
        terms.append(value)
    terms = [jnp.sum(v, axis=0, keepdims=True) for v in terms]
    pad[...] = jnp.zeros((PL, PL), F32)
    for i, v in enumerate(terms):
        pad[i : i + 1, :] = v + pltpu.roll(v, 64, 1)
    back = pad[...].T
    field = [back[0:NB, i : i + 1] for i in range(3)]
    tide = [back[0:NB, 3 + i : 4 + i] for i in range(6)]
    offset = [pos[c] - centre[c] for c in range(3)]
    for c, (i, j, k) in enumerate(((0, 3, 4), (3, 1, 5), (4, 5, 2))):
        out_ref[c] = field[c] + tide[i] * offset[0] + tide[j] * offset[1] + tide[k] * offset[2]


def split3(v):
    high = v.astype(BF16).astype(F32)
    rest = v - high
    mid = rest.astype(BF16).astype(F32)
    return high, mid, rest - mid


def prep_kernel(y_ref, t0, t1, t2, t3, tall, tab):
    me = y_ref[0]
    wide = 2 * PL
    tiles = []
    for i, t in enumerate((t0, t1, t2, t3)):
        tall[i * NB : (i + 1) * NB] = t[0:NB]
        tiles.append(t[NB])
    left = lax.broadcasted_iota(I32, (4, PL), 1) < 64
    code, cnt = [], []
    for a, b in ((tiles[0], tiles[1]), (tiles[2], tiles[3])):
        code.append(jnp.where(left, a, pltpu.roll(b, 64, 1)))
        cnt.append(jnp.where(left, pltpu.roll(a, 64, 1), b))
    code = jnp.concatenate(code, axis=1).astype(I32)
    cnt = jnp.concatenate(cnt, axis=1)[0:1]
    lane = lax.broadcasted_iota(I32, (1, wide), 1)
    valid = (lane & 63) < NB
    flag = [jnp.where(((code[k : k + 1] >> 9) == me) & valid, 1.0, 0.0) for k in range(K)]
    local = [(code[k : k + 1] & 511).astype(F32) for k in range(K)]
    count = (flag[0] + flag[1]) + (flag[2] + flag[3])
    full = jnp.where(count > 2.5, 1.0, 0.0)
    half = jnp.where((count > 0.5) & (count < 2.5), 1.0, 0.0)
    group = lane >> 6
    mine = group == 0
    lists = [jnp.where(m, v, 0.0) for v in (full, half) for m in (~mine, mine)]
    marks = jnp.concatenate(lists + [jnp.zeros((12, wide), F32)], axis=0).astype(BF16)
    a = lax.broadcasted_iota(I32, (wide, wide), 0)
    b = lax.broadcasted_iota(I32, (wide, wide), 1)
    before = jnp.dot(marks, jnp.where(a < b, 1.0, 0.0).astype(BF16), preferred_element_type=F32)
    sizes = [jnp.sum(v, axis=1, keepdims=True) for v in lists]
    place, begin = jnp.full((1, wide), -1.0, F32), jnp.zeros((1, 1), F32)
    for i, v in enumerate(lists):
        place = jnp.where(v > 0.5, begin + before[i : i + 1], place)
        begin = begin + sizes[i]
    moved = jnp.where(a == place.astype(I32), 1.0, 0.0).astype(BF16)
    bucket = lane & 63
    home = ((group - 1) & (NY - 1)) * NB + bucket
    slot, ins, outs = [], jnp.zeros((1, wide), F32), jnp.zeros((1, wide), F32)
    for k in range(K):
        slot.append(jnp.where(flag[k] > 0.5, ins, count + outs))
        ins, outs = ins + flag[k], outs + (1.0 - flag[k])
    fields = []
    for j in range(K):
        pick = jnp.zeros((1, wide), F32)
        for k in range(K):
            pick = pick + jnp.where(slot[k] == float(j), local[k], 0.0)
        fields.append(pick)
    fields += [cnt, home.astype(F32), count, (group * NB + bucket).astype(F32)]
    load = jnp.concatenate(fields, axis=0)
    high = load.astype(BF16).astype(F32)
    both = jnp.concatenate([high, load - high], axis=0).astype(BF16)
    out = lax.dot_general(both, moved, (((1,), (1,)), ((), ())), preferred_element_type=F32)
    out = out[0:8] + out[8:16]
    sizes = jnp.concatenate([jnp.broadcast_to(v, (1, wide)) for v in sizes + [begin] * 4], axis=0)
    tab[...] = jnp.concatenate([out, sizes], axis=0).astype(I32)


def near_kernel(first, *refs):
    (table, tall, src_ref), refs = refs[:3], refs[3:]
    outs, (out_ref, hold, spots, tab, sem) = refs[:-5], refs[-5:]
    if not first:
        kept, outs = outs[0], outs[1:]
    copies = [pltpu.make_async_copy(table, tab, sem.at[0]), pltpu.make_async_copy(hold, spots, sem.at[1])]
    copies[0].start()
    for z in range(NZ):
        hold[z : z + 1, :] = src_ref[z * (TILES + 1) + TILES][0:1].astype(I32)
    copies[1].start()
    out_ref[...] = jnp.zeros(out_ref.shape, F32) if first else kept[...]
    for copy in copies:
        copy.wait()
    lane1 = lax.broadcasted_iota(I32, (1, PL), 1)
    sub4 = lax.broadcasted_iota(I32, (4, PL), 0)
    lane4 = lax.broadcasted_iota(I32, (4, PL), 1)
    spatial = sub4 < 3
    one = jnp.ones((4, PL), F32)
    zero4 = jnp.zeros((4, PL), F32)
    zero8 = jnp.zeros((8, PL), F32)

    def square(v):
        return jnp.sum(jnp.where(spatial, v * v, 0.0), axis=0, keepdims=True)

    def mix(a, b):
        return jnp.where(spatial, a, b)

    def stack(*v):
        return jnp.concatenate(v, axis=0).astype(BF16)

    row_base = 0 if first else (NY - 1) * NB

    def job(e, width):
        n = tab[6, e]
        t = tall[tab[7, e]]
        th, tm, tl = split3(t)
        qh, qm, ql = split3(square(t))
        u = stack(mix(th, one), mix(th, one), mix(tm, one), mix(tm, qh), mix(th, qm), mix(tl, ql), zero8)
        vs, gs = [], []
        for k in range(width):
            z, bucket = tab[k, e] >> 6, tab[k, e] & 63
            begin = spots[z, bucket]
            shift = begin & (PL - 1)
            tile = z * (TILES + 1) + (begin >> 7)
            s = jnp.concatenate([src_ref[tile], src_ref[tile + 1]], axis=0)
            s = pltpu.roll(s, (PL - shift) & (PL - 1), 1)
            s = jnp.where(lane4 < PL - shift, s[0:4], s[4:8])
            live = jnp.where(k < n, spots[z, 64 + bucket], 0)
            sh, sm, sl = split3(-2.0 * s)
            qh, qm, ql = split3(square(s) + SOFT)
            vs.append(stack(mix(sh, qh), mix(sm, qm), mix(sh, ql), mix(sm, one), mix(sl, one), mix(sh, one), zero8))
            w = jnp.where(lane1 < live, s[3:4], 0.0)
            gs.append(stack(*split3(mix(s * w, w)), zero4))
        v = jnp.concatenate(vs, axis=1)
        g = jnp.concatenate(gs, axis=1)
        dist = lax.dot_general(v, u, (((0,), (0,)), ((), ())), preferred_element_type=F32)
        inv = lax.rsqrt(dist)
        f = inv * inv * inv
        high = f.astype(BF16)
        low = (f - high.astype(F32)).astype(BF16)
        o = jnp.dot(g, jnp.concatenate([high, low], axis=1), preferred_element_type=F32)
        o = o[:, :PL] + o[:, PL:]
        a = o[0:4] + o[4:8] + o[8:12]
        out_ref[tab[5, e] - row_base] = jnp.where(lane4 < tab[4, e], a - t * a[3:4], 0.0)

    sizes = [tab[8 + i, 0] for i in range(4)]

    def run(begin, size, width, step):
        def body(i, _):
            for j in range(step):
                job(begin + jnp.minimum(step * i + j, size - 1), width)

        lax.fori_loop(0, (size + step - 1) // step, body, None)

    def whole_steps(size, step):
        return (size + step - 1) // step * step

    n_full, n_half = sizes[0] + sizes[1], sizes[2] + sizes[3]
    early_full = jnp.minimum(n_full, jnp.maximum(whole_steps(sizes[0], UNROLL[0]), FULL_SLOTS))
    early_half = jnp.minimum(n_half, whole_steps(sizes[2], UNROLL[1]))
    if first:
        run(jnp.int32(0), early_full, 4, UNROLL[0])
        run(n_full, early_half, 2, UNROLL[1])
    else:
        run(early_full, n_full - early_full, 4, UNROLL_OWN[0])
        run(n_full + early_half, n_half - early_half, 2, UNROLL_OWN[1])
    if first:
        outs[-1][...] = out_ref[(NY - 1) * NB : NY * NB]
        outs = outs[:-1]
    for i, o in enumerate(outs):
        for c in range(3):
            o[c] = out_ref[i * NB : (i + 1) * NB, c, :]


def final_kernel(cnt_ref, far_ref, p0, p1, p2, p3, out_ref):
    live = lax.broadcasted_iota(I32, (NB, PL), 1) < column_of(cnt_ref[...], NB)
    for c in range(3):
        near = (p0[c] + p1[c]) + (p2[c] + p3[c])
        out_ref[c] = jnp.where(live, far_ref[c] + near, 0.0)


def along_y(k):
    return [(NZ * y + z, NZ * ((y + k) % NY) + z) for y in range(NY) for z in range(NZ)]


def along_x(k):
    return [(2 * x + c, 2 * ((x + k) % NX) + c) for x in range(NX) for c in range(2)]


def call(kernel, outs, in_specs, out_specs, name, mib, scratch=()):
    return pl.pallas_call(
        kernel,
        out_shape=[jax.ShapeDtypeStruct(shape, dtype) for shape, dtype in outs],
        in_specs=in_specs,
        out_specs=out_specs,
        scratch_shapes=scratch,
        compiler_params=pltpu.CompilerParams(vmem_limit_bytes=mib * MIB),
        name=name,
    )


def per_device(positions, masses, counts, dest_ids, near_list, cell_list, cell_centers, cell_mass):
    pos = jnp.transpose(positions[0], (1, 0, 2))
    cnt = counts[0]
    src, tgt, cells = call(
        pack_kernel,
        (((NZ, TILES + 1, 4, PL), F32), ((NB + 1, 4, PL), F32), ((16, 4, PL), F32)),
        [pl.BlockSpec(memory_space=pltpu.HBM)] * 7,
        [vspec()] * 3,
        "pack",
        8,
        [
            pltpu.VMEM((3, NB, PL), F32),
            pltpu.VMEM((NB, PL), F32),
            pltpu.VMEM((1, NB), I32),
            pltpu.VMEM((1, NB), I32),
            pltpu.VMEM((K, NB), I32),
            pltpu.VMEM((3, 2048), F32),
            pltpu.VMEM((1, 2048), F32),
            pltpu.SMEM((1, NB), I32),
            pltpu.VMEM((NB, 8, PL), F32),
            pltpu.SemaphoreType.DMA((8,)),
        ],
    )(
        *[
            pltpu.with_memory_space_constraint(v, pltpu.HBM)
            for v in (pos, masses[0], cnt, dest_ids, near_list[0].T, cell_centers, cell_mass[None])
        ]
    )
    z_rows = [[NZ * y + NZ - 1 - z for z in range(NZ)] for y in range(NY)]
    window = lax.all_to_all(src, "space", 0, 0, axis_index_groups=z_rows, tiled=True)
    tgts = [tgt] + [lax.ppermute(tgt, "space", along_y(k)) for k in (1, -1)]
    tgts.append(lax.ppermute(tgts[1], "space", along_y(1)))
    pair = jnp.stack([cells, lax.ppermute(cells, "slab", [(i, i ^ 1) for i in range(2 * NX)])])
    pairs = [pair] + [lax.ppermute(pair, "slab", along_x(k)) for k in (1, -1)]
    pairs.append(lax.ppermute(pairs[1], "slab", along_x(1)))
    me = (lax.axis_index("space") // NZ).astype(I32).reshape(1)
    place = lax.axis_index("slab").astype(I32).reshape(1)
    tall, tab = call(
        prep_kernel,
        (((NY * NB, 4, PL), F32), ((16, 2 * PL), I32)),
        [sspec()] + [vspec()] * 4,
        [vspec(), vspec()],
        "prep",
        8,
    )(me, *tgts)
    tall, tab, *pairs = lax.optimization_barrier((tall, tab, *pairs))
    window = window.reshape(NZ * (TILES + 1), 4, PL)

    def near(first, *arrays):
        partial = ((3, NB, PL), F32)
        kept = ((NB, 4, PL), F32)
        outs = (partial,) * (NY - 1) + (kept,) if first else (partial,)
        return call(
            functools.partial(near_kernel, first),
            outs,
            [vspec()] * len(arrays),
            [vspec()] * len(outs),
            "near",
            32,
            [
                pltpu.VMEM(((NY if first else 1) * NB, 4, PL), F32),
                pltpu.VMEM((NZ, PL), I32),
                pltpu.SMEM((NZ, PL), I32),
                pltpu.SMEM((16, 2 * PL), I32),
                pltpu.SemaphoreType.DMA((2,)),
            ],
        )(*arrays)

    *sent, kept = near(True, tab, tall, window)
    back = [lax.ppermute(sent[i], "space", along_y(-k)) for i, k in ((2, 2), (0, 1), (1, -1))]
    *pairs, kept, sent[0] = lax.optimization_barrier((*pairs, kept, sent[0]))
    (far,) = call(
        far_kernel,
        (((3, NB, PL), F32),),
        [sspec()] + [vspec()] * 7,
        [vspec()],
        "far",
        16,
        [pltpu.VMEM((PL, PL), F32)],
    )(place, pos, cnt, cell_list[0].T, *pairs)
    (own,) = near(False, tab, tall, window, kept)
    (out,) = call(
        final_kernel,
        (((3, NB, PL), F32),),
        [vspec()] * 6,
        [vspec()],
        "final",
        8,
    )(cnt, far, own, *back)
    return jnp.transpose(out, (1, 0, 2))[None]


def solution(mesh):
    in_specs = (
        P("slab", "space", None, None),
        P("slab", "space", None),
        P("slab", "space", None),
        P("slab", "space"),
        P("slab", "space", None),
        P("slab", "space", None),
        P(None, "slab"),
        P("slab"),
    )
    return jax.shard_map(
        per_device,
        mesh=mesh,
        in_specs=in_specs,
        out_specs=P("slab", "space", None, None),
        check_vma=False,
    )
```

```python
import functools

import jax
import jax.numpy as jnp
from jax import lax
from jax.experimental import pallas as pl
from jax.experimental.pallas import tpu as pltpu
from jax.sharding import PartitionSpec as P

NB = 48
PL = 128
K = 4
LC = 32
NY = 4
NZ = 8
NX = 4
SOFT = 0.01
UNROLL = (18, 20)
UNROLL_OWN = (12, 8)
MIB = 1 << 20
TILES = 36
F32 = jnp.float32
I32 = jnp.int32
BF16 = jnp.bfloat16
VMEM = pltpu.VMEM
SMEM = pltpu.SMEM


def vspec():
    return pl.BlockSpec(memory_space=VMEM)


def sspec():
    return pl.BlockSpec(memory_space=SMEM)


def column_of(row, n):
    square = jnp.broadcast_to(row, (n, n))
    diag = lax.broadcasted_iota(I32, (n, n), 0) == lax.broadcasted_iota(I32, (n, n), 1)
    return jnp.sum(jnp.where(diag, square, jnp.zeros_like(square)), axis=1, keepdims=True)


def pack_kernel(*refs):
    ins, (src_ref, tgt_ref, cell_ref), holds = refs[:7], refs[7:10], refs[10:18]
    full, sem = refs[18:]
    copies = [pltpu.make_async_copy(ins[i], holds[i], sem.at[i]) for i in range(7)]
    copies.append(pltpu.make_async_copy(ins[2], holds[7], sem.at[7]))
    for copy in copies:
        copy.start()
    for copy in copies:
        copy.wait()
    pos_ref, mass_ref, cnt_ref, dest_ref, near_ref, ctr_ref, cm_ref, cnt_smem = holds
    counts = cnt_ref[...]
    cnt = column_of(counts, NB)
    near = near_ref[...]
    off = (near >= NB).astype(I32) + (near >= 2 * NB).astype(I32)
    dev = (dest_ref[...] + off - 1) & (NY * NZ - 1)
    code = (dev >> 3) * 512 + ((NZ - 1) - (dev & (NZ - 1))) * 64 + (near - off * NB)
    gap = jnp.zeros((4, 64 - NB), I32)
    info = jnp.concatenate([code, gap, jnp.broadcast_to(counts, (4, NB)), gap], axis=1)
    lane = lax.broadcasted_iota(I32, (NB, PL), 1)
    weight = jnp.where(lane < cnt, mass_ref[...], 0.0)
    for c in range(3):
        value = pos_ref[c]
        tgt_ref[0:NB, c, :] = value
        full[:, c, :] = value
    full[:, 3, :] = weight
    lane4 = lax.broadcasted_iota(I32, (4, PL), 1)
    carry, begin = jnp.zeros((4, PL), F32), jnp.int32(0)
    for b in range(NB):
        shift, tile = begin & (PL - 1), begin >> 7
        turned = pltpu.roll(full[b], shift, 1)[0:4]
        merged = jnp.where(lane4 >= shift, turned, carry)
        src_ref[0, tile] = merged
        begin = begin + cnt_smem[0, b]
        carry = jnp.where((begin >> 7) != tile, turned, merged)
    square = (NB, NB)
    earlier = lax.broadcasted_iota(I32, square, 0) < lax.broadcasted_iota(I32, square, 1)
    starts = jnp.sum(jnp.where(earlier, cnt, 0), axis=0, keepdims=True)
    places = jnp.concatenate([starts, gap[0:1], counts, gap[0:1]], axis=1)
    src_ref[0, TILES] = jnp.broadcast_to(places, (4, PL)).astype(F32)
    for z in range(1, NZ):
        src_ref[z] = src_ref[0]
    tgt_ref[0:NB, 3, :] = jnp.zeros((NB, PL), F32)
    tgt_ref[NB] = info.astype(F32)
    for j in range(16):
        part = slice(j * PL, (j + 1) * PL)
        cell_ref[j, 0:3, :] = ctr_ref[:, part]
        cell_ref[j, 3:4, :] = cm_ref[0:1, part]


def far_kernel(place_ref, pos_hbm, cnt_hbm, list_hbm, c0, c1, c2, c3, out_ref, pad, pos_ref, cnt_ref, list_ref, sem):
    xs, cs = place_ref[0] >> 1, place_ref[0] & 1
    moves = ((pos_hbm, pos_ref), (cnt_hbm, cnt_ref), (list_hbm, list_ref))
    copies = [pltpu.make_async_copy(a, b, sem.at[i]) for i, (a, b) in enumerate(moves)]
    for copy in copies:
        copy.start()
    tables = []
    for c in range(4):
        whole = jnp.concatenate([ref[i, :, c, :] for ref in (c0, c1, c2, c3) for i in range(2)], axis=0)
        whole = whole.T
        high = whole.astype(BF16)
        low = (whole - high.astype(F32)).astype(BF16)
        tables.append(jnp.concatenate([high, low], axis=1))
    tables = jnp.concatenate(tables, axis=0)
    for copy in copies:
        copy.wait()
    lane = lax.broadcasted_iota(I32, (NB, PL), 1)
    cnt = column_of(cnt_ref[...], NB)
    live = lane < cnt
    total = jnp.maximum(cnt, 1).astype(F32)
    pos = [pos_ref[c] for c in range(3)]
    centre = [jnp.sum(jnp.where(live, v, 0.0), axis=1, keepdims=True) / total for v in pos]
    diag = lax.broadcasted_iota(I32, (NB, PL), 0) == (lane & 63)
    ctr = [jnp.sum(jnp.where(diag, v, 0.0), axis=0, keepdims=True) for v in centre]
    wide = jnp.concatenate([list_ref[...], jnp.zeros((LC, PL - NB), I32)], axis=1)
    twice = wide + pltpu.roll(wide, 64, 1)
    half = lax.broadcasted_iota(I32, (1, PL), 1) < 64
    ids = [jnp.where(half, twice[2 * j : 2 * j + 1], twice[2 * j + 1 : 2 * j + 2]) for j in range(LC // 2)]
    ids = jnp.concatenate(ids, axis=0)
    slab = ids >> 11
    dx = ((slab >> 1) - xs) & (NX - 1)
    order = jnp.where(dx == 3, 1, jnp.where(dx == 0, 0, dx + 1))
    rows = (order * 2 + ((slab & 1) ^ cs)) * 16 + ((ids >> 7) & 15)
    lanes = ids & (PL - 1)
    sub = lax.broadcasted_iota(I32, (PL, 2 * PL), 0)
    got = [[] for _ in range(4)]
    for j in range(0, LC // 2, 2):
        r2 = jnp.concatenate([rows[j : j + 1], rows[j + 1 : j + 2]], axis=1)
        l2 = jnp.concatenate([lanes[j : j + 1], lanes[j + 1 : j + 2]], axis=1)
        hot = jnp.where(sub == r2, 1.0, 0.0).astype(BF16)
        hot = jnp.concatenate([hot, hot], axis=0)
        found = jnp.dot(tables, hot, preferred_element_type=F32)
        pick = sub == l2
        for c in range(4):
            value = jnp.sum(jnp.where(pick, found[c * PL : (c + 1) * PL], 0.0), axis=0, keepdims=True)
            got[c] += [value[:, :PL], value[:, PL:]]
    cells = [jnp.concatenate(v, axis=0) for v in got]
    rel = [ctr[c] - cells[c] for c in range(3)]
    dist = rel[0] * rel[0] + rel[1] * rel[1] + rel[2] * rel[2] + 1.0
    inv = lax.rsqrt(dist)
    cube = cells[3] * (inv * inv * inv)
    fifth = 3.0 * cube * (inv * inv)
    terms = [-(cube * rel[c]) for c in range(3)]
    for a, b in ((0, 0), (1, 1), (2, 2), (0, 1), (0, 2), (1, 2)):
        value = fifth * rel[a] * rel[b]
        if a == b:
            value = value - cube
        terms.append(value)
    terms = [jnp.sum(v, axis=0, keepdims=True) for v in terms]
    pad[...] = jnp.zeros((PL, PL), F32)
    for i, v in enumerate(terms):
        pad[i : i + 1, :] = v + pltpu.roll(v, 64, 1)
    back = pad[...].T
    field = [back[0:NB, i : i + 1] for i in range(3)]
    tide = [back[0:NB, 3 + i : 4 + i] for i in range(6)]
    offset = [pos[c] - centre[c] for c in range(3)]
    for c, (i, j, k) in enumerate(((0, 3, 4), (3, 1, 5), (4, 5, 2))):
        out_ref[c] = field[c] + tide[i] * offset[0] + tide[j] * offset[1] + tide[k] * offset[2]


def split3(v):
    high = v.astype(BF16).astype(F32)
    rest = v - high
    mid = rest.astype(BF16).astype(F32)
    return high, mid, rest - mid


def prep_kernel(y_ref, t0, t1, t2, t3, tall, tab):
    me = y_ref[0]
    wide = 2 * PL
    tiles = []
    for i, t in enumerate((t0, t1, t2, t3)):
        tall[i * NB : (i + 1) * NB] = t[0:NB]
        tiles.append(t[NB])
    left = lax.broadcasted_iota(I32, (4, PL), 1) < 64
    code, cnt = [], []
    for a, b in ((tiles[0], tiles[1]), (tiles[2], tiles[3])):
        code.append(jnp.where(left, a, pltpu.roll(b, 64, 1)))
        cnt.append(jnp.where(left, pltpu.roll(a, 64, 1), b))
    code = jnp.concatenate(code, axis=1).astype(I32)
    cnt = jnp.concatenate(cnt, axis=1)[0:1]
    lane = lax.broadcasted_iota(I32, (1, wide), 1)
    valid = (lane & 63) < NB
    flag = [jnp.where(((code[k : k + 1] >> 9) == me) & valid, 1.0, 0.0) for k in range(K)]
    local = [(code[k : k + 1] & 511).astype(F32) for k in range(K)]
    count = (flag[0] + flag[1]) + (flag[2] + flag[3])
    full = jnp.where(count > 2.5, 1.0, 0.0)
    half = jnp.where((count > 0.5) & (count < 2.5), 1.0, 0.0)
    group = lane >> 6
    mine = group == 0
    lists = [jnp.where(m, v, 0.0) for v in (full, half) for m in (~mine, mine)]
    marks = jnp.concatenate(lists + [jnp.zeros((12, wide), F32)], axis=0).astype(BF16)
    a = lax.broadcasted_iota(I32, (wide, wide), 0)
    b = lax.broadcasted_iota(I32, (wide, wide), 1)
    before = jnp.dot(marks, jnp.where(a < b, 1.0, 0.0).astype(BF16), preferred_element_type=F32)
    sizes = [jnp.sum(v, axis=1, keepdims=True) for v in lists]
    place, begin = jnp.full((1, wide), -1.0, F32), jnp.zeros((1, 1), F32)
    for i, v in enumerate(lists):
        place = jnp.where(v > 0.5, begin + before[i : i + 1], place)
        begin = begin + sizes[i]
    moved = jnp.where(a == place.astype(I32), 1.0, 0.0).astype(BF16)
    bucket = lane & 63
    home = ((group - 1) & (NY - 1)) * NB + bucket
    slot, ins, outs = [], jnp.zeros((1, wide), F32), jnp.zeros((1, wide), F32)
    for k in range(K):
        slot.append(jnp.where(flag[k] > 0.5, ins, count + outs))
        ins, outs = ins + flag[k], outs + (1.0 - flag[k])
    fields = []
    for j in range(K):
        pick = jnp.zeros((1, wide), F32)
        for k in range(K):
            pick = pick + jnp.where(slot[k] == float(j), local[k], 0.0)
        fields.append(pick)
    fields += [cnt, home.astype(F32), count, (group * NB + bucket).astype(F32)]
    load = jnp.concatenate(fields, axis=0)
    high = load.astype(BF16).astype(F32)
    both = jnp.concatenate([high, load - high], axis=0).astype(BF16)
    out = lax.dot_general(both, moved, (((1,), (1,)), ((), ())), preferred_element_type=F32)
    out = out[0:8] + out[8:16]
    sizes = jnp.concatenate([jnp.broadcast_to(v, (1, wide)) for v in sizes + [begin] * 4], axis=0)
    tab[...] = jnp.concatenate([out, sizes], axis=0).astype(I32)


def near_kernel(first, *refs):
    (table, tall, src_ref), refs = refs[:3], refs[3:]
    outs, (out_ref, hold, spots, tab, sem) = refs[:-5], refs[-5:]
    if not first:
        kept, outs = outs[0], outs[1:]
    copies = [pltpu.make_async_copy(table, tab, sem.at[0]), pltpu.make_async_copy(hold, spots, sem.at[1])]
    copies[0].start()
    for z in range(NZ):
        hold[z : z + 1, :] = src_ref[z * (TILES + 1) + TILES][0:1].astype(I32)
    copies[1].start()
    out_ref[...] = jnp.zeros(out_ref.shape, F32) if first else kept[...]
    for copy in copies:
        copy.wait()
    lane1 = lax.broadcasted_iota(I32, (1, PL), 1)
    sub4 = lax.broadcasted_iota(I32, (4, PL), 0)
    lane4 = lax.broadcasted_iota(I32, (4, PL), 1)
    spatial = sub4 < 3
    one = jnp.ones((4, PL), F32)
    zero4 = jnp.zeros((4, PL), F32)
    zero8 = jnp.zeros((8, PL), F32)

    def square(v):
        return jnp.sum(jnp.where(spatial, v * v, 0.0), axis=0, keepdims=True)

    def mix(a, b):
        return jnp.where(spatial, a, b)

    def stack(*v):
        return jnp.concatenate(v, axis=0).astype(BF16)

    row_base = 0 if first else (NY - 1) * NB

    def job(e, width):
        n = tab[6, e]
        t = tall[tab[7, e]]
        th, tm, tl = split3(t)
        qh, qm, ql = split3(square(t))
        u = stack(mix(th, one), mix(th, one), mix(tm, one), mix(tm, qh), mix(th, qm), mix(tl, ql), zero8)
        vs, gs = [], []
        for k in range(width):
            z, bucket = tab[k, e] >> 6, tab[k, e] & 63
            begin = spots[z, bucket]
            shift = begin & (PL - 1)
            tile = z * (TILES + 1) + (begin >> 7)
            s = jnp.concatenate([src_ref[tile], src_ref[tile + 1]], axis=0)
            s = pltpu.roll(s, (PL - shift) & (PL - 1), 1)
            s = jnp.where(lane4 < PL - shift, s[0:4], s[4:8])
            live = jnp.where(k < n, spots[z, 64 + bucket], 0)
            sh, sm, sl = split3(-2.0 * s)
            qh, qm, ql = split3(square(s) + SOFT)
            vs.append(stack(mix(sh, qh), mix(sm, qm), mix(sh, ql), mix(sm, one), mix(sl, one), mix(sh, one), zero8))
            w = jnp.where(lane1 < live, s[3:4], 0.0)
            gs.append(stack(*split3(mix(s * w, w)), zero4))
        v = jnp.concatenate(vs, axis=1)
        g = jnp.concatenate(gs, axis=1)
        dist = lax.dot_general(v, u, (((0,), (0,)), ((), ())), preferred_element_type=F32)
        inv = lax.rsqrt(dist)
        f = inv * inv * inv
        high = f.astype(BF16)
        low = (f - high.astype(F32)).astype(BF16)
        o = jnp.dot(g, jnp.concatenate([high, low], axis=1), preferred_element_type=F32)
        o = o[:, :PL] + o[:, PL:]
        a = o[0:4] + o[4:8] + o[8:12]
        out_ref[tab[5, e] - row_base] = jnp.where(lane4 < tab[4, e], a - t * a[3:4], 0.0)

    sizes = [tab[8 + i, 0] for i in range(4)]

    def run(begin, size, width, step):
        def body(i, _):
            for j in range(step):
                job(begin + jnp.minimum(step * i + j, size - 1), width)

        lax.fori_loop(0, (size + step - 1) // step, body, None)

    def whole_steps(size, step):
        return (size + step - 1) // step * step

    n_full, n_half = sizes[0] + sizes[1], sizes[2] + sizes[3]
    early_full = jnp.minimum(n_full, whole_steps(sizes[0], UNROLL[0]))
    early_half = jnp.minimum(n_half, whole_steps(sizes[2], UNROLL[1]))
    if first:
        run(jnp.int32(0), early_full, 4, UNROLL[0])
        run(n_full, early_half, 2, UNROLL[1])
    else:
        run(early_full, n_full - early_full, 4, UNROLL_OWN[0])
        run(n_full + early_half, n_half - early_half, 2, UNROLL_OWN[1])
    if first:
        outs[-1][...] = out_ref[(NY - 1) * NB : NY * NB]
        outs = outs[:-1]
    for i, o in enumerate(outs):
        for c in range(3):
            o[c] = out_ref[i * NB : (i + 1) * NB, c, :]


def final_kernel(cnt_ref, far_ref, p0, p1, p2, p3, out_ref):
    live = lax.broadcasted_iota(I32, (NB, PL), 1) < column_of(cnt_ref[...], NB)
    for c in range(3):
        near = (p0[c] + p1[c]) + (p2[c] + p3[c])
        out_ref[c] = jnp.where(live, far_ref[c] + near, 0.0)


def along_y(k):
    return [(NZ * y + z, NZ * ((y + k) % NY) + z) for y in range(NY) for z in range(NZ)]


def along_x(k):
    return [(2 * x + c, 2 * ((x + k) % NX) + c) for x in range(NX) for c in range(2)]


def call(kernel, outs, in_specs, out_specs, name, mib, scratch=()):
    return pl.pallas_call(
        kernel,
        out_shape=[jax.ShapeDtypeStruct(shape, dtype) for shape, dtype in outs],
        in_specs=in_specs,
        out_specs=out_specs,
        scratch_shapes=scratch,
        compiler_params=pltpu.CompilerParams(vmem_limit_bytes=mib * MIB),
        name=name,
    )


def per_device(positions, masses, counts, dest_ids, near_list, cell_list, cell_centers, cell_mass):
    pos = jnp.transpose(positions[0], (1, 0, 2))
    cnt = counts[0]
    src, tgt, cells = call(
        pack_kernel,
        (((NZ, TILES + 1, 4, PL), F32), ((NB + 1, 4, PL), F32), ((16, 4, PL), F32)),
        [pl.BlockSpec(memory_space=pltpu.HBM)] * 7,
        [vspec()] * 3,
        "pack",
        8,
        [
            pltpu.VMEM((3, NB, PL), F32),
            pltpu.VMEM((NB, PL), F32),
            pltpu.VMEM((1, NB), I32),
            pltpu.VMEM((1, NB), I32),
            pltpu.VMEM((K, NB), I32),
            pltpu.VMEM((3, 2048), F32),
            pltpu.VMEM((1, 2048), F32),
            pltpu.SMEM((1, NB), I32),
            pltpu.VMEM((NB, 8, PL), F32),
            pltpu.SemaphoreType.DMA((8,)),
        ],
    )(
        *[
            pltpu.with_memory_space_constraint(v, pltpu.HBM)
            for v in (pos, masses[0], cnt, dest_ids, near_list[0].T, cell_centers, cell_mass[None])
        ]
    )
    z_rows = [[NZ * y + NZ - 1 - z for z in range(NZ)] for y in range(NY)]
    window = lax.all_to_all(src, "space", 0, 0, axis_index_groups=z_rows, tiled=True)
    tgts = [tgt] + [lax.ppermute(tgt, "space", along_y(k)) for k in (1, -1)]
    tgts.append(lax.ppermute(tgts[1], "space", along_y(1)))
    pair = jnp.stack([cells, lax.ppermute(cells, "slab", [(i, i ^ 1) for i in range(2 * NX)])])
    pairs = [pair] + [lax.ppermute(pair, "slab", along_x(k)) for k in (1, -1)]
    pairs.append(lax.ppermute(pairs[1], "slab", along_x(1)))
    me = (lax.axis_index("space") // NZ).astype(I32).reshape(1)
    place = lax.axis_index("slab").astype(I32).reshape(1)
    tall, tab = call(
        prep_kernel,
        (((NY * NB, 4, PL), F32), ((16, 2 * PL), I32)),
        [sspec()] + [vspec()] * 4,
        [vspec(), vspec()],
        "prep",
        8,
    )(me, *tgts)
    (far,) = call(
        far_kernel,
        (((3, NB, PL), F32),),
        [sspec()] + [pl.BlockSpec(memory_space=pltpu.HBM)] * 3 + [vspec()] * 4,
        [vspec()],
        "far",
        16,
        [
            pltpu.VMEM((PL, PL), F32),
            pltpu.VMEM((3, NB, PL), F32),
            pltpu.VMEM((1, NB), I32),
            pltpu.VMEM((LC, NB), I32),
            pltpu.SemaphoreType.DMA((3,)),
        ],
    )(place, *[pltpu.with_memory_space_constraint(v, pltpu.HBM) for v in (pos, cnt, cell_list[0].T)], *pairs)
    tall, tab, far = lax.optimization_barrier((tall, tab, far))
    window = window.reshape(NZ * (TILES + 1), 4, PL)

    def near(first, *arrays):
        partial = ((3, NB, PL), F32)
        kept = ((NB, 4, PL), F32)
        outs = (partial,) * (NY - 1) + (kept,) if first else (partial,)
        return call(
            functools.partial(near_kernel, first),
            outs,
            [vspec()] * len(arrays),
            [vspec()] * len(outs),
            "near",
            32,
            [
                pltpu.VMEM(((NY if first else 1) * NB, 4, PL), F32),
                pltpu.VMEM((NZ, PL), I32),
                pltpu.SMEM((NZ, PL), I32),
                pltpu.SMEM((16, 2 * PL), I32),
                pltpu.SemaphoreType.DMA((2,)),
            ],
        )(*arrays)

    *sent, kept = near(True, tab, tall, window)
    back = [lax.ppermute(sent[i], "space", along_y(-k)) for i, k in ((2, 2), (0, 1), (1, -1))]
    (own,) = near(False, tab, tall, window, kept)
    (out,) = call(
        final_kernel,
        (((3, NB, PL), F32),),
        [vspec()] * 6,
        [vspec()],
        "final",
        8,
    )(cnt, far, own, *back)
    return jnp.transpose(out, (1, 0, 2))[None]


def solution(mesh):
    in_specs = (
        P("slab", "space", None, None),
        P("slab", "space", None),
        P("slab", "space", None),
        P("slab", "space"),
        P("slab", "space", None),
        P("slab", "space", None),
        P(None, "slab"),
        P("slab"),
    )
    return jax.shard_map(
        per_device,
        mesh=mesh,
        in_specs=in_specs,
        out_specs=P("slab", "space", None, None),
        check_vma=False,
    )
```

```python
import functools

import jax
import jax.numpy as jnp
from jax import lax
from jax.experimental import pallas as pl
from jax.experimental.pallas import tpu as pltpu
from jax.sharding import PartitionSpec as P

NB = 48
PL = 128
K = 4
LC = 32
NY = 4
NZ = 8
NX = 4
SOFT = 0.01
UNROLL = (18, 20)
UNROLL_OWN = (12, 8)
MIB = 1 << 20
TILES = 36
F32 = jnp.float32
I32 = jnp.int32
BF16 = jnp.bfloat16
VMEM = pltpu.VMEM
SMEM = pltpu.SMEM


def vspec():
    return pl.BlockSpec(memory_space=VMEM)


def sspec():
    return pl.BlockSpec(memory_space=SMEM)


def column_of(row, n):
    square = jnp.broadcast_to(row, (n, n))
    diag = lax.broadcasted_iota(I32, (n, n), 0) == lax.broadcasted_iota(I32, (n, n), 1)
    return jnp.sum(jnp.where(diag, square, jnp.zeros_like(square)), axis=1, keepdims=True)


def pack_kernel(*refs):
    ins, (src_ref, tgt_ref, cell_ref), holds = refs[:7], refs[7:10], refs[10:18]
    full, sem = refs[18:]
    copies = [pltpu.make_async_copy(ins[i], holds[i], sem.at[i]) for i in range(7)]
    copies.append(pltpu.make_async_copy(ins[2], holds[7], sem.at[7]))
    for copy in copies:
        copy.start()
    for copy in copies:
        copy.wait()
    pos_ref, mass_ref, cnt_ref, dest_ref, near_ref, ctr_ref, cm_ref, cnt_smem = holds
    counts = cnt_ref[...]
    cnt = column_of(counts, NB)
    near = near_ref[...]
    off = (near >= NB).astype(I32) + (near >= 2 * NB).astype(I32)
    dev = (dest_ref[...] + off - 1) & (NY * NZ - 1)
    code = (dev >> 3) * 512 + ((NZ - 1) - (dev & (NZ - 1))) * 64 + (near - off * NB)
    gap = jnp.zeros((4, 64 - NB), I32)
    info = jnp.concatenate([code, gap, jnp.broadcast_to(counts, (4, NB)), gap], axis=1)
    lane = lax.broadcasted_iota(I32, (NB, PL), 1)
    weight = jnp.where(lane < cnt, mass_ref[...], 0.0)
    for c in range(3):
        value = pos_ref[c]
        tgt_ref[0:NB, c, :] = value
        full[:, c, :] = value
    full[:, 3, :] = weight
    lane4 = lax.broadcasted_iota(I32, (4, PL), 1)
    carry, begin = jnp.zeros((4, PL), F32), jnp.int32(0)
    for b in range(NB):
        shift, tile = begin & (PL - 1), begin >> 7
        turned = pltpu.roll(full[b], shift, 1)[0:4]
        merged = jnp.where(lane4 >= shift, turned, carry)
        src_ref[0, tile] = merged
        begin = begin + cnt_smem[0, b]
        carry = jnp.where((begin >> 7) != tile, turned, merged)
    square = (NB, NB)
    earlier = lax.broadcasted_iota(I32, square, 0) < lax.broadcasted_iota(I32, square, 1)
    starts = jnp.sum(jnp.where(earlier, cnt, 0), axis=0, keepdims=True)
    places = jnp.concatenate([starts, gap[0:1], counts, gap[0:1]], axis=1)
    src_ref[0, TILES] = jnp.broadcast_to(places, (4, PL)).astype(F32)
    for z in range(1, NZ):
        src_ref[z] = src_ref[0]
    tgt_ref[0:NB, 3, :] = jnp.zeros((NB, PL), F32)
    tgt_ref[NB] = info.astype(F32)
    for j in range(16):
        part = slice(j * PL, (j + 1) * PL)
        cell_ref[j, 0:3, :] = ctr_ref[:, part]
        cell_ref[j, 3:4, :] = cm_ref[0:1, part]


def far_kernel(place_ref, pos_ref, cnt_ref, list_ref, c0, c1, c2, c3, out_ref, pad):
    xs, cs = place_ref[0] >> 1, place_ref[0] & 1
    lane = lax.broadcasted_iota(I32, (NB, PL), 1)
    cnt = column_of(cnt_ref[...], NB)
    live = lane < cnt
    total = jnp.maximum(cnt, 1).astype(F32)
    pos = [pos_ref[c] for c in range(3)]
    centre = [jnp.sum(jnp.where(live, v, 0.0), axis=1, keepdims=True) / total for v in pos]
    diag = lax.broadcasted_iota(I32, (NB, PL), 0) == (lane & 63)
    ctr = [jnp.sum(jnp.where(diag, v, 0.0), axis=0, keepdims=True) for v in centre]
    wide = jnp.concatenate([list_ref[...], jnp.zeros((LC, PL - NB), I32)], axis=1)
    twice = wide + pltpu.roll(wide, 64, 1)
    half = lax.broadcasted_iota(I32, (1, PL), 1) < 64
    ids = [jnp.where(half, twice[2 * j : 2 * j + 1], twice[2 * j + 1 : 2 * j + 2]) for j in range(LC // 2)]
    ids = jnp.concatenate(ids, axis=0)
    slab = ids >> 11
    dx = ((slab >> 1) - xs) & (NX - 1)
    order = jnp.where(dx == 3, 1, jnp.where(dx == 0, 0, dx + 1))
    rows = (order * 2 + ((slab & 1) ^ cs)) * 16 + ((ids >> 7) & 15)
    lanes = ids & (PL - 1)
    tables = []
    for c in range(4):
        whole = jnp.concatenate([ref[i, :, c, :] for ref in (c0, c1, c2, c3) for i in range(2)], axis=0)
        whole = whole.T
        high = whole.astype(BF16)
        low = (whole - high.astype(F32)).astype(BF16)
        tables.append(jnp.concatenate([high, low], axis=1))
    tables = jnp.concatenate(tables, axis=0)
    sub = lax.broadcasted_iota(I32, (PL, 2 * PL), 0)
    got = [[] for _ in range(4)]
    for j in range(0, LC // 2, 2):
        r2 = jnp.concatenate([rows[j : j + 1], rows[j + 1 : j + 2]], axis=1)
        l2 = jnp.concatenate([lanes[j : j + 1], lanes[j + 1 : j + 2]], axis=1)
        hot = jnp.where(sub == r2, 1.0, 0.0).astype(BF16)
        hot = jnp.concatenate([hot, hot], axis=0)
        found = jnp.dot(tables, hot, preferred_element_type=F32)
        pick = sub == l2
        for c in range(4):
            value = jnp.sum(jnp.where(pick, found[c * PL : (c + 1) * PL], 0.0), axis=0, keepdims=True)
            got[c] += [value[:, :PL], value[:, PL:]]
    cells = [jnp.concatenate(v, axis=0) for v in got]
    rel = [ctr[c] - cells[c] for c in range(3)]
    dist = rel[0] * rel[0] + rel[1] * rel[1] + rel[2] * rel[2] + 1.0
    inv = lax.rsqrt(dist)
    cube = cells[3] * (inv * inv * inv)
    fifth = 3.0 * cube * (inv * inv)
    terms = [-(cube * rel[c]) for c in range(3)]
    for a, b in ((0, 0), (1, 1), (2, 2), (0, 1), (0, 2), (1, 2)):
        value = fifth * rel[a] * rel[b]
        if a == b:
            value = value - cube
        terms.append(value)
    terms = [jnp.sum(v, axis=0, keepdims=True) for v in terms]
    pad[...] = jnp.zeros((PL, PL), F32)
    for i, v in enumerate(terms):
        pad[i : i + 1, :] = v + pltpu.roll(v, 64, 1)
    back = pad[...].T
    field = [back[0:NB, i : i + 1] for i in range(3)]
    tide = [back[0:NB, 3 + i : 4 + i] for i in range(6)]
    offset = [pos[c] - centre[c] for c in range(3)]
    for c, (i, j, k) in enumerate(((0, 3, 4), (3, 1, 5), (4, 5, 2))):
        out_ref[c] = field[c] + tide[i] * offset[0] + tide[j] * offset[1] + tide[k] * offset[2]


def split3(v):
    high = v.astype(BF16).astype(F32)
    rest = v - high
    mid = rest.astype(BF16).astype(F32)
    return high, mid, rest - mid


def prep_kernel(y_ref, t0, t1, t2, t3, tall, tab):
    me = y_ref[0]
    wide = 2 * PL
    tiles = []
    for i, t in enumerate((t0, t1, t2, t3)):
        tall[i * NB : (i + 1) * NB] = t[0:NB]
        tiles.append(t[NB])
    left = lax.broadcasted_iota(I32, (4, PL), 1) < 64
    code, cnt = [], []
    for a, b in ((tiles[0], tiles[1]), (tiles[2], tiles[3])):
        code.append(jnp.where(left, a, pltpu.roll(b, 64, 1)))
        cnt.append(jnp.where(left, pltpu.roll(a, 64, 1), b))
    code = jnp.concatenate(code, axis=1).astype(I32)
    cnt = jnp.concatenate(cnt, axis=1)[0:1]
    lane = lax.broadcasted_iota(I32, (1, wide), 1)
    valid = (lane & 63) < NB
    flag = [jnp.where(((code[k : k + 1] >> 9) == me) & valid, 1.0, 0.0) for k in range(K)]
    local = [(code[k : k + 1] & 511).astype(F32) for k in range(K)]
    count = (flag[0] + flag[1]) + (flag[2] + flag[3])
    full = jnp.where(count > 2.5, 1.0, 0.0)
    half = jnp.where((count > 0.5) & (count < 2.5), 1.0, 0.0)
    group = lane >> 6
    mine = group == 0
    lists = [jnp.where(m, v, 0.0) for v in (full, half) for m in (~mine, mine)]
    marks = jnp.concatenate(lists + [jnp.zeros((12, wide), F32)], axis=0).astype(BF16)
    a = lax.broadcasted_iota(I32, (wide, wide), 0)
    b = lax.broadcasted_iota(I32, (wide, wide), 1)
    before = jnp.dot(marks, jnp.where(a < b, 1.0, 0.0).astype(BF16), preferred_element_type=F32)
    sizes = [jnp.sum(v, axis=1, keepdims=True) for v in lists]
    place, begin = jnp.full((1, wide), -1.0, F32), jnp.zeros((1, 1), F32)
    for i, v in enumerate(lists):
        place = jnp.where(v > 0.5, begin + before[i : i + 1], place)
        begin = begin + sizes[i]
    moved = jnp.where(a == place.astype(I32), 1.0, 0.0).astype(BF16)
    bucket = lane & 63
    home = ((group - 1) & (NY - 1)) * NB + bucket
    slot, ins, outs = [], jnp.zeros((1, wide), F32), jnp.zeros((1, wide), F32)
    for k in range(K):
        slot.append(jnp.where(flag[k] > 0.5, ins, count + outs))
        ins, outs = ins + flag[k], outs + (1.0 - flag[k])
    fields = []
    for j in range(K):
        pick = jnp.zeros((1, wide), F32)
        for k in range(K):
            pick = pick + jnp.where(slot[k] == float(j), local[k], 0.0)
        fields.append(pick)
    fields += [cnt, home.astype(F32), count, (group * NB + bucket).astype(F32)]
    load = jnp.concatenate(fields, axis=0)
    high = load.astype(BF16).astype(F32)
    both = jnp.concatenate([high, load - high], axis=0).astype(BF16)
    out = lax.dot_general(both, moved, (((1,), (1,)), ((), ())), preferred_element_type=F32)
    out = out[0:8] + out[8:16]
    sizes = jnp.concatenate([jnp.broadcast_to(v, (1, wide)) for v in sizes + [begin] * 4], axis=0)
    tab[...] = jnp.concatenate([out, sizes], axis=0).astype(I32)


def near_kernel(first, *refs):
    (table, tall, src_ref), refs = refs[:3], refs[3:]
    outs, (out_ref, hold, spots, tab, sem) = refs[:-5], refs[-5:]
    if not first:
        kept, outs = outs[0], outs[1:]
    copies = [pltpu.make_async_copy(table, tab, sem.at[0]), pltpu.make_async_copy(hold, spots, sem.at[1])]
    copies[0].start()
    for z in range(NZ):
        hold[z : z + 1, :] = src_ref[z * (TILES + 1) + TILES][0:1].astype(I32)
    copies[1].start()
    out_ref[...] = jnp.zeros(out_ref.shape, F32) if first else kept[...]
    for copy in copies:
        copy.wait()
    lane1 = lax.broadcasted_iota(I32, (1, PL), 1)
    sub4 = lax.broadcasted_iota(I32, (4, PL), 0)
    lane4 = lax.broadcasted_iota(I32, (4, PL), 1)
    spatial = sub4 < 3
    one = jnp.ones((4, PL), F32)
    zero4 = jnp.zeros((4, PL), F32)
    zero8 = jnp.zeros((8, PL), F32)

    def square(v):
        return jnp.sum(jnp.where(spatial, v * v, 0.0), axis=0, keepdims=True)

    def mix(a, b):
        return jnp.where(spatial, a, b)

    def stack(*v):
        return jnp.concatenate(v, axis=0).astype(BF16)

    row_base = 0 if first else (NY - 1) * NB

    def job(e, width):
        n = tab[6, e]
        t = tall[tab[7, e]]
        th, tm, tl = split3(t)
        qh, qm, ql = split3(square(t))
        u = stack(mix(th, one), mix(th, one), mix(tm, one), mix(tm, qh), mix(th, qm), mix(tl, ql), zero8)
        vs, gs = [], []
        for k in range(width):
            z, bucket = tab[k, e] >> 6, tab[k, e] & 63
            begin = spots[z, bucket]
            shift = begin & (PL - 1)
            tile = z * (TILES + 1) + (begin >> 7)
            s = jnp.concatenate([src_ref[tile], src_ref[tile + 1]], axis=0)
            s = pltpu.roll(s, (PL - shift) & (PL - 1), 1)
            s = jnp.where(lane4 < PL - shift, s[0:4], s[4:8])
            live = jnp.where(k < n, spots[z, 64 + bucket], 0)
            sh, sm, sl = split3(-2.0 * s)
            qh, qm, ql = split3(square(s) + SOFT)
            vs.append(stack(mix(sh, qh), mix(sm, qm), mix(sh, ql), mix(sm, one), mix(sl, one), mix(sh, one), zero8))
            w = jnp.where(lane1 < live, s[3:4], 0.0)
            gs.append(stack(*split3(mix(s * w, w)), zero4))
        v = jnp.concatenate(vs, axis=1)
        g = jnp.concatenate(gs, axis=1)
        dist = lax.dot_general(v, u, (((0,), (0,)), ((), ())), preferred_element_type=F32)
        inv = lax.rsqrt(dist)
        f = inv * inv * inv
        high = f.astype(BF16)
        low = (f - high.astype(F32)).astype(BF16)
        o = jnp.dot(g, jnp.concatenate([high, low], axis=1), preferred_element_type=F32)
        o = o[:, :PL] + o[:, PL:]
        a = o[0:4] + o[4:8] + o[8:12]
        out_ref[tab[5, e] - row_base] = jnp.where(lane4 < tab[4, e], a - t * a[3:4], 0.0)

    sizes = [tab[8 + i, 0] for i in range(4)]

    def run(begin, size, width, step):
        def body(i, _):
            for j in range(step):
                job(begin + jnp.minimum(step * i + j, size - 1), width)

        lax.fori_loop(0, (size + step - 1) // step, body, None)

    def whole_steps(size, step):
        return (size + step - 1) // step * step

    n_full, n_half = sizes[0] + sizes[1], sizes[2] + sizes[3]
    early_full = jnp.minimum(n_full, whole_steps(sizes[0], UNROLL[0]))
    early_half = jnp.minimum(n_half, whole_steps(sizes[2], UNROLL[1]))
    if first:
        run(jnp.int32(0), early_full, 4, UNROLL[0])
        run(n_full, early_half, 2, UNROLL[1])
    else:
        run(early_full, n_full - early_full, 4, UNROLL_OWN[0])
        run(n_full + early_half, n_half - early_half, 2, UNROLL_OWN[1])
    if first:
        outs[-1][...] = out_ref[(NY - 1) * NB : NY * NB]
        outs = outs[:-1]
    for i, o in enumerate(outs):
        for c in range(3):
            o[c] = out_ref[i * NB : (i + 1) * NB, c, :]


def final_kernel(cnt_ref, far_ref, p0, p1, p2, p3, out_ref):
    live = lax.broadcasted_iota(I32, (NB, PL), 1) < column_of(cnt_ref[...], NB)
    for c in range(3):
        near = (p0[c] + p1[c]) + (p2[c] + p3[c])
        out_ref[c] = jnp.where(live, far_ref[c] + near, 0.0)


def along_y(k):
    return [(NZ * y + z, NZ * ((y + k) % NY) + z) for y in range(NY) for z in range(NZ)]


def along_x(k):
    return [(2 * x + c, 2 * ((x + k) % NX) + c) for x in range(NX) for c in range(2)]


def call(kernel, outs, in_specs, out_specs, name, mib, scratch=()):
    return pl.pallas_call(
        kernel,
        out_shape=[jax.ShapeDtypeStruct(shape, dtype) for shape, dtype in outs],
        in_specs=in_specs,
        out_specs=out_specs,
        scratch_shapes=scratch,
        compiler_params=pltpu.CompilerParams(vmem_limit_bytes=mib * MIB),
        name=name,
    )


def per_device(positions, masses, counts, dest_ids, near_list, cell_list, cell_centers, cell_mass):
    pos = jnp.transpose(positions[0], (1, 0, 2))
    cnt = counts[0]
    src, tgt, cells = call(
        pack_kernel,
        (((NZ, TILES + 1, 4, PL), F32), ((NB + 1, 4, PL), F32), ((16, 4, PL), F32)),
        [pl.BlockSpec(memory_space=pltpu.HBM)] * 7,
        [vspec()] * 3,
        "pack",
        8,
        [
            pltpu.VMEM((3, NB, PL), F32),
            pltpu.VMEM((NB, PL), F32),
            pltpu.VMEM((1, NB), I32),
            pltpu.VMEM((1, NB), I32),
            pltpu.VMEM((K, NB), I32),
            pltpu.VMEM((3, 2048), F32),
            pltpu.VMEM((1, 2048), F32),
            pltpu.SMEM((1, NB), I32),
            pltpu.VMEM((NB, 8, PL), F32),
            pltpu.SemaphoreType.DMA((8,)),
        ],
    )(
        *[
            pltpu.with_memory_space_constraint(v, pltpu.HBM)
            for v in (pos, masses[0], cnt, dest_ids, near_list[0].T, cell_centers, cell_mass[None])
        ]
    )
    z_rows = [[NZ * y + NZ - 1 - z for z in range(NZ)] for y in range(NY)]
    window = lax.all_to_all(src, "space", 0, 0, axis_index_groups=z_rows, tiled=True)
    tgts = [tgt] + [lax.ppermute(tgt, "space", along_y(k)) for k in (1, -1)]
    tgts.append(lax.ppermute(tgts[1], "space", along_y(1)))
    pair = jnp.stack([cells, lax.ppermute(cells, "slab", [(i, i ^ 1) for i in range(2 * NX)])])
    first = lax.ppermute(pair, "slab", along_x(1))
    pair, first = lax.optimization_barrier((pair, first))
    third = lax.ppermute(first, "slab", along_x(1))
    pairs = [pair, first, lax.ppermute(pair, "slab", along_x(-1)), third]
    me = (lax.axis_index("space") // NZ).astype(I32).reshape(1)
    place = lax.axis_index("slab").astype(I32).reshape(1)
    tall, tab = call(
        prep_kernel,
        (((NY * NB, 4, PL), F32), ((16, 2 * PL), I32)),
        [sspec()] + [vspec()] * 4,
        [vspec(), vspec()],
        "prep",
        8,
    )(me, *tgts)
    (far,) = call(
        far_kernel,
        (((3, NB, PL), F32),),
        [sspec()] + [vspec()] * 7,
        [vspec()],
        "far",
        16,
        [pltpu.VMEM((PL, PL), F32)],
    )(place, pos, cnt, cell_list[0].T, *pairs)
    tall, tab, far = lax.optimization_barrier((tall, tab, far))
    window = window.reshape(NZ * (TILES + 1), 4, PL)

    def near(first, *arrays):
        partial = ((3, NB, PL), F32)
        kept = ((NB, 4, PL), F32)
        outs = (partial,) * (NY - 1) + (kept,) if first else (partial,)
        return call(
            functools.partial(near_kernel, first),
            outs,
            [vspec()] * len(arrays),
            [vspec()] * len(outs),
            "near",
            32,
            [
                pltpu.VMEM(((NY if first else 1) * NB, 4, PL), F32),
                pltpu.VMEM((NZ, PL), I32),
                pltpu.SMEM((NZ, PL), I32),
                pltpu.SMEM((16, 2 * PL), I32),
                pltpu.SemaphoreType.DMA((2,)),
            ],
        )(*arrays)

    *sent, kept = near(True, tab, tall, window)
    back = [lax.ppermute(sent[i], "space", along_y(-k)) for i, k in ((2, 2), (0, 1), (1, -1))]
    (own,) = near(False, tab, tall, window, kept)
    (out,) = call(
        final_kernel,
        (((3, NB, PL), F32),),
        [vspec()] * 6,
        [vspec()],
        "final",
        8,
    )(cnt, far, own, *back)
    return jnp.transpose(out, (1, 0, 2))[None]


def solution(mesh):
    in_specs = (
        P("slab", "space", None, None),
        P("slab", "space", None),
        P("slab", "space", None),
        P("slab", "space"),
        P("slab", "space", None),
        P("slab", "space", None),
        P(None, "slab"),
        P("slab"),
    )
    return jax.shard_map(
        per_device,
        mesh=mesh,
        in_specs=in_specs,
        out_specs=P("slab", "space", None, None),
        check_vma=False,
    )
```

```python
import functools

import jax
import jax.numpy as jnp
from jax import lax
from jax.experimental import pallas as pl
from jax.experimental.pallas import tpu as pltpu
from jax.sharding import PartitionSpec as P

NB = 48
PL = 128
K = 4
LC = 32
NY = 4
NZ = 8
NX = 4
SOFT = 0.01
UNROLL = (18, 20)
UNROLL_OWN = (12, 8)
MIB = 1 << 20
TILES = 36
F32 = jnp.float32
I32 = jnp.int32
BF16 = jnp.bfloat16
VMEM = pltpu.VMEM
SMEM = pltpu.SMEM


def vspec():
    return pl.BlockSpec(memory_space=VMEM)


def sspec():
    return pl.BlockSpec(memory_space=SMEM)


def column_of(row, n):
    square = jnp.broadcast_to(row, (n, n))
    diag = lax.broadcasted_iota(I32, (n, n), 0) == lax.broadcasted_iota(I32, (n, n), 1)
    return jnp.sum(jnp.where(diag, square, jnp.zeros_like(square)), axis=1, keepdims=True)


def pack_kernel(*refs):
    ins, (src_ref, tgt_ref, cell_ref), holds = refs[:7], refs[7:10], refs[10:18]
    full, sem = refs[18:]
    copies = [pltpu.make_async_copy(ins[i], holds[i], sem.at[i]) for i in range(7)]
    copies.append(pltpu.make_async_copy(ins[2], holds[7], sem.at[7]))
    for copy in copies:
        copy.start()
    for copy in copies:
        copy.wait()
    pos_ref, mass_ref, cnt_ref, dest_ref, near_ref, ctr_ref, cm_ref, cnt_smem = holds
    counts = cnt_ref[...]
    cnt = column_of(counts, NB)
    near = near_ref[...]
    off = (near >= NB).astype(I32) + (near >= 2 * NB).astype(I32)
    dev = (dest_ref[...] + off - 1) & (NY * NZ - 1)
    code = (dev >> 3) * 512 + ((NZ - 1) - (dev & (NZ - 1))) * 64 + (near - off * NB)
    gap = jnp.zeros((4, 64 - NB), I32)
    info = jnp.concatenate([code, gap, jnp.broadcast_to(counts, (4, NB)), gap], axis=1)
    lane = lax.broadcasted_iota(I32, (NB, PL), 1)
    weight = jnp.where(lane < cnt, mass_ref[...], 0.0)
    for c in range(3):
        value = pos_ref[c]
        tgt_ref[0:NB, c, :] = value
        full[:, c, :] = value
    full[:, 3, :] = weight
    lane4 = lax.broadcasted_iota(I32, (4, PL), 1)
    carry, begin = jnp.zeros((4, PL), F32), jnp.int32(0)
    for b in range(NB):
        shift, tile = begin & (PL - 1), begin >> 7
        turned = pltpu.roll(full[b], shift, 1)[0:4]
        merged = jnp.where(lane4 >= shift, turned, carry)
        src_ref[0, tile] = merged
        begin = begin + cnt_smem[0, b]
        carry = jnp.where((begin >> 7) != tile, turned, merged)
    square = (NB, NB)
    earlier = lax.broadcasted_iota(I32, square, 0) < lax.broadcasted_iota(I32, square, 1)
    starts = jnp.sum(jnp.where(earlier, cnt, 0), axis=0, keepdims=True)
    places = jnp.concatenate([starts, gap[0:1], counts, gap[0:1]], axis=1)
    src_ref[0, TILES] = jnp.broadcast_to(places, (4, PL)).astype(F32)
    for z in range(1, NZ):
        src_ref[z] = src_ref[0]
    tgt_ref[0:NB, 3, :] = jnp.zeros((NB, PL), F32)
    tgt_ref[NB] = info.astype(F32)
    for j in range(16):
        part = slice(j * PL, (j + 1) * PL)
        cell_ref[j, 0:3, :] = ctr_ref[:, part]
        cell_ref[j, 3:4, :] = cm_ref[0:1, part]


def far_kernel(place_ref, pos_ref, cnt_ref, list_ref, c0, c1, c2, c3, out_ref, pad):
    xs, cs = place_ref[0] >> 1, place_ref[0] & 1
    lane = lax.broadcasted_iota(I32, (NB, PL), 1)
    cnt = column_of(cnt_ref[...], NB)
    live = lane < cnt
    total = jnp.maximum(cnt, 1).astype(F32)
    pos = [pos_ref[c] for c in range(3)]
    centre = [jnp.sum(jnp.where(live, v, 0.0), axis=1, keepdims=True) / total for v in pos]
    diag = lax.broadcasted_iota(I32, (NB, PL), 0) == (lane & 63)
    ctr = [jnp.sum(jnp.where(diag, v, 0.0), axis=0, keepdims=True) for v in centre]
    wide = jnp.concatenate([list_ref[...], jnp.zeros((LC, PL - NB), I32)], axis=1)
    twice = wide + pltpu.roll(wide, 64, 1)
    half = lax.broadcasted_iota(I32, (1, PL), 1) < 64
    ids = [jnp.where(half, twice[2 * j : 2 * j + 1], twice[2 * j + 1 : 2 * j + 2]) for j in range(LC // 2)]
    ids = jnp.concatenate(ids, axis=0)
    slab = ids >> 11
    dx = ((slab >> 1) - xs) & (NX - 1)
    order = jnp.where(dx == 3, 1, jnp.where(dx == 0, 0, dx + 1))
    rows = (order * 2 + ((slab & 1) ^ cs)) * 16 + ((ids >> 7) & 15)
    lanes = ids & (PL - 1)
    tables = []
    for c in range(4):
        whole = jnp.concatenate([ref[i, :, c, :] for ref in (c0, c1, c2, c3) for i in range(2)], axis=0)
        whole = whole.T
        high = whole.astype(BF16)
        low = (whole - high.astype(F32)).astype(BF16)
        tables.append(jnp.concatenate([high, low], axis=1))
    tables = jnp.concatenate(tables, axis=0)
    sub = lax.broadcasted_iota(I32, (PL, 2 * PL), 0)
    got = [[] for _ in range(4)]
    for j in range(0, LC // 2, 2):
        r2 = jnp.concatenate([rows[j : j + 1], rows[j + 1 : j + 2]], axis=1)
        l2 = jnp.concatenate([lanes[j : j + 1], lanes[j + 1 : j + 2]], axis=1)
        hot = jnp.where(sub == r2, 1.0, 0.0).astype(BF16)
        hot = jnp.concatenate([hot, hot], axis=0)
        found = jnp.dot(tables, hot, preferred_element_type=F32)
        pick = sub == l2
        for c in range(4):
            value = jnp.sum(jnp.where(pick, found[c * PL : (c + 1) * PL], 0.0), axis=0, keepdims=True)
            got[c] += [value[:, :PL], value[:, PL:]]
    cells = [jnp.concatenate(v, axis=0) for v in got]
    rel = [ctr[c] - cells[c] for c in range(3)]
    dist = rel[0] * rel[0] + rel[1] * rel[1] + rel[2] * rel[2] + 1.0
    inv = lax.rsqrt(dist)
    cube = cells[3] * (inv * inv * inv)
    fifth = 3.0 * cube * (inv * inv)
    terms = [-(cube * rel[c]) for c in range(3)]
    for a, b in ((0, 0), (1, 1), (2, 2), (0, 1), (0, 2), (1, 2)):
        value = fifth * rel[a] * rel[b]
        if a == b:
            value = value - cube
        terms.append(value)
    terms = [jnp.sum(v, axis=0, keepdims=True) for v in terms]
    pad[...] = jnp.zeros((PL, PL), F32)
    for i, v in enumerate(terms):
        pad[i : i + 1, :] = v + pltpu.roll(v, 64, 1)
    back = pad[...].T
    field = [back[0:NB, i : i + 1] for i in range(3)]
    tide = [back[0:NB, 3 + i : 4 + i] for i in range(6)]
    offset = [pos[c] - centre[c] for c in range(3)]
    for c, (i, j, k) in enumerate(((0, 3, 4), (3, 1, 5), (4, 5, 2))):
        out_ref[c] = field[c] + tide[i] * offset[0] + tide[j] * offset[1] + tide[k] * offset[2]


def split3(v):
    high = v.astype(BF16).astype(F32)
    rest = v - high
    mid = rest.astype(BF16).astype(F32)
    return high, mid, rest - mid


def prep_kernel(y_ref, t0, t1, t2, t3, tall, tab):
    me = y_ref[0]
    wide = 2 * PL
    tiles = []
    for i, t in enumerate((t0, t1, t2, t3)):
        tall[i * NB : (i + 1) * NB] = t[0:NB]
        tiles.append(t[NB])
    left = lax.broadcasted_iota(I32, (4, PL), 1) < 64
    code, cnt = [], []
    for a, b in ((tiles[0], tiles[1]), (tiles[2], tiles[3])):
        code.append(jnp.where(left, a, pltpu.roll(b, 64, 1)))
        cnt.append(jnp.where(left, pltpu.roll(a, 64, 1), b))
    code = jnp.concatenate(code, axis=1).astype(I32)
    cnt = jnp.concatenate(cnt, axis=1)[0:1]
    lane = lax.broadcasted_iota(I32, (1, wide), 1)
    valid = (lane & 63) < NB
    flag = [jnp.where(((code[k : k + 1] >> 9) == me) & valid, 1.0, 0.0) for k in range(K)]
    local = [(code[k : k + 1] & 511).astype(F32) for k in range(K)]
    count = (flag[0] + flag[1]) + (flag[2] + flag[3])
    full = jnp.where(count > 2.5, 1.0, 0.0)
    half = jnp.where((count > 0.5) & (count < 2.5), 1.0, 0.0)
    group = lane >> 6
    mine = group == 0
    lists = [jnp.where(m, v, 0.0) for v in (full, half) for m in (~mine, mine)]
    marks = jnp.concatenate(lists + [jnp.zeros((12, wide), F32)], axis=0).astype(BF16)
    a = lax.broadcasted_iota(I32, (wide, wide), 0)
    b = lax.broadcasted_iota(I32, (wide, wide), 1)
    before = jnp.dot(marks, jnp.where(a < b, 1.0, 0.0).astype(BF16), preferred_element_type=F32)
    sizes = [jnp.sum(v, axis=1, keepdims=True) for v in lists]
    place, begin = jnp.full((1, wide), -1.0, F32), jnp.zeros((1, 1), F32)
    for i, v in enumerate(lists):
        place = jnp.where(v > 0.5, begin + before[i : i + 1], place)
        begin = begin + sizes[i]
    moved = jnp.where(a == place.astype(I32), 1.0, 0.0).astype(BF16)
    bucket = lane & 63
    home = ((group - 1) & (NY - 1)) * NB + bucket
    slot, ins, outs = [], jnp.zeros((1, wide), F32), jnp.zeros((1, wide), F32)
    for k in range(K):
        slot.append(jnp.where(flag[k] > 0.5, ins, count + outs))
        ins, outs = ins + flag[k], outs + (1.0 - flag[k])
    fields = []
    for j in range(K):
        pick = jnp.zeros((1, wide), F32)
        for k in range(K):
            pick = pick + jnp.where(slot[k] == float(j), local[k], 0.0)
        fields.append(pick)
    fields += [cnt, home.astype(F32), count, (group * NB + bucket).astype(F32)]
    load = jnp.concatenate(fields, axis=0)
    high = load.astype(BF16).astype(F32)
    both = jnp.concatenate([high, load - high], axis=0).astype(BF16)
    out = lax.dot_general(both, moved, (((1,), (1,)), ((), ())), preferred_element_type=F32)
    out = out[0:8] + out[8:16]
    sizes = jnp.concatenate([jnp.broadcast_to(v, (1, wide)) for v in sizes + [begin] * 4], axis=0)
    tab[...] = jnp.concatenate([out, sizes], axis=0).astype(I32)


def near_kernel(first, *refs):
    (table, tall, src_ref), refs = refs[:3], refs[3:]
    outs, (out_ref, hold, spots, tab, sem) = refs[:-5], refs[-5:]
    if not first:
        kept, outs = outs[0], outs[1:]
    copies = [pltpu.make_async_copy(table, tab, sem.at[0]), pltpu.make_async_copy(hold, spots, sem.at[1])]
    copies[0].start()
    for z in range(NZ):
        hold[z : z + 1, :] = src_ref[z * (TILES + 1) + TILES][0:1].astype(I32)
    copies[1].start()
    out_ref[...] = jnp.zeros(out_ref.shape, F32) if first else kept[...]
    for copy in copies:
        copy.wait()
    lane1 = lax.broadcasted_iota(I32, (1, PL), 1)
    sub4 = lax.broadcasted_iota(I32, (4, PL), 0)
    lane4 = lax.broadcasted_iota(I32, (4, PL), 1)
    spatial = sub4 < 3
    one = jnp.ones((4, PL), F32)
    zero4 = jnp.zeros((4, PL), F32)
    zero8 = jnp.zeros((8, PL), F32)

    def square(v):
        return jnp.sum(jnp.where(spatial, v * v, 0.0), axis=0, keepdims=True)

    def mix(a, b):
        return jnp.where(spatial, a, b)

    def stack(*v):
        return jnp.concatenate(v, axis=0).astype(BF16)

    row_base = 0 if first else (NY - 1) * NB

    def job(e, width):
        n = tab[6, e]
        t = tall[tab[7, e]]
        th, tm, tl = split3(t)
        qh, qm, ql = split3(square(t))
        u = stack(mix(th, one), mix(th, one), mix(tm, one), mix(tm, qh), mix(th, qm), mix(tl, ql), zero8)
        vs, gs = [], []
        for k in range(width):
            z, bucket = tab[k, e] >> 6, tab[k, e] & 63
            begin = spots[z, bucket]
            shift = begin & (PL - 1)
            tile = z * (TILES + 1) + (begin >> 7)
            s = jnp.concatenate([src_ref[tile], src_ref[tile + 1]], axis=0)
            s = pltpu.roll(s, (PL - shift) & (PL - 1), 1)
            s = jnp.where(lane4 < PL - shift, s[0:4], s[4:8])
            live = jnp.where(k < n, spots[z, 64 + bucket], 0)
            sh, sm, sl = split3(-2.0 * s)
            qh, qm, ql = split3(square(s) + SOFT)
            vs.append(stack(mix(sh, qh), mix(sm, qm), mix(sh, ql), mix(sm, one), mix(sl, one), mix(sh, one), zero8))
            w = jnp.where(lane1 < live, s[3:4], 0.0)
            gs.append(stack(*split3(mix(s * w, w)), zero4))
        v = jnp.concatenate(vs, axis=1)
        g = jnp.concatenate(gs, axis=1)
        dist = lax.dot_general(v, u, (((0,), (0,)), ((), ())), preferred_element_type=F32)
        inv = lax.rsqrt(dist)
        f = inv * inv * inv
        high = f.astype(BF16)
        low = (f - high.astype(F32)).astype(BF16)
        o = jnp.dot(g, jnp.concatenate([high, low], axis=1), preferred_element_type=F32)
        o = o[:, :PL] + o[:, PL:]
        a = o[0:4] + o[4:8] + o[8:12]
        out_ref[tab[5, e] - row_base] = jnp.where(lane4 < tab[4, e], a - t * a[3:4], 0.0)

    sizes = [tab[8 + i, 0] for i in range(4)]

    def run(begin, size, width, step):
        def body(i, _):
            for j in range(step):
                job(begin + jnp.minimum(step * i + j, size - 1), width)

        lax.fori_loop(0, (size + step - 1) // step, body, None)

    def whole_steps(size, step):
        return (size + step - 1) // step * step

    n_full, n_half = sizes[0] + sizes[1], sizes[2] + sizes[3]
    early_full = jnp.minimum(n_full, whole_steps(sizes[0], UNROLL[0]))
    early_half = jnp.minimum(n_half, whole_steps(sizes[2], UNROLL[1]))
    if first:
        run(jnp.int32(0), early_full, 4, UNROLL[0])
        run(n_full, early_half, 2, UNROLL[1])
    else:
        run(early_full, n_full - early_full, 4, UNROLL_OWN[0])
        run(n_full + early_half, n_half - early_half, 2, UNROLL_OWN[1])
    if first:
        outs[-1][...] = out_ref[(NY - 1) * NB : NY * NB]
        outs = outs[:-1]
    for i, o in enumerate(outs):
        for c in range(3):
            o[c] = out_ref[i * NB : (i + 1) * NB, c, :]


def final_kernel(cnt_ref, far_ref, p0, p1, p2, p3, out_ref):
    live = lax.broadcasted_iota(I32, (NB, PL), 1) < column_of(cnt_ref[...], NB)
    for c in range(3):
        near = (p0[c] + p1[c]) + (p2[c] + p3[c])
        out_ref[c] = jnp.where(live, far_ref[c] + near, 0.0)


def along_y(k):
    return [(NZ * y + z, NZ * ((y + k) % NY) + z) for y in range(NY) for z in range(NZ)]


def along_x(k):
    return [(2 * x + c, 2 * ((x + k) % NX) + c) for x in range(NX) for c in range(2)]


def call(kernel, outs, in_specs, out_specs, name, mib, scratch=()):
    return pl.pallas_call(
        kernel,
        out_shape=[jax.ShapeDtypeStruct(shape, dtype) for shape, dtype in outs],
        in_specs=in_specs,
        out_specs=out_specs,
        scratch_shapes=scratch,
        compiler_params=pltpu.CompilerParams(vmem_limit_bytes=mib * MIB),
        name=name,
    )


def per_device(positions, masses, counts, dest_ids, near_list, cell_list, cell_centers, cell_mass):
    pos = jnp.transpose(positions[0], (1, 0, 2))
    cnt = counts[0]
    src, tgt, cells = call(
        pack_kernel,
        (((NZ, TILES + 1, 4, PL), F32), ((NB + 1, 4, PL), F32), ((16, 4, PL), F32)),
        [pl.BlockSpec(memory_space=pltpu.HBM)] * 7,
        [vspec()] * 3,
        "pack",
        8,
        [
            pltpu.VMEM((3, NB, PL), F32),
            pltpu.VMEM((NB, PL), F32),
            pltpu.VMEM((1, NB), I32),
            pltpu.VMEM((1, NB), I32),
            pltpu.VMEM((K, NB), I32),
            pltpu.VMEM((3, 2048), F32),
            pltpu.VMEM((1, 2048), F32),
            pltpu.SMEM((1, NB), I32),
            pltpu.VMEM((NB, 8, PL), F32),
            pltpu.SemaphoreType.DMA((8,)),
        ],
    )(
        *[
            pltpu.with_memory_space_constraint(v, pltpu.HBM)
            for v in (pos, masses[0], cnt, dest_ids, near_list[0].T, cell_centers, cell_mass[None])
        ]
    )
    z_rows = [[NZ * y + NZ - 1 - z for z in range(NZ)] for y in range(NY)]
    window = lax.all_to_all(src, "space", 0, 0, axis_index_groups=z_rows, tiled=True)
    tgts = [tgt] + [lax.ppermute(tgt, "space", along_y(k)) for k in (1, -1)]
    tgts.append(lax.ppermute(tgts[1], "space", along_y(1)))
    pair = jnp.stack([cells, lax.ppermute(cells, "slab", [(i, i ^ 1) for i in range(2 * NX)])])
    first = lax.ppermute(pair, "slab", along_x(1))
    third = lax.ppermute(first, "slab", along_x(1))
    pair, tgts[2] = lax.optimization_barrier((pair, tgts[2]))
    pairs = [pair, first, lax.ppermute(pair, "slab", along_x(-1)), third]
    me = (lax.axis_index("space") // NZ).astype(I32).reshape(1)
    place = lax.axis_index("slab").astype(I32).reshape(1)
    tall, tab = call(
        prep_kernel,
        (((NY * NB, 4, PL), F32), ((16, 2 * PL), I32)),
        [sspec()] + [vspec()] * 4,
        [vspec(), vspec()],
        "prep",
        8,
    )(me, *tgts)
    (far,) = call(
        far_kernel,
        (((3, NB, PL), F32),),
        [sspec()] + [vspec()] * 7,
        [vspec()],
        "far",
        16,
        [pltpu.VMEM((PL, PL), F32)],
    )(place, pos, cnt, cell_list[0].T, *pairs)
    tall, tab, far = lax.optimization_barrier((tall, tab, far))
    window = window.reshape(NZ * (TILES + 1), 4, PL)

    def near(first, *arrays):
        partial = ((3, NB, PL), F32)
        kept = ((NB, 4, PL), F32)
        outs = (partial,) * (NY - 1) + (kept,) if first else (partial,)
        return call(
            functools.partial(near_kernel, first),
            outs,
            [vspec()] * len(arrays),
            [vspec()] * len(outs),
            "near",
            32,
            [
                pltpu.VMEM(((NY if first else 1) * NB, 4, PL), F32),
                pltpu.VMEM((NZ, PL), I32),
                pltpu.SMEM((NZ, PL), I32),
                pltpu.SMEM((16, 2 * PL), I32),
                pltpu.SemaphoreType.DMA((2,)),
            ],
        )(*arrays)

    *sent, kept = near(True, tab, tall, window)
    back = [lax.ppermute(sent[i], "space", along_y(-k)) for i, k in ((2, 2), (0, 1), (1, -1))]
    (own,) = near(False, tab, tall, window, kept)
    (out,) = call(
        final_kernel,
        (((3, NB, PL), F32),),
        [vspec()] * 6,
        [vspec()],
        "final",
        8,
    )(cnt, far, own, *back)
    return jnp.transpose(out, (1, 0, 2))[None]


def solution(mesh):
    in_specs = (
        P("slab", "space", None, None),
        P("slab", "space", None),
        P("slab", "space", None),
        P("slab", "space"),
        P("slab", "space", None),
        P("slab", "space", None),
        P(None, "slab"),
        P("slab"),
    )
    return jax.shard_map(
        per_device,
        mesh=mesh,
        in_specs=in_specs,
        out_specs=P("slab", "space", None, None),
        check_vma=False,
    )
```

```python
import functools

import jax
import jax.numpy as jnp
from jax import lax
from jax.experimental import pallas as pl
from jax.experimental.pallas import tpu as pltpu
from jax.sharding import PartitionSpec as P

NB = 48
PL = 128
K = 4
LC = 32
NY = 4
NZ = 8
NX = 4
SOFT = 0.01
UNROLL = (18, 20)
UNROLL_OWN = (12, 8)
MIB = 1 << 20
TILES = 36
F32 = jnp.float32
I32 = jnp.int32
BF16 = jnp.bfloat16
VMEM = pltpu.VMEM
SMEM = pltpu.SMEM


def vspec():
    return pl.BlockSpec(memory_space=VMEM)


def sspec():
    return pl.BlockSpec(memory_space=SMEM)


def column_of(row, n):
    square = jnp.broadcast_to(row, (n, n))
    diag = lax.broadcasted_iota(I32, (n, n), 0) == lax.broadcasted_iota(I32, (n, n), 1)
    return jnp.sum(jnp.where(diag, square, jnp.zeros_like(square)), axis=1, keepdims=True)


def pack_kernel(*refs):
    ins, (src_ref, tgt_ref, cell_ref, pos_ref, cnt_ref, list_ref) = refs[:8], refs[8:14]
    mass_ref, dest_ref, near_ref, ctr_ref, cm_ref, cnt_smem, full, sem = refs[14:]
    goals = (pos_ref, mass_ref, cnt_ref, dest_ref, near_ref, ctr_ref, cm_ref, list_ref)
    copies = [pltpu.make_async_copy(ins[i], goals[i], sem.at[i]) for i in range(8)]
    copies.append(pltpu.make_async_copy(ins[2], cnt_smem, sem.at[8]))
    for copy in copies:
        copy.start()
    for copy in copies:
        copy.wait()
    counts = cnt_ref[...]
    cnt = column_of(counts, NB)
    near = near_ref[...]
    off = (near >= NB).astype(I32) + (near >= 2 * NB).astype(I32)
    dev = (dest_ref[...] + off - 1) & (NY * NZ - 1)
    code = (dev >> 3) * 512 + ((NZ - 1) - (dev & (NZ - 1))) * 64 + (near - off * NB)
    gap = jnp.zeros((4, 64 - NB), I32)
    info = jnp.concatenate([code, gap, jnp.broadcast_to(counts, (4, NB)), gap], axis=1)
    lane = lax.broadcasted_iota(I32, (NB, PL), 1)
    weight = jnp.where(lane < cnt, mass_ref[...], 0.0)
    for c in range(3):
        value = pos_ref[c]
        tgt_ref[0:NB, c, :] = value
        full[:, c, :] = value
    full[:, 3, :] = weight
    lane4 = lax.broadcasted_iota(I32, (4, PL), 1)
    carry, begin = jnp.zeros((4, PL), F32), jnp.int32(0)
    for b in range(NB):
        shift, tile = begin & (PL - 1), begin >> 7
        turned = pltpu.roll(full[b], shift, 1)[0:4]
        merged = jnp.where(lane4 >= shift, turned, carry)
        src_ref[0, tile] = merged
        begin = begin + cnt_smem[0, b]
        carry = jnp.where((begin >> 7) != tile, turned, merged)
    square = (NB, NB)
    earlier = lax.broadcasted_iota(I32, square, 0) < lax.broadcasted_iota(I32, square, 1)
    starts = jnp.sum(jnp.where(earlier, cnt, 0), axis=0, keepdims=True)
    places = jnp.concatenate([starts, gap[0:1], counts, gap[0:1]], axis=1)
    src_ref[0, TILES] = jnp.broadcast_to(places, (4, PL)).astype(F32)
    for z in range(1, NZ):
        src_ref[z] = src_ref[0]
    tgt_ref[0:NB, 3, :] = jnp.zeros((NB, PL), F32)
    tgt_ref[NB] = info.astype(F32)
    for j in range(16):
        part = slice(j * PL, (j + 1) * PL)
        cell_ref[j, 0:3, :] = ctr_ref[:, part]
        cell_ref[j, 3:4, :] = cm_ref[0:1, part]


def far_kernel(place_ref, pos_ref, cnt_ref, list_ref, c0, c1, c2, c3, out_ref, pad):
    xs, cs = place_ref[0] >> 1, place_ref[0] & 1
    lane = lax.broadcasted_iota(I32, (NB, PL), 1)
    cnt = column_of(cnt_ref[...], NB)
    live = lane < cnt
    total = jnp.maximum(cnt, 1).astype(F32)
    pos = [pos_ref[c] for c in range(3)]
    centre = [jnp.sum(jnp.where(live, v, 0.0), axis=1, keepdims=True) / total for v in pos]
    diag = lax.broadcasted_iota(I32, (NB, PL), 0) == (lane & 63)
    ctr = [jnp.sum(jnp.where(diag, v, 0.0), axis=0, keepdims=True) for v in centre]
    wide = jnp.concatenate([list_ref[...], jnp.zeros((LC, PL - NB), I32)], axis=1)
    twice = wide + pltpu.roll(wide, 64, 1)
    half = lax.broadcasted_iota(I32, (1, PL), 1) < 64
    ids = [jnp.where(half, twice[2 * j : 2 * j + 1], twice[2 * j + 1 : 2 * j + 2]) for j in range(LC // 2)]
    ids = jnp.concatenate(ids, axis=0)
    slab = ids >> 11
    dx = ((slab >> 1) - xs) & (NX - 1)
    order = jnp.where(dx == 3, 1, jnp.where(dx == 0, 0, dx + 1))
    rows = (order * 2 + ((slab & 1) ^ cs)) * 16 + ((ids >> 7) & 15)
    lanes = ids & (PL - 1)
    tables = []
    for c in range(4):
        whole = jnp.concatenate([ref[i, :, c, :] for ref in (c0, c1, c2, c3) for i in range(2)], axis=0)
        whole = whole.T
        high = whole.astype(BF16)
        low = (whole - high.astype(F32)).astype(BF16)
        tables.append(jnp.concatenate([high, low], axis=1))
    tables = jnp.concatenate(tables, axis=0)
    sub = lax.broadcasted_iota(I32, (PL, 2 * PL), 0)
    got = [[] for _ in range(4)]
    for j in range(0, LC // 2, 2):
        r2 = jnp.concatenate([rows[j : j + 1], rows[j + 1 : j + 2]], axis=1)
        l2 = jnp.concatenate([lanes[j : j + 1], lanes[j + 1 : j + 2]], axis=1)
        hot = jnp.where(sub == r2, 1.0, 0.0).astype(BF16)
        hot = jnp.concatenate([hot, hot], axis=0)
        found = jnp.dot(tables, hot, preferred_element_type=F32)
        pick = sub == l2
        for c in range(4):
            value = jnp.sum(jnp.where(pick, found[c * PL : (c + 1) * PL], 0.0), axis=0, keepdims=True)
            got[c] += [value[:, :PL], value[:, PL:]]
    cells = [jnp.concatenate(v, axis=0) for v in got]
    rel = [ctr[c] - cells[c] for c in range(3)]
    dist = rel[0] * rel[0] + rel[1] * rel[1] + rel[2] * rel[2] + 1.0
    inv = lax.rsqrt(dist)
    cube = cells[3] * (inv * inv * inv)
    fifth = 3.0 * cube * (inv * inv)
    terms = [-(cube * rel[c]) for c in range(3)]
    for a, b in ((0, 0), (1, 1), (2, 2), (0, 1), (0, 2), (1, 2)):
        value = fifth * rel[a] * rel[b]
        if a == b:
            value = value - cube
        terms.append(value)
    terms = [jnp.sum(v, axis=0, keepdims=True) for v in terms]
    pad[...] = jnp.zeros((PL, PL), F32)
    for i, v in enumerate(terms):
        pad[i : i + 1, :] = v + pltpu.roll(v, 64, 1)
    back = pad[...].T
    field = [back[0:NB, i : i + 1] for i in range(3)]
    tide = [back[0:NB, 3 + i : 4 + i] for i in range(6)]
    offset = [pos[c] - centre[c] for c in range(3)]
    for c, (i, j, k) in enumerate(((0, 3, 4), (3, 1, 5), (4, 5, 2))):
        out_ref[c] = field[c] + tide[i] * offset[0] + tide[j] * offset[1] + tide[k] * offset[2]


def split3(v):
    high = v.astype(BF16).astype(F32)
    rest = v - high
    mid = rest.astype(BF16).astype(F32)
    return high, mid, rest - mid


def prep_kernel(y_ref, t0, t1, t2, t3, tall, tab):
    me = y_ref[0]
    wide = 2 * PL
    tiles = []
    for i, t in enumerate((t0, t1, t2, t3)):
        tall[i * NB : (i + 1) * NB] = t[0:NB]
        tiles.append(t[NB])
    left = lax.broadcasted_iota(I32, (4, PL), 1) < 64
    code, cnt = [], []
    for a, b in ((tiles[0], tiles[1]), (tiles[2], tiles[3])):
        code.append(jnp.where(left, a, pltpu.roll(b, 64, 1)))
        cnt.append(jnp.where(left, pltpu.roll(a, 64, 1), b))
    code = jnp.concatenate(code, axis=1).astype(I32)
    cnt = jnp.concatenate(cnt, axis=1)[0:1]
    lane = lax.broadcasted_iota(I32, (1, wide), 1)
    valid = (lane & 63) < NB
    flag = [jnp.where(((code[k : k + 1] >> 9) == me) & valid, 1.0, 0.0) for k in range(K)]
    local = [(code[k : k + 1] & 511).astype(F32) for k in range(K)]
    count = (flag[0] + flag[1]) + (flag[2] + flag[3])
    full = jnp.where(count > 2.5, 1.0, 0.0)
    half = jnp.where((count > 0.5) & (count < 2.5), 1.0, 0.0)
    group = lane >> 6
    mine = group == 0
    lists = [jnp.where(m, v, 0.0) for v in (full, half) for m in (~mine, mine)]
    marks = jnp.concatenate(lists + [jnp.zeros((12, wide), F32)], axis=0).astype(BF16)
    a = lax.broadcasted_iota(I32, (wide, wide), 0)
    b = lax.broadcasted_iota(I32, (wide, wide), 1)
    before = jnp.dot(marks, jnp.where(a < b, 1.0, 0.0).astype(BF16), preferred_element_type=F32)
    sizes = [jnp.sum(v, axis=1, keepdims=True) for v in lists]
    place, begin = jnp.full((1, wide), -1.0, F32), jnp.zeros((1, 1), F32)
    for i, v in enumerate(lists):
        place = jnp.where(v > 0.5, begin + before[i : i + 1], place)
        begin = begin + sizes[i]
    moved = jnp.where(a == place.astype(I32), 1.0, 0.0).astype(BF16)
    bucket = lane & 63
    home = ((group - 1) & (NY - 1)) * NB + bucket
    slot, ins, outs = [], jnp.zeros((1, wide), F32), jnp.zeros((1, wide), F32)
    for k in range(K):
        slot.append(jnp.where(flag[k] > 0.5, ins, count + outs))
        ins, outs = ins + flag[k], outs + (1.0 - flag[k])
    fields = []
    for j in range(K):
        pick = jnp.zeros((1, wide), F32)
        for k in range(K):
            pick = pick + jnp.where(slot[k] == float(j), local[k], 0.0)
        fields.append(pick)
    fields += [cnt, home.astype(F32), count, (group * NB + bucket).astype(F32)]
    load = jnp.concatenate(fields, axis=0)
    high = load.astype(BF16).astype(F32)
    both = jnp.concatenate([high, load - high], axis=0).astype(BF16)
    out = lax.dot_general(both, moved, (((1,), (1,)), ((), ())), preferred_element_type=F32)
    out = out[0:8] + out[8:16]
    sizes = jnp.concatenate([jnp.broadcast_to(v, (1, wide)) for v in sizes + [begin] * 4], axis=0)
    tab[...] = jnp.concatenate([out, sizes], axis=0).astype(I32)


def near_kernel(first, *refs):
    (table, tall, src_ref), refs = refs[:3], refs[3:]
    outs, (out_ref, hold, spots, tab, sem) = refs[:-5], refs[-5:]
    if not first:
        kept, outs = outs[0], outs[1:]
    copies = [pltpu.make_async_copy(table, tab, sem.at[0]), pltpu.make_async_copy(hold, spots, sem.at[1])]
    copies[0].start()
    for z in range(NZ):
        hold[z : z + 1, :] = src_ref[z * (TILES + 1) + TILES][0:1].astype(I32)
    copies[1].start()
    out_ref[...] = jnp.zeros(out_ref.shape, F32) if first else kept[...]
    for copy in copies:
        copy.wait()
    lane1 = lax.broadcasted_iota(I32, (1, PL), 1)
    sub4 = lax.broadcasted_iota(I32, (4, PL), 0)
    lane4 = lax.broadcasted_iota(I32, (4, PL), 1)
    spatial = sub4 < 3
    one = jnp.ones((4, PL), F32)
    zero4 = jnp.zeros((4, PL), F32)
    zero8 = jnp.zeros((8, PL), F32)

    def square(v):
        return jnp.sum(jnp.where(spatial, v * v, 0.0), axis=0, keepdims=True)

    def mix(a, b):
        return jnp.where(spatial, a, b)

    def stack(*v):
        return jnp.concatenate(v, axis=0).astype(BF16)

    row_base = 0 if first else (NY - 1) * NB

    def job(e, width):
        n = tab[6, e]
        t = tall[tab[7, e]]
        th, tm, tl = split3(t)
        qh, qm, ql = split3(square(t))
        u = stack(mix(th, one), mix(th, one), mix(tm, one), mix(tm, qh), mix(th, qm), mix(tl, ql), zero8)
        vs, gs = [], []
        for k in range(width):
            z, bucket = tab[k, e] >> 6, tab[k, e] & 63
            begin = spots[z, bucket]
            shift = begin & (PL - 1)
            tile = z * (TILES + 1) + (begin >> 7)
            s = jnp.concatenate([src_ref[tile], src_ref[tile + 1]], axis=0)
            s = pltpu.roll(s, (PL - shift) & (PL - 1), 1)
            s = jnp.where(lane4 < PL - shift, s[0:4], s[4:8])
            live = jnp.where(k < n, spots[z, 64 + bucket], 0)
            sh, sm, sl = split3(-2.0 * s)
            qh, qm, ql = split3(square(s) + SOFT)
            vs.append(stack(mix(sh, qh), mix(sm, qm), mix(sh, ql), mix(sm, one), mix(sl, one), mix(sh, one), zero8))
            w = jnp.where(lane1 < live, s[3:4], 0.0)
            gs.append(stack(*split3(mix(s * w, w)), zero4))
        v = jnp.concatenate(vs, axis=1)
        g = jnp.concatenate(gs, axis=1)
        dist = lax.dot_general(v, u, (((0,), (0,)), ((), ())), preferred_element_type=F32)
        inv = lax.rsqrt(dist)
        f = inv * inv * inv
        high = f.astype(BF16)
        low = (f - high.astype(F32)).astype(BF16)
        o = jnp.dot(g, jnp.concatenate([high, low], axis=1), preferred_element_type=F32)
        o = o[:, :PL] + o[:, PL:]
        a = o[0:4] + o[4:8] + o[8:12]
        out_ref[tab[5, e] - row_base] = jnp.where(lane4 < tab[4, e], a - t * a[3:4], 0.0)

    sizes = [tab[8 + i, 0] for i in range(4)]

    def run(begin, size, width, step):
        def body(i, _):
            for j in range(step):
                job(begin + jnp.minimum(step * i + j, size - 1), width)

        lax.fori_loop(0, (size + step - 1) // step, body, None)

    def whole_steps(size, step):
        return (size + step - 1) // step * step

    n_full, n_half = sizes[0] + sizes[1], sizes[2] + sizes[3]
    early_full = jnp.minimum(n_full, whole_steps(sizes[0], UNROLL[0]))
    early_half = jnp.minimum(n_half, whole_steps(sizes[2], UNROLL[1]))
    if first:
        run(jnp.int32(0), early_full, 4, UNROLL[0])
        run(n_full, early_half, 2, UNROLL[1])
    else:
        run(early_full, n_full - early_full, 4, UNROLL_OWN[0])
        run(n_full + early_half, n_half - early_half, 2, UNROLL_OWN[1])
    if first:
        outs[-1][...] = out_ref[(NY - 1) * NB : NY * NB]
        outs = outs[:-1]
    for i, o in enumerate(outs):
        for c in range(3):
            o[c] = out_ref[i * NB : (i + 1) * NB, c, :]


def final_kernel(cnt_ref, far_ref, p0, p1, p2, p3, out_ref):
    live = lax.broadcasted_iota(I32, (NB, PL), 1) < column_of(cnt_ref[...], NB)
    for c in range(3):
        near = (p0[c] + p1[c]) + (p2[c] + p3[c])
        out_ref[c] = jnp.where(live, far_ref[c] + near, 0.0)


def along_y(k):
    return [(NZ * y + z, NZ * ((y + k) % NY) + z) for y in range(NY) for z in range(NZ)]


def along_x(k):
    return [(2 * x + c, 2 * ((x + k) % NX) + c) for x in range(NX) for c in range(2)]


def call(kernel, outs, in_specs, out_specs, name, mib, scratch=()):
    return pl.pallas_call(
        kernel,
        out_shape=[jax.ShapeDtypeStruct(shape, dtype) for shape, dtype in outs],
        in_specs=in_specs,
        out_specs=out_specs,
        scratch_shapes=scratch,
        compiler_params=pltpu.CompilerParams(vmem_limit_bytes=mib * MIB),
        name=name,
    )


def per_device(positions, masses, counts, dest_ids, near_list, cell_list, cell_centers, cell_mass):
    pos = jnp.transpose(positions[0], (1, 0, 2))
    cnt = counts[0]
    src, tgt, cells, pos, cnt, cell_ids = call(
        pack_kernel,
        (((NZ, TILES + 1, 4, PL), F32), ((NB + 1, 4, PL), F32), ((16, 4, PL), F32), ((3, NB, PL), F32), ((1, NB), I32), ((LC, NB), I32)),
        [pl.BlockSpec(memory_space=pltpu.HBM)] * 8,
        [vspec()] * 6,
        "pack",
        8,
        [
            pltpu.VMEM((NB, PL), F32),
            pltpu.VMEM((1, NB), I32),
            pltpu.VMEM((K, NB), I32),
            pltpu.VMEM((3, 2048), F32),
            pltpu.VMEM((1, 2048), F32),
            pltpu.SMEM((1, NB), I32),
            pltpu.VMEM((NB, 8, PL), F32),
            pltpu.SemaphoreType.DMA((9,)),
        ],
    )(
        *[
            pltpu.with_memory_space_constraint(v, pltpu.HBM)
            for v in (pos, masses[0], cnt, dest_ids, near_list[0].T, cell_centers, cell_mass[None], cell_list[0].T)
        ]
    )
    z_rows = [[NZ * y + NZ - 1 - z for z in range(NZ)] for y in range(NY)]
    window = lax.all_to_all(src, "space", 0, 0, axis_index_groups=z_rows, tiled=True)
    tgts = [tgt] + [lax.ppermute(tgt, "space", along_y(k)) for k in (1, -1)]
    tgts.append(lax.ppermute(tgts[1], "space", along_y(1)))
    pair = jnp.stack([cells, lax.ppermute(cells, "slab", [(i, i ^ 1) for i in range(2 * NX)])])
    pairs = [pair] + [lax.ppermute(pair, "slab", along_x(k)) for k in (1, -1)]
    pairs.append(lax.ppermute(pairs[1], "slab", along_x(1)))
    me = (lax.axis_index("space") // NZ).astype(I32).reshape(1)
    place = lax.axis_index("slab").astype(I32).reshape(1)
    tall, tab = call(
        prep_kernel,
        (((NY * NB, 4, PL), F32), ((16, 2 * PL), I32)),
        [sspec()] + [vspec()] * 4,
        [vspec(), vspec()],
        "prep",
        8,
    )(me, *tgts)
    (far,) = call(
        far_kernel,
        (((3, NB, PL), F32),),
        [sspec()] + [vspec()] * 7,
        [vspec()],
        "far",
        16,
        [pltpu.VMEM((PL, PL), F32)],
    )(place, pos, cnt, cell_ids, *pairs)
    tall, tab, far = lax.optimization_barrier((tall, tab, far))
    window = window.reshape(NZ * (TILES + 1), 4, PL)

    def near(first, *arrays):
        partial = ((3, NB, PL), F32)
        kept = ((NB, 4, PL), F32)
        outs = (partial,) * (NY - 1) + (kept,) if first else (partial,)
        return call(
            functools.partial(near_kernel, first),
            outs,
            [vspec()] * len(arrays),
            [vspec()] * len(outs),
            "near",
            32,
            [
                pltpu.VMEM(((NY if first else 1) * NB, 4, PL), F32),
                pltpu.VMEM((NZ, PL), I32),
                pltpu.SMEM((NZ, PL), I32),
                pltpu.SMEM((16, 2 * PL), I32),
                pltpu.SemaphoreType.DMA((2,)),
            ],
        )(*arrays)

    *sent, kept = near(True, tab, tall, window)
    back = [lax.ppermute(sent[i], "space", along_y(-k)) for i, k in ((2, 2), (0, 1), (1, -1))]
    (own,) = near(False, tab, tall, window, kept)
    (out,) = call(
        final_kernel,
        (((3, NB, PL), F32),),
        [vspec()] * 6,
        [vspec()],
        "final",
        8,
    )(cnt, far, own, *back)
    return jnp.transpose(out, (1, 0, 2))[None]


def solution(mesh):
    in_specs = (
        P("slab", "space", None, None),
        P("slab", "space", None),
        P("slab", "space", None),
        P("slab", "space"),
        P("slab", "space", None),
        P("slab", "space", None),
        P(None, "slab"),
        P("slab"),
    )
    return jax.shard_map(
        per_device,
        mesh=mesh,
        in_specs=in_specs,
        out_specs=P("slab", "space", None, None),
        check_vma=False,
    )
```
